32 devices in a mesh: replica: 8 (over y, x, core), tensor: 4 (over z).
Axes of the slice: x: 2, y: 2, z: 4, core: 2. Of those that a mesh axis runs over, the one named last changes fastest.
Arguments:
- x_in: bfloat16 [4096, 4096], P('replica', 'tensor'), may hold values from -6 to 6
- gate_z: bfloat16 [4096, 4096], P('replica', 'tensor'), may hold values from -6 to 6
- b_proj: bfloat16 [4096, 1024], P('replica', 'tensor'), may hold values from -2 to 2
- c_proj: bfloat16 [4096, 1024], P('replica', 'tensor'), may hold values from -2 to 2
- dt_raw: float32 [4096, 64], P('replica', 'tensor'), may hold values from -5 to 5
- a_log: float32 [64], P('tensor'), may hold values from 0 to 2.77
- dt_bias: float32 [64], P('tensor'), may hold values from -6 to -2
- skip_d: float32 [64], P('tensor'), may hold values from 0.5 to 1.5
- norm_gain: float32 [4096], P('tensor'), may hold values from 0.5 to 1.5
- out_weight: bfloat16 [8, 2048, 4096], P('replica', None, 'tensor'), may hold values from -0.125 to 0.125
- global_weight: float32 [2048, 4096], P('replica', 'tensor'), may hold values from -0.09375 to 0.09375
- momentum: float32 [2048, 4096], P('replica', 'tensor'), may hold values from -0.04 to 0.04
- target: bfloat16 [4096, 2048], P(('replica', 'tensor')), may hold values from -6 to 6
Outputs:
- grad_x: bfloat16 [4096, 4096], P('replica', 'tensor')
- new_weight: bfloat16 [2048, 4096], P(None, 'tensor')
- new_global: float32 [2048, 4096], P('replica', 'tensor')
- new_momentum: float32 [2048, 4096], P('replica', 'tensor')
The draws below stay inside these ranges and needn't reach their ends.
All inputs are finite; a program needn't handle non-finite values.
Results may differ from the reference program's by a relative error of at most 0.0085.
Values may be sent and summed in bfloat16 or wider, within the bound.
No kernel may reach another device: no remote copies, remote signals or barrier semaphores. Data moves between devices by JAX's collectives and lax.ppermute only.
A program may use at most 128 MiB of HBM per device.

```python
import jax
import jax.numpy as jnp
from jax import lax

D = 2048
HEADS = 64
HEAD_DIM = 64
STATE = 128
GROUPS = 8
SPAN = 256
TOK = 512
INNER = 4096
REPLICAS = 8


def strengthened(drawn, stream_key, source, target, blocks, factor):
    def block_of(position):
        return (jnp.arange(drawn.shape[position]) // (drawn.shape[position] // blocks)).reshape((-1,) + (1,) * (drawn.ndim - 1 - position))

    one_side = jax.random.permutation(stream_key, blocks)[block_of(target)]
    second = (block_of(target) + blocks // 2) % blocks
    return jnp.where((block_of(source) == one_side) | (block_of(source) == second), factor * drawn, drawn)


def block_scale(own_key, shape, cuts, least, largest):
    loudness = 1.0
    for axis_at, shards_of in cuts:
        steps = jax.random.uniform(jax.random.fold_in(jax.random.fold_in(own_key, 6), axis_at), (shards_of,), jnp.float32, least / len(cuts), largest / len(cuts))
        loudness = loudness * jnp.repeat(jnp.exp(steps), shape[axis_at] // shards_of).reshape((-1,) + (1,) * (len(shape) - 1 - axis_at))
    return loudness


def scatter_about(stream_key, extent, deviation, most, cuts=(), held_as=jnp.bfloat16):
    values = jax.random.normal(stream_key, extent, jnp.float32) * deviation
    if len(cuts) > 0:
        values = block_scale(stream_key, extent, cuts, -0.22, 0.18) * values
    return jnp.clip(values, min=-most, max=most).astype(held_as)


def bell_draw_with(rng, extent, scale, reach, split, heavy, kind=jnp.bfloat16):
    drawn = scale * jax.random.normal(rng, extent, jnp.float32)
    if split:
        drawn = drawn * block_scale(rng, extent, split, -0.22, 0.18)
    return jnp.clip(strengthened(drawn, jax.random.fold_in(rng, 3), *heavy), -reach, reach).astype(kind)


def setup_inputs(seed: int = 0) -> dict:
    seeds = jax.random.split(jax.random.key(seed), 14)
    return {
        "x_in": scatter_about(seeds[0], (REPLICAS * TOK, INNER), 1.0, 6.0, ((0, 8), (1, 4))),
        "gate_z": scatter_about(seeds[1], (REPLICAS * TOK, INNER), 1.0, 6.0, ((0, 8), (1, 4))),
        "b_proj": scatter_about(seeds[2], (REPLICAS * TOK, GROUPS * STATE), 0.3, 2.0, ((0, 8), (1, 4))),
        "c_proj": scatter_about(seeds[3], (REPLICAS * TOK, GROUPS * STATE), 0.3, 2.0, ((0, 8), (1, 4))),
        "dt_raw": scatter_about(seeds[4], (REPLICAS * TOK, HEADS), 1.0, 5.0, ((0, 8), (1, 4)), jnp.float32),
        "a_log": jnp.clip(2.77 * jax.random.uniform(seeds[5], (HEADS,), jnp.float32) ** block_scale(seeds[5], (HEADS,), ((0, 4),), -0.2, 0.2), 0.0, 2.77),
        "dt_bias": jnp.clip(-6.0 + 4.0 * jax.random.uniform(seeds[6], (HEADS,), jnp.float32) ** block_scale(seeds[6], (HEADS,), ((0, 4),), -0.2, 0.2), -6.0, -2.0),
        "skip_d": jnp.clip(0.5 + 1.0 * jax.random.uniform(seeds[7], (HEADS,), jnp.float32) ** block_scale(seeds[7], (HEADS,), ((0, 4),), -0.2, 0.2), 0.5, 1.5),
        "norm_gain": jnp.clip(1.0 + 0.1 * jax.random.normal(seeds[8], (INNER,), jnp.float32), 0.5, 1.5),
        "out_weight": bell_draw_with(seeds[9], (REPLICAS, D, INNER), INNER ** -0.5, 0.125, ((0, 8), (2, 4)), (0, 1, 8, 2.0)),
        "global_weight": scatter_about(seeds[10], (D, INNER), INNER ** -0.5, 0.09375, ((0, 8), (1, 4)), jnp.float32),
        "momentum": scatter_about(seeds[11], (D, INNER), 0.005, 0.04, ((0, 8), (1, 4)), jnp.float32),
        "target": scatter_about(seeds[12], (REPLICAS * TOK, D), 1.0, 6.0, ((0, 32),)),
    }


inner_rate = 0.001
outer_rate = 0.7
outer_beta = 0.9
clip_rms = 0.005

def gated_ssd(inputs_f, gate_z, b_proj, c_proj, dt_raw, a_log, dt_bias, skip_d, norm_gain):
    tokens = inputs_f.shape[0]
    head_count = a_log.shape[0]
    group_count = b_proj.shape[1] // STATE
    per_group = head_count // group_count
    block_count = tokens // SPAN
    values = inputs_f.reshape(block_count, SPAN, group_count, per_group, HEAD_DIM)
    step_size = jax.nn.softplus(dt_raw.astype(jnp.float32) + dt_bias).reshape(block_count, SPAN, group_count, per_group)
    log_decay = (-jnp.exp(a_log)).reshape(group_count, per_group) * step_size
    cum_decay = jnp.cumsum(log_decay, axis=1)
    key_proj = b_proj.astype(jnp.float32).reshape(block_count, SPAN, group_count, STATE)
    query_proj = c_proj.astype(jnp.float32).reshape(block_count, SPAN, group_count, STATE)
    scores = jnp.einsum('clgn,csgn->cgls', query_proj, key_proj)
    cumulative = cum_decay.transpose(0, 2, 3, 1)
    gap_decay = cumulative[..., :, None] - cumulative[..., None, :]
    causal_mask = jnp.tril(jnp.ones((SPAN, SPAN), dtype=bool))
    decay_table = jnp.where(causal_mask, jnp.exp(jnp.where(causal_mask, gap_decay, 0.0)), 0.0)
    weights = scores[:, :, None] * decay_table * step_size.transpose(0, 2, 3, 1)[..., None, :]
    inside = jnp.einsum('cgrls,csgrp->clgrp', weights, values)
    tail_weight = jnp.exp(cum_decay[:, -1:] - cum_decay) * step_size
    states = jnp.einsum('csgn,csgr,csgrp->cgrpn', key_proj, tail_weight, values)
    span_fade = jnp.exp(cum_decay[:, -1])

    def carry_state(carried, inputs_pair):
        fade_now, state_now = inputs_pair
        return (fade_now[..., None, None] * carried + state_now, carried)
    _, entering = lax.scan(carry_state, jnp.zeros(states.shape[1:], jnp.float32), (span_fade, states))
    outside = jnp.einsum('clgn,cgrpn->clgrp', query_proj, entering) * jnp.exp(cum_decay)[..., None]
    ssd_out = inside + outside + skip_d.reshape(group_count, per_group)[..., None] * values
    width = per_group * HEAD_DIM
    gated_vals = ssd_out.reshape(tokens, group_count, width) * jax.nn.silu(gate_z.astype(jnp.float32)).reshape(tokens, group_count, width)
    inv_norm = lax.rsqrt(lax.optimization_barrier(jnp.mean(gated_vals * gated_vals, axis=-1, keepdims=True)) + 1e-05)
    return (gated_vals * inv_norm).reshape(tokens, head_count * HEAD_DIM) * norm_gain

def reference(x_in, gate_z, b_proj, c_proj, dt_raw, a_log, dt_bias, skip_d, norm_gain, out_weight, global_weight, momentum, target):
    replicas = out_weight.shape[0]
    width = x_in.shape[1]

    def per_replica(total_sum, pieces):
        x_rep, z_rep, b_rep, c_rep, dt_rep, w_rep, t_rep = pieces

        def forward(inputs_f):
            return gated_ssd(inputs_f, z_rep, b_rep, c_rep, dt_rep, a_log, dt_bias, skip_d, norm_gain)
        normed_f, pull_back = jax.vjp(forward, x_rep.astype(jnp.float32))
        normed = normed_f.astype(jnp.bfloat16)
        layer_out = lax.dot_general(normed, w_rep, (((1,), (1,)), ((), ())), preferred_element_type=jnp.float32)
        cotangent = (layer_out - t_rep.astype(jnp.float32)).astype(jnp.bfloat16)
        d_normed = jnp.dot(cotangent, w_rep, preferred_element_type=jnp.float32)
        weight_grad = lax.dot_general(cotangent, normed, (((0,), (0,)), ((), ())), preferred_element_type=jnp.float32)
        local_new = w_rep.astype(jnp.float32) - inner_rate * weight_grad
        grad_input = pull_back(d_normed)[0].astype(jnp.bfloat16)
        return (total_sum + local_new, grad_input)
    pieces = (x_in.reshape(replicas, TOK, width), gate_z.reshape(replicas, TOK, width), b_proj.reshape(replicas, TOK, -1), c_proj.reshape(replicas, TOK, -1), dt_raw.reshape(replicas, TOK, -1), out_weight, target.reshape(replicas, TOK, -1))
    total_sum, grads = lax.scan(per_replica, jnp.zeros(out_weight.shape[1:], jnp.float32), pieces)
    grad_x = grads.reshape(replicas * TOK, width)
    delta = global_weight - total_sum / replicas
    factor = jnp.minimum(1.0, clip_rms / jnp.sqrt(jnp.mean(delta * delta) + 1e-06))
    clipped = factor * delta
    new_momentum = outer_beta * momentum + clipped
    new_global = global_weight - outer_rate * (clipped + outer_beta * new_momentum)
    return (grad_x, new_global.astype(jnp.bfloat16), new_global, new_momentum)
```

```python
import functools

import jax
import jax.numpy as jnp
from jax import lax
from jax.experimental import pallas as pl
from jax.experimental.pallas import tpu as pltpu
from jax.sharding import PartitionSpec as P

HEAD_DIM = 64
STATE = 128
SPAN = 256
HALF = SPAN // 2

inner_rate = 0.001
outer_rate = 0.7
outer_beta = 0.9
clip_rms = 0.005
LOG2E = 1.4426950408889634

F32 = jnp.float32
BF16 = jnp.bfloat16
NN = (((1,), (0,)), ((), ()))
NT = (((1,), (1,)), ((), ()))
TN = (((0,), (0,)), ((), ()))


def exact_dot(a, b, dims):
    return lax.dot_general(a, b, dims, precision=lax.Precision.HIGHEST, preferred_element_type=F32)


def fast_dot(a, b, dims):
    return lax.dot_general(a, b, dims, preferred_element_type=F32)


def silu(z):
    return z * (1.0 / (1.0 + jnp.exp(-z)))


def softplus(v):
    return jnp.maximum(v, 0.0) + jnp.log1p(jnp.exp(-jnp.abs(v)))


def head_tables(dt_ref, a_ref, bias_ref, per_group):
    first = pl.program_id(0) * per_group
    tokens, heads = dt_ref.shape
    pick = lax.broadcasted_iota(jnp.int32, (per_group, heads), 1) == (
        lax.broadcasted_iota(jnp.int32, (per_group, heads), 0) + first
    )
    dt = exact_dot(pick.astype(F32), dt_ref[...], NT)
    row = lax.broadcasted_iota(jnp.int32, (per_group, tokens), 0)
    bias = jnp.zeros((per_group, tokens), F32)
    a_log = jnp.zeros((per_group, tokens), F32)
    for h in range(per_group):
        bias = jnp.where(row == h, bias_ref[first + h], bias)
        a_log = jnp.where(row == h, a_ref[first + h], a_log)
    step = softplus(dt + bias)
    return step, -jnp.exp(a_log) * step * LOG2E


def span_tables(step, rate, lo, per_group, width):
    s_at = lax.broadcasted_iota(jnp.int32, (SPAN, SPAN), 0)
    t_at = lax.broadcasted_iota(jnp.int32, (SPAN, SPAN), 1)
    upper = (s_at <= t_at).astype(F32)
    step_k = step[:, lo : lo + SPAN]
    cum = exact_dot(rate[:, lo : lo + SPAN], upper, NN)
    cum_col = exact_dot((s_at == t_at).astype(F32), cum, NT)
    spread = (
        lax.broadcasted_iota(jnp.int32, (per_group, width), 1) // HEAD_DIM
        == lax.broadcasted_iota(jnp.int32, (per_group, width), 0)
    ).astype(F32)
    step_x = exact_dot(step_k, spread, TN)
    fade_x = exact_dot(jnp.exp2(cum), spread, TN)
    tail_x = exact_dot(jnp.exp2(cum[:, SPAN - 1 :] - cum) * step_k, spread, TN)
    return cum, cum_col, step_x, fade_x, tail_x


def forward_kernel(dt_ref, x_ref, z_ref, b_ref, c_ref, gain_ref, a_ref, bias_ref, skip_ref, normed_ref, inv_ref):
    tokens, width = x_ref.shape
    per_group = width // HEAD_DIM
    first = pl.program_id(0) * per_group
    step, rate = head_tables(dt_ref, a_ref, bias_ref, per_group)
    causal = lax.broadcasted_iota(jnp.int32, (HALF, HALF), 0) >= lax.broadcasted_iota(jnp.int32, (HALF, HALF), 1)
    spans = tokens // SPAN
    entering = None
    for k in range(spans):
        rows = slice(k * SPAN, (k + 1) * SPAN)
        cum, cum_col, step_x, fade_x, tail_x = span_tables(step, rate, k * SPAN, per_group, width)
        x = x_ref[rows, :].astype(F32)
        b, c = b_ref[rows, :], c_ref[rows, :]
        scores = fast_dot(c, b, NT)
        stepped = (x * step_x).astype(BF16)
        pieces = []
        for h in range(per_group):
            channels = slice(h * HEAD_DIM, (h + 1) * HEAD_DIM)
            col, line = cum_col[:, h : h + 1], cum[h : h + 1, :]
            top = jnp.exp2(jnp.where(causal, col[:HALF] - line[:, :HALF], -1e30)) * scores[:HALF, :HALF]
            left = jnp.exp2(col[HALF:] - line[:, :HALF]) * scores[HALF:, :HALF]
            low = jnp.exp2(jnp.where(causal, col[HALF:] - line[:, HALF:], -1e30)) * scores[HALF:, HALF:]
            bottom = jnp.concatenate([left, low], axis=1)
            value = stepped[:, channels]
            inside = jnp.concatenate(
                [fast_dot(top.astype(BF16), value[:HALF], NN), fast_dot(bottom.astype(BF16), value, NN)], axis=0
            )
            pieces.append(inside + skip_ref[first + h] * x[:, channels])
        ssd = jnp.concatenate(pieces, axis=1)
        if entering is not None:
            ssd = ssd + fast_dot(c, entering.astype(BF16), NN) * fade_x
        if k + 1 < spans:
            state = fast_dot(b, (x * tail_x).astype(BF16), TN)
            entering = state if entering is None else entering * fade_x[SPAN - 1 :, :] + state
        gated = ssd * silu(z_ref[rows, :].astype(F32))
        inv = lax.rsqrt(jnp.mean(gated * gated, axis=1, keepdims=True) + 1e-05)
        normed_ref[rows, :] = (gated * inv * gain_ref[...]).astype(BF16)
        inv_ref[0, rows, :] = inv


def backward_kernel(
    dt_ref, dn_ref, normed_ref, inv_ref, z_ref, b_ref, c_ref, gain_ref, a_ref, bias_ref, skip_ref, dx_ref
):
    tokens, width = dn_ref.shape
    per_group = width // HEAD_DIM
    first = pl.program_id(0) * per_group
    step, rate = head_tables(dt_ref, a_ref, bias_ref, per_group)
    causal = lax.broadcasted_iota(jnp.int32, (HALF, HALF), 1) >= lax.broadcasted_iota(jnp.int32, (HALF, HALF), 0)
    spans = tokens // SPAN
    d_state = None
    for k in reversed(range(spans)):
        rows = slice(k * SPAN, (k + 1) * SPAN)
        cum, cum_col, step_x, fade_x, tail_x = span_tables(step, rate, k * SPAN, per_group, width)
        dn = dn_ref[rows, :].astype(F32)
        gain = gain_ref[...]
        normed = normed_ref[rows, :].astype(F32)
        shared = jnp.mean(normed * dn, axis=1, keepdims=True)
        d_gated = inv_ref[0, rows, :] * (gain * dn - (normed / gain) * shared)
        d_ssd = d_gated * silu(z_ref[rows, :].astype(F32))
        d_low = d_ssd.astype(BF16)
        b, c = b_ref[rows, :], c_ref[rows, :]
        scores = fast_dot(b, c, NT)
        pieces = []
        skips = []
        for h in range(per_group):
            channels = slice(h * HEAD_DIM, (h + 1) * HEAD_DIM)
            col, line = cum_col[:, h : h + 1], cum[h : h + 1, :]
            high = jnp.exp2(jnp.where(causal, line[:, :HALF] - col[:HALF], -1e30)) * scores[:HALF, :HALF]
            right = jnp.exp2(line[:, HALF:] - col[:HALF]) * scores[:HALF, HALF:]
            low = jnp.exp2(jnp.where(causal, line[:, HALF:] - col[HALF:], -1e30)) * scores[HALF:, HALF:]
            top = jnp.concatenate([high, right], axis=1)
            value = d_low[:, channels]
            pieces.append(
                jnp.concatenate(
                    [fast_dot(top.astype(BF16), value, NN), fast_dot(low.astype(BF16), value[HALF:], NN)], axis=0
                )
            )
            skips.append(skip_ref[first + h] * d_ssd[:, channels])
        dx = jnp.concatenate(pieces, axis=1) * step_x + jnp.concatenate(skips, axis=1)
        if d_state is not None:
            dx = dx + fast_dot(b, d_state.astype(BF16), NN) * tail_x
        dx_ref[rows, :] = dx.astype(BF16)
        if k > 0:
            own = fast_dot(c, (d_ssd * fade_x).astype(BF16), TN)
            d_state = own if d_state is None else own + d_state * fade_x[SPAN - 1 :, :]


def group_call(kernel, dt_raw, wide, narrow, gain, scalars, outs, out_specs, cost):
    tokens, heads = dt_raw.shape
    groups = narrow[0].shape[1] // STATE
    width = heads * HEAD_DIM // groups
    wide_spec = pl.BlockSpec((tokens, width), lambda g: (0, g))
    state_spec = pl.BlockSpec((tokens, STATE), lambda g: (0, g))
    inv_spec = pl.BlockSpec((1, tokens, 1), lambda g: (g, 0, 0))
    whole = pl.BlockSpec((tokens, heads), lambda g: (0, 0))
    specs = [whole]
    specs += [inv_spec if v.ndim == 3 else wide_spec for v in wide]
    specs += [state_spec] * len(narrow)
    specs += [pl.BlockSpec((1, width), lambda g: (0, g))]
    specs += [pl.BlockSpec(memory_space=pltpu.SMEM)] * len(scalars)
    return pl.pallas_call(
        kernel,
        grid=(groups,),
        in_specs=specs,
        out_specs=[{"wide": wide_spec, "inv": inv_spec}[s] for s in out_specs],
        out_shape=outs,
        cost_estimate=cost,
        compiler_params=pltpu.CompilerParams(vmem_limit_bytes=48 * 1024 * 1024),
    )(dt_raw, *wide, *narrow, gain.reshape(1, -1), *scalars)


def shards(
    x_in,
    gate_z,
    b_proj,
    c_proj,
    dt_raw,
    a_log,
    dt_bias,
    skip_d,
    norm_gain,
    out_weight,
    global_weight,
    momentum,
    target,
):
    weight = out_weight[0]
    tokens, inner = x_in.shape
    groups = b_proj.shape[1] // STATE
    cost = pl.CostEstimate(flops=3 * tokens * inner * SPAN * 2, bytes_accessed=8 * tokens * inner, transcendentals=tokens * SPAN * 16)
    scalars = (a_log, dt_bias, skip_d)
    normed, inv = group_call(
        forward_kernel,
        dt_raw,
        [x_in, gate_z],
        [b_proj, c_proj],
        norm_gain,
        scalars,
        [jax.ShapeDtypeStruct((tokens, inner), BF16), jax.ShapeDtypeStruct((groups, tokens, 1), F32)],
        ["wide", "inv"],
        cost,
    )
    kept = global_weight - outer_rate * outer_beta * outer_beta * momentum
    kept_all = lax.all_gather(kept.astype(BF16), "replica", axis=0, tiled=True)

    layer_part = lax.psum_scatter(
        lax.dot_general(normed, weight, NT, preferred_element_type=F32).astype(BF16),
        "tensor",
        scatter_dimension=0,
        tiled=True,
    )
    cotangent_part = (layer_part.astype(F32) - target.astype(F32)).astype(BF16)
    cotangent = lax.all_gather(cotangent_part, "tensor", axis=0, tiled=True)
    weight_grad = lax.dot_general(cotangent, normed, TN, preferred_element_type=F32)
    local_new = (weight.astype(F32) - inner_rate * weight_grad).astype(BF16)
    summed = lax.psum_scatter(local_new, "replica", scatter_dimension=0, tiled=True)
    replicas = lax.axis_size("replica")
    delta = global_weight - summed.astype(F32) / replicas
    delta_all = lax.all_gather(delta.astype(BF16), "replica", axis=0, tiled=True)

    d_normed = lax.dot_general(cotangent, weight, NN, preferred_element_type=F32)
    (grad_input,) = group_call(
        backward_kernel,
        dt_raw,
        [d_normed, normed, inv, gate_z],
        [b_proj, c_proj],
        norm_gain,
        scalars,
        [jax.ShapeDtypeStruct((tokens, inner), BF16)],
        ["wide"],
        cost,
    )

    wide_delta = delta_all.astype(F32)
    own_sum = jnp.sum(wide_delta * wide_delta)
    sums = lax.all_gather(jnp.full((8, 128), own_sum, F32), "tensor", axis=0, tiled=False)
    square_sum = jnp.sum(sums[:, 0, 0])
    entry_count = delta_all.shape[0] * delta_all.shape[1] * lax.axis_size("tensor")
    factor = jnp.minimum(1.0, clip_rms / jnp.sqrt(square_sum / entry_count + 1e-06))
    clipped = factor * delta
    new_momentum = outer_beta * momentum + clipped
    new_global = global_weight - outer_rate * (clipped + outer_beta * new_momentum)
    new_weight = (kept_all.astype(F32) - (outer_rate * (1.0 + outer_beta)) * factor * wide_delta).astype(BF16)
    return (grad_input, new_weight, new_global, new_momentum)


def solution(mesh):
    placed = (
        P("replica", "tensor"),
        P("replica", "tensor"),
        P("replica", "tensor"),
        P("replica", "tensor"),
        P("replica", "tensor"),
        P("tensor"),
        P("tensor"),
        P("tensor"),
        P("tensor"),
        P("replica", None, "tensor"),
        P("replica", "tensor"),
        P("replica", "tensor"),
        P(("replica", "tensor"), None),
    )
    return jax.shard_map(
        shards,
        mesh=mesh,
        in_specs=placed,
        out_specs=(
            P("replica", "tensor"),
            P(None, "tensor"),
            P("replica", "tensor"),
            P("replica", "tensor"),
        ),
        check_vma=False,
    )
```

```python
import functools

import jax
import jax.numpy as jnp
from jax import lax
from jax.experimental import pallas as pl
from jax.experimental.pallas import tpu as pltpu
from jax.sharding import PartitionSpec as P

HEAD_DIM = 64
STATE = 128
SPAN = 256
HALF = SPAN // 2

inner_rate = 0.001
outer_rate = 0.7
outer_beta = 0.9
clip_rms = 0.005
LOG2E = 1.4426950408889634
DEPTH = 2

F32 = jnp.float32
BF16 = jnp.bfloat16
NN = (((1,), (0,)), ((), ()))
NT = (((1,), (1,)), ((), ()))
TN = (((0,), (0,)), ((), ()))


def exact_dot(a, b, dims):
    return lax.dot_general(a, b, dims, precision=lax.Precision.HIGHEST, preferred_element_type=F32)


def fast_dot(a, b, dims):
    return lax.dot_general(a, b, dims, preferred_element_type=F32)


def silu(z):
    return z * (1.0 / (1.0 + jnp.exp(-z)))


def softplus(v):
    return jnp.maximum(v, 0.0) + jnp.log1p(jnp.exp(-jnp.abs(v)))


def head_tables(dt_ref, a_ref, bias_ref, per_group):
    first = pl.program_id(0) * per_group
    tokens, heads = dt_ref.shape
    pick = lax.broadcasted_iota(jnp.int32, (per_group, heads), 1) == (
        lax.broadcasted_iota(jnp.int32, (per_group, heads), 0) + first
    )
    dt = exact_dot(pick.astype(F32), dt_ref[...], NT)
    row = lax.broadcasted_iota(jnp.int32, (per_group, tokens), 0)
    bias = jnp.zeros((per_group, tokens), F32)
    a_log = jnp.zeros((per_group, tokens), F32)
    for h in range(per_group):
        bias = jnp.where(row == h, bias_ref[first + h], bias)
        a_log = jnp.where(row == h, a_ref[first + h], a_log)
    step = softplus(dt + bias)
    return step, -jnp.exp(a_log) * step * LOG2E


def span_tables(step, rate, lo, per_group, width):
    s_at = lax.broadcasted_iota(jnp.int32, (SPAN, SPAN), 0)
    t_at = lax.broadcasted_iota(jnp.int32, (SPAN, SPAN), 1)
    upper = (s_at <= t_at).astype(F32)
    step_k = step[:, lo : lo + SPAN]
    cum = exact_dot(rate[:, lo : lo + SPAN], upper, NN)
    cum_col = exact_dot((s_at == t_at).astype(F32), cum, NT)
    spread = (
        lax.broadcasted_iota(jnp.int32, (per_group, width), 1) // HEAD_DIM
        == lax.broadcasted_iota(jnp.int32, (per_group, width), 0)
    ).astype(F32)
    step_x = exact_dot(step_k, spread, TN)
    fade_x = exact_dot(jnp.exp2(cum), spread, TN)
    tail_x = exact_dot(jnp.exp2(cum[:, SPAN - 1 :] - cum) * step_k, spread, TN)
    return cum, cum_col, step_x, fade_x, tail_x


def forward_kernel(
    place_ref, dt_ref, x_ref, z_ref, b_ref, c_ref, gain_ref, a_ref, bias_ref, skip_ref, weight_ref, target_ref,
    normed_ref, inv_ref, *part_refs_and_total
):
    *part_refs, total_ref = part_refs_and_total
    tokens, width = x_ref.shape
    per_group = width // HEAD_DIM
    first = pl.program_id(0) * per_group
    step, rate = head_tables(dt_ref, a_ref, bias_ref, per_group)
    causal = lax.broadcasted_iota(jnp.int32, (HALF, HALF), 0) >= lax.broadcasted_iota(jnp.int32, (HALF, HALF), 1)
    spans = tokens // SPAN
    entering = None
    for k in range(spans):
        rows = slice(k * SPAN, (k + 1) * SPAN)
        cum, cum_col, step_x, fade_x, tail_x = span_tables(step, rate, k * SPAN, per_group, width)
        x = x_ref[rows, :].astype(F32)
        b, c = b_ref[rows, :], c_ref[rows, :]
        scores = fast_dot(c, b, NT)
        stepped = (x * step_x).astype(BF16)
        pieces = []
        for h in range(per_group):
            channels = slice(h * HEAD_DIM, (h + 1) * HEAD_DIM)
            col, line = cum_col[:, h : h + 1], cum[h : h + 1, :]
            top = jnp.exp2(jnp.where(causal, col[:HALF] - line[:, :HALF], -1e30)) * scores[:HALF, :HALF]
            left = jnp.exp2(col[HALF:] - line[:, :HALF]) * scores[HALF:, :HALF]
            low = jnp.exp2(jnp.where(causal, col[HALF:] - line[:, HALF:], -1e30)) * scores[HALF:, HALF:]
            bottom = jnp.concatenate([left, low], axis=1)
            value = stepped[:, channels]
            inside = jnp.concatenate(
                [fast_dot(top.astype(BF16), value[:HALF], NN), fast_dot(bottom.astype(BF16), value, NN)], axis=0
            )
            pieces.append(inside + skip_ref[first + h] * x[:, channels])
        ssd = jnp.concatenate(pieces, axis=1)
        if entering is not None:
            ssd = ssd + fast_dot(c, entering.astype(BF16), NN) * fade_x
        if k + 1 < spans:
            state = fast_dot(b, (x * tail_x).astype(BF16), TN)
            entering = state if entering is None else entering * fade_x[SPAN - 1 :, :] + state
        gated = ssd * silu(z_ref[rows, :].astype(F32))
        inv = lax.rsqrt(jnp.mean(gated * gated, axis=1, keepdims=True) + 1e-05)
        normed_ref[rows, :] = (gated * inv * gain_ref[...]).astype(BF16)
        inv_ref[0, rows, :] = inv

    replicas, owned, _ = weight_ref.shape
    chunks = len(part_refs)
    piece = owned // chunks
    for n in range(chunks):
        weight = weight_ref[:, n * piece : (n + 1) * piece, :].reshape(replicas * piece, width)
        part = fast_dot(normed_ref[...], weight, NT)

        @pl.when(pl.program_id(0) == 0)
        def _():
            total_ref[n] = part

        @pl.when(pl.program_id(0) > 0)
        def _():
            total_ref[n] = total_ref[n] + part

        @pl.when(pl.program_id(0) == pl.num_programs(0) - 1)
        def _():
            held = target_ref.shape[0]
            own = pl.ds(pl.multiple_of(place_ref[0] * held, held), held)
            goal = jnp.concatenate(
                [target_ref[:, r * owned + n * piece : r * owned + (n + 1) * piece] for r in range(replicas)], axis=1
            )
            total_ref[n, own, :] = total_ref[n, own, :] - goal.astype(F32)
            part_refs[n][...] = total_ref[n].astype(BF16)


def gradient_kernel(place_ref, mid_ref, sent_ref, normed_ref, weight_ref, cot_ref, keep_ref, send_ref):
    middle = place_ref[1] == 1
    cot = jnp.where(middle, mid_ref[...], sent_ref[...])
    cot_ref[...] = cot
    replicas, piece, width = weight_ref.shape
    grad = fast_dot(cot, normed_ref[...], TN)
    new = weight_ref[...].reshape(replicas * piece, width).astype(F32) - inner_rate * grad
    new = new.astype(BF16).reshape(replicas // 2, 2, piece, width)
    odd = place_ref[2] == 1
    keep_ref[...] = jnp.where(odd, new[:, 1], new[:, 0])
    send_ref[...] = jnp.where(odd, new[:, 0], new[:, 1])


def backward_kernel(
    dt_ref, normed_ref, inv_ref, z_ref, b_ref, c_ref, gain_ref, a_ref, bias_ref, skip_ref, weight_ref, *refs
):
    *cot_refs, dx_ref, dn_ref = refs
    tokens, width = normed_ref.shape
    per_group = width // HEAD_DIM
    first = pl.program_id(0) * per_group
    replicas, owned, _ = weight_ref.shape
    piece = owned // len(cot_refs)
    d_normed = None
    for n, cot_ref in enumerate(cot_refs):
        weight = weight_ref[:, n * piece : (n + 1) * piece, :].reshape(replicas * piece, width)
        term = fast_dot(cot_ref[...], weight, NN)
        d_normed = term if d_normed is None else d_normed + term
    dn_ref[...] = d_normed
    step, rate = head_tables(dt_ref, a_ref, bias_ref, per_group)
    causal = lax.broadcasted_iota(jnp.int32, (HALF, HALF), 1) >= lax.broadcasted_iota(jnp.int32, (HALF, HALF), 0)
    spans = tokens // SPAN
    d_state = None
    for k in reversed(range(spans)):
        rows = slice(k * SPAN, (k + 1) * SPAN)
        cum, cum_col, step_x, fade_x, tail_x = span_tables(step, rate, k * SPAN, per_group, width)
        dn = dn_ref[rows, :]
        gain = gain_ref[...]
        normed = normed_ref[rows, :].astype(F32)
        shared = jnp.mean(normed * dn, axis=1, keepdims=True)
        d_gated = inv_ref[0, rows, :] * (gain * dn - (normed / gain) * shared)
        d_ssd = d_gated * silu(z_ref[rows, :].astype(F32))
        d_low = d_ssd.astype(BF16)
        b, c = b_ref[rows, :], c_ref[rows, :]
        scores = fast_dot(b, c, NT)
        pieces = []
        skips = []
        for h in range(per_group):
            channels = slice(h * HEAD_DIM, (h + 1) * HEAD_DIM)
            col, line = cum_col[:, h : h + 1], cum[h : h + 1, :]
            high = jnp.exp2(jnp.where(causal, line[:, :HALF] - col[:HALF], -1e30)) * scores[:HALF, :HALF]
            right = jnp.exp2(line[:, HALF:] - col[:HALF]) * scores[:HALF, HALF:]
            low = jnp.exp2(jnp.where(causal, line[:, HALF:] - col[HALF:], -1e30)) * scores[HALF:, HALF:]
            top = jnp.concatenate([high, right], axis=1)
            value = d_low[:, channels]
            pieces.append(
                jnp.concatenate(
                    [fast_dot(top.astype(BF16), value, NN), fast_dot(low.astype(BF16), value[HALF:], NN)], axis=0
                )
            )
            skips.append(skip_ref[first + h] * d_ssd[:, channels])
        dx = jnp.concatenate(pieces, axis=1) * step_x + jnp.concatenate(skips, axis=1)
        if d_state is not None:
            dx = dx + fast_dot(b, d_state.astype(BF16), NN) * tail_x
        dx_ref[rows, :] = dx.astype(BF16)
        if k > 0:
            own = fast_dot(c, (d_ssd * fade_x).astype(BF16), TN)
            d_state = own if d_state is None else own + d_state * fade_x[SPAN - 1 :, :]


def inward(axis_size):
    half = axis_size // 2
    hops = [[(s, s + 1), (axis_size - 1 - s, axis_size - 2 - s)] for s in range(half - 1)]
    return hops, [(half - 1, half), (half, half - 1)]


def add16(a, b):
    return (a.astype(F32) + b.astype(F32)).astype(BF16)


def after(value, *others):
    return lax.optimization_barrier((value, *others))[0]


def shards(
    x_in,
    gate_z,
    b_proj,
    c_proj,
    dt_raw,
    a_log,
    dt_bias,
    skip_d,
    norm_gain,
    out_weight,
    global_weight,
    momentum,
    target,
):
    tokens, inner = x_in.shape
    features = out_weight.shape[1]
    replicas = lax.axis_size("replica")
    heads_over = lax.axis_size("tensor")
    groups = b_proj.shape[1] // STATE
    heads = dt_raw.shape[1]
    width = inner // groups
    owned = features // replicas
    chunks = max(1, min(4, owned // 16))
    piece = owned // chunks
    span_rows = replicas * piece
    place = lax.axis_index("tensor")
    me = lax.axis_index("replica")
    in_middle = (place == heads_over // 2 - 1) | (place == heads_over // 2)
    places = jnp.stack([place, in_middle.astype(jnp.int32), lax.rem(me, 2)]).astype(jnp.int32)
    weight = out_weight[0].reshape(replicas, owned, inner)
    gain = norm_gain.reshape(1, inner)

    smem = pl.BlockSpec(memory_space=pltpu.SMEM)
    by_group = pl.BlockSpec((tokens, width), lambda g: (0, g))
    by_state = pl.BlockSpec((tokens, STATE), lambda g: (0, g))
    inv_spec = pl.BlockSpec((1, tokens, 1), lambda g: (g, 0, 0))
    all_heads = pl.BlockSpec((tokens, heads), lambda g: (0, 0))
    gain_spec = pl.BlockSpec((1, width), lambda g: (0, g))
    weight_spec = pl.BlockSpec((replicas, owned, width), lambda g: (0, 0, g))
    chunk_spec = pl.BlockSpec((tokens, span_rows), lambda g: (0, 0))
    params = pltpu.CompilerParams(vmem_limit_bytes=56 * 1024 * 1024)
    cost = pl.CostEstimate(
        flops=2 * tokens * inner * (features + 3 * SPAN),
        bytes_accessed=2 * inner * (features + 4 * tokens),
        transcendentals=tokens * SPAN * heads,
    )

    kept = global_weight - outer_rate * outer_beta * outer_beta * momentum
    kept_all = lax.all_gather(kept.astype(BF16), "replica", axis=0, tiled=True)

    normed, inv, *parts = pl.pallas_call(
        forward_kernel,
        grid=(groups,),
        in_specs=[smem, all_heads, by_group, by_group, by_state, by_state, gain_spec, smem, smem, smem, weight_spec,
                  pl.BlockSpec(target.shape, lambda g: (0, 0))],
        out_specs=[by_group, inv_spec] + [chunk_spec] * chunks,
        out_shape=[jax.ShapeDtypeStruct((tokens, inner), BF16), jax.ShapeDtypeStruct((groups, tokens, 1), F32)]
        + [jax.ShapeDtypeStruct((tokens, span_rows), BF16)] * chunks,
        scratch_shapes=[pltpu.VMEM((chunks, tokens, span_rows), F32)],
        cost_estimate=cost,
        compiler_params=params,
    )(places, dt_raw, x_in, gate_z, b_proj, c_proj, gain, a_log, dt_bias, skip_d, weight, target)

    in_hops, across = inward(heads_over)
    first_landed = []
    cots, deltas, gathered = [], [], []
    for n in range(chunks):
        held = parts[n]
        if n >= DEPTH:
            held = after(held, first_landed[n - DEPTH])
        for at, pairs in enumerate(in_hops):
            landed = lax.ppermute(held, "tensor", pairs)
            if at == 0:
                first_landed.append(landed)
            held = add16(held, landed)
        mid = add16(held, lax.ppermute(held, "tensor", across))
        out = mid
        for pairs in reversed(in_hops):
            back = lax.ppermute(out, "tensor", [(b, a) for a, b in pairs])
            out = jnp.where(in_middle, mid, back) if pairs is not in_hops[0] else back

        col_tile = min(inner, 512)
        cot, keep, send = pl.pallas_call(
            gradient_kernel,
            grid=(inner // col_tile,),
            in_specs=[smem, chunk_spec, chunk_spec, pl.BlockSpec((tokens, col_tile), lambda i: (0, i)),
                      pl.BlockSpec((replicas, piece, col_tile), lambda i, n=n: (0, n, i))],
            out_specs=[chunk_spec] + [pl.BlockSpec((replicas // 2, piece, col_tile), lambda i: (0, 0, i))] * 2,
            out_shape=[jax.ShapeDtypeStruct((tokens, span_rows), BF16)]
            + [jax.ShapeDtypeStruct((replicas // 2, piece, inner), BF16)] * 2,
            cost_estimate=pl.CostEstimate(
                flops=2 * tokens * span_rows * inner, bytes_accessed=2 * (tokens + 2 * span_rows) * inner, transcendentals=0
            ),
            compiler_params=params,
        )(places, mid, out, normed, weight)
        cots.append(cot)

        landed = [lax.ppermute(send, "replica", [(r, r ^ 1) for r in range(replicas)])]
        mine = [keep]
        bit = 1
        left = replicas // 2
        while left > 1:
            bits = 2 if left >= 4 else 1
            ways = 1 << bits
            my = lax.rem(lax.div(me, 1 << bit), ways)
            terms = [t.reshape(left // ways, ways, piece, inner) for t in mine + landed]

            def total(mask):
                at = lax.bitwise_xor(my, jnp.int32(mask))
                cut = [lax.dynamic_index_in_dim(t, at, 1, keepdims=False).astype(F32) for t in terms]
                return functools.reduce(jnp.add, cut).astype(BF16)

            landed = [
                lax.ppermute(total(mask), "replica", [(r, r ^ (mask << bit)) for r in range(replicas)])
                for mask in range(1, ways)
            ]
            mine = [total(0)]
            bit += bits
            left //= ways
        summed = functools.reduce(jnp.add, [t.reshape(piece, inner).astype(F32) for t in mine + landed])
        delta = global_weight[n * piece : (n + 1) * piece] - summed / replicas
        deltas.append(delta)
        gathered.append(lax.all_gather(delta.astype(BF16), "replica", axis=0, tiled=True))

    (grad_input,) = pl.pallas_call(
        backward_kernel,
        grid=(groups,),
        in_specs=[all_heads, by_group, inv_spec, by_group, by_state, by_state, gain_spec, smem, smem, smem, weight_spec]
        + [chunk_spec] * chunks,
        out_specs=[by_group],
        out_shape=[jax.ShapeDtypeStruct((tokens, inner), BF16)],
        scratch_shapes=[pltpu.VMEM((tokens, width), F32)],
        cost_estimate=cost,
        compiler_params=params,
    )(dt_raw, normed, inv, gate_z, b_proj, c_proj, gain, a_log, dt_bias, skip_d, weight, *cots)

    square_sum = functools.reduce(jnp.add, [jnp.sum(d * d) for d in deltas])
    spread = jnp.full((8, 128), square_sum, F32)
    for pairs in [[(r, r ^ (1 << bit)) for r in range(replicas)] for bit in range(replicas.bit_length() - 1)]:
        spread = spread + lax.ppermute(spread, "replica", pairs)
    for bit in range(heads_over.bit_length() - 1):
        spread = spread + lax.ppermute(spread, "tensor", [(t, t ^ (1 << bit)) for t in range(heads_over)])
    entry_count = features * inner * heads_over
    factor = jnp.minimum(1.0, clip_rms / jnp.sqrt(spread[0, 0] / entry_count + 1e-06))
    clipped = factor * jnp.concatenate(deltas, axis=0)
    new_momentum = outer_beta * momentum + clipped
    new_global = global_weight - outer_rate * (clipped + outer_beta * new_momentum)
    scale = (outer_rate * (1.0 + outer_beta)) * factor
    new_weight = pl.pallas_call(
        weight_kernel,
        grid=(replicas,),
        in_specs=[smem, pl.BlockSpec((owned, inner), lambda r: (r, 0))]
        + [pl.BlockSpec((piece, inner), lambda r: (r, 0))] * chunks,
        out_specs=pl.BlockSpec((owned, inner), lambda r: (r, 0)),
        out_shape=jax.ShapeDtypeStruct((features, inner), BF16),
        cost_estimate=pl.CostEstimate(flops=2 * features * inner, bytes_accessed=6 * features * inner, transcendentals=0),
        compiler_params=params,
    )(scale.reshape(1), kept_all, *gathered)
    return (grad_input, new_weight, new_global, new_momentum)


def weight_kernel(scale_ref, kept_ref, *refs):
    *delta_refs, new_ref = refs
    piece = delta_refs[0].shape[0]
    for n, delta_ref in enumerate(delta_refs):
        rows = slice(n * piece, (n + 1) * piece)
        new = kept_ref[rows, :].astype(F32) - scale_ref[0] * delta_ref[...].astype(F32)
        new_ref[rows, :] = new.astype(BF16)


def solution(mesh):
    placed = (
        P("replica", "tensor"),
        P("replica", "tensor"),
        P("replica", "tensor"),
        P("replica", "tensor"),
        P("replica", "tensor"),
        P("tensor"),
        P("tensor"),
        P("tensor"),
        P("tensor"),
        P("replica", None, "tensor"),
        P("replica", "tensor"),
        P("replica", "tensor"),
        P(("replica", "tensor"), None),
    )
    return jax.shard_map(
        shards,
        mesh=mesh,
        in_specs=placed,
        out_specs=(
            P("replica", "tensor"),
            P(None, "tensor"),
            P("replica", "tensor"),
            P("replica", "tensor"),
        ),
        check_vma=False,
    )
```

```python
import functools

import jax
import jax.numpy as jnp
from jax import lax
from jax.experimental import pallas as pl
from jax.experimental.pallas import tpu as pltpu
from jax.sharding import PartitionSpec as P

HEAD_DIM = 64
STATE = 128
SPAN = 256
HALF = SPAN // 2
LANES = 128

inner_rate = 0.001
outer_rate = 0.7
outer_beta = 0.9
clip_rms = 0.005
LOG2E = 1.4426950408889634
DEPTH = 2

F32 = jnp.float32
BF16 = jnp.bfloat16
NN = (((1,), (0,)), ((), ()))
NT = (((1,), (1,)), ((), ()))
TN = (((0,), (0,)), ((), ()))


def dot(a, b, dims):
    return lax.dot_general(a, b, dims, preferred_element_type=F32)


def silu(z):
    return z * (1.0 / (1.0 + jnp.exp(-z)))


def softplus(v):
    return jnp.maximum(v, 0.0) + jnp.log1p(jnp.exp(-jnp.abs(v)))


def iota(shape, axis):
    return lax.broadcasted_iota(jnp.int32, shape, axis)


def thirds(v):
    high = v.astype(BF16).astype(F32)
    middle = (v - high).astype(BF16).astype(F32)
    return jnp.concatenate([high, middle, v - high - middle], axis=0).astype(BF16)


def by_head(refs, first, per_group, tokens):
    row = iota((per_group, tokens), 0)
    rows = []
    for ref in refs:
        value = jnp.zeros((per_group, tokens), F32)
        for h in range(per_group):
            value = jnp.where(row == h, ref[first + h], value)
        rows.append(value)
    return rows


def head_tables(dt_ref, a_ref, bias_ref, per_group):
    first = pl.program_id(0) * per_group
    bias, a_log = by_head([bias_ref, a_ref], first, per_group, dt_ref.shape[1])
    step = softplus(dt_ref[...] + bias)
    return step, -jnp.exp(a_log) * step * LOG2E


def span_tables(step, rate, lo, per_group, width):
    upper = (iota((SPAN, SPAN), 0) <= iota((SPAN, SPAN), 1)).astype(BF16)
    step_k = step[:, lo : lo + SPAN]
    sums = dot(thirds(rate[:, lo : lo + SPAN]), upper, NN)
    cum = sums[:per_group] + sums[per_group : 2 * per_group] + sums[2 * per_group :]
    spread = (iota((3 * per_group, width), 1) // HEAD_DIM == iota((3 * per_group, width), 0) % per_group).astype(BF16)
    turn = (iota((3 * per_group, per_group), 1) == iota((3 * per_group, per_group), 0) % per_group).astype(BF16)
    cum_col = dot(thirds(cum), turn, TN)
    step_x = dot(thirds(step_k), spread, TN)
    fade_x = dot(thirds(jnp.exp2(cum)), spread, TN)
    tail_x = dot(thirds(jnp.exp2(cum[:, SPAN - 1 :] - cum) * step_k), spread, TN)
    return cum, cum_col, step_x, fade_x, tail_x


def skip_row(skip_ref, first, per_group, width):
    head = iota((1, width), 1) // HEAD_DIM
    row = jnp.zeros((1, width), F32)
    for h in range(per_group):
        row = jnp.where(head == h, skip_ref[first + h], row)
    return row


def decay(gap, mask=None):
    return jnp.exp2(gap if mask is None else jnp.where(mask, gap, -1e30))


def even_odd(v):
    first = iota(v.shape, 1) % (2 * HEAD_DIM) < HEAD_DIM
    return jnp.where(first, v, 0.0).astype(BF16), jnp.where(first, 0.0, v).astype(BF16)


def forward_kernel(dt_ref, x_ref, z_ref, b_ref, c_ref, gain_ref, a_ref, bias_ref, skip_ref, normed_ref, inv_ref):
    tokens, width = x_ref.shape
    per_group = width // HEAD_DIM
    step, rate = head_tables(dt_ref, a_ref, bias_ref, per_group)
    skip = skip_row(skip_ref, pl.program_id(0) * per_group, per_group, width)
    causal = iota((HALF, HALF), 0) >= iota((HALF, HALF), 1)
    spans = tokens // SPAN
    entering = None
    for k in range(spans):
        rows = slice(k * SPAN, (k + 1) * SPAN)
        cum, cum_col, step_x, fade_x, tail_x = span_tables(step, rate, k * SPAN, per_group, width)
        x = x_ref[rows, :].astype(F32)
        b, c = b_ref[rows, :], c_ref[rows, :]
        scores = dot(c, b, NT)
        values = even_odd(x * step_x)
        pieces = []
        for pair in range(per_group // 2):
            lanes = slice(2 * pair * HEAD_DIM, 2 * (pair + 1) * HEAD_DIM)
            tops, bottoms = [], []
            for h in (2 * pair, 2 * pair + 1):
                col, line = cum_col[:, h : h + 1], cum[h : h + 1, :]
                top = decay(col[:HALF] - line[:, :HALF], causal) * scores[:HALF, :HALF]
                left = decay(col[HALF:] - line[:, :HALF]) * scores[HALF:, :HALF]
                low = decay(col[HALF:] - line[:, HALF:], causal) * scores[HALF:, HALF:]
                tops.append(top.astype(BF16))
                bottoms += [left.astype(BF16), low.astype(BF16)]
            upper_values = jnp.concatenate([v[:HALF, lanes] for v in values], axis=0)
            all_values = jnp.concatenate([v[:, lanes] for v in values], axis=0)
            pieces.append(
                jnp.concatenate(
                    [
                        dot(jnp.concatenate(tops, axis=1), upper_values, NN),
                        dot(jnp.concatenate(bottoms, axis=1), all_values, NN),
                    ],
                    axis=0,
                )
            )
        ssd = jnp.concatenate(pieces, axis=1) + skip * x
        if entering is not None:
            ssd = ssd + dot(c, entering.astype(BF16), NN) * fade_x
        if k + 1 < spans:
            state = dot(b, (x * tail_x).astype(BF16), TN)
            entering = state if entering is None else entering * fade_x[SPAN - 1 :, :] + state
        gated = ssd * silu(z_ref[rows, :].astype(F32))
        inv = lax.rsqrt(jnp.mean(gated * gated, axis=1, keepdims=True) + 1e-05)
        normed_ref[rows, :] = (gated * inv * gain_ref[...]).astype(BF16)
        inv_ref[0, rows, :] = inv


def project_kernel(chunk, place_ref, weight_ref, normed_ref, target_ref, part_ref):
    owners, piece, inner = weight_ref.shape
    held, lanes = target_ref.shape
    owned = lanes // owners
    part = dot(weight_ref[...].reshape(owners * piece, inner), normed_ref[...], NT)
    goal = jnp.concatenate(
        [target_ref[:, o * owned + chunk * piece : o * owned + (chunk + 1) * piece] for o in range(owners)], axis=1
    )
    eye = (iota((held, held), 0) == iota((held, held), 1)).astype(BF16)
    turned = dot(goal, eye, TN)
    tiled = jnp.concatenate([turned] * (part.shape[1] // held), axis=1)
    part = part - jnp.where(iota(part.shape, 1) // held == place_ref[0], tiled, 0.0)
    part_ref[...] = part.astype(BF16)


def gradient_kernel(count, split, place_ref, *refs):
    cot_refs, (normed_ref, weight_ref), outs = refs[: 2 * count], refs[2 * count : 2 * count + 2], refs[2 * count + 2 :]
    middle = place_ref[1] == 1
    owners, rows, inner = weight_ref.shape
    piece = rows // count
    for n in range(count):
        cot = jnp.where(middle, cot_refs[2 * n][...], cot_refs[2 * n + 1][...])
        weight = weight_ref[:, n * piece : (n + 1) * piece, :].reshape(owners * piece, inner).astype(F32)
        new = (weight - inner_rate * dot(cot, normed_ref[...], NN)).astype(BF16).reshape(owners, piece, inner)
        at = slice(n * piece, (n + 1) * piece)
        if split:
            odd = place_ref[2] == 1
            outs[0][0, at, :] = jnp.where(odd, new[1], new[0])
            outs[1][0, at, :] = jnp.where(odd, new[0], new[1])
        else:
            outs[0][:, at, :] = new


def backward_kernel(
    place_ref, dt_ref, normed_ref, inv_ref, z_ref, b_ref, c_ref, gain_ref, a_ref, bias_ref, skip_ref, weight_ref, *refs
):
    *cot_refs, dx_ref, dn_ref = refs
    tokens, width = normed_ref.shape
    per_group = width // HEAD_DIM
    replicas, owned, _ = weight_ref.shape
    chunks = len(cot_refs) // 2
    piece = owned // chunks
    middle = place_ref[1] == 1
    for n in range(chunks):
        weight = weight_ref[:, n * piece : (n + 1) * piece, :].reshape(replicas * piece, width)
        term = dot(jnp.where(middle, cot_refs[2 * n][...], cot_refs[2 * n + 1][...]), weight, TN)
        dn_ref[...] = term if n == 0 else dn_ref[...] + term
    step, rate = head_tables(dt_ref, a_ref, bias_ref, per_group)
    skip = skip_row(skip_ref, pl.program_id(0) * per_group, per_group, width)
    causal = iota((HALF, HALF), 1) >= iota((HALF, HALF), 0)
    spans = tokens // SPAN
    d_state = None
    for k in reversed(range(spans)):
        rows = slice(k * SPAN, (k + 1) * SPAN)
        cum, cum_col, step_x, fade_x, tail_x = span_tables(step, rate, k * SPAN, per_group, width)
        dn = dn_ref[rows, :]
        gain = gain_ref[...]
        normed = normed_ref[rows, :].astype(F32)
        shared = jnp.mean(normed * dn, axis=1, keepdims=True)
        d_gated = inv_ref[0, rows, :] * (gain * dn - (normed / gain) * shared)
        d_ssd = d_gated * silu(z_ref[rows, :].astype(F32))
        values = even_odd(d_ssd)
        b, c = b_ref[rows, :], c_ref[rows, :]
        scores = dot(b, c, NT)
        pieces = []
        for pair in range(per_group // 2):
            lanes = slice(2 * pair * HEAD_DIM, 2 * (pair + 1) * HEAD_DIM)
            tops, bottoms = [], []
            for h in (2 * pair, 2 * pair + 1):
                col, line = cum_col[:, h : h + 1], cum[h : h + 1, :]
                high = decay(line[:, :HALF] - col[:HALF], causal) * scores[:HALF, :HALF]
                right = decay(line[:, HALF:] - col[:HALF]) * scores[:HALF, HALF:]
                low = decay(line[:, HALF:] - col[HALF:], causal) * scores[HALF:, HALF:]
                tops += [high.astype(BF16), right.astype(BF16)]
                bottoms.append(low.astype(BF16))
            lower_values = jnp.concatenate([v[HALF:, lanes] for v in values], axis=0)
            all_values = jnp.concatenate([v[:, lanes] for v in values], axis=0)
            pieces.append(
                jnp.concatenate(
                    [
                        dot(jnp.concatenate(tops, axis=1), all_values, NN),
                        dot(jnp.concatenate(bottoms, axis=1), lower_values, NN),
                    ],
                    axis=0,
                )
            )
        dx = jnp.concatenate(pieces, axis=1) * step_x + skip * d_ssd
        if d_state is not None:
            dx = dx + dot(b, d_state.astype(BF16), NN) * tail_x
        dx_ref[rows, :] = dx.astype(BF16)
        if k > 0:
            own = dot(c, (d_ssd * fade_x).astype(BF16), TN)
            d_state = own if d_state is None else own + d_state * fade_x[SPAN - 1 :, :]


def weight_kernel(place_ref, scale_ref, kept_ref, whole_ref, *refs):
    *pair_refs, new_ref = refs
    mine = lax.rem(pl.program_id(0), 2) == place_ref[2]
    pieces = [whole_ref[...]]
    for own_ref, other_ref in zip(pair_refs[::2], pair_refs[1::2]):
        pieces.append(jnp.where(mine, own_ref[0], other_ref[0]))
    lo = 0
    for piece in pieces:
        rows = slice(lo, lo + piece.shape[0])
        lo += piece.shape[0]
        new_ref[rows, :] = (kept_ref[rows, :].astype(F32) - scale_ref[0] * piece.astype(F32)).astype(BF16)


def inward(axis_size):
    half = axis_size // 2
    hops = [[(s, s + 1), (axis_size - 1 - s, axis_size - 2 - s)] for s in range(half - 1)]
    return hops, [(half - 1, half), (half, half - 1)]


def add16(a, b):
    return (a.astype(F32) + b.astype(F32)).astype(BF16)


def after(value, *others):
    return lax.optimization_barrier((value, *others))[0]


def stages(replicas):
    bit, left, found = 1, replicas // 2, []
    while left > 1:
        bits = 2 if left >= 4 else 1
        found.append((bit, bits))
        bit, left = bit + bits, left >> bits
    return found


def reduce_rows(keep, send, replicas, me):
    _, piece, inner = keep.shape
    mine, landed = keep, [lax.ppermute(send, "replica", [(r, r ^ 1) for r in range(replicas)])]
    left = replicas // 2
    for bit, bits in stages(replicas):
        ways = 1 << bits
        my = lax.rem(lax.div(me, 1 << bit), ways)
        terms = [t.reshape(left // ways, ways, piece, inner) for t in [mine] + landed]

        def total(mask):
            at = lax.bitwise_xor(my, jnp.int32(mask))
            cut = [lax.dynamic_index_in_dim(t, at, 1, keepdims=False).astype(F32) for t in terms]
            return functools.reduce(jnp.add, cut).astype(BF16)

        landed = [
            lax.ppermute(total(mask), "replica", [(r, r ^ (mask << bit)) for r in range(replicas)])
            for mask in range(1, ways)
        ]
        mine = total(0)
        left //= ways
    return functools.reduce(jnp.add, [t.reshape(piece, inner).astype(F32) for t in [mine] + landed])


def gather_rows(rows, replicas):
    held = rows[None]
    for bit, bits in stages(replicas):
        parts = [held] + [
            lax.ppermute(held, "replica", [(r, r ^ (mask << bit)) for r in range(replicas)]) for mask in range(1, 1 << bits)
        ]
        held = jnp.concatenate(parts, axis=0)
    return held, lax.ppermute(held, "replica", [(r, r ^ 1) for r in range(replicas)])


def shards(
    x_in,
    gate_z,
    b_proj,
    c_proj,
    dt_raw,
    a_log,
    dt_bias,
    skip_d,
    norm_gain,
    out_weight,
    global_weight,
    momentum,
    target,
):
    tokens, inner = x_in.shape
    features = out_weight.shape[1]
    replicas = lax.axis_size("replica")
    heads_over = lax.axis_size("tensor")
    groups = b_proj.shape[1] // STATE
    heads = dt_raw.shape[1]
    width = inner // groups
    owned = features // replicas
    chunks = max(2, min(4, owned // 16))
    batches = [list(range(max(1, chunks - 2)))] + [[n] for n in range(max(1, chunks - 2), chunks)]
    piece = owned // chunks
    span_rows = replicas * piece
    place = lax.axis_index("tensor")
    me = lax.axis_index("replica")
    in_middle = (place == heads_over // 2 - 1) | (place == heads_over // 2)
    places = jnp.stack([place, in_middle.astype(jnp.int32), lax.rem(me, 2), lax.div(me, 2)]).astype(jnp.int32)
    weight = out_weight[0].reshape(replicas, owned, inner)
    gain = norm_gain.reshape(1, inner)
    dt_rows = dt_raw.T

    smem = pl.BlockSpec(memory_space=pltpu.SMEM)
    by_group = pl.BlockSpec((tokens, width), lambda g: (0, g))
    by_state = pl.BlockSpec((tokens, STATE), lambda g: (0, g))
    inv_spec = pl.BlockSpec((1, tokens, 1), lambda g: (g, 0, 0))
    dt_spec = pl.BlockSpec((heads // groups, tokens), lambda g: (g, 0))
    gain_spec = pl.BlockSpec((1, width), lambda g: (0, g))
    weight_spec = pl.BlockSpec((replicas, owned, width), lambda g: (0, 0, g))
    normed_spec = pl.BlockSpec((tokens, inner), lambda i: (0, 0))
    by_chip = pl.BlockSpec((2 * piece, tokens), lambda i: (i, 0))
    params = pltpu.CompilerParams(vmem_limit_bytes=56 * 1024 * 1024)
    cost = pl.CostEstimate(
        flops=2 * tokens * inner * 4 * SPAN, bytes_accessed=8 * inner * tokens, transcendentals=tokens * SPAN * heads
    )

    kept = global_weight - outer_rate * outer_beta * outer_beta * momentum
    kept_all = lax.all_gather(kept.astype(BF16), "replica", axis=0, tiled=True)

    normed, inv = pl.pallas_call(
        forward_kernel,
        grid=(groups,),
        in_specs=[dt_spec, by_group, by_group, by_state, by_state, gain_spec, smem, smem, smem],
        out_specs=[by_group, inv_spec],
        out_shape=[jax.ShapeDtypeStruct((tokens, inner), BF16), jax.ShapeDtypeStruct((groups, tokens, 1), F32)],
        cost_estimate=cost,
        compiler_params=params,
    )(dt_rows, x_in, gate_z, b_proj, c_proj, gain, a_log, dt_bias, skip_d)

    owners = min(replicas, max(2, LANES // owned))

    def project(n):
        return pl.pallas_call(
            functools.partial(project_kernel, n),
            grid=(replicas // owners,),
            in_specs=[
                smem,
                pl.BlockSpec((owners, piece, inner), lambda i: (i, n, 0)),
                normed_spec,
                pl.BlockSpec((target.shape[0], owners * owned), lambda i: (0, i)),
            ],
            out_specs=pl.BlockSpec((owners * piece, tokens), lambda i: (i, 0)),
            out_shape=jax.ShapeDtypeStruct((span_rows, tokens), BF16),
            cost_estimate=pl.CostEstimate(
                flops=2 * tokens * span_rows * inner, bytes_accessed=2 * (tokens + span_rows) * inner, transcendentals=0
            ),
            compiler_params=params,
        )(places, weight, normed, target)

    in_hops, across = inward(heads_over)
    first_landed = []
    cots = []

    def sum_over_heads(n):
        held = project(n)
        if n >= DEPTH:
            held = after(held, first_landed[n - DEPTH])
        for at, pairs in enumerate(in_hops):
            landed = lax.ppermute(held, "tensor", pairs)
            if at == 0:
                first_landed.append(landed)
            held = add16(held, landed)
        mid = add16(held, lax.ppermute(held, "tensor", across))
        out = mid
        for pairs in reversed(in_hops):
            back = lax.ppermute(out, "tensor", [(b, a) for a, b in pairs])
            out = back if pairs is in_hops[0] else jnp.where(in_middle, mid, back)
        return [mid, out]

    def updated(batch, split):
        rows = len(batch) * piece
        shape = (replicas // 2 if split else replicas, rows, inner)
        out_spec = pl.BlockSpec((1 if split else 2, rows, inner), lambda i: (i, 0, 0))
        count = 2 if split else 1
        return pl.pallas_call(
            functools.partial(gradient_kernel, len(batch), split),
            grid=(replicas // 2,),
            in_specs=[smem]
            + [by_chip] * (2 * len(batch))
            + [normed_spec, pl.BlockSpec((2, rows, inner), lambda i: (i, batch[0] // len(batch), 0))],
            out_specs=[out_spec] * count,
            out_shape=[jax.ShapeDtypeStruct(shape, BF16)] * count,
            cost_estimate=pl.CostEstimate(
                flops=2 * tokens * replicas * rows * inner,
                bytes_accessed=2 * (tokens + 2 * replicas * rows) * inner,
                transcendentals=0,
            ),
            compiler_params=params,
        )(places, *[c for n in batch for c in cots[n]], normed, weight)

    deltas, gathered = [], []
    for batch in batches:
        for n in batch:
            cots.append(sum_over_heads(n))
        here = global_weight[batch[0] * piece : (batch[-1] + 1) * piece]
        if batch is batches[0]:
            (new,) = updated(batch, False)
            new = after(new, kept_all)
            summed = lax.psum_scatter(new.reshape(-1, inner), "replica", scatter_dimension=0, tiled=True).astype(F32)
            deltas.append(here - summed / replicas)
            gathered.append(lax.all_gather(deltas[-1].astype(BF16), "replica", axis=0, tiled=True))
        else:
            summed = reduce_rows(*updated(batch, True), replicas, me)
            deltas.append(here - summed / replicas)
            gathered += gather_rows(deltas[-1].astype(BF16), replicas)

    (grad_input,) = pl.pallas_call(
        backward_kernel,
        grid=(groups,),
        in_specs=[smem, dt_spec, by_group, inv_spec, by_group, by_state, by_state, gain_spec, smem, smem, smem, weight_spec]
        + [pl.BlockSpec((span_rows, tokens), lambda g: (0, 0))] * (2 * chunks),
        out_specs=[by_group],
        out_shape=[jax.ShapeDtypeStruct((tokens, inner), BF16)],
        scratch_shapes=[pltpu.VMEM((tokens, width), F32)],
        cost_estimate=cost,
        compiler_params=params,
    )(places, dt_rows, normed, inv, gate_z, b_proj, c_proj, gain, a_log, dt_bias, skip_d, weight, *[c for p in cots for c in p])

    square_sum = functools.reduce(jnp.add, [jnp.sum(d * d) for d in deltas])
    spread = jnp.full((8, LANES), square_sum, F32)
    for axis, size in (("replica", replicas), ("tensor", heads_over)):
        for bit in range(size.bit_length() - 1):
            spread = spread + lax.ppermute(spread, axis, [(r, r ^ (1 << bit)) for r in range(size)])
    entry_count = features * inner * heads_over
    factor = jnp.minimum(1.0, clip_rms / jnp.sqrt(spread[0, 0] / entry_count + 1e-06))
    clipped = factor * jnp.concatenate(deltas, axis=0)
    new_momentum = outer_beta * momentum + clipped
    new_global = global_weight - outer_rate * (clipped + outer_beta * new_momentum)
    scale = (outer_rate * (1.0 + outer_beta)) * factor
    chip_spec = pl.BlockSpec((1, piece, inner), lambda r, place: (lax.bitwise_xor(lax.div(r, 2), place[3]), 0, 0))
    new_weight = pl.pallas_call(
        weight_kernel,
        grid_spec=pltpu.PrefetchScalarGridSpec(
            num_scalar_prefetch=1,
            grid=(replicas,),
            in_specs=[
                smem,
                pl.BlockSpec((owned, inner), lambda r, place: (r, 0)),
                pl.BlockSpec((len(batches[0]) * piece, inner), lambda r, place: (r, 0)),
            ]
            + [chip_spec] * (len(gathered) - 1),
            out_specs=pl.BlockSpec((owned, inner), lambda r, place: (r, 0)),
        ),
        out_shape=jax.ShapeDtypeStruct((features, inner), BF16),
        cost_estimate=pl.CostEstimate(flops=2 * features * inner, bytes_accessed=6 * features * inner, transcendentals=0),
        compiler_params=params,
    )(places, scale.reshape(1), kept_all, *gathered)
    return (grad_input, new_weight, new_global, new_momentum)


def solution(mesh):
    placed = (
        P("replica", "tensor"),
        P("replica", "tensor"),
        P("replica", "tensor"),
        P("replica", "tensor"),
        P("replica", "tensor"),
        P("tensor"),
        P("tensor"),
        P("tensor"),
        P("tensor"),
        P("replica", None, "tensor"),
        P("replica", "tensor"),
        P("replica", "tensor"),
        P(("replica", "tensor"), None),
    )
    return jax.shard_map(
        shards,
        mesh=mesh,
        in_specs=placed,
        out_specs=(
            P("replica", "tensor"),
            P(None, "tensor"),
            P("replica", "tensor"),
            P("replica", "tensor"),
        ),
        check_vma=False,
    )
```

```python
import functools

import jax
import jax.numpy as jnp
from jax import lax
from jax.experimental import pallas as pl
from jax.experimental.pallas import tpu as pltpu
from jax.sharding import PartitionSpec as P

HEAD_DIM = 64
STATE = 128
SPAN = 256
HALF = SPAN // 2
LANES = 128

inner_rate = 0.001
outer_rate = 0.7
outer_beta = 0.9
clip_rms = 0.005
LOG2E = 1.4426950408889634
DEPTH = 2

F32 = jnp.float32
BF16 = jnp.bfloat16
NN = (((1,), (0,)), ((), ()))
NT = (((1,), (1,)), ((), ()))
TN = (((0,), (0,)), ((), ()))


def dot(a, b, dims):
    return lax.dot_general(a, b, dims, preferred_element_type=F32)


def silu(z):
    return z * (1.0 / (1.0 + jnp.exp(-z)))


def softplus(v):
    return jnp.maximum(v, 0.0) + jnp.log1p(jnp.exp(-jnp.abs(v)))


def iota(shape, axis):
    return lax.broadcasted_iota(jnp.int32, shape, axis)


def thirds(v):
    high = v.astype(BF16).astype(F32)
    middle = (v - high).astype(BF16).astype(F32)
    return jnp.concatenate([high, middle, v - high - middle], axis=0).astype(BF16)


def by_head(refs, first, per_group, tokens):
    row = iota((per_group, tokens), 0)
    rows = []
    for ref in refs:
        value = jnp.zeros((per_group, tokens), F32)
        for h in range(per_group):
            value = jnp.where(row == h, ref[first + h], value)
        rows.append(value)
    return rows


def head_tables(dt_ref, a_ref, bias_ref, per_group):
    first = pl.program_id(0) * per_group
    bias, a_log = by_head([bias_ref, a_ref], first, per_group, dt_ref.shape[1])
    step = softplus(dt_ref[...] + bias)
    return step, -jnp.exp(a_log) * step * LOG2E


def span_tables(step, rate, lo, per_group, width):
    upper = (iota((SPAN, SPAN), 0) <= iota((SPAN, SPAN), 1)).astype(BF16)
    step_k = step[:, lo : lo + SPAN]
    sums = dot(thirds(rate[:, lo : lo + SPAN]), upper, NN)
    cum = sums[:per_group] + sums[per_group : 2 * per_group] + sums[2 * per_group :]
    spread = (iota((3 * per_group, width), 1) // HEAD_DIM == iota((3 * per_group, width), 0) % per_group).astype(BF16)
    turn = (iota((3 * per_group, per_group), 1) == iota((3 * per_group, per_group), 0) % per_group).astype(BF16)
    cum_col = dot(thirds(cum), turn, TN)
    step_x = dot(thirds(step_k), spread, TN)
    fade_x = dot(thirds(jnp.exp2(cum)), spread, TN)
    tail_x = dot(thirds(jnp.exp2(cum[:, SPAN - 1 :] - cum) * step_k), spread, TN)
    return cum, cum_col, step_x, fade_x, tail_x


def skip_row(skip_ref, first, per_group, width):
    head = iota((1, width), 1) // HEAD_DIM
    row = jnp.zeros((1, width), F32)
    for h in range(per_group):
        row = jnp.where(head == h, skip_ref[first + h], row)
    return row


def decay(gap, mask=None):
    return jnp.exp2(gap if mask is None else jnp.where(mask, gap, -1e30))


def even_odd(v):
    first = iota(v.shape, 1) % (2 * HEAD_DIM) < HEAD_DIM
    return jnp.where(first, v, 0.0).astype(BF16), jnp.where(first, 0.0, v).astype(BF16)


def forward_kernel(dt_ref, x_ref, z_ref, b_ref, c_ref, gain_ref, a_ref, bias_ref, skip_ref, normed_ref, inv_ref):
    tokens, width = x_ref.shape
    per_group = width // HEAD_DIM
    step, rate = head_tables(dt_ref, a_ref, bias_ref, per_group)
    skip = skip_row(skip_ref, pl.program_id(0) * per_group, per_group, width)
    causal = iota((HALF, HALF), 0) >= iota((HALF, HALF), 1)
    spans = tokens // SPAN
    entering = None
    for k in range(spans):
        rows = slice(k * SPAN, (k + 1) * SPAN)
        cum, cum_col, step_x, fade_x, tail_x = span_tables(step, rate, k * SPAN, per_group, width)
        x = x_ref[rows, :].astype(F32)
        b, c = b_ref[rows, :], c_ref[rows, :]
        scores = dot(c, b, NT)
        values = even_odd(x * step_x)
        pieces = []
        for pair in range(per_group // 2):
            lanes = slice(2 * pair * HEAD_DIM, 2 * (pair + 1) * HEAD_DIM)
            tops, bottoms = [], []
            for h in (2 * pair, 2 * pair + 1):
                col, line = cum_col[:, h : h + 1], cum[h : h + 1, :]
                top = decay(col[:HALF] - line[:, :HALF], causal) * scores[:HALF, :HALF]
                left = decay(col[HALF:] - line[:, :HALF]) * scores[HALF:, :HALF]
                low = decay(col[HALF:] - line[:, HALF:], causal) * scores[HALF:, HALF:]
                tops.append(top.astype(BF16))
                bottoms += [left.astype(BF16), low.astype(BF16)]
            upper_values = jnp.concatenate([v[:HALF, lanes] for v in values], axis=0)
            all_values = jnp.concatenate([v[:, lanes] for v in values], axis=0)
            pieces.append(
                jnp.concatenate(
                    [
                        dot(jnp.concatenate(tops, axis=1), upper_values, NN),
                        dot(jnp.concatenate(bottoms, axis=1), all_values, NN),
                    ],
                    axis=0,
                )
            )
        ssd = jnp.concatenate(pieces, axis=1) + skip * x
        if entering is not None:
            ssd = ssd + dot(c, entering.astype(BF16), NN) * fade_x
        if k + 1 < spans:
            state = dot(b, (x * tail_x).astype(BF16), TN)
            entering = state if entering is None else entering * fade_x[SPAN - 1 :, :] + state
        gated = ssd * silu(z_ref[rows, :].astype(F32))
        inv = lax.rsqrt(jnp.mean(gated * gated, axis=1, keepdims=True) + 1e-05)
        normed_ref[rows, :] = (gated * inv * gain_ref[...]).astype(BF16)
        inv_ref[0, rows, :] = inv


def project_kernel(chunks, place_ref, weight_ref, normed_ref, target_ref, *part_refs):
    replicas, owned, inner = weight_ref.shape
    held, features = target_ref.shape
    piece = part_refs[0].shape[0] // replicas
    tokens = normed_ref.shape[0]
    eye = (iota((held, held), 0) == iota((held, held), 1)).astype(BF16)
    turned = dot(target_ref[...], eye, TN).reshape(replicas, owned, held)
    here = iota((replicas * piece, tokens), 1) // held == place_ref[0]
    for n, part_ref in zip(chunks, part_refs):
        at = slice(n * piece, (n + 1) * piece)
        part = dot(weight_ref[:, at, :].reshape(replicas * piece, inner), normed_ref[...], NT)
        goal = jnp.concatenate([turned[:, at, :].reshape(replicas * piece, held)] * (tokens // held), axis=1)
        part_ref[...] = (part - jnp.where(here, goal, 0.0)).astype(BF16)


def add_kernel(a_ref, b_ref, sum_ref):
    sum_ref[...] = (a_ref[...].astype(F32) + b_ref[...].astype(F32)).astype(BF16)


def gradient_kernel(batch, place_ref, *refs):
    count = len(batch)
    cot_refs, (normed_ref, weight_ref, keep_ref, send_ref) = refs[: 2 * count], refs[2 * count :]
    middle = place_ref[1] == 1
    odd = place_ref[2] == 1
    replicas, _, inner = weight_ref.shape
    piece = keep_ref.shape[1] // count
    tile = min(inner, 512)
    for n, chunk in enumerate(batch):
        cot = jnp.where(middle, cot_refs[2 * n][...], cot_refs[2 * n + 1][...])
        rows = slice(chunk * piece, (chunk + 1) * piece)
        at = slice(n * piece, (n + 1) * piece)
        for lo in range(0, inner, tile):
            cols = slice(lo, lo + tile)
            weight = weight_ref[:, rows, cols].reshape(replicas * piece, tile).astype(F32)
            new = weight - inner_rate * dot(cot, normed_ref[:, cols], NN)
            new = new.astype(BF16).reshape(replicas // 2, 2, piece, tile)
            keep_ref[:, at, cols] = jnp.where(odd, new[:, 1], new[:, 0])
            send_ref[:, at, cols] = jnp.where(odd, new[:, 0], new[:, 1])


def backward_kernel(
    place_ref, dt_ref, normed_ref, inv_ref, z_ref, b_ref, c_ref, gain_ref, a_ref, bias_ref, skip_ref, weight_ref, *refs
):
    *cot_refs, dx_ref, dn_ref = refs
    tokens, width = normed_ref.shape
    per_group = width // HEAD_DIM
    replicas, owned, _ = weight_ref.shape
    chunks = len(cot_refs) // 2
    piece = owned // chunks
    middle = place_ref[1] == 1
    for n in range(chunks):
        weight = weight_ref[:, n * piece : (n + 1) * piece, :].reshape(replicas * piece, width)
        term = dot(jnp.where(middle, cot_refs[2 * n][...], cot_refs[2 * n + 1][...]), weight, TN)
        dn_ref[...] = term if n == 0 else dn_ref[...] + term
    step, rate = head_tables(dt_ref, a_ref, bias_ref, per_group)
    skip = skip_row(skip_ref, pl.program_id(0) * per_group, per_group, width)
    causal = iota((HALF, HALF), 1) >= iota((HALF, HALF), 0)
    spans = tokens // SPAN
    d_state = None
    for k in reversed(range(spans)):
        rows = slice(k * SPAN, (k + 1) * SPAN)
        cum, cum_col, step_x, fade_x, tail_x = span_tables(step, rate, k * SPAN, per_group, width)
        dn = dn_ref[rows, :]
        gain = gain_ref[...]
        normed = normed_ref[rows, :].astype(F32)
        shared = jnp.mean(normed * dn, axis=1, keepdims=True)
        d_gated = inv_ref[0, rows, :] * (gain * dn - (normed / gain) * shared)
        d_ssd = d_gated * silu(z_ref[rows, :].astype(F32))
        values = even_odd(d_ssd)
        b, c = b_ref[rows, :], c_ref[rows, :]
        scores = dot(b, c, NT)
        pieces = []
        for pair in range(per_group // 2):
            lanes = slice(2 * pair * HEAD_DIM, 2 * (pair + 1) * HEAD_DIM)
            tops, bottoms = [], []
            for h in (2 * pair, 2 * pair + 1):
                col, line = cum_col[:, h : h + 1], cum[h : h + 1, :]
                high = decay(line[:, :HALF] - col[:HALF], causal) * scores[:HALF, :HALF]
                right = decay(line[:, HALF:] - col[:HALF]) * scores[:HALF, HALF:]
                low = decay(line[:, HALF:] - col[HALF:], causal) * scores[HALF:, HALF:]
                tops += [high.astype(BF16), right.astype(BF16)]
                bottoms.append(low.astype(BF16))
            lower_values = jnp.concatenate([v[HALF:, lanes] for v in values], axis=0)
            all_values = jnp.concatenate([v[:, lanes] for v in values], axis=0)
            pieces.append(
                jnp.concatenate(
                    [
                        dot(jnp.concatenate(tops, axis=1), all_values, NN),
                        dot(jnp.concatenate(bottoms, axis=1), lower_values, NN),
                    ],
                    axis=0,
                )
            )
        dx = jnp.concatenate(pieces, axis=1) * step_x + skip * d_ssd
        if d_state is not None:
            dx = dx + dot(b, d_state.astype(BF16), NN) * tail_x
        dx_ref[rows, :] = dx.astype(BF16)
        if k > 0:
            own = dot(c, (d_ssd * fade_x).astype(BF16), TN)
            d_state = own if d_state is None else own + d_state * fade_x[SPAN - 1 :, :]


def weight_kernel(place_ref, scale_ref, kept_ref, whole_ref, *refs):
    *pair_refs, new_ref = refs
    mine = lax.rem(pl.program_id(0), 2) == place_ref[2]
    pieces = [whole_ref[...]]
    for own_ref, other_ref in zip(pair_refs[::2], pair_refs[1::2]):
        pieces.append(jnp.where(mine, own_ref[0], other_ref[0]))
    lo = 0
    for piece in pieces:
        rows = slice(lo, lo + piece.shape[0])
        lo += piece.shape[0]
        new_ref[rows, :] = (kept_ref[rows, :].astype(F32) - scale_ref[0] * piece.astype(F32)).astype(BF16)


def inward(axis_size):
    half = axis_size // 2
    hops = [[(s, s + 1), (axis_size - 1 - s, axis_size - 2 - s)] for s in range(half - 1)]
    return hops, [(half - 1, half), (half, half - 1)]


def after(value, *others):
    return lax.optimization_barrier((value, *others))[0]


def stages(replicas):
    bit, left, found = 1, replicas // 2, []
    while left > 1:
        bits = 2 if left >= 4 else 1
        found.append((bit, bits))
        bit, left = bit + bits, left >> bits
    return found


def reduce_rows(keep, send, replicas, me):
    _, piece, inner = keep.shape
    mine, landed = keep, [lax.ppermute(send, "replica", [(r, r ^ 1) for r in range(replicas)])]
    left = replicas // 2
    for bit, bits in stages(replicas):
        ways = 1 << bits
        my = lax.rem(lax.div(me, 1 << bit), ways)
        terms = [t.reshape(left // ways, ways, piece, inner) for t in [mine] + landed]

        def total(mask):
            at = lax.bitwise_xor(my, jnp.int32(mask))
            cut = [lax.dynamic_index_in_dim(t, at, 1, keepdims=False).astype(F32) for t in terms]
            return functools.reduce(jnp.add, cut).astype(BF16)

        landed = [
            lax.ppermute(total(mask), "replica", [(r, r ^ (mask << bit)) for r in range(replicas)])
            for mask in range(1, ways)
        ]
        mine = total(0)
        left //= ways
    return functools.reduce(jnp.add, [t.reshape(piece, inner).astype(F32) for t in [mine] + landed])


def gather_rows(rows, replicas):
    held = rows[None]
    for bit, bits in stages(replicas):
        parts = [held] + [
            lax.ppermute(held, "replica", [(r, r ^ (mask << bit)) for r in range(replicas)]) for mask in range(1, 1 << bits)
        ]
        held = jnp.concatenate(parts, axis=0)
    return held, lax.ppermute(held, "replica", [(r, r ^ 1) for r in range(replicas)])


def shards(
    x_in,
    gate_z,
    b_proj,
    c_proj,
    dt_raw,
    a_log,
    dt_bias,
    skip_d,
    norm_gain,
    out_weight,
    global_weight,
    momentum,
    target,
):
    tokens, inner = x_in.shape
    features = out_weight.shape[1]
    replicas = lax.axis_size("replica")
    heads_over = lax.axis_size("tensor")
    groups = b_proj.shape[1] // STATE
    heads = dt_raw.shape[1]
    width = inner // groups
    owned = features // replicas
    chunks = max(2, min(4, owned // 16))
    batches = [list(range(max(1, chunks - 2)))] + [[n] for n in range(max(1, chunks - 2), chunks)]
    piece = owned // chunks
    span_rows = replicas * piece
    place = lax.axis_index("tensor")
    me = lax.axis_index("replica")
    in_middle = (place == heads_over // 2 - 1) | (place == heads_over // 2)
    places = jnp.stack([place, in_middle.astype(jnp.int32), lax.rem(me, 2), lax.div(me, 2)]).astype(jnp.int32)
    weight = out_weight[0].reshape(replicas, owned, inner)
    gain = norm_gain.reshape(1, inner)
    dt_rows = dt_raw.T

    smem = pl.BlockSpec(memory_space=pltpu.SMEM)
    vmem = pl.BlockSpec(memory_space=pltpu.VMEM)
    by_group = pl.BlockSpec((tokens, width), lambda g: (0, g))
    by_state = pl.BlockSpec((tokens, STATE), lambda g: (0, g))
    inv_spec = pl.BlockSpec((1, tokens, 1), lambda g: (g, 0, 0))
    dt_spec = pl.BlockSpec((heads // groups, tokens), lambda g: (g, 0))
    gain_spec = pl.BlockSpec((1, width), lambda g: (0, g))
    weight_spec = pl.BlockSpec((replicas, owned, width), lambda g: (0, 0, g))
    params = pltpu.CompilerParams(vmem_limit_bytes=28 * 1024 * 1024)
    small = pltpu.CompilerParams(vmem_limit_bytes=16 * 1024 * 1024)
    cost = pl.CostEstimate(
        flops=2 * tokens * inner * 4 * SPAN, bytes_accessed=8 * inner * tokens, transcendentals=tokens * SPAN * heads
    )

    kept = global_weight - outer_rate * outer_beta * outer_beta * momentum
    kept_all = lax.all_gather(kept.astype(BF16), "replica", axis=0, tiled=True)

    normed, inv = pl.pallas_call(
        forward_kernel,
        grid=(groups,),
        in_specs=[dt_spec, by_group, by_group, by_state, by_state, gain_spec, smem, smem, smem],
        out_specs=[by_group, inv_spec],
        out_shape=[jax.ShapeDtypeStruct((tokens, inner), BF16), jax.ShapeDtypeStruct((groups, tokens, 1), F32)],
        cost_estimate=cost,
        compiler_params=params,
    )(dt_rows, x_in, gate_z, b_proj, c_proj, gain, a_log, dt_bias, skip_d)

    def project(picked):
        return pl.pallas_call(
            functools.partial(project_kernel, picked),
            in_specs=[smem, vmem, vmem, vmem],
            out_specs=[vmem] * len(picked),
            out_shape=[jax.ShapeDtypeStruct((span_rows, tokens), BF16)] * len(picked),
            cost_estimate=pl.CostEstimate(
                flops=2 * tokens * span_rows * inner * len(picked), bytes_accessed=2 * tokens * inner, transcendentals=0
            ),
            compiler_params=small,
        )(places, weight, normed, target)

    def add(a, b):
        return pl.pallas_call(
            add_kernel,
            in_specs=[vmem, vmem],
            out_specs=vmem,
            out_shape=jax.ShapeDtypeStruct(a.shape, BF16),
            cost_estimate=pl.CostEstimate(flops=a.size, bytes_accessed=2 * a.size, transcendentals=0),
            compiler_params=small,
        )(a, b)

    def updated(batch):
        shape = jax.ShapeDtypeStruct((replicas // 2, len(batch) * piece, inner), BF16)
        return pl.pallas_call(
            functools.partial(gradient_kernel, batch),
            in_specs=[smem] + [vmem] * (2 * len(batch) + 2),
            out_specs=[vmem] * 2,
            out_shape=[shape] * 2,
            cost_estimate=pl.CostEstimate(
                flops=2 * tokens * len(batch) * span_rows * inner, bytes_accessed=2 * tokens * inner, transcendentals=0
            ),
            compiler_params=small,
        )(places, *[c for n in batch for c in cots[n]], normed, weight)

    in_hops, across = inward(heads_over)
    parts = list(project([0]))
    parts += project(list(range(1, chunks)))
    landed_first, sums, cots = {}, {}, {}
    last = parts[-1]

    def hop_in(n):
        held = parts[n] if n < DEPTH or not in_hops else after(parts[n], landed_first[n - DEPTH])
        landed_first[n] = lax.ppermute(held, "tensor", in_hops[0]) if in_hops else held

    def sum_side(n):
        held = parts[n]
        for at, pairs in enumerate(in_hops):
            landed = landed_first[n] if at == 0 else lax.ppermute(held, "tensor", pairs)
            held = add(after(held, last), landed)
        return held

    def sum_all(n):
        mid = add(after(sums[n], last), lax.ppermute(sums[n], "tensor", across))
        out = mid
        for pairs in reversed(in_hops):
            back = lax.ppermute(out, "tensor", [(b, a) for a, b in pairs])
            out = back if pairs is in_hops[0] else jnp.where(in_middle, mid, back)
        return mid, out

    deltas, gathered = [], []
    pending = list(batches)
    for n in range(chunks):
        hop_in(n)
    for t in range(chunks + 2):
        if t < chunks:
            last = sums[t] = sum_side(t)
        if 1 <= t <= chunks:
            cots[t - 1] = sum_all(t - 1)
            last = cots[t - 1][0]
        if pending and t - 2 == pending[0][-1]:
            batch = pending.pop(0)
            if batch[0] == 0:
                last = after(last, kept_all)
            elif len(deltas) > 0:
                last = after(last, deltas[0])
            cots[batch[0]] = (after(cots[batch[0]][0], last), cots[batch[0]][1])
            keep, send = updated(batch)
            last = keep
            here = global_weight[batch[0] * piece : (batch[-1] + 1) * piece]
            deltas.append(here - reduce_rows(keep, send, replicas, me) / replicas)
            if batch[0] == 0:
                gathered.append(lax.all_gather(deltas[-1].astype(BF16), "replica", axis=0, tiled=True))
            else:
                gathered += gather_rows(deltas[-1].astype(BF16), replicas)

    (grad_input,) = pl.pallas_call(
        backward_kernel,
        grid=(groups,),
        in_specs=[smem, dt_spec, by_group, inv_spec, by_group, by_state, by_state, gain_spec, smem, smem, smem, weight_spec]
        + [vmem] * (2 * chunks),
        out_specs=[by_group],
        out_shape=[jax.ShapeDtypeStruct((tokens, inner), BF16)],
        scratch_shapes=[pltpu.VMEM((tokens, width), F32)],
        cost_estimate=cost,
        compiler_params=params,
    )(places, dt_rows, normed, inv, gate_z, b_proj, c_proj, gain, a_log, dt_bias, skip_d, weight, after(cots[0][0], deltas[-1]), *[c for n in range(chunks) for c in cots[n]][1:])

    square_sum = functools.reduce(jnp.add, [jnp.sum(d * d) for d in deltas])
    spread = jnp.full((8, LANES), square_sum, F32)
    for axis, size in (("replica", replicas), ("tensor", heads_over)):
        for bit in range(size.bit_length() - 1):
            spread = spread + lax.ppermute(spread, axis, [(r, r ^ (1 << bit)) for r in range(size)])
    entry_count = features * inner * heads_over
    factor = jnp.minimum(1.0, clip_rms / jnp.sqrt(spread[0, 0] / entry_count + 1e-06))
    clipped = factor * jnp.concatenate(deltas, axis=0)
    new_momentum = outer_beta * momentum + clipped
    new_global = global_weight - outer_rate * (clipped + outer_beta * new_momentum)
    scale = (outer_rate * (1.0 + outer_beta)) * factor
    chip_spec = pl.BlockSpec((1, piece, inner), lambda r, place: (lax.bitwise_xor(lax.div(r, 2), place[3]), 0, 0))
    new_weight = pl.pallas_call(
        weight_kernel,
        grid_spec=pltpu.PrefetchScalarGridSpec(
            num_scalar_prefetch=1,
            grid=(replicas,),
            in_specs=[
                smem,
                pl.BlockSpec((owned, inner), lambda r, place: (r, 0)),
                pl.BlockSpec((len(batches[0]) * piece, inner), lambda r, place: (r, 0)),
            ]
            + [chip_spec] * (len(gathered) - 1),
            out_specs=pl.BlockSpec((owned, inner), lambda r, place: (r, 0)),
        ),
        out_shape=jax.ShapeDtypeStruct((features, inner), BF16),
        cost_estimate=pl.CostEstimate(flops=2 * features * inner, bytes_accessed=6 * features * inner, transcendentals=0),
        compiler_params=params,
    )(places, scale.reshape(1), kept_all, *gathered)
    return (grad_input, new_weight, new_global, new_momentum)


def solution(mesh):
    placed = (
        P("replica", "tensor"),
        P("replica", "tensor"),
        P("replica", "tensor"),
        P("replica", "tensor"),
        P("replica", "tensor"),
        P("tensor"),
        P("tensor"),
        P("tensor"),
        P("tensor"),
        P("replica", None, "tensor"),
        P("replica", "tensor"),
        P("replica", "tensor"),
        P(("replica", "tensor"), None),
    )
    return jax.shard_map(
        shards,
        mesh=mesh,
        in_specs=placed,
        out_specs=(
            P("replica", "tensor"),
            P(None, "tensor"),
            P("replica", "tensor"),
            P("replica", "tensor"),
        ),
        check_vma=False,
    )
```

```python
import functools

import jax
import jax.numpy as jnp
from jax import lax
from jax.experimental import pallas as pl
from jax.experimental.pallas import tpu as pltpu
from jax.sharding import PartitionSpec as P

HEAD_DIM = 64
STATE = 128
SPAN = 256
HALF = SPAN // 2
LANES = 128

inner_rate = 0.001
outer_rate = 0.7
outer_beta = 0.9
clip_rms = 0.005
LOG2E = 1.4426950408889634
NOTE = 16

F32 = jnp.float32
BF16 = jnp.bfloat16
NN = (((1,), (0,)), ((), ()))
NT = (((1,), (1,)), ((), ()))
TN = (((0,), (0,)), ((), ()))


def dot(a, b, dims):
    return lax.dot_general(a, b, dims, preferred_element_type=F32)


def silu(z):
    return z * (1.0 / (1.0 + jnp.exp(-z)))


def softplus(v):
    return jnp.maximum(v, 0.0) + jnp.log1p(jnp.exp(-jnp.abs(v)))


def iota(shape, axis):
    return lax.broadcasted_iota(jnp.int32, shape, axis)


def thirds(v):
    high = v.astype(BF16).astype(F32)
    middle = (v - high).astype(BF16).astype(F32)
    return jnp.concatenate([high, middle, v - high - middle], axis=0).astype(BF16)


def by_head(refs, first, per_group, tokens):
    row = iota((per_group, tokens), 0)
    rows = []
    for ref in refs:
        value = jnp.zeros((per_group, tokens), F32)
        for h in range(per_group):
            value = jnp.where(row == h, ref[first + h], value)
        rows.append(value)
    return rows


def head_tables(dt_ref, a_ref, bias_ref, first, per_group):
    bias, a_log = by_head([bias_ref, a_ref], first, per_group, dt_ref.shape[1])
    step = softplus(dt_ref[...] + bias)
    return step, -jnp.exp(a_log) * step * LOG2E


def span_tables(step, rate, lo, per_group, width):
    upper = (iota((SPAN, SPAN), 0) <= iota((SPAN, SPAN), 1)).astype(BF16)
    step_k = step[:, lo : lo + SPAN]
    sums = dot(thirds(rate[:, lo : lo + SPAN]), upper, NN)
    cum = sums[:per_group] + sums[per_group : 2 * per_group] + sums[2 * per_group :]
    spread = (iota((3 * per_group, width), 1) // HEAD_DIM == iota((3 * per_group, width), 0) % per_group).astype(BF16)
    turn = (iota((3 * per_group, per_group), 1) == iota((3 * per_group, per_group), 0) % per_group).astype(BF16)
    cum_col = dot(thirds(cum), turn, TN)
    step_x = dot(thirds(step_k), spread, TN)
    fade_x = dot(thirds(jnp.exp2(cum)), spread, TN)
    tail_x = dot(thirds(jnp.exp2(cum[:, SPAN - 1 :] - cum) * step_k), spread, TN)
    return cum, cum_col, step_x, fade_x, tail_x


def skip_row(skip_ref, first, per_group, width):
    head = iota((1, width), 1) // HEAD_DIM
    row = jnp.zeros((1, width), F32)
    for h in range(per_group):
        row = jnp.where(head == h, skip_ref[first + h], row)
    return row


def decay(gap, mask=None):
    return jnp.exp2(gap if mask is None else jnp.where(mask, gap, -1e30))


def even_odd(v):
    first = iota(v.shape, 1) % (2 * HEAD_DIM) < HEAD_DIM
    return jnp.where(first, v, 0.0).astype(BF16), jnp.where(first, 0.0, v).astype(BF16)


def forward_kernel(
    count, dt_ref, x_ref, z_ref, b_ref, c_ref, gain_ref, a_ref, bias_ref, skip_ref, *refs
):
    loads = [pltpu.make_async_copy(refs[n], refs[count + n], refs[-1].at[n]) for n in range(count)]
    normed_ref, inv_ref = refs[2 * count : 2 * count + 2]

    @pl.when(pl.program_id(0) == 0)
    def _():
        for load in loads:
            load.start()

    tokens, width = x_ref.shape
    per_group = width // HEAD_DIM
    first = pl.program_id(0) * per_group
    lanes_here = pl.ds(pl.multiple_of(pl.program_id(0) * width, LANES), width)
    step, rate = head_tables(dt_ref, a_ref, bias_ref, first, per_group)
    skip = skip_row(skip_ref, first, per_group, width)
    causal = iota((HALF, HALF), 0) >= iota((HALF, HALF), 1)
    spans = tokens // SPAN
    entering = None
    for k in range(spans):
        rows = slice(k * SPAN, (k + 1) * SPAN)
        cum, cum_col, step_x, fade_x, tail_x = span_tables(step, rate, k * SPAN, per_group, width)
        x = x_ref[rows, :].astype(F32)
        b, c = b_ref[rows, :], c_ref[rows, :]
        scores = dot(c, b, NT)
        values = even_odd(x * step_x)
        pieces = []
        for pair in range(per_group // 2):
            lanes = slice(2 * pair * HEAD_DIM, 2 * (pair + 1) * HEAD_DIM)
            tops, bottoms = [], []
            for h in (2 * pair, 2 * pair + 1):
                col, line = cum_col[:, h : h + 1], cum[h : h + 1, :]
                top = decay(col[:HALF] - line[:, :HALF], causal) * scores[:HALF, :HALF]
                left = decay(col[HALF:] - line[:, :HALF]) * scores[HALF:, :HALF]
                low = decay(col[HALF:] - line[:, HALF:], causal) * scores[HALF:, HALF:]
                tops.append(top.astype(BF16))
                bottoms += [left.astype(BF16), low.astype(BF16)]
            upper_values = jnp.concatenate([v[:HALF, lanes] for v in values], axis=0)
            all_values = jnp.concatenate([v[:, lanes] for v in values], axis=0)
            pieces.append(
                jnp.concatenate(
                    [
                        dot(jnp.concatenate(tops, axis=1), upper_values, NN),
                        dot(jnp.concatenate(bottoms, axis=1), all_values, NN),
                    ],
                    axis=0,
                )
            )
        ssd = jnp.concatenate(pieces, axis=1) + skip * x
        if entering is not None:
            ssd = ssd + dot(c, entering.astype(BF16), NN) * fade_x
        if k + 1 < spans:
            state = dot(b, (x * tail_x).astype(BF16), TN)
            entering = state if entering is None else entering * fade_x[SPAN - 1 :, :] + state
        gated = ssd * silu(z_ref[rows, :].astype(F32))
        inv = lax.rsqrt(jnp.mean(gated * gated, axis=1, keepdims=True) + 1e-05)
        normed_ref[rows, lanes_here] = (gated * inv * gain_ref[...]).astype(BF16)
        inv_ref[pl.program_id(0), rows, :] = inv

    @pl.when(pl.program_id(0) == pl.num_programs(0) - 1)
    def _():
        for load in loads:
            load.wait()


def project_kernel(chunks, place_ref, weight_ref, normed_ref, target_ref, *part_refs):
    replicas, owned, inner = weight_ref.shape
    held, features = target_ref.shape
    piece = part_refs[0].shape[0] // replicas
    tokens = normed_ref.shape[0]
    eye = (iota((held, held), 0) == iota((held, held), 1)).astype(BF16)
    turned = dot(target_ref[...], eye, TN).reshape(replicas, owned, held)
    here = iota((replicas * piece, tokens), 1) // held == place_ref[0]
    for n, part_ref in zip(chunks, part_refs):
        at = slice(n * piece, (n + 1) * piece)
        part = dot(weight_ref[:, at, :].reshape(replicas * piece, inner), normed_ref[...], NT)
        goal = jnp.concatenate([turned[:, at, :].reshape(replicas * piece, held)] * (tokens // held), axis=1)
        part_ref[...] = (part - jnp.where(here, goal, 0.0)).astype(BF16)


def add_kernel(a_ref, b_ref, sum_ref):
    sum_ref[...] = (a_ref[...].astype(F32) + b_ref[...].astype(F32)).astype(BF16)


def gradient_kernel(batch, place_ref, *refs):
    count = len(batch)
    cot_refs, (normed_ref, weight_ref, keep_ref, send_ref) = refs[: 2 * count], refs[2 * count :]
    middle = place_ref[1] == 1
    odd = place_ref[2] == 1
    replicas, _, inner = weight_ref.shape
    piece = keep_ref.shape[1] // count
    tile = min(inner, 512)
    for n, chunk in enumerate(batch):
        cot = jnp.where(middle, cot_refs[2 * n][...], cot_refs[2 * n + 1][...])
        rows = slice(chunk * piece, (chunk + 1) * piece)
        at = slice(n * piece, (n + 1) * piece)
        for lo in range(0, inner, tile):
            cols = slice(lo, lo + tile)
            weight = weight_ref[:, rows, cols].reshape(replicas * piece, tile).astype(F32)
            new = weight - inner_rate * dot(cot, normed_ref[:, cols], NN)
            new = new.astype(BF16).reshape(replicas // 2, 2, piece, tile)
            keep_ref[:, at, cols] = jnp.where(odd, new[:, 1], new[:, 0])
            send_ref[:, at, cols] = jnp.where(odd, new[:, 0], new[:, 1])


def backward_kernel(
    begin, place_ref, dt_ref, z_ref, b_ref, c_ref, gain_ref, a_ref, bias_ref, skip_ref, normed_ref, inv_ref, weight_ref, *refs
):
    *cot_refs, dx_ref, dn_ref = refs
    if len(cot_refs) % 2:
        cot_refs = cot_refs[:-1]
    tokens, width = z_ref.shape
    per_group = width // HEAD_DIM
    group = pl.program_id(0) + begin
    first = group * per_group
    here = pl.ds(pl.multiple_of(group * width, LANES), width)
    replicas, owned, _ = weight_ref.shape
    chunks = len(cot_refs) // 2
    piece = owned // chunks
    middle = place_ref[1] == 1
    for n in range(chunks):
        weight = weight_ref[:, n * piece : (n + 1) * piece, here].reshape(replicas * piece, width)
        term = dot(jnp.where(middle, cot_refs[2 * n][...], cot_refs[2 * n + 1][...]), weight, TN)
        dn_ref[...] = term if n == 0 else dn_ref[...] + term
    step, rate = head_tables(dt_ref, a_ref, bias_ref, first, per_group)
    skip = skip_row(skip_ref, first, per_group, width)
    causal = iota((HALF, HALF), 1) >= iota((HALF, HALF), 0)
    spans = tokens // SPAN
    d_state = None
    for k in reversed(range(spans)):
        rows = slice(k * SPAN, (k + 1) * SPAN)
        cum, cum_col, step_x, fade_x, tail_x = span_tables(step, rate, k * SPAN, per_group, width)
        dn = dn_ref[rows, :]
        gain = gain_ref[...]
        normed = normed_ref[rows, here].astype(F32)
        shared = jnp.mean(normed * dn, axis=1, keepdims=True)
        d_gated = inv_ref[group, rows, :] * (gain * dn - (normed / gain) * shared)
        d_ssd = d_gated * silu(z_ref[rows, :].astype(F32))
        values = even_odd(d_ssd)
        b, c = b_ref[rows, :], c_ref[rows, :]
        scores = dot(b, c, NT)
        pieces = []
        for pair in range(per_group // 2):
            lanes = slice(2 * pair * HEAD_DIM, 2 * (pair + 1) * HEAD_DIM)
            tops, bottoms = [], []
            for h in (2 * pair, 2 * pair + 1):
                col, line = cum_col[:, h : h + 1], cum[h : h + 1, :]
                high = decay(line[:, :HALF] - col[:HALF], causal) * scores[:HALF, :HALF]
                right = decay(line[:, HALF:] - col[:HALF]) * scores[:HALF, HALF:]
                low = decay(line[:, HALF:] - col[HALF:], causal) * scores[HALF:, HALF:]
                tops += [high.astype(BF16), right.astype(BF16)]
                bottoms.append(low.astype(BF16))
            lower_values = jnp.concatenate([v[HALF:, lanes] for v in values], axis=0)
            all_values = jnp.concatenate([v[:, lanes] for v in values], axis=0)
            pieces.append(
                jnp.concatenate(
                    [
                        dot(jnp.concatenate(tops, axis=1), all_values, NN),
                        dot(jnp.concatenate(bottoms, axis=1), lower_values, NN),
                    ],
                    axis=0,
                )
            )
        dx = jnp.concatenate(pieces, axis=1) * step_x + skip * d_ssd
        if d_state is not None:
            dx = dx + dot(b, d_state.astype(BF16), NN) * tail_x
        dx_ref[rows, :] = dx.astype(BF16)
        if k > 0:
            own = dot(c, (d_ssd * fade_x).astype(BF16), TN)
            d_state = own if d_state is None else own + d_state * fade_x[SPAN - 1 :, :]


def pick_kernel(count, place_ref, *refs):
    terms, outs = refs[:count], refs[count:]
    my = lax.rem(lax.div(place_ref[3], place_ref[4]), len(outs))
    for mask, out_ref in enumerate(outs):
        at = lax.bitwise_xor(my, jnp.int32(mask))
        total = terms[0][:, at].astype(F32)
        for term in terms[1:]:
            total = total + term[:, at].astype(F32)
        out_ref[...] = total.astype(BF16)


def delta_kernel(count, lo, replicas, global_ref, before_ref, *refs):
    terms, (delta_ref, sent_ref, squares_ref) = refs[:count], refs[count:]
    rows, inner = delta_ref.shape
    total = terms[0][0].astype(F32)
    for term in terms[1:]:
        total = total + term[0].astype(F32)
    delta = global_ref[lo : lo + rows, :] - total / replicas
    delta_ref[...] = delta
    sent_ref[:rows, :] = delta.astype(BF16)
    squares = jnp.sum(delta * delta, axis=0, keepdims=True)
    squares = before_ref[...] + jnp.broadcast_to(jnp.sum(squares, axis=1, keepdims=True), before_ref.shape)
    squares_ref[...] = squares
    if sent_ref.shape[0] > rows:
        at = iota((NOTE, LANES), 0)
        value = jnp.broadcast_to(squares[:1, :], (NOTE, LANES))
        high = value.astype(BF16).astype(F32)
        middle = (value - high).astype(BF16).astype(F32)
        note = jnp.where(at == 0, high, jnp.where(at == 1, middle, jnp.where(at == 2, value - high - middle, 0.0)))
        sent_ref[rows:, :] = jnp.concatenate([note] * (inner // LANES), axis=1).astype(BF16)


def join_kernel(*refs):
    *parts, out_ref = refs
    lo = 0
    for part in parts:
        out_ref[lo : lo + part.shape[0]] = part[...]
        lo += part.shape[0]


def tree(values):
    while len(values) > 1:
        values = [a + b for a, b in zip(values[::2], values[1::2])]
    return values[0]


def squares_kernel(own_ref, other_ref, out_ref):
    sides = []
    for ref in (own_ref, other_ref):
        rows = ref.shape[1] - NOTE
        notes = [ref[p, rows:, :LANES].astype(F32) for p in range(ref.shape[0])]
        sides.append(tree([note[0:1] + note[1:2] + note[2:3] for note in notes]))
    out_ref[...] = jnp.broadcast_to(sides[0] + sides[1], out_ref.shape)


def weight_kernel(sizes, entries, place_ref, kept_ref, whole_ref, global_ref, momentum_ref, *refs):
    count = len(sizes)
    pairs, deltas, squares = refs[: 2 * count - 2], refs[2 * count - 2 : 3 * count - 2], refs[3 * count - 2 : -3]
    new_ref, new_global_ref, new_momentum_ref = refs[-3:]
    mean = tree([ref[:1, :1] for ref in squares]) / entries
    factor = jnp.minimum(1.0, clip_rms / jnp.sqrt(mean + 1e-06))
    r = pl.program_id(0)
    owned = new_ref.shape[0]
    at_chip = lax.bitwise_xor(lax.div(r, 2), place_ref[3])
    mine = lax.rem(r, 2) == place_ref[2]
    scale = (outer_rate * (1.0 + outer_beta)) * factor
    lo = 0
    for n, size in enumerate(sizes):
        if n == 0:
            piece = whole_ref[...]
        else:
            piece = jnp.where(mine, pairs[2 * n - 2][at_chip, :size, :], pairs[2 * n - 1][at_chip, :size, :])
        kept = kept_ref[pl.ds(pl.multiple_of(r * owned + lo, 16), size), :]
        new_ref[lo : lo + size, :] = (kept.astype(F32) - scale * piece.astype(F32)).astype(BF16)
        lo += size

    @pl.when(r == 0)
    def _():
        lo = 0
        for n, size in enumerate(sizes):
            rows = slice(lo, lo + size)
            lo += size
            clipped = factor * deltas[n][...]
            new_momentum = outer_beta * momentum_ref[rows, :] + clipped
            new_momentum_ref[rows, :] = new_momentum
            new_global_ref[rows, :] = global_ref[rows, :] - outer_rate * (clipped + outer_beta * new_momentum)


def inward(axis_size):
    half = axis_size // 2
    hops = [[(s, s + 1), (axis_size - 1 - s, axis_size - 2 - s)] for s in range(half - 1)]
    return hops, [(half - 1, half), (half, half - 1)]


def in_turn(kernel, inputs, waits, outs):
    def body(*refs):
        end = inputs + waits + outs
        refs[end][...] = jnp.zeros_like(refs[end])
        kernel(*refs[:inputs], *refs[inputs + waits : end], *refs[end + 1 :])

    return body


def stages(replicas):
    bit, left, found = 1, replicas // 2, []
    while left > 1:
        bits = 2 if left >= 4 else 1
        found.append((bit, bits))
        bit, left = bit + bits, left >> bits
    return found


def shards(
    x_in,
    gate_z,
    b_proj,
    c_proj,
    dt_raw,
    a_log,
    dt_bias,
    skip_d,
    norm_gain,
    out_weight,
    global_weight,
    momentum,
    target,
):
    tokens, inner = x_in.shape
    features = out_weight.shape[1]
    replicas = lax.axis_size("replica")
    heads_over = lax.axis_size("tensor")
    groups = b_proj.shape[1] // STATE
    heads = dt_raw.shape[1]
    width = inner // groups
    owned = features // replicas
    chunks = max(2, min(4, owned // 16))
    batches = [list(range(max(1, chunks - 2)))] + [[n] for n in range(max(1, chunks - 2), chunks)]
    piece = owned // chunks
    span_rows = replicas * piece
    place = lax.axis_index("tensor")
    me = lax.axis_index("replica")
    in_middle = (place == heads_over // 2 - 1) | (place == heads_over // 2)
    one = jnp.int32(1)
    places = jnp.stack([place, in_middle.astype(jnp.int32), lax.rem(me, 2), lax.div(me, 2), one]).astype(jnp.int32)
    stored = out_weight[0].reshape(replicas, owned, inner)
    gain = norm_gain.reshape(1, inner)
    dt_rows = dt_raw.T

    smem = pl.BlockSpec(memory_space=pltpu.SMEM)
    vmem = pl.BlockSpec(memory_space=pltpu.VMEM)
    anywhere = pl.BlockSpec(memory_space=pl.ANY)
    inv_spec = pl.BlockSpec((1, tokens, 1), lambda g: (g, 0, 0))
    large = pltpu.CompilerParams(vmem_limit_bytes=30 * 1024 * 1024)
    small = pltpu.CompilerParams(vmem_limit_bytes=16 * 1024 * 1024)
    cost = pl.CostEstimate(
        flops=2 * tokens * inner * 4 * SPAN, bytes_accessed=8 * inner * tokens, transcendentals=tokens * SPAN * heads
    )

    turn = []

    def run(kernel, inputs, in_specs, outs, out_specs, waits=(), **options):
        waits = [*turn[-1:], *waits]
        done = jax.ShapeDtypeStruct((8, LANES), F32)
        *results, ran = pl.pallas_call(
            in_turn(kernel, len(inputs), len(waits), len(outs)),
            in_specs=[*in_specs, *[vmem] * len(waits)],
            out_specs=[*out_specs, vmem],
            out_shape=[*outs, done],
            **options,
        )(*inputs, *waits)
        turn.append(ran)
        return results

    def step(kernel, operands, outs, flops, waits=(), out_specs=None, scalars=()):
        return run(
            kernel,
            [*scalars, *operands],
            [smem] * len(scalars) + [vmem] * len(operands),
            outs,
            out_specs or [vmem] * len(outs),
            waits,
            cost_estimate=pl.CostEstimate(flops=flops, bytes_accessed=4 * sum(o.size for o in outs), transcendentals=0),
            compiler_params=small,
        )

    def shape(*dims, dtype=BF16):
        return jax.ShapeDtypeStruct(dims, dtype)

    def in_hbm(*arrays):
        return [pltpu.with_memory_space_constraint(a, pltpu.HBM) for a in arrays]

    kept = global_weight - outer_rate * outer_beta * outer_beta * momentum
    kept_all = lax.all_gather(kept.astype(BF16), "replica", axis=0, tiled=True)

    def group_specs(begin):
        wide = pl.BlockSpec((tokens, width), lambda g: (0, g + begin))
        state = pl.BlockSpec((tokens, STATE), lambda g: (0, g + begin))
        dt = pl.BlockSpec((heads // groups, tokens), lambda g: (g + begin, 0))
        return wide, state, dt, pl.BlockSpec((1, width), lambda g: (0, g + begin))

    by_group, by_state, dt_spec, gain_spec = group_specs(0)
    shared = in_hbm(dt_rows, gate_z, b_proj, c_proj, gain, a_log, dt_bias, skip_d)
    later = [stored, target, global_weight, momentum]
    weight, goal, own_global, own_momentum, normed, inv = run(
        functools.partial(forward_kernel, len(later)),
        [shared[0], *in_hbm(x_in), *shared[1:], *in_hbm(*later)],
        [dt_spec, by_group, by_group, by_state, by_state, gain_spec, smem, smem, smem] + [anywhere] * len(later),
        [pltpu.VMEM(v.shape, v.dtype) for v in later] + [pltpu.VMEM((tokens, inner), BF16), pltpu.VMEM((groups, tokens, 1), F32)],
        [vmem] * (len(later) + 2),
        grid=(groups,),
        scratch_shapes=[pltpu.SemaphoreType.DMA((len(later),))],
        cost_estimate=cost,
        compiler_params=large,
    )

    part = shape(span_rows, tokens)
    chunk_flops = 2 * tokens * span_rows * inner

    def project(picked):
        return step(
            functools.partial(project_kernel, picked),
            [weight, normed, goal],
            [part] * len(picked),
            len(picked) * chunk_flops,
            scalars=[places],
        )

    in_hops, across = inward(heads_over)
    parts = project([0])
    parts += project(list(range(1, chunks)))
    first_landed = [lax.ppermute(p, "tensor", in_hops[0]) if in_hops else None for p in parts]
    sums, cots = {}, {}

    def sum_side(n):
        held = parts[n]
        for at, pairs in enumerate(in_hops):
            landed = first_landed[n] if at == 0 else lax.ppermute(held, "tensor", pairs)
            (held,) = step(add_kernel, [held, landed], [part], part.size)
        sums[n] = held

    def sum_all(n):
        (mid,) = step(add_kernel, [sums[n], lax.ppermute(sums[n], "tensor", across)], [part], part.size)
        out = mid
        for pairs in reversed(in_hops):
            back = lax.ppermute(out, "tensor", [(b, a) for a, b in pairs])
            out = back if pairs is in_hops[0] else jnp.where(in_middle, mid, back)
        cots[n] = (mid, out)

    def exchange(value, mask):
        return lax.ppermute(value, "replica", [(r, r ^ mask) for r in range(replicas)])

    terms, deltas, gathered = {}, {}, {}
    squares = {-1: jnp.zeros((8, LANES), F32)}

    def send_rows(b):
        batch = batches[b]
        rows = len(batch) * piece
        keep, send = step(
            functools.partial(gradient_kernel, batch),
            [c for n in batch for c in cots[n]] + [normed, weight],
            [shape(replicas // 2, rows, inner)] * 2,
            len(batch) * chunk_flops,
            waits=[kept_all[:NOTE, :LANES]] if b == 0 else [],
            scalars=[places],
        )
        held, left = [keep, exchange(send, 1)], replicas // 2
        for bit, bits in stages(replicas):
            ways = 1 << bits
            left //= ways
            cut = [h.reshape(left, ways, rows, inner) for h in held]
            picked = step(
                functools.partial(pick_kernel, len(cut)),
                cut,
                [shape(left, rows, inner)] * ways,
                replicas * rows * inner,
                scalars=[places.at[4].set(1 << (bit - 1))] if bit > 1 else [places],
            )
            held = [picked[0]] + [exchange(picked[mask], mask << bit) for mask in range(1, ways)]
        terms[b] = held

    def own_rows(b):
        batch = batches[b]
        rows = len(batch) * piece
        sent_rows = rows + NOTE if b == len(batches) - 1 else rows
        delta, sent, total = step(
            functools.partial(delta_kernel, len(terms[b]), batch[0] * piece, replicas),
            [own_global, squares[b - 1], *terms[b]],
            [shape(rows, inner, dtype=F32), shape(sent_rows, inner), shape(8, LANES, dtype=F32)],
            4 * rows * inner,
            out_specs=[vmem, vmem if b else pl.BlockSpec((rows, inner)), vmem],
        )
        deltas[b], squares[b] = delta, total
        if b == 0:
            gathered[b] = [lax.all_gather(sent, "replica", axis=0, tiled=True)]
        else:
            gathered[b] = [sent[None]]
            (bit, bits), *_ = stages(replicas)
            gathered[b] += [exchange(gathered[b][0], mask << bit) for mask in range(1, 1 << bits)]

    def join(b):
        for at, (bit, bits) in enumerate(stages(replicas)):
            if at > 0:
                gathered[b] = [held] + [exchange(held, mask << bit) for mask in range(1, 1 << bits)]
            one = gathered[b][0]
            (held,) = step(join_kernel, gathered[b], [shape(len(gathered[b]) * one.shape[0], *one.shape[1:])], one.size)
        gathered[b] = [held, exchange(held, 1)]

    def backward(begin, count, so_far):
        wide, state, dt, gain_here = group_specs(begin)
        operands = [places, *shared, normed, inv, weight] + [c for n in range(chunks) for c in cots[n]]
        specs = [smem, dt, wide, state, state, gain_here, smem, smem, smem, vmem, vmem, vmem] + [vmem] * (2 * chunks)
        aliases = {}
        if so_far is not None:
            aliases = {len(operands): 0}
            operands.append(so_far)
            specs.append(anywhere)
        (grad,) = run(
            functools.partial(backward_kernel, begin),
            operands,
            specs,
            [shape(tokens, inner)],
            [wide],
            grid=(count,),
            scratch_shapes=[pltpu.VMEM((tokens, width), F32)],
            input_output_aliases=aliases,
            cost_estimate=cost,
            compiler_params=large,
        )
        return grad

    begun = 0
    for t in range(chunks + 2):
        if t < chunks:
            sum_side(t)
        if 1 <= t <= chunks:
            sum_all(t - 1)
        if begun < len(batches) and t - 2 == batches[begun][-1]:
            send_rows(begun)
            if begun > 0:
                own_rows(begun - 1)
            begun += 1
    half = groups // 2
    end = len(batches) - 1
    grad_input = backward(0, half, None) if half else None
    own_rows(end)
    for b in range(1, end):
        join(b)
    grad_input = backward(half, groups - half, grad_input)
    join(end)
    (column,) = step(squares_kernel, gathered[end], [shape(8, LANES, dtype=F32)], NOTE * inner)
    columns = [column] + [
        lax.ppermute(column, "tensor", [(t, t ^ mask) for t in range(heads_over)]) for mask in range(1, heads_over)
    ]

    sizes = [len(batch) * piece for batch in batches]
    row_spec = pl.BlockSpec((owned, inner), lambda r: (r, 0))
    held_spec = pl.BlockSpec((owned, inner), lambda r: (0, 0))
    pairs = [v for b in range(1, end + 1) for v in gathered[b]]
    new_weight, new_global, new_momentum = run(
        functools.partial(weight_kernel, sizes, features * inner * heads_over),
        [places, kept_all, *in_hbm(*gathered[0]), own_global, own_momentum, *pairs, *[deltas[b] for b in range(end + 1)], *columns],
        [smem, vmem, pl.BlockSpec((sizes[0], inner), lambda r: (r, 0)), vmem, vmem]
        + [vmem] * (len(pairs) + len(sizes) + len(columns)),
        [shape(features, inner), shape(owned, inner, dtype=F32), shape(owned, inner, dtype=F32)],
        [row_spec, held_spec, held_spec],
        grid=(replicas,),
        cost_estimate=pl.CostEstimate(flops=2 * features * inner, bytes_accessed=6 * features * inner, transcendentals=0),
        compiler_params=pltpu.CompilerParams(vmem_limit_bytes=24 * 1024 * 1024),
    )
    return (grad_input, new_weight, new_global, new_momentum)


def solution(mesh):
    placed = (
        P("replica", "tensor"),
        P("replica", "tensor"),
        P("replica", "tensor"),
        P("replica", "tensor"),
        P("replica", "tensor"),
        P("tensor"),
        P("tensor"),
        P("tensor"),
        P("tensor"),
        P("replica", None, "tensor"),
        P("replica", "tensor"),
        P("replica", "tensor"),
        P(("replica", "tensor"), None),
    )
    return jax.shard_map(
        shards,
        mesh=mesh,
        in_specs=placed,
        out_specs=(
            P("replica", "tensor"),
            P(None, "tensor"),
            P("replica", "tensor"),
            P("replica", "tensor"),
        ),
        check_vma=False,
    )
```

```python
import functools

import jax
import jax.numpy as jnp
from jax import lax
from jax.experimental import pallas as pl
from jax.experimental.pallas import tpu as pltpu
from jax.sharding import PartitionSpec as P

HEAD_DIM = 64
STATE = 128
SPAN = 256
HALF = SPAN // 2
LANES = 128

inner_rate = 0.001
outer_rate = 0.7
outer_beta = 0.9
clip_rms = 0.005
LOG2E = 1.4426950408889634
NOTE = 16

F32 = jnp.float32
BF16 = jnp.bfloat16
NN = (((1,), (0,)), ((), ()))
NT = (((1,), (1,)), ((), ()))
TN = (((0,), (0,)), ((), ()))


def dot(a, b, dims):
    return lax.dot_general(a, b, dims, preferred_element_type=F32)


def silu(z):
    return z * (1.0 / (1.0 + jnp.exp(-z)))


def softplus(v):
    return jnp.maximum(v, 0.0) + jnp.log1p(jnp.exp(-jnp.abs(v)))


def iota(shape, axis):
    return lax.broadcasted_iota(jnp.int32, shape, axis)


def thirds(v):
    high = v.astype(BF16).astype(F32)
    middle = (v - high).astype(BF16).astype(F32)
    return jnp.concatenate([high, middle, v - high - middle], axis=0).astype(BF16)


def by_head(refs, first, per_group, tokens):
    row = iota((per_group, tokens), 0)
    rows = []
    for ref in refs:
        value = jnp.zeros((per_group, tokens), F32)
        for h in range(per_group):
            value = jnp.where(row == h, ref[first + h], value)
        rows.append(value)
    return rows


def head_tables(dt_ref, a_ref, bias_ref, first, per_group):
    bias, a_log = by_head([bias_ref, a_ref], first, per_group, dt_ref.shape[1])
    step = softplus(dt_ref[...] + bias)
    return step, -jnp.exp(a_log) * step * LOG2E


def span_tables(step, rate, lo, per_group, width):
    upper = (iota((SPAN, SPAN), 0) <= iota((SPAN, SPAN), 1)).astype(BF16)
    step_k = step[:, lo : lo + SPAN]
    sums = dot(thirds(rate[:, lo : lo + SPAN]), upper, NN)
    cum = sums[:per_group] + sums[per_group : 2 * per_group] + sums[2 * per_group :]
    spread = (iota((3 * per_group, width), 1) // HEAD_DIM == iota((3 * per_group, width), 0) % per_group).astype(BF16)
    turn = (iota((3 * per_group, per_group), 1) == iota((3 * per_group, per_group), 0) % per_group).astype(BF16)
    cum_col = dot(thirds(cum), turn, TN)
    step_x = dot(thirds(step_k), spread, TN)
    fade_x = dot(thirds(jnp.exp2(cum)), spread, TN)
    tail_x = dot(thirds(jnp.exp2(cum[:, SPAN - 1 :] - cum) * step_k), spread, TN)
    return cum, cum_col, step_x, fade_x, tail_x


def skip_row(skip_ref, first, per_group, width):
    head = iota((1, width), 1) // HEAD_DIM
    row = jnp.zeros((1, width), F32)
    for h in range(per_group):
        row = jnp.where(head == h, skip_ref[first + h], row)
    return row


def decay(gap, mask=None):
    return jnp.exp2(gap if mask is None else jnp.where(mask, gap, -1e30))


def even_odd(v):
    first = iota(v.shape, 1) % (2 * HEAD_DIM) < HEAD_DIM
    return jnp.where(first, v, 0.0).astype(BF16), jnp.where(first, 0.0, v).astype(BF16)


def forward_kernel(
    count, dt_ref, x_ref, z_ref, b_ref, c_ref, gain_ref, a_ref, bias_ref, skip_ref, *refs
):
    loads = [pltpu.make_async_copy(refs[n], refs[count + n], refs[-1].at[n]) for n in range(count)]
    normed_ref, inv_ref = refs[2 * count : 2 * count + 2]

    @pl.when(pl.program_id(0) == 0)
    def _():
        for load in loads:
            load.start()

    tokens, width = x_ref.shape
    per_group = width // HEAD_DIM
    first = pl.program_id(0) * per_group
    lanes_here = pl.ds(pl.multiple_of(pl.program_id(0) * width, LANES), width)
    step, rate = head_tables(dt_ref, a_ref, bias_ref, first, per_group)
    skip = skip_row(skip_ref, first, per_group, width)
    causal = iota((HALF, HALF), 0) >= iota((HALF, HALF), 1)
    spans = tokens // SPAN
    entering = None
    for k in range(spans):
        rows = slice(k * SPAN, (k + 1) * SPAN)
        cum, cum_col, step_x, fade_x, tail_x = span_tables(step, rate, k * SPAN, per_group, width)
        x = x_ref[rows, :].astype(F32)
        b, c = b_ref[rows, :], c_ref[rows, :]
        scores = dot(c, b, NT)
        values = even_odd(x * step_x)
        pieces = []
        for pair in range(per_group // 2):
            lanes = slice(2 * pair * HEAD_DIM, 2 * (pair + 1) * HEAD_DIM)
            tops, bottoms = [], []
            for h in (2 * pair, 2 * pair + 1):
                col, line = cum_col[:, h : h + 1], cum[h : h + 1, :]
                top = decay(col[:HALF] - line[:, :HALF], causal) * scores[:HALF, :HALF]
                left = decay(col[HALF:] - line[:, :HALF]) * scores[HALF:, :HALF]
                low = decay(col[HALF:] - line[:, HALF:], causal) * scores[HALF:, HALF:]
                tops.append(top.astype(BF16))
                bottoms += [left.astype(BF16), low.astype(BF16)]
            upper_values = jnp.concatenate([v[:HALF, lanes] for v in values], axis=0)
            all_values = jnp.concatenate([v[:, lanes] for v in values], axis=0)
            pieces.append(
                jnp.concatenate(
                    [
                        dot(jnp.concatenate(tops, axis=1), upper_values, NN),
                        dot(jnp.concatenate(bottoms, axis=1), all_values, NN),
                    ],
                    axis=0,
                )
            )
        ssd = jnp.concatenate(pieces, axis=1) + skip * x
        if entering is not None:
            ssd = ssd + dot(c, entering.astype(BF16), NN) * fade_x
        if k + 1 < spans:
            state = dot(b, (x * tail_x).astype(BF16), TN)
            entering = state if entering is None else entering * fade_x[SPAN - 1 :, :] + state
        gated = ssd * silu(z_ref[rows, :].astype(F32))
        inv = lax.rsqrt(jnp.mean(gated * gated, axis=1, keepdims=True) + 1e-05)
        normed_ref[rows, lanes_here] = (gated * inv * gain_ref[...]).astype(BF16)
        inv_ref[pl.program_id(0), rows, :] = inv

    @pl.when(pl.program_id(0) == pl.num_programs(0) - 1)
    def _():
        for load in loads:
            load.wait()


def kept_kernel(chunks, place_ref, weight_ref, normed_ref, target_ref, global_ref, momentum_ref, *refs):
    *part_refs, kept_ref = refs
    kept = global_ref[...] - outer_rate * outer_beta * outer_beta * momentum_ref[...]
    kept_ref[...] = kept.astype(BF16)
    project_kernel(chunks, place_ref, weight_ref, normed_ref, target_ref, *part_refs)


def project_kernel(chunks, place_ref, weight_ref, normed_ref, target_ref, *part_refs):
    replicas, owned, inner = weight_ref.shape
    held, features = target_ref.shape
    piece = part_refs[0].shape[0] // replicas
    tokens = normed_ref.shape[0]
    eye = (iota((held, held), 0) == iota((held, held), 1)).astype(BF16)
    turned = dot(target_ref[...], eye, TN).reshape(replicas, owned, held)
    here = iota((replicas * piece, tokens), 1) // held == place_ref[0]
    for n, part_ref in zip(chunks, part_refs):
        at = slice(n * piece, (n + 1) * piece)
        part = dot(weight_ref[:, at, :].reshape(replicas * piece, inner), normed_ref[...], NT)
        goal = jnp.concatenate([turned[:, at, :].reshape(replicas * piece, held)] * (tokens // held), axis=1)
        part_ref[...] = (part - jnp.where(here, goal, 0.0)).astype(BF16)


def add_kernel(a_ref, b_ref, sum_ref):
    sum_ref[...] = (a_ref[...].astype(F32) + b_ref[...].astype(F32)).astype(BF16)


def gradient_kernel(batch, place_ref, *refs):
    count = len(batch)
    cot_refs, (normed_ref, weight_ref, keep_ref, send_ref) = refs[: 2 * count], refs[2 * count :]
    middle = place_ref[1] == 1
    odd = place_ref[2] == 1
    replicas, _, inner = weight_ref.shape
    piece = keep_ref.shape[1] // count
    tile = min(inner, 512)
    for n, chunk in enumerate(batch):
        cot = jnp.where(middle, cot_refs[2 * n][...], cot_refs[2 * n + 1][...])
        rows = slice(chunk * piece, (chunk + 1) * piece)
        at = slice(n * piece, (n + 1) * piece)
        for lo in range(0, inner, tile):
            cols = slice(lo, lo + tile)
            weight = weight_ref[:, rows, cols].reshape(replicas * piece, tile).astype(F32)
            new = weight - inner_rate * dot(cot, normed_ref[:, cols], NN)
            new = new.astype(BF16).reshape(replicas // 2, 2, piece, tile)
            keep_ref[:, at, cols] = jnp.where(odd, new[:, 1], new[:, 0])
            send_ref[:, at, cols] = jnp.where(odd, new[:, 0], new[:, 1])


def backward_kernel(
    begin, place_ref, dt_ref, z_ref, b_ref, c_ref, gain_ref, a_ref, bias_ref, skip_ref, normed_ref, inv_ref, weight_ref, *refs
):
    *cot_refs, dx_ref, dn_ref = refs
    if len(cot_refs) % 2:
        cot_refs = cot_refs[:-1]
    tokens, width = z_ref.shape
    per_group = width // HEAD_DIM
    group = pl.program_id(0) + begin
    first = group * per_group
    here = pl.ds(pl.multiple_of(group * width, LANES), width)
    replicas, owned, _ = weight_ref.shape
    chunks = len(cot_refs) // 2
    piece = owned // chunks
    middle = place_ref[1] == 1
    for n in range(chunks):
        weight = weight_ref[:, n * piece : (n + 1) * piece, here].reshape(replicas * piece, width)
        term = dot(jnp.where(middle, cot_refs[2 * n][...], cot_refs[2 * n + 1][...]), weight, TN)
        dn_ref[...] = term if n == 0 else dn_ref[...] + term
    step, rate = head_tables(dt_ref, a_ref, bias_ref, first, per_group)
    skip = skip_row(skip_ref, first, per_group, width)
    causal = iota((HALF, HALF), 1) >= iota((HALF, HALF), 0)
    spans = tokens // SPAN
    d_state = None
    for k in reversed(range(spans)):
        rows = slice(k * SPAN, (k + 1) * SPAN)
        cum, cum_col, step_x, fade_x, tail_x = span_tables(step, rate, k * SPAN, per_group, width)
        dn = dn_ref[rows, :]
        gain = gain_ref[...]
        normed = normed_ref[rows, here].astype(F32)
        shared = jnp.mean(normed * dn, axis=1, keepdims=True)
        d_gated = inv_ref[group, rows, :] * (gain * dn - (normed / gain) * shared)
        d_ssd = d_gated * silu(z_ref[rows, :].astype(F32))
        values = even_odd(d_ssd)
        b, c = b_ref[rows, :], c_ref[rows, :]
        scores = dot(b, c, NT)
        pieces = []
        for pair in range(per_group // 2):
            lanes = slice(2 * pair * HEAD_DIM, 2 * (pair + 1) * HEAD_DIM)
            tops, bottoms = [], []
            for h in (2 * pair, 2 * pair + 1):
                col, line = cum_col[:, h : h + 1], cum[h : h + 1, :]
                high = decay(line[:, :HALF] - col[:HALF], causal) * scores[:HALF, :HALF]
                right = decay(line[:, HALF:] - col[:HALF]) * scores[:HALF, HALF:]
                low = decay(line[:, HALF:] - col[HALF:], causal) * scores[HALF:, HALF:]
                tops += [high.astype(BF16), right.astype(BF16)]
                bottoms.append(low.astype(BF16))
            lower_values = jnp.concatenate([v[HALF:, lanes] for v in values], axis=0)
            all_values = jnp.concatenate([v[:, lanes] for v in values], axis=0)
            pieces.append(
                jnp.concatenate(
                    [
                        dot(jnp.concatenate(tops, axis=1), all_values, NN),
                        dot(jnp.concatenate(bottoms, axis=1), lower_values, NN),
                    ],
                    axis=0,
                )
            )
        dx = jnp.concatenate(pieces, axis=1) * step_x + skip * d_ssd
        if d_state is not None:
            dx = dx + dot(b, d_state.astype(BF16), NN) * tail_x
        dx_ref[rows, :] = dx.astype(BF16)
        if k > 0:
            own = dot(c, (d_ssd * fade_x).astype(BF16), TN)
            d_state = own if d_state is None else own + d_state * fade_x[SPAN - 1 :, :]


def pick_kernel(count, place_ref, *refs):
    terms, outs = refs[:count], refs[count:]
    my = lax.rem(lax.div(place_ref[3], place_ref[4]), len(outs))
    for mask, out_ref in enumerate(outs):
        at = lax.bitwise_xor(my, jnp.int32(mask))
        total = terms[0][:, at].astype(F32)
        for term in terms[1:]:
            total = total + term[:, at].astype(F32)
        out_ref[...] = total.astype(BF16)


def delta_kernel(count, lo, replicas, global_ref, before_ref, *refs):
    terms, (delta_ref, sent_ref, squares_ref) = refs[:count], refs[count:]
    rows, inner = delta_ref.shape
    total = terms[0][0].astype(F32)
    for term in terms[1:]:
        total = total + term[0].astype(F32)
    delta = global_ref[lo : lo + rows, :] - total / replicas
    delta_ref[...] = delta
    sent_ref[:rows, :] = delta.astype(BF16)
    squares = jnp.sum(delta * delta, axis=0, keepdims=True)
    squares = before_ref[...] + jnp.broadcast_to(jnp.sum(squares, axis=1, keepdims=True), before_ref.shape)
    squares_ref[...] = squares
    if sent_ref.shape[0] > rows:
        at = iota((NOTE, LANES), 0)
        value = jnp.broadcast_to(squares[:1, :], (NOTE, LANES))
        high = value.astype(BF16).astype(F32)
        middle = (value - high).astype(BF16).astype(F32)
        note = jnp.where(at == 0, high, jnp.where(at == 1, middle, jnp.where(at == 2, value - high - middle, 0.0)))
        sent_ref[rows:, :] = jnp.concatenate([note] * (inner // LANES), axis=1).astype(BF16)


def join_kernel(*refs):
    *parts, out_ref = refs
    lo = 0
    for part in parts:
        out_ref[lo : lo + part.shape[0]] = part[...]
        lo += part.shape[0]


def tree(values):
    while len(values) > 1:
        values = [a + b for a, b in zip(values[::2], values[1::2])]
    return values[0]


def squares_kernel(own_ref, other_ref, out_ref):
    sides = []
    for ref in (own_ref, other_ref):
        rows = ref.shape[1] - NOTE
        notes = [ref[p, rows:, :LANES].astype(F32) for p in range(ref.shape[0])]
        sides.append(tree([note[0:1] + note[1:2] + note[2:3] for note in notes]))
    out_ref[...] = jnp.broadcast_to(sides[0] + sides[1], out_ref.shape)


def weight_kernel(sizes, entries, place_ref, global_ref, momentum_ref, *refs):
    count = len(sizes)
    pairs, deltas, squares = refs[: 2 * count + 2], refs[2 * count + 2 : 3 * count + 2], refs[3 * count + 2 : -3]
    new_ref, new_global_ref, new_momentum_ref = refs[-3:]
    mean = tree([ref[:1, :1] for ref in squares]) / entries
    factor = jnp.minimum(1.0, clip_rms / jnp.sqrt(mean + 1e-06))
    at_chip = lax.bitwise_xor(pl.program_id(0), place_ref[3])
    owned = new_ref.shape[0] // 2
    scale = (outer_rate * (1.0 + outer_beta)) * factor

    def one_core(core, side):
        lo = 0
        for n, size in enumerate(sizes):
            kept = pairs[side][at_chip, lo : lo + size, :].astype(F32)
            delta = pairs[2 * n + 2 + side][at_chip, :size, :].astype(F32)
            new_ref[core * owned + lo : core * owned + lo + size, :] = (kept - scale * delta).astype(BF16)
            lo += size

    for own_core in range(2):

        @pl.when(place_ref[2] == own_core)
        def _():
            one_core(own_core, 0)
            one_core(1 - own_core, 1)

    @pl.when(pl.program_id(0) == 0)
    def _():
        lo = 0
        for n, size in enumerate(sizes):
            rows = slice(lo, lo + size)
            lo += size
            clipped = factor * deltas[n][...]
            new_momentum = outer_beta * momentum_ref[rows, :] + clipped
            new_momentum_ref[rows, :] = new_momentum
            new_global_ref[rows, :] = global_ref[rows, :] - outer_rate * (clipped + outer_beta * new_momentum)


def inward(axis_size):
    half = axis_size // 2
    hops = [[(s, s + 1), (axis_size - 1 - s, axis_size - 2 - s)] for s in range(half - 1)]
    return hops, [(half - 1, half), (half, half - 1)]


def in_turn(kernel, inputs, waits, outs):
    def body(*refs):
        end = inputs + waits + outs
        refs[end][...] = jnp.zeros_like(refs[end])
        kernel(*refs[:inputs], *refs[inputs + waits : end], *refs[end + 1 :])

    return body


def stages(replicas):
    bit, left, found = 1, replicas // 2, []
    while left > 1:
        bits = 2 if left >= 4 else 1
        found.append((bit, bits))
        bit, left = bit + bits, left >> bits
    return found


def shards(
    x_in,
    gate_z,
    b_proj,
    c_proj,
    dt_raw,
    a_log,
    dt_bias,
    skip_d,
    norm_gain,
    out_weight,
    global_weight,
    momentum,
    target,
):
    tokens, inner = x_in.shape
    features = out_weight.shape[1]
    replicas = lax.axis_size("replica")
    heads_over = lax.axis_size("tensor")
    groups = b_proj.shape[1] // STATE
    heads = dt_raw.shape[1]
    width = inner // groups
    owned = features // replicas
    chunks = max(2, min(4, owned // 16))
    batches = [list(range(max(1, chunks - 2)))] + [[n] for n in range(max(1, chunks - 2), chunks)]
    piece = owned // chunks
    span_rows = replicas * piece
    place = lax.axis_index("tensor")
    me = lax.axis_index("replica")
    in_middle = (place == heads_over // 2 - 1) | (place == heads_over // 2)
    one = jnp.int32(1)
    places = jnp.stack([place, in_middle.astype(jnp.int32), lax.rem(me, 2), lax.div(me, 2), one]).astype(jnp.int32)
    stored = out_weight[0].reshape(replicas, owned, inner)
    gain = norm_gain.reshape(1, inner)
    dt_rows = dt_raw.T

    smem = pl.BlockSpec(memory_space=pltpu.SMEM)
    vmem = pl.BlockSpec(memory_space=pltpu.VMEM)
    anywhere = pl.BlockSpec(memory_space=pl.ANY)
    inv_spec = pl.BlockSpec((1, tokens, 1), lambda g: (g, 0, 0))
    large = pltpu.CompilerParams(vmem_limit_bytes=20 * 1024 * 1024)
    small = pltpu.CompilerParams(vmem_limit_bytes=12 * 1024 * 1024)
    small_cost = pl.CostEstimate(flops=1, bytes_accessed=1, transcendentals=0)

    turn = []

    def run(kernel, inputs, in_specs, outs, out_specs, **options):
        waits = turn[-1:]
        done = jax.ShapeDtypeStruct((8, LANES), F32)
        *results, ran = pl.pallas_call(
            in_turn(kernel, len(inputs), len(waits), len(outs)),
            in_specs=[*in_specs, *[vmem] * len(waits)],
            out_specs=[*out_specs, vmem],
            out_shape=[*outs, done],
            **options,
        )(*inputs, *waits)
        turn.append(ran)
        return results

    def step(kernel, operands, outs, flops, scalars=()):
        return run(
            kernel,
            [*scalars, *operands],
            [smem] * len(scalars) + [vmem] * len(operands),
            outs,
            [vmem] * len(outs),
            cost_estimate=small_cost,
            compiler_params=small,
        )

    def shape(*dims, dtype=BF16):
        return jax.ShapeDtypeStruct(dims, dtype)

    def in_hbm(*arrays):
        return [pltpu.with_memory_space_constraint(a, pltpu.HBM) for a in arrays]

    def group_specs(begin):
        wide = pl.BlockSpec((tokens, width), lambda g: (0, g + begin))
        state = pl.BlockSpec((tokens, STATE), lambda g: (0, g + begin))
        dt = pl.BlockSpec((heads // groups, tokens), lambda g: (g + begin, 0))
        return wide, state, dt, pl.BlockSpec((1, width), lambda g: (0, g + begin))

    by_group, by_state, dt_spec, gain_spec = group_specs(0)
    shared = in_hbm(dt_rows, gate_z, b_proj, c_proj, gain, a_log, dt_bias, skip_d)
    later = [stored, target, global_weight, momentum]
    weight, goal, own_global, own_momentum, normed, inv = run(
        functools.partial(forward_kernel, len(later)),
        [shared[0], *in_hbm(x_in), *shared[1:], *in_hbm(*later)],
        [dt_spec, by_group, by_group, by_state, by_state, gain_spec, smem, smem, smem] + [anywhere] * len(later),
        [pltpu.VMEM(v.shape, v.dtype) for v in later] + [pltpu.VMEM((tokens, inner), BF16), pltpu.VMEM((groups, tokens, 1), F32)],
        [vmem] * (len(later) + 2),
        grid=(groups,),
        scratch_shapes=[pltpu.SemaphoreType.DMA((len(later),))],
        cost_estimate=small_cost,
        compiler_params=large,
    )

    part = shape(span_rows, tokens)
    chunk_flops = 2 * tokens * span_rows * inner

    def project(picked):
        return step(
            functools.partial(project_kernel, picked),
            [weight, normed, goal],
            [part] * len(picked),
            len(picked) * chunk_flops,
            scalars=[places],
        )

    in_hops, across = inward(heads_over)
    parts = project([0])
    *others, kept = step(
        functools.partial(kept_kernel, list(range(1, chunks))),
        [weight, normed, goal, own_global, own_momentum],
        [part] * (chunks - 1) + [shape(owned, inner)],
        (chunks - 1) * chunk_flops,
        scalars=[places],
    )
    parts += others
    first_landed = [lax.ppermute(p, "tensor", in_hops[0]) if in_hops else None for p in parts]
    sums, cots = {}, {}

    def sum_side(n):
        held = parts[n]
        for at, pairs in enumerate(in_hops):
            landed = first_landed[n] if at == 0 else lax.ppermute(held, "tensor", pairs)
            (held,) = step(add_kernel, [held, landed], [part], part.size)
        sums[n] = held

    def sum_all(n):
        (mid,) = step(add_kernel, [sums[n], lax.ppermute(sums[n], "tensor", across)], [part], part.size)
        out = mid
        for pairs in reversed(in_hops):
            back = lax.ppermute(out, "tensor", [(b, a) for a, b in pairs])
            out = back if pairs is in_hops[0] else jnp.where(in_middle, mid, back)
        cots[n] = (mid, out)

    def exchange(value, mask):
        return lax.ppermute(value, "replica", [(r, r ^ mask) for r in range(replicas)])

    terms, deltas, gathered = {}, {}, {}
    squares = {-1: jnp.zeros((8, LANES), F32)}

    def send_rows(b):
        batch = batches[b]
        rows = len(batch) * piece
        keep, send = step(
            functools.partial(gradient_kernel, batch),
            [c for n in batch for c in cots[n]] + [normed, weight],
            [shape(replicas // 2, rows, inner)] * 2,
            len(batch) * chunk_flops,
            scalars=[places],
        )
        held, left = [keep, exchange(send, 1)], replicas // 2
        for bit, bits in stages(replicas):
            ways = 1 << bits
            left //= ways
            cut = [h.reshape(left, ways, rows, inner) for h in held]
            picked = step(
                functools.partial(pick_kernel, len(cut)),
                cut,
                [shape(left, rows, inner)] * ways,
                replicas * rows * inner,
                scalars=[places.at[4].set(1 << (bit - 1))] if bit > 1 else [places],
            )
            held = [picked[0]] + [exchange(picked[mask], mask << bit) for mask in range(1, ways)]
        terms[b] = held

    def own_rows(b):
        batch = batches[b]
        rows = len(batch) * piece
        sent_rows = rows + NOTE if b == len(batches) - 1 else rows
        delta, sent, total = step(
            functools.partial(delta_kernel, len(terms[b]), batch[0] * piece, replicas),
            [own_global, squares[b - 1], *terms[b]],
            [shape(rows, inner, dtype=F32), shape(sent_rows, inner), shape(8, LANES, dtype=F32)],
            4 * rows * inner,
        )
        deltas[b], squares[b] = delta, total
        spread_rows(b, sent)

    def spread_rows(b, sent):
        (bit, bits), *_ = stages(replicas)
        gathered[b] = [sent[None]] + [exchange(sent[None], mask << bit) for mask in range(1, 1 << bits)]

    def join(b):
        for at, (bit, bits) in enumerate(stages(replicas)):
            if at > 0:
                gathered[b] = [held] + [exchange(held, mask << bit) for mask in range(1, 1 << bits)]
            one = gathered[b][0]
            (held,) = step(join_kernel, gathered[b], [shape(len(gathered[b]) * one.shape[0], *one.shape[1:])], one.size)
        gathered[b] = [held, exchange(held, 1)]

    def backward(begin, count, so_far):
        wide, state, dt, gain_here = group_specs(begin)
        operands = [places, *shared, normed, inv, weight] + [c for n in range(chunks) for c in cots[n]]
        specs = [smem, dt, wide, state, state, gain_here, smem, smem, smem, vmem, vmem, vmem] + [vmem] * (2 * chunks)
        aliases = {}
        if so_far is not None:
            aliases = {len(operands): 0}
            operands.append(so_far)
            specs.append(anywhere)
        (grad,) = run(
            functools.partial(backward_kernel, begin),
            operands,
            specs,
            [shape(tokens, inner)],
            [wide],
            grid=(count,),
            scratch_shapes=[pltpu.VMEM((tokens, width), F32)],
            input_output_aliases=aliases,
            cost_estimate=small_cost,
            compiler_params=large,
        )
        return grad

    spread_rows("kept", kept)
    begun = 0
    for t in range(chunks + 2):
        if t < chunks:
            sum_side(t)
        if 1 <= t <= chunks:
            sum_all(t - 1)
        if t == chunks - 2:
            join("kept")
        if begun < len(batches) and t - 2 == batches[begun][-1]:
            send_rows(begun)
            if begun > 0:
                own_rows(begun - 1)
            begun += 1
    half = groups // 2
    end = len(batches) - 1
    if end > 1:
        join(0)
    grad_input = backward(0, half, None) if half else None
    own_rows(end)
    for b in range(1 if end > 1 else 0, end):
        join(b)
    grad_input = backward(half, groups - half, grad_input)
    join(end)
    (column,) = step(squares_kernel, gathered[end], [shape(8, LANES, dtype=F32)], NOTE * inner)
    columns = [column] + [
        lax.ppermute(column, "tensor", [(t, t ^ mask) for t in range(heads_over)]) for mask in range(1, heads_over)
    ]

    sizes = [len(batch) * piece for batch in batches]
    pair_spec = pl.BlockSpec((2 * owned, inner), lambda r: (r, 0))
    held_spec = pl.BlockSpec((owned, inner), lambda r: (0, 0))
    inputs = [own_global, own_momentum, *gathered["kept"], *[v for b in range(end + 1) for v in gathered[b]]]
    inputs += [*[deltas[b] for b in range(end + 1)], *columns]
    new_weight, new_global, new_momentum = run(
        functools.partial(weight_kernel, sizes, features * inner * heads_over),
        [places, *inputs],
        [smem] + [vmem] * len(inputs),
        [shape(features, inner), shape(owned, inner, dtype=F32), shape(owned, inner, dtype=F32)],
        [pair_spec, held_spec, held_spec],
        grid=(replicas // 2,),
        cost_estimate=small_cost,
        compiler_params=small,
    )
    return (grad_input, new_weight, new_global, new_momentum)


def solution(mesh):
    placed = (
        P("replica", "tensor"),
        P("replica", "tensor"),
        P("replica", "tensor"),
        P("replica", "tensor"),
        P("replica", "tensor"),
        P("tensor"),
        P("tensor"),
        P("tensor"),
        P("tensor"),
        P("replica", None, "tensor"),
        P("replica", "tensor"),
        P("replica", "tensor"),
        P(("replica", "tensor"), None),
    )
    return jax.shard_map(
        shards,
        mesh=mesh,
        in_specs=placed,
        out_specs=(
            P("replica", "tensor"),
            P(None, "tensor"),
            P("replica", "tensor"),
            P("replica", "tensor"),
        ),
        check_vma=False,
    )
```

```python
import functools

import jax
import jax.numpy as jnp
from jax import lax
from jax.experimental import pallas as pl
from jax.experimental.pallas import tpu as pltpu
from jax.sharding import PartitionSpec as P

HEAD_DIM = 64
STATE = 128
SPAN = 256
HALF = SPAN // 2
LANES = 128

inner_rate = 0.001
outer_rate = 0.7
outer_beta = 0.9
clip_rms = 0.005
LOG2E = 1.4426950408889634

F32 = jnp.float32
BF16 = jnp.bfloat16
NN = (((1,), (0,)), ((), ()))
NT = (((1,), (1,)), ((), ()))
TN = (((0,), (0,)), ((), ()))


def dot(a, b, dims):
    return lax.dot_general(a, b, dims, preferred_element_type=F32)


def silu(z):
    return z * (1.0 / (1.0 + jnp.exp(-z)))


def softplus(v):
    return jnp.maximum(v, 0.0) + jnp.log1p(jnp.exp(-jnp.abs(v)))


def iota(shape, axis):
    return lax.broadcasted_iota(jnp.int32, shape, axis)


def thirds(v):
    high = v.astype(BF16).astype(F32)
    middle = (v - high).astype(BF16).astype(F32)
    return jnp.concatenate([high, middle, v - high - middle], axis=0).astype(BF16)


def by_head(refs, first, per_group, tokens):
    row = iota((per_group, tokens), 0)
    rows = []
    for ref in refs:
        value = jnp.zeros((per_group, tokens), F32)
        for h in range(per_group):
            value = jnp.where(row == h, ref[first + h], value)
        rows.append(value)
    return rows


def head_tables(dt_ref, a_ref, bias_ref, first, per_group):
    bias, a_log = by_head([bias_ref, a_ref], first, per_group, dt_ref.shape[1])
    step = softplus(dt_ref[...] + bias)
    return step, -jnp.exp(a_log) * step * LOG2E


def span_tables(step, rate, lo, per_group, width):
    upper = (iota((SPAN, SPAN), 0) <= iota((SPAN, SPAN), 1)).astype(BF16)
    step_k = step[:, lo : lo + SPAN]
    sums = dot(thirds(rate[:, lo : lo + SPAN]), upper, NN)
    cum = sums[:per_group] + sums[per_group : 2 * per_group] + sums[2 * per_group :]
    spread = (iota((3 * per_group, width), 1) // HEAD_DIM == iota((3 * per_group, width), 0) % per_group).astype(BF16)
    turn = (iota((3 * per_group, per_group), 1) == iota((3 * per_group, per_group), 0) % per_group).astype(BF16)
    cum_col = dot(thirds(cum), turn, TN)
    step_x = dot(thirds(step_k), spread, TN)
    fade_x = dot(thirds(jnp.exp2(cum)), spread, TN)
    tail_x = dot(thirds(jnp.exp2(cum[:, SPAN - 1 :] - cum) * step_k), spread, TN)
    return cum, cum_col, step_x, fade_x, tail_x


def skip_row(skip_ref, first, per_group, width):
    head = iota((1, width), 1) // HEAD_DIM
    row = jnp.zeros((1, width), F32)
    for h in range(per_group):
        row = jnp.where(head == h, skip_ref[first + h], row)
    return row


def decay(gap, mask=None):
    return jnp.exp2(gap if mask is None else jnp.where(mask, gap, -1e30))


def even_odd(v):
    first = iota(v.shape, 1) % (2 * HEAD_DIM) < HEAD_DIM
    return jnp.where(first, v, 0.0).astype(BF16), jnp.where(first, 0.0, v).astype(BF16)


def forward_kernel(
    count, dt_ref, x_ref, z_ref, b_ref, c_ref, gain_ref, a_ref, bias_ref, skip_ref, *refs
):
    loads = [pltpu.make_async_copy(refs[n], refs[count + n], refs[-1].at[n]) for n in range(count)]
    normed_ref, inv_ref = refs[2 * count : 2 * count + 2]

    @pl.when(pl.program_id(0) == 0)
    def _():
        for load in loads:
            load.start()

    tokens, width = x_ref.shape
    per_group = width // HEAD_DIM
    first = pl.program_id(0) * per_group
    lanes_here = pl.ds(pl.multiple_of(pl.program_id(0) * width, LANES), width)
    step, rate = head_tables(dt_ref, a_ref, bias_ref, first, per_group)
    skip = skip_row(skip_ref, first, per_group, width)
    causal = iota((HALF, HALF), 0) >= iota((HALF, HALF), 1)
    spans = tokens // SPAN
    entering = None
    for k in range(spans):
        rows = slice(k * SPAN, (k + 1) * SPAN)
        cum, cum_col, step_x, fade_x, tail_x = span_tables(step, rate, k * SPAN, per_group, width)
        x = x_ref[rows, :].astype(F32)
        b, c = b_ref[rows, :], c_ref[rows, :]
        scores = dot(c, b, NT)
        values = even_odd(x * step_x)
        pieces = []
        for pair in range(per_group // 2):
            lanes = slice(2 * pair * HEAD_DIM, 2 * (pair + 1) * HEAD_DIM)
            tops, bottoms = [], []
            for h in (2 * pair, 2 * pair + 1):
                col, line = cum_col[:, h : h + 1], cum[h : h + 1, :]
                top = decay(col[:HALF] - line[:, :HALF], causal) * scores[:HALF, :HALF]
                left = decay(col[HALF:] - line[:, :HALF]) * scores[HALF:, :HALF]
                low = decay(col[HALF:] - line[:, HALF:], causal) * scores[HALF:, HALF:]
                tops.append(top.astype(BF16))
                bottoms += [left.astype(BF16), low.astype(BF16)]
            upper_values = jnp.concatenate([v[:HALF, lanes] for v in values], axis=0)
            all_values = jnp.concatenate([v[:, lanes] for v in values], axis=0)
            pieces.append(
                jnp.concatenate(
                    [
                        dot(jnp.concatenate(tops, axis=1), upper_values, NN),
                        dot(jnp.concatenate(bottoms, axis=1), all_values, NN),
                    ],
                    axis=0,
                )
            )
        ssd = jnp.concatenate(pieces, axis=1) + skip * x
        if entering is not None:
            ssd = ssd + dot(c, entering.astype(BF16), NN) * fade_x
        if k + 1 < spans:
            state = dot(b, (x * tail_x).astype(BF16), TN)
            entering = state if entering is None else entering * fade_x[SPAN - 1 :, :] + state
        gated = ssd * silu(z_ref[rows, :].astype(F32))
        inv = lax.rsqrt(jnp.mean(gated * gated, axis=1, keepdims=True) + 1e-05)
        normed_ref[rows, lanes_here] = (gated * inv * gain_ref[...]).astype(BF16)
        inv_ref[pl.program_id(0), rows, :] = inv

    @pl.when(pl.program_id(0) == pl.num_programs(0) - 1)
    def _():
        for load in loads:
            load.wait()


def kept_kernel(global_ref, momentum_ref, kept_ref):
    kept_ref[...] = (global_ref[...] - outer_rate * outer_beta * outer_beta * momentum_ref[...]).astype(BF16)


def project_kernel(chunks, place_ref, weight_ref, normed_ref, target_ref, *part_refs):
    replicas, owned, inner = weight_ref.shape
    held, features = target_ref.shape
    piece = part_refs[0].shape[0] // replicas
    tokens = normed_ref.shape[0]
    eye = (iota((held, held), 0) == iota((held, held), 1)).astype(BF16)
    turned = dot(target_ref[...], eye, TN).reshape(replicas, owned, held)
    here = iota((replicas * piece, tokens), 1) // held == place_ref[0]
    for n, part_ref in zip(chunks, part_refs):
        at = slice(n * piece, (n + 1) * piece)
        part = dot(weight_ref[:, at, :].reshape(replicas * piece, inner), normed_ref[...], NT)
        goal = jnp.concatenate([turned[:, at, :].reshape(replicas * piece, held)] * (tokens // held), axis=1)
        part_ref[...] = (part - jnp.where(here, goal, 0.0)).astype(BF16)


def add_kernel(a_ref, b_ref, sum_ref):
    sum_ref[...] = (a_ref[...].astype(F32) + b_ref[...].astype(F32)).astype(BF16)


def add_squares_kernel(a_ref, b_ref, sum_ref):
    sum_ref[...] = a_ref[...] + b_ref[...]


def gradient_kernel(batch, place_ref, *refs):
    count = len(batch)
    cot_refs, (normed_ref, weight_ref, keep_ref, send_ref) = refs[: 2 * count], refs[2 * count :]
    middle = place_ref[1] == 1
    odd = place_ref[2] == 1
    replicas, _, inner = weight_ref.shape
    piece = keep_ref.shape[1] // count
    tile = min(inner, 512)
    for n, chunk in enumerate(batch):
        cot = jnp.where(middle, cot_refs[2 * n][...], cot_refs[2 * n + 1][...])
        rows = slice(chunk * piece, (chunk + 1) * piece)
        at = slice(n * piece, (n + 1) * piece)
        for lo in range(0, inner, tile):
            cols = slice(lo, lo + tile)
            weight = weight_ref[:, rows, cols].reshape(replicas * piece, tile).astype(F32)
            new = weight - inner_rate * dot(cot, normed_ref[:, cols], NN)
            new = new.astype(BF16).reshape(replicas // 2, 2, piece, tile)
            keep_ref[:, at, cols] = jnp.where(odd, new[:, 1], new[:, 0])
            send_ref[:, at, cols] = jnp.where(odd, new[:, 0], new[:, 1])


def backward_kernel(
    begin, place_ref, dt_ref, z_ref, b_ref, c_ref, gain_ref, a_ref, bias_ref, skip_ref, normed_ref, inv_ref, weight_ref, *refs
):
    *cot_refs, dx_ref, dn_ref = refs
    if len(cot_refs) % 2:
        cot_refs = cot_refs[:-1]
    tokens, width = z_ref.shape
    per_group = width // HEAD_DIM
    group = pl.program_id(0) + begin
    first = group * per_group
    here = pl.ds(pl.multiple_of(group * width, LANES), width)
    replicas, owned, _ = weight_ref.shape
    chunks = len(cot_refs) // 2
    piece = owned // chunks
    middle = place_ref[1] == 1
    for n in range(chunks):
        weight = weight_ref[:, n * piece : (n + 1) * piece, here].reshape(replicas * piece, width)
        term = dot(jnp.where(middle, cot_refs[2 * n][...], cot_refs[2 * n + 1][...]), weight, TN)
        dn_ref[...] = term if n == 0 else dn_ref[...] + term
    step, rate = head_tables(dt_ref, a_ref, bias_ref, first, per_group)
    skip = skip_row(skip_ref, first, per_group, width)
    causal = iota((HALF, HALF), 1) >= iota((HALF, HALF), 0)
    spans = tokens // SPAN
    d_state = None
    for k in reversed(range(spans)):
        rows = slice(k * SPAN, (k + 1) * SPAN)
        cum, cum_col, step_x, fade_x, tail_x = span_tables(step, rate, k * SPAN, per_group, width)
        dn = dn_ref[rows, :]
        gain = gain_ref[...]
        normed = normed_ref[rows, here].astype(F32)
        shared = jnp.mean(normed * dn, axis=1, keepdims=True)
        d_gated = inv_ref[group, rows, :] * (gain * dn - (normed / gain) * shared)
        d_ssd = d_gated * silu(z_ref[rows, :].astype(F32))
        values = even_odd(d_ssd)
        b, c = b_ref[rows, :], c_ref[rows, :]
        scores = dot(b, c, NT)
        pieces = []
        for pair in range(per_group // 2):
            lanes = slice(2 * pair * HEAD_DIM, 2 * (pair + 1) * HEAD_DIM)
            tops, bottoms = [], []
            for h in (2 * pair, 2 * pair + 1):
                col, line = cum_col[:, h : h + 1], cum[h : h + 1, :]
                high = decay(line[:, :HALF] - col[:HALF], causal) * scores[:HALF, :HALF]
                right = decay(line[:, HALF:] - col[:HALF]) * scores[:HALF, HALF:]
                low = decay(line[:, HALF:] - col[HALF:], causal) * scores[HALF:, HALF:]
                tops += [high.astype(BF16), right.astype(BF16)]
                bottoms.append(low.astype(BF16))
            lower_values = jnp.concatenate([v[HALF:, lanes] for v in values], axis=0)
            all_values = jnp.concatenate([v[:, lanes] for v in values], axis=0)
            pieces.append(
                jnp.concatenate(
                    [
                        dot(jnp.concatenate(tops, axis=1), all_values, NN),
                        dot(jnp.concatenate(bottoms, axis=1), lower_values, NN),
                    ],
                    axis=0,
                )
            )
        dx = jnp.concatenate(pieces, axis=1) * step_x + skip * d_ssd
        if d_state is not None:
            dx = dx + dot(b, d_state.astype(BF16), NN) * tail_x
        dx_ref[rows, :] = dx.astype(BF16)
        if k > 0:
            own = dot(c, (d_ssd * fade_x).astype(BF16), TN)
            d_state = own if d_state is None else own + d_state * fade_x[SPAN - 1 :, :]


def pick_kernel(count, place_ref, *refs):
    terms, outs = refs[:count], refs[count:]
    my = lax.rem(lax.div(place_ref[3], place_ref[4]), len(outs))
    for mask, out_ref in enumerate(outs):
        at = lax.bitwise_xor(my, jnp.int32(mask))
        total = terms[0][:, at].astype(F32)
        for term in terms[1:]:
            total = total + term[:, at].astype(F32)
        out_ref[...] = total.astype(BF16)


def delta_kernel(count, lo, replicas, global_ref, before_ref, *refs):
    terms, (delta_ref, sent_ref, squares_ref) = refs[:count], refs[count:]
    rows, inner = delta_ref.shape
    total = terms[0][0].astype(F32)
    for term in terms[1:]:
        total = total + term[0].astype(F32)
    delta = global_ref[lo : lo + rows, :] - total / replicas
    delta_ref[...] = delta
    sent_ref[...] = delta.astype(BF16)
    squares = jnp.sum(delta * delta, axis=0, keepdims=True)
    squares = before_ref[...] + jnp.broadcast_to(jnp.sum(squares, axis=1, keepdims=True), before_ref.shape)
    squares_ref[...] = squares


def join_kernel(*refs):
    *parts, out_ref = refs
    lo = 0
    for part in parts:
        out_ref[lo : lo + part.shape[0]] = part[...]
        lo += part.shape[0]


def weight_kernel(sizes, entries, place_ref, global_ref, momentum_ref, *refs):
    count = len(sizes)
    pairs, deltas, squares = refs[: 2 * count + 2], refs[2 * count + 2 : 3 * count + 2], refs[3 * count + 2 : -3]
    new_ref, new_global_ref, new_momentum_ref = refs[-3:]
    mean = (squares[0][:1, :1] + squares[1][:1, :1]) / entries
    factor = jnp.minimum(1.0, clip_rms / jnp.sqrt(mean + 1e-06))
    at_chip = lax.bitwise_xor(pl.program_id(0), place_ref[3])
    owned = new_ref.shape[0] // 2
    scale = (outer_rate * (1.0 + outer_beta)) * factor

    def one_core(core, side):
        lo = 0
        for n, size in enumerate(sizes):
            kept = pairs[side][at_chip, lo : lo + size, :].astype(F32)
            delta = pairs[2 * n + 2 + side][at_chip, :size, :].astype(F32)
            new_ref[core * owned + lo : core * owned + lo + size, :] = (kept - scale * delta).astype(BF16)
            lo += size

    for own_core in range(2):

        @pl.when(place_ref[2] == own_core)
        def _():
            one_core(own_core, 0)
            one_core(1 - own_core, 1)

    @pl.when(pl.program_id(0) == 0)
    def _():
        lo = 0
        for n, size in enumerate(sizes):
            rows = slice(lo, lo + size)
            lo += size
            clipped = factor * deltas[n][...]
            new_momentum = outer_beta * momentum_ref[rows, :] + clipped
            new_momentum_ref[rows, :] = new_momentum
            new_global_ref[rows, :] = global_ref[rows, :] - outer_rate * (clipped + outer_beta * new_momentum)


def inward(axis_size):
    half = axis_size // 2
    hops = [[(s, s + 1), (axis_size - 1 - s, axis_size - 2 - s)] for s in range(half - 1)]
    return hops, [(half - 1, half), (half, half - 1)]


def in_turn(kernel, inputs, waits, outs):
    def body(*refs):
        end = inputs + waits + outs
        refs[end][...] = jnp.zeros_like(refs[end])
        kernel(*refs[:inputs], *refs[inputs + waits : end], *refs[end + 1 :])

    return body


def stages(replicas):
    bit, left, found = 1, replicas // 2, []
    while left > 1:
        bits = 2 if left >= 4 else 1
        found.append((bit, bits))
        bit, left = bit + bits, left >> bits
    return found


def shards(
    x_in,
    gate_z,
    b_proj,
    c_proj,
    dt_raw,
    a_log,
    dt_bias,
    skip_d,
    norm_gain,
    out_weight,
    global_weight,
    momentum,
    target,
):
    tokens, inner = x_in.shape
    features = out_weight.shape[1]
    replicas = lax.axis_size("replica")
    heads_over = lax.axis_size("tensor")
    groups = b_proj.shape[1] // STATE
    heads = dt_raw.shape[1]
    width = inner // groups
    owned = features // replicas
    chunks = max(2, min(4, owned // 16))
    batches = [list(range(chunks // 2)), list(range(chunks // 2, chunks))]
    piece = owned // chunks
    span_rows = replicas * piece
    place = lax.axis_index("tensor")
    me = lax.axis_index("replica")
    in_middle = (place == heads_over // 2 - 1) | (place == heads_over // 2)
    one = jnp.int32(1)
    places = jnp.stack([place, in_middle.astype(jnp.int32), lax.rem(me, 2), lax.div(me, 2), one]).astype(jnp.int32)
    stored = out_weight[0].reshape(replicas, owned, inner)
    gain = norm_gain.reshape(1, inner)
    dt_rows = dt_raw.T

    smem = pl.BlockSpec(memory_space=pltpu.SMEM)
    vmem = pl.BlockSpec(memory_space=pltpu.VMEM)
    anywhere = pl.BlockSpec(memory_space=pl.ANY)
    inv_spec = pl.BlockSpec((1, tokens, 1), lambda g: (g, 0, 0))
    large = pltpu.CompilerParams(vmem_limit_bytes=20 * 1024 * 1024)
    small = pltpu.CompilerParams(vmem_limit_bytes=12 * 1024 * 1024)
    small_cost = pl.CostEstimate(flops=1, bytes_accessed=1, transcendentals=0)

    turn = []

    def run(kernel, inputs, in_specs, outs, out_specs, waits=(), **options):
        waits = [*turn[-1:], *waits]
        done = jax.ShapeDtypeStruct((8, LANES), F32)
        *results, ran = pl.pallas_call(
            in_turn(kernel, len(inputs), len(waits), len(outs)),
            in_specs=[*in_specs, *[vmem] * len(waits)],
            out_specs=[*out_specs, vmem],
            out_shape=[*outs, done],
            **options,
        )(*inputs, *waits)
        turn.append(ran)
        return results

    def step(kernel, operands, outs, scalars=(), waits=()):
        return run(
            kernel,
            [*scalars, *operands],
            [smem] * len(scalars) + [vmem] * len(operands),
            outs,
            [vmem] * len(outs),
            waits,
            cost_estimate=small_cost,
            compiler_params=small,
        )

    def shape(*dims, dtype=BF16):
        return jax.ShapeDtypeStruct(dims, dtype)

    def in_hbm(*arrays):
        return [pltpu.with_memory_space_constraint(a, pltpu.HBM) for a in arrays]

    def group_specs(begin):
        wide = pl.BlockSpec((tokens, width), lambda g: (0, g + begin))
        state = pl.BlockSpec((tokens, STATE), lambda g: (0, g + begin))
        dt = pl.BlockSpec((heads // groups, tokens), lambda g: (g + begin, 0))
        return wide, state, dt, pl.BlockSpec((1, width), lambda g: (0, g + begin))

    def exchange(value, mask):
        return lax.ppermute(value, "replica", [(r, r ^ mask) for r in range(replicas)])

    gathered = {}

    def spread_rows(b, sent):
        (bit, bits), *_ = stages(replicas)
        gathered[b] = [sent[None]] + [exchange(sent[None], mask << bit) for mask in range(1, 1 << bits)]

    def join(b, waits=()):
        for at, (bit, bits) in enumerate(stages(replicas)):
            if at > 0:
                gathered[b] = [held] + [exchange(held, mask << bit) for mask in range(1, 1 << bits)]
            one = gathered[b][0]
            out = shape(len(gathered[b]) * one.shape[0], *one.shape[1:])
            (held,) = step(join_kernel, gathered[b], [out], waits=waits if at == 0 else ())
        gathered[b] = [held, exchange(held, 1)]

    by_group, by_state, dt_spec, gain_spec = group_specs(0)
    shared = in_hbm(dt_rows, gate_z, b_proj, c_proj, gain, a_log, dt_bias, skip_d)
    later = [stored, target, global_weight, momentum]
    (kept,) = step(kept_kernel, in_hbm(global_weight, momentum), [shape(owned, inner)])
    spread_rows("kept", kept)
    weight, goal, own_global, own_momentum, normed, inv = run(
        functools.partial(forward_kernel, len(later)),
        [shared[0], *in_hbm(x_in), *shared[1:], *in_hbm(*later)],
        [dt_spec, by_group, by_group, by_state, by_state, gain_spec, smem, smem, smem] + [anywhere] * len(later),
        [pltpu.VMEM(v.shape, v.dtype) for v in later] + [pltpu.VMEM((tokens, inner), BF16), pltpu.VMEM((groups, tokens, 1), F32)],
        [vmem] * (len(later) + 2),
        grid=(groups,),
        scratch_shapes=[pltpu.SemaphoreType.DMA((len(later),))],
        cost_estimate=small_cost,
        compiler_params=large,
    )

    part = shape(span_rows, tokens)

    def project(picked):
        kernel = functools.partial(project_kernel, picked)
        return step(kernel, [weight, normed, goal], [part] * len(picked), scalars=[places])

    in_hops, across = inward(heads_over)
    parts = project([0])
    parts += project(list(range(1, chunks)))
    first_landed = [lax.ppermute(p, "tensor", in_hops[0]) if in_hops else None for p in parts]
    sums, cots = {}, {}

    def sum_side(n):
        held = parts[n]
        for at, pairs in enumerate(in_hops):
            landed = first_landed[n] if at == 0 else lax.ppermute(held, "tensor", pairs)
            (held,) = step(add_kernel, [held, landed], [part])
        sums[n] = held

    def sum_all(n):
        (mid,) = step(add_kernel, [sums[n], lax.ppermute(sums[n], "tensor", across)], [part])
        out = mid
        for pairs in reversed(in_hops):
            back = lax.ppermute(out, "tensor", [(b, a) for a, b in pairs])
            out = back if pairs is in_hops[0] else jnp.where(in_middle, mid, back)
        cots[n] = (mid, out)

    terms, deltas = {}, {}
    tile = shape(8, LANES, dtype=F32)
    squares = {-1: jnp.zeros((8, LANES), F32)}

    def send_rows(b):
        batch = batches[b]
        rows = len(batch) * piece
        keep, send = step(
            functools.partial(gradient_kernel, batch),
            [c for n in batch for c in cots[n]] + [normed, weight],
            [shape(replicas // 2, rows, inner)] * 2,
            scalars=[places],
        )
        held, left = [keep, exchange(send, 1)], replicas // 2
        for bit, bits in stages(replicas):
            ways = 1 << bits
            left //= ways
            cut = [h.reshape(left, ways, rows, inner) for h in held]
            picked = step(
                functools.partial(pick_kernel, len(cut)),
                cut,
                [shape(left, rows, inner)] * ways,
                scalars=[places.at[4].set(1 << (bit - 1))] if bit > 1 else [places],
            )
            held = [picked[0]] + [exchange(picked[mask], mask << bit) for mask in range(1, ways)]
        terms[b] = held

    def own_rows(b, waits=()):
        batch = batches[b]
        rows = len(batch) * piece
        deltas[b], sent, squares[b] = step(
            functools.partial(delta_kernel, len(terms[b]), batch[0] * piece, replicas),
            [own_global, squares[b - 1], *terms[b]],
            [shape(rows, inner, dtype=F32), shape(rows, inner), tile],
            waits=waits,
        )
        spread_rows(b, sent)

    def backward(begin, count, so_far):
        wide, state, dt, gain_here = group_specs(begin)
        operands = [places, *shared, normed, inv, weight] + [c for n in range(chunks) for c in cots[n]]
        specs = [smem, dt, wide, state, state, gain_here, smem, smem, smem, vmem, vmem, vmem] + [vmem] * (2 * chunks)
        aliases = {}
        if so_far is not None:
            aliases = {len(operands): 0}
            operands.append(so_far)
            specs.append(anywhere)
        (grad,) = run(
            functools.partial(backward_kernel, begin),
            operands,
            specs,
            [shape(tokens, inner)],
            [wide],
            grid=(count,),
            scratch_shapes=[pltpu.VMEM((tokens, width), F32)],
            input_output_aliases=aliases,
            cost_estimate=small_cost,
            compiler_params=large,
        )
        return grad

    first, second = range(2)
    for t in range(chunks + 2):
        if t < chunks:
            sum_side(t)
        if t == 0:
            join("kept")
        if 1 <= t <= chunks:
            sum_all(t - 1)
        if t - 2 == batches[first][-1]:
            send_rows(first)
    own_rows(first, gathered["kept"][1:])
    send_rows(second)
    half = groups // 2
    grad_input = backward(0, half, None) if half else None
    join(first)
    grad_input = backward(half, groups - half, grad_input)
    own_rows(second, gathered[first][1:])
    total = squares[second]
    for axis, bits in (("tensor", range(heads_over.bit_length() - 1)), ("replica", range(1, replicas.bit_length() - 1))):
        for bit in bits:
            pairs = [(r, r ^ (1 << bit)) for r in range(lax.axis_size(axis))]
            (total,) = step(add_squares_kernel, [total, lax.ppermute(total, axis, pairs)], [tile])
    join(second)
    columns = [total, exchange(total, 1)]

    sizes = [len(batch) * piece for batch in batches]
    pair_spec = pl.BlockSpec((2 * owned, inner), lambda r: (r, 0))
    held_spec = pl.BlockSpec((owned, inner), lambda r: (0, 0))
    inputs = [own_global, own_momentum, *gathered["kept"], *gathered[first], *gathered[second]]
    inputs += [deltas[first], deltas[second], *columns]
    new_weight, new_global, new_momentum = run(
        functools.partial(weight_kernel, sizes, features * inner * heads_over),
        [places, *inputs],
        [smem] + [vmem] * len(inputs),
        [shape(features, inner), shape(owned, inner, dtype=F32), shape(owned, inner, dtype=F32)],
        [pair_spec, held_spec, held_spec],
        grid=(replicas // 2,),
        cost_estimate=small_cost,
        compiler_params=small,
    )
    return (grad_input, new_weight, new_global, new_momentum)


def solution(mesh):
    placed = (
        P("replica", "tensor"),
        P("replica", "tensor"),
        P("replica", "tensor"),
        P("replica", "tensor"),
        P("replica", "tensor"),
        P("tensor"),
        P("tensor"),
        P("tensor"),
        P("tensor"),
        P("replica", None, "tensor"),
        P("replica", "tensor"),
        P("replica", "tensor"),
        P(("replica", "tensor"), None),
    )
    return jax.shard_map(
        shards,
        mesh=mesh,
        in_specs=placed,
        out_specs=(
            P("replica", "tensor"),
            P(None, "tensor"),
            P("replica", "tensor"),
            P("replica", "tensor"),
        ),
        check_vma=False,
    )
```

```python
import functools

import jax
import jax.numpy as jnp
from jax import lax
from jax.experimental import pallas as pl
from jax.experimental.pallas import tpu as pltpu
from jax.sharding import PartitionSpec as P

HEAD_DIM = 64
STATE = 128
SPAN = 256
HALF = SPAN // 2
LANES = 128

inner_rate = 0.001
outer_rate = 0.7
outer_beta = 0.9
clip_rms = 0.005
LOG2E = 1.4426950408889634

F32 = jnp.float32
BF16 = jnp.bfloat16
NN = (((1,), (0,)), ((), ()))
NT = (((1,), (1,)), ((), ()))
TN = (((0,), (0,)), ((), ()))


def dot(a, b, dims):
    return lax.dot_general(a, b, dims, preferred_element_type=F32)


def silu(z):
    return z * (1.0 / (1.0 + jnp.exp(-z)))


def softplus(v):
    return jnp.maximum(v, 0.0) + jnp.log1p(jnp.exp(-jnp.abs(v)))


def iota(shape, axis):
    return lax.broadcasted_iota(jnp.int32, shape, axis)


def thirds(v):
    high = v.astype(BF16).astype(F32)
    middle = (v - high).astype(BF16).astype(F32)
    return jnp.concatenate([high, middle, v - high - middle], axis=0).astype(BF16)


def by_head(refs, first, per_group, tokens):
    row = iota((per_group, tokens), 0)
    rows = []
    for ref in refs:
        value = jnp.zeros((per_group, tokens), F32)
        for h in range(per_group):
            value = jnp.where(row == h, ref[first + h], value)
        rows.append(value)
    return rows


def head_tables(dt_ref, a_ref, bias_ref, first, per_group):
    bias, a_log = by_head([bias_ref, a_ref], first, per_group, dt_ref.shape[1])
    step = softplus(dt_ref[...] + bias)
    return step, -jnp.exp(a_log) * step * LOG2E


def span_tables(step, rate, lo, per_group, width):
    upper = (iota((SPAN, SPAN), 0) <= iota((SPAN, SPAN), 1)).astype(BF16)
    step_k = step[:, lo : lo + SPAN]
    sums = dot(thirds(rate[:, lo : lo + SPAN]), upper, NN)
    cum = sums[:per_group] + sums[per_group : 2 * per_group] + sums[2 * per_group :]
    spread = (iota((3 * per_group, width), 1) // HEAD_DIM == iota((3 * per_group, width), 0) % per_group).astype(BF16)
    turn = (iota((3 * per_group, per_group), 1) == iota((3 * per_group, per_group), 0) % per_group).astype(BF16)
    cum_col = dot(thirds(cum), turn, TN)
    step_x = dot(thirds(step_k), spread, TN)
    fade_x = dot(thirds(jnp.exp2(cum)), spread, TN)
    tail_x = dot(thirds(jnp.exp2(cum[:, SPAN - 1 :] - cum) * step_k), spread, TN)
    return cum, cum_col, step_x, fade_x, tail_x


def skip_row(skip_ref, first, per_group, width):
    head = iota((1, width), 1) // HEAD_DIM
    row = jnp.zeros((1, width), F32)
    for h in range(per_group):
        row = jnp.where(head == h, skip_ref[first + h], row)
    return row


def decay(gap, mask=None):
    return jnp.exp2(gap if mask is None else jnp.where(mask, gap, -1e30))


def even_odd(v):
    first = iota(v.shape, 1) % (2 * HEAD_DIM) < HEAD_DIM
    return jnp.where(first, v, 0.0).astype(BF16), jnp.where(first, 0.0, v).astype(BF16)


def forward_kernel(
    count, dt_ref, x_ref, z_ref, b_ref, c_ref, gain_ref, a_ref, bias_ref, skip_ref, *refs
):
    loads = [pltpu.make_async_copy(refs[n], refs[count + n], refs[-1].at[n]) for n in range(count)]
    normed_ref, inv_ref = refs[2 * count : 2 * count + 2]

    @pl.when(pl.program_id(0) == 0)
    def _():
        for load in loads:
            load.start()

    tokens, width = x_ref.shape
    per_group = width // HEAD_DIM
    first = pl.program_id(0) * per_group
    lanes_here = pl.ds(pl.multiple_of(pl.program_id(0) * width, LANES), width)
    step, rate = head_tables(dt_ref, a_ref, bias_ref, first, per_group)
    skip = skip_row(skip_ref, first, per_group, width)
    causal = iota((HALF, HALF), 0) >= iota((HALF, HALF), 1)
    spans = tokens // SPAN
    entering = None
    for k in range(spans):
        rows = slice(k * SPAN, (k + 1) * SPAN)
        cum, cum_col, step_x, fade_x, tail_x = span_tables(step, rate, k * SPAN, per_group, width)
        x = x_ref[rows, :].astype(F32)
        b, c = b_ref[rows, :], c_ref[rows, :]
        scores = dot(c, b, NT)
        values = even_odd(x * step_x)
        pieces = []
        for pair in range(per_group // 2):
            lanes = slice(2 * pair * HEAD_DIM, 2 * (pair + 1) * HEAD_DIM)
            tops, bottoms = [], []
            for h in (2 * pair, 2 * pair + 1):
                col, line = cum_col[:, h : h + 1], cum[h : h + 1, :]
                top = decay(col[:HALF] - line[:, :HALF], causal) * scores[:HALF, :HALF]
                left = decay(col[HALF:] - line[:, :HALF]) * scores[HALF:, :HALF]
                low = decay(col[HALF:] - line[:, HALF:], causal) * scores[HALF:, HALF:]
                tops.append(top.astype(BF16))
                bottoms += [left.astype(BF16), low.astype(BF16)]
            upper_values = jnp.concatenate([v[:HALF, lanes] for v in values], axis=0)
            all_values = jnp.concatenate([v[:, lanes] for v in values], axis=0)
            pieces.append(
                jnp.concatenate(
                    [
                        dot(jnp.concatenate(tops, axis=1), upper_values, NN),
                        dot(jnp.concatenate(bottoms, axis=1), all_values, NN),
                    ],
                    axis=0,
                )
            )
        ssd = jnp.concatenate(pieces, axis=1) + skip * x
        if entering is not None:
            ssd = ssd + dot(c, entering.astype(BF16), NN) * fade_x
        if k + 1 < spans:
            state = dot(b, (x * tail_x).astype(BF16), TN)
            entering = state if entering is None else entering * fade_x[SPAN - 1 :, :] + state
        gated = ssd * silu(z_ref[rows, :].astype(F32))
        inv = lax.rsqrt(jnp.mean(gated * gated, axis=1, keepdims=True) + 1e-05)
        normed_ref[rows, lanes_here] = (gated * inv * gain_ref[...]).astype(BF16)
        inv_ref[pl.program_id(0), rows, :] = inv

    @pl.when(pl.program_id(0) == pl.num_programs(0) - 1)
    def _():
        for load in loads:
            load.wait()


def kept_kernel(global_ref, momentum_ref, kept_ref):
    kept_ref[...] = (global_ref[...] - outer_rate * outer_beta * outer_beta * momentum_ref[...]).astype(BF16)


def project_kernel(chunks, place_ref, weight_ref, normed_ref, target_ref, *part_refs):
    replicas, owned, inner = weight_ref.shape
    held, features = target_ref.shape
    piece = part_refs[0].shape[0] // replicas
    tokens = normed_ref.shape[0]
    eye = (iota((held, held), 0) == iota((held, held), 1)).astype(BF16)
    turned = dot(target_ref[...], eye, TN).reshape(replicas, owned, held)
    here = iota((replicas * piece, tokens), 1) // held == place_ref[0]
    for n, part_ref in zip(chunks, part_refs):
        at = slice(n * piece, (n + 1) * piece)
        part = dot(weight_ref[:, at, :].reshape(replicas * piece, inner), normed_ref[...], NT)
        goal = jnp.concatenate([turned[:, at, :].reshape(replicas * piece, held)] * (tokens // held), axis=1)
        part_ref[...] = (part - jnp.where(here, goal, 0.0)).astype(BF16)


def add_kernel(a_ref, b_ref, sum_ref):
    sum_ref[...] = (a_ref[...].astype(F32) + b_ref[...].astype(F32)).astype(BF16)


def add_squares_kernel(a_ref, b_ref, sum_ref):
    sum_ref[...] = a_ref[...] + b_ref[...]


def gradient_kernel(batch, place_ref, *refs):
    count = len(batch)
    cot_refs, (normed_ref, weight_ref, keep_ref, send_ref) = refs[: 2 * count], refs[2 * count :]
    middle = place_ref[1] == 1
    odd = place_ref[2] == 1
    replicas, _, inner = weight_ref.shape
    piece = keep_ref.shape[1] // count
    tile = min(inner, 512)
    for n, chunk in enumerate(batch):
        cot = jnp.where(middle, cot_refs[2 * n][...], cot_refs[2 * n + 1][...])
        rows = slice(chunk * piece, (chunk + 1) * piece)
        at = slice(n * piece, (n + 1) * piece)
        for lo in range(0, inner, tile):
            cols = slice(lo, lo + tile)
            weight = weight_ref[:, rows, cols].reshape(replicas * piece, tile).astype(F32)
            new = weight - inner_rate * dot(cot, normed_ref[:, cols], NN)
            new = new.astype(BF16).reshape(replicas // 2, 2, piece, tile)
            keep_ref[:, at, cols] = jnp.where(odd, new[:, 1], new[:, 0])
            send_ref[:, at, cols] = jnp.where(odd, new[:, 0], new[:, 1])


def backward_kernel(
    begin, place_ref, dt_ref, z_ref, b_ref, c_ref, gain_ref, a_ref, bias_ref, skip_ref, normed_ref, inv_ref, weight_ref, *refs
):
    *cot_refs, dx_ref, dn_ref = refs
    if len(cot_refs) % 2:
        cot_refs = cot_refs[:-1]
    tokens, width = z_ref.shape
    per_group = width // HEAD_DIM
    group = pl.program_id(0) + begin
    first = group * per_group
    here = pl.ds(pl.multiple_of(group * width, LANES), width)
    replicas, owned, _ = weight_ref.shape
    chunks = len(cot_refs) // 2
    piece = owned // chunks
    middle = place_ref[1] == 1
    for n in range(chunks):
        weight = weight_ref[:, n * piece : (n + 1) * piece, here].reshape(replicas * piece, width)
        term = dot(jnp.where(middle, cot_refs[2 * n][...], cot_refs[2 * n + 1][...]), weight, TN)
        dn_ref[...] = term if n == 0 else dn_ref[...] + term
    step, rate = head_tables(dt_ref, a_ref, bias_ref, first, per_group)
    skip = skip_row(skip_ref, first, per_group, width)
    causal = iota((HALF, HALF), 1) >= iota((HALF, HALF), 0)
    spans = tokens // SPAN
    d_state = None
    for k in reversed(range(spans)):
        rows = slice(k * SPAN, (k + 1) * SPAN)
        cum, cum_col, step_x, fade_x, tail_x = span_tables(step, rate, k * SPAN, per_group, width)
        dn = dn_ref[rows, :]
        gain = gain_ref[...]
        normed = normed_ref[rows, here].astype(F32)
        shared = jnp.mean(normed * dn, axis=1, keepdims=True)
        d_gated = inv_ref[group, rows, :] * (gain * dn - (normed / gain) * shared)
        d_ssd = d_gated * silu(z_ref[rows, :].astype(F32))
        values = even_odd(d_ssd)
        b, c = b_ref[rows, :], c_ref[rows, :]
        scores = dot(b, c, NT)
        pieces = []
        for pair in range(per_group // 2):
            lanes = slice(2 * pair * HEAD_DIM, 2 * (pair + 1) * HEAD_DIM)
            tops, bottoms = [], []
            for h in (2 * pair, 2 * pair + 1):
                col, line = cum_col[:, h : h + 1], cum[h : h + 1, :]
                high = decay(line[:, :HALF] - col[:HALF], causal) * scores[:HALF, :HALF]
                right = decay(line[:, HALF:] - col[:HALF]) * scores[:HALF, HALF:]
                low = decay(line[:, HALF:] - col[HALF:], causal) * scores[HALF:, HALF:]
                tops += [high.astype(BF16), right.astype(BF16)]
                bottoms.append(low.astype(BF16))
            lower_values = jnp.concatenate([v[HALF:, lanes] for v in values], axis=0)
            all_values = jnp.concatenate([v[:, lanes] for v in values], axis=0)
            pieces.append(
                jnp.concatenate(
                    [
                        dot(jnp.concatenate(tops, axis=1), all_values, NN),
                        dot(jnp.concatenate(bottoms, axis=1), lower_values, NN),
                    ],
                    axis=0,
                )
            )
        dx = jnp.concatenate(pieces, axis=1) * step_x + skip * d_ssd
        if d_state is not None:
            dx = dx + dot(b, d_state.astype(BF16), NN) * tail_x
        dx_ref[rows, :] = dx.astype(BF16)
        if k > 0:
            own = dot(c, (d_ssd * fade_x).astype(BF16), TN)
            d_state = own if d_state is None else own + d_state * fade_x[SPAN - 1 :, :]


def pick_kernel(count, place_ref, *refs):
    terms, outs = refs[:count], refs[count:]
    my = lax.rem(lax.div(place_ref[3], place_ref[4]), len(outs))
    for mask, out_ref in enumerate(outs):
        at = lax.bitwise_xor(my, jnp.int32(mask))
        total = terms[0][:, at].astype(F32)
        for term in terms[1:]:
            total = total + term[:, at].astype(F32)
        out_ref[...] = total.astype(BF16)


def delta_kernel(count, lo, replicas, global_ref, before_ref, *refs):
    terms, (delta_ref, sent_ref, squares_ref) = refs[:count], refs[count:]
    rows, inner = delta_ref.shape
    total = terms[0][0].astype(F32)
    for term in terms[1:]:
        total = total + term[0].astype(F32)
    delta = global_ref[lo : lo + rows, :] - total / replicas
    delta_ref[...] = delta
    sent_ref[...] = delta.astype(BF16)
    squares = jnp.sum(delta * delta, axis=0, keepdims=True)
    squares = before_ref[...] + jnp.broadcast_to(jnp.sum(squares, axis=1, keepdims=True), before_ref.shape)
    squares_ref[...] = squares


def join_kernel(*refs):
    *parts, out_ref = refs
    lo = 0
    for part in parts:
        out_ref[lo : lo + part.shape[0]] = part[...]
        lo += part.shape[0]


def weight_kernel(sizes, entries, place_ref, global_ref, momentum_ref, *refs):
    count = len(sizes)
    pairs, deltas, squares = refs[: 2 * count + 2], refs[2 * count + 2 : 3 * count + 2], refs[3 * count + 2 : -3]
    new_ref, new_global_ref, new_momentum_ref = refs[-3:]
    mean = (squares[0][:1, :1] + squares[1][:1, :1]) / entries
    factor = jnp.minimum(1.0, clip_rms / jnp.sqrt(mean + 1e-06))
    at_chip = lax.bitwise_xor(pl.program_id(0), place_ref[3])
    owned = new_ref.shape[0] // 2
    scale = (outer_rate * (1.0 + outer_beta)) * factor

    def one_core(core, side):
        lo = 0
        for n, size in enumerate(sizes):
            kept = pairs[side][at_chip, lo : lo + size, :].astype(F32)
            delta = pairs[2 * n + 2 + side][at_chip, :size, :].astype(F32)
            new_ref[core * owned + lo : core * owned + lo + size, :] = (kept - scale * delta).astype(BF16)
            lo += size

    for own_core in range(2):

        @pl.when(place_ref[2] == own_core)
        def _():
            one_core(own_core, 0)
            one_core(1 - own_core, 1)

    @pl.when(pl.program_id(0) == 0)
    def _():
        lo = 0
        for n, size in enumerate(sizes):
            rows = slice(lo, lo + size)
            lo += size
            clipped = factor * deltas[n][...]
            new_momentum = outer_beta * momentum_ref[rows, :] + clipped
            new_momentum_ref[rows, :] = new_momentum
            new_global_ref[rows, :] = global_ref[rows, :] - outer_rate * (clipped + outer_beta * new_momentum)


def inward(axis_size):
    half = axis_size // 2
    hops = [[(s, s + 1), (axis_size - 1 - s, axis_size - 2 - s)] for s in range(half - 1)]
    return hops, [(half - 1, half), (half, half - 1)]


def in_turn(kernel, inputs, waits, outs):
    def body(*refs):
        end = inputs + waits + outs
        refs[end][...] = jnp.zeros_like(refs[end])
        kernel(*refs[:inputs], *refs[inputs + waits : end], *refs[end + 1 :])

    return body


def stages(replicas):
    bit, left, found = 1, replicas // 2, []
    while left > 1:
        bits = 2 if left >= 4 else 1
        found.append((bit, bits))
        bit, left = bit + bits, left >> bits
    return found


def shards(
    x_in,
    gate_z,
    b_proj,
    c_proj,
    dt_raw,
    a_log,
    dt_bias,
    skip_d,
    norm_gain,
    out_weight,
    global_weight,
    momentum,
    target,
):
    tokens, inner = x_in.shape
    features = out_weight.shape[1]
    replicas = lax.axis_size("replica")
    heads_over = lax.axis_size("tensor")
    groups = b_proj.shape[1] // STATE
    heads = dt_raw.shape[1]
    width = inner // groups
    owned = features // replicas
    chunks = max(2, min(4, owned // 16))
    batches = [list(range(chunks // 2)), list(range(chunks // 2, chunks))]
    piece = owned // chunks
    span_rows = replicas * piece
    place = lax.axis_index("tensor")
    me = lax.axis_index("replica")
    in_middle = (place == heads_over // 2 - 1) | (place == heads_over // 2)
    one = jnp.int32(1)
    places = jnp.stack([place, in_middle.astype(jnp.int32), lax.rem(me, 2), lax.div(me, 2), one]).astype(jnp.int32)
    stored = out_weight[0].reshape(replicas, owned, inner)
    gain = norm_gain.reshape(1, inner)
    dt_rows = dt_raw.T

    smem = pl.BlockSpec(memory_space=pltpu.SMEM)
    vmem = pl.BlockSpec(memory_space=pltpu.VMEM)
    anywhere = pl.BlockSpec(memory_space=pl.ANY)
    inv_spec = pl.BlockSpec((1, tokens, 1), lambda g: (g, 0, 0))
    large = pltpu.CompilerParams(vmem_limit_bytes=20 * 1024 * 1024)
    small = pltpu.CompilerParams(vmem_limit_bytes=12 * 1024 * 1024)
    small_cost = pl.CostEstimate(flops=1, bytes_accessed=1, transcendentals=0)
    large_cost = pl.CostEstimate(flops=30_000_000_000, bytes_accessed=1, transcendentals=0)

    turn = []

    def run(kernel, inputs, in_specs, outs, out_specs, waits=(), **options):
        waits = [*turn[-1:], *waits]
        done = jax.ShapeDtypeStruct((8, LANES), F32)
        *results, ran = pl.pallas_call(
            in_turn(kernel, len(inputs), len(waits), len(outs)),
            in_specs=[*in_specs, *[vmem] * len(waits)],
            out_specs=[*out_specs, vmem],
            out_shape=[*outs, done],
            **options,
        )(*inputs, *waits)
        turn.append(ran)
        return results

    def step(kernel, operands, outs, scalars=(), waits=(), cost=small_cost):
        return run(
            kernel,
            [*scalars, *operands],
            [smem] * len(scalars) + [vmem] * len(operands),
            outs,
            [vmem] * len(outs),
            waits,
            cost_estimate=cost,
            compiler_params=small,
        )

    def shape(*dims, dtype=BF16):
        return jax.ShapeDtypeStruct(dims, dtype)

    def in_hbm(*arrays):
        return [pltpu.with_memory_space_constraint(a, pltpu.HBM) for a in arrays]

    def group_specs(begin):
        wide = pl.BlockSpec((tokens, width), lambda g: (0, g + begin))
        state = pl.BlockSpec((tokens, STATE), lambda g: (0, g + begin))
        dt = pl.BlockSpec((heads // groups, tokens), lambda g: (g + begin, 0))
        return wide, state, dt, pl.BlockSpec((1, width), lambda g: (0, g + begin))

    def exchange(value, mask):
        return lax.ppermute(value, "replica", [(r, r ^ mask) for r in range(replicas)])

    gathered = {}

    def spread_rows(b, sent):
        (bit, bits), *_ = stages(replicas)
        gathered[b] = [sent[None]] + [exchange(sent[None], mask << bit) for mask in range(1, 1 << bits)]

    def join(b, waits=()):
        for at, (bit, bits) in enumerate(stages(replicas)):
            if at > 0:
                gathered[b] = [held] + [exchange(held, mask << bit) for mask in range(1, 1 << bits)]
            one = gathered[b][0]
            out = shape(len(gathered[b]) * one.shape[0], *one.shape[1:])
            (held,) = step(join_kernel, gathered[b], [out], waits=waits if at == 0 else ())
        gathered[b] = [held, exchange(held, 1)]

    by_group, by_state, dt_spec, gain_spec = group_specs(0)
    shared = in_hbm(dt_rows, gate_z, b_proj, c_proj, gain, a_log, dt_bias, skip_d)
    later = [stored, target, global_weight, momentum]
    (kept,) = step(kept_kernel, in_hbm(global_weight, momentum), [shape(owned, inner)])
    spread_rows("kept", kept)
    weight, goal, own_global, own_momentum, normed, inv = run(
        functools.partial(forward_kernel, len(later)),
        [shared[0], *in_hbm(x_in), *shared[1:], *in_hbm(*later)],
        [dt_spec, by_group, by_group, by_state, by_state, gain_spec, smem, smem, smem] + [anywhere] * len(later),
        [pltpu.VMEM(v.shape, v.dtype) for v in later] + [pltpu.VMEM((tokens, inner), BF16), pltpu.VMEM((groups, tokens, 1), F32)],
        [vmem] * (len(later) + 2),
        grid=(groups,),
        scratch_shapes=[pltpu.SemaphoreType.DMA((len(later),))],
        cost_estimate=small_cost,
        compiler_params=large,
    )

    part = shape(span_rows, tokens)

    def project(picked):
        kernel = functools.partial(project_kernel, picked)
        return step(kernel, [weight, normed, goal], [part] * len(picked), scalars=[places])

    in_hops, across = inward(heads_over)
    parts = project([0])
    parts += project(list(range(1, chunks)))
    first_landed = [lax.ppermute(p, "tensor", in_hops[0]) if in_hops else None for p in parts]
    sums, cots = {}, {}

    def sum_side(n):
        held = parts[n]
        for at, pairs in enumerate(in_hops):
            landed = first_landed[n] if at == 0 else lax.ppermute(held, "tensor", pairs)
            (held,) = step(add_kernel, [held, landed], [part])
        sums[n] = held

    def sum_all(n, waits=(), cost=small_cost):
        landed = lax.ppermute(sums[n], "tensor", across)
        (mid,) = step(add_kernel, [sums[n], landed], [part], waits=waits, cost=cost)
        out = mid
        for pairs in reversed(in_hops):
            back = lax.ppermute(out, "tensor", [(b, a) for a, b in pairs])
            out = back if pairs is in_hops[0] else jnp.where(in_middle, mid, back)
        cots[n] = (mid, out)

    terms, deltas = {}, {}
    tile = shape(8, LANES, dtype=F32)
    squares = {-1: jnp.zeros((8, LANES), F32)}

    def new_rows(b, waits=()):
        batch = batches[b]
        rows = len(batch) * piece
        keep, send = step(
            functools.partial(gradient_kernel, batch),
            [c for n in batch for c in cots[n]] + [normed, weight],
            [shape(replicas // 2, rows, inner)] * 2,
            scalars=[places],
            waits=waits,
        )
        return [keep, exchange(send, 1)]

    def send_rows(b, held):
        rows, left = len(batches[b]) * piece, replicas // 2
        for bit, bits in stages(replicas):
            ways = 1 << bits
            left //= ways
            cut = [h.reshape(left, ways, rows, inner) for h in held]
            picked = step(
                functools.partial(pick_kernel, len(cut)),
                cut,
                [shape(left, rows, inner)] * ways,
                scalars=[places.at[4].set(1 << (bit - 1))] if bit > 1 else [places],
            )
            held = [picked[0]] + [exchange(picked[mask], mask << bit) for mask in range(1, ways)]
        terms[b] = held

    def own_rows(b, cost=small_cost):
        batch = batches[b]
        rows = len(batch) * piece
        deltas[b], sent, squares[b] = step(
            functools.partial(delta_kernel, len(terms[b]), batch[0] * piece, replicas),
            [own_global, squares[b - 1], *terms[b]],
            [shape(rows, inner, dtype=F32), shape(rows, inner), tile],
            cost=cost,
        )
        spread_rows(b, sent)

    def backward(begin, count, so_far):
        wide, state, dt, gain_here = group_specs(begin)
        operands = [places, *shared, normed, inv, weight] + [c for n in range(chunks) for c in cots[n]]
        specs = [smem, dt, wide, state, state, gain_here, smem, smem, smem, vmem, vmem, vmem] + [vmem] * (2 * chunks)
        aliases = {}
        if so_far is not None:
            aliases = {len(operands): 0}
            operands.append(so_far)
            specs.append(anywhere)
        (grad,) = run(
            functools.partial(backward_kernel, begin),
            operands,
            specs,
            [shape(tokens, inner)],
            [wide],
            grid=(count,),
            scratch_shapes=[pltpu.VMEM((tokens, width), F32)],
            input_output_aliases=aliases,
            cost_estimate=large_cost,
            compiler_params=large,
        )
        return grad

    first, second = range(2)
    for t in range(chunks):
        sum_side(t)
        if t == 0:
            join("kept")
        else:
            sum_all(t - 1)
    held_first = new_rows(first)
    sum_all(chunks - 1, [cots[chunks - 2][1], gathered["kept"][1]], large_cost)
    send_rows(first, held_first)
    held_second = new_rows(second)
    own_rows(first, large_cost)
    send_rows(second, held_second)
    half = groups // 2
    grad_input = backward(0, half, None) if half else None
    join(first)
    grad_input = backward(half, groups - half, grad_input)
    own_rows(second)
    total = squares[second]
    for axis, bits in (("tensor", range(heads_over.bit_length() - 1)), ("replica", range(1, replicas.bit_length() - 1))):
        for bit in bits:
            pairs = [(r, r ^ (1 << bit)) for r in range(lax.axis_size(axis))]
            (total,) = step(add_squares_kernel, [total, lax.ppermute(total, axis, pairs)], [tile])
    join(second, gathered[first][1:])
    columns = [total, exchange(total, 1)]

    sizes = [len(batch) * piece for batch in batches]
    pair_spec = pl.BlockSpec((2 * owned, inner), lambda r: (r, 0))
    held_spec = pl.BlockSpec((owned, inner), lambda r: (0, 0))
    inputs = [own_global, own_momentum, *gathered["kept"], *gathered[first], *gathered[second]]
    inputs += [deltas[first], deltas[second], *columns]
    new_weight, new_global, new_momentum = run(
        functools.partial(weight_kernel, sizes, features * inner * heads_over),
        [places, *inputs],
        [smem] + [vmem] * len(inputs),
        [shape(features, inner), shape(owned, inner, dtype=F32), shape(owned, inner, dtype=F32)],
        [pair_spec, held_spec, held_spec],
        grid=(replicas // 2,),
        cost_estimate=small_cost,
        compiler_params=small,
    )
    return (grad_input, new_weight, new_global, new_momentum)


def solution(mesh):
    placed = (
        P("replica", "tensor"),
        P("replica", "tensor"),
        P("replica", "tensor"),
        P("replica", "tensor"),
        P("replica", "tensor"),
        P("tensor"),
        P("tensor"),
        P("tensor"),
        P("tensor"),
        P("replica", None, "tensor"),
        P("replica", "tensor"),
        P("replica", "tensor"),
        P(("replica", "tensor"), None),
    )
    return jax.shard_map(
        shards,
        mesh=mesh,
        in_specs=placed,
        out_specs=(
            P("replica", "tensor"),
            P(None, "tensor"),
            P("replica", "tensor"),
            P("replica", "tensor"),
        ),
        check_vma=False,
    )
```

```python
import functools

import jax
import jax.numpy as jnp
from jax import lax
from jax.experimental import pallas as pl
from jax.experimental.pallas import tpu as pltpu
from jax.sharding import PartitionSpec as P

HEAD_DIM = 64
STATE = 128
SPAN = 256
HALF = SPAN // 2
LANES = 128

inner_rate = 0.001
outer_rate = 0.7
outer_beta = 0.9
clip_rms = 0.005
LOG2E = 1.4426950408889634

F32 = jnp.float32
BF16 = jnp.bfloat16
NN = (((1,), (0,)), ((), ()))
NT = (((1,), (1,)), ((), ()))
TN = (((0,), (0,)), ((), ()))


def dot(a, b, dims):
    return lax.dot_general(a, b, dims, preferred_element_type=F32)


def silu(z):
    return z * (1.0 / (1.0 + jnp.exp(-z)))


def softplus(v):
    return jnp.maximum(v, 0.0) + jnp.log1p(jnp.exp(-jnp.abs(v)))


def iota(shape, axis):
    return lax.broadcasted_iota(jnp.int32, shape, axis)


def thirds(v):
    high = v.astype(BF16).astype(F32)
    middle = (v - high).astype(BF16).astype(F32)
    return jnp.concatenate([high, middle, v - high - middle], axis=0).astype(BF16)


def by_head(refs, first, per_group, tokens):
    row = iota((per_group, tokens), 0)
    rows = []
    for ref in refs:
        value = jnp.zeros((per_group, tokens), F32)
        for h in range(per_group):
            value = jnp.where(row == h, ref[first + h], value)
        rows.append(value)
    return rows


def head_tables(dt_ref, a_ref, bias_ref, first, per_group):
    bias, a_log = by_head([bias_ref, a_ref], first, per_group, dt_ref.shape[1])
    step = softplus(dt_ref[...] + bias)
    return step, -jnp.exp(a_log) * step * LOG2E


def span_tables(step, rate, lo, per_group, width):
    upper = (iota((SPAN, SPAN), 0) <= iota((SPAN, SPAN), 1)).astype(BF16)
    step_k = step[:, lo : lo + SPAN]
    sums = dot(thirds(rate[:, lo : lo + SPAN]), upper, NN)
    cum = sums[:per_group] + sums[per_group : 2 * per_group] + sums[2 * per_group :]
    spread = (iota((3 * per_group, width), 1) // HEAD_DIM == iota((3 * per_group, width), 0) % per_group).astype(BF16)
    turn = (iota((3 * per_group, per_group), 1) == iota((3 * per_group, per_group), 0) % per_group).astype(BF16)
    cum_col = dot(thirds(cum), turn, TN)
    step_x = dot(thirds(step_k), spread, TN)
    fade_x = dot(thirds(jnp.exp2(cum)), spread, TN)
    tail_x = dot(thirds(jnp.exp2(cum[:, SPAN - 1 :] - cum) * step_k), spread, TN)
    return cum, cum_col, step_x, fade_x, tail_x


def skip_row(skip_ref, first, per_group, width):
    head = iota((1, width), 1) // HEAD_DIM
    row = jnp.zeros((1, width), F32)
    for h in range(per_group):
        row = jnp.where(head == h, skip_ref[first + h], row)
    return row


def decay(gap, mask=None):
    return jnp.exp2(gap if mask is None else jnp.where(mask, gap, -1e30))


def even_odd(v):
    first = iota(v.shape, 1) % (2 * HEAD_DIM) < HEAD_DIM
    return jnp.where(first, v, 0.0).astype(BF16), jnp.where(first, 0.0, v).astype(BF16)


def forward_kernel(
    count, dt_ref, x_ref, z_ref, b_ref, c_ref, gain_ref, a_ref, bias_ref, skip_ref, *refs
):
    loads = [pltpu.make_async_copy(refs[n], refs[count + n], refs[-1].at[n]) for n in range(count)]
    normed_ref, inv_ref = refs[2 * count : 2 * count + 2]

    @pl.when(pl.program_id(0) == 0)
    def _():
        for load in loads:
            load.start()

    tokens, width = x_ref.shape
    per_group = width // HEAD_DIM
    first = pl.program_id(0) * per_group
    lanes_here = pl.ds(pl.multiple_of(pl.program_id(0) * width, LANES), width)
    step, rate = head_tables(dt_ref, a_ref, bias_ref, first, per_group)
    skip = skip_row(skip_ref, first, per_group, width)
    causal = iota((HALF, HALF), 0) >= iota((HALF, HALF), 1)
    spans = tokens // SPAN
    entering = None
    for k in range(spans):
        rows = slice(k * SPAN, (k + 1) * SPAN)
        cum, cum_col, step_x, fade_x, tail_x = span_tables(step, rate, k * SPAN, per_group, width)
        x = x_ref[rows, :].astype(F32)
        b, c = b_ref[rows, :], c_ref[rows, :]
        scores = dot(c, b, NT)
        values = even_odd(x * step_x)
        pieces = []
        for pair in range(per_group // 2):
            lanes = slice(2 * pair * HEAD_DIM, 2 * (pair + 1) * HEAD_DIM)
            tops, bottoms = [], []
            for h in (2 * pair, 2 * pair + 1):
                col, line = cum_col[:, h : h + 1], cum[h : h + 1, :]
                top = decay(col[:HALF] - line[:, :HALF], causal) * scores[:HALF, :HALF]
                left = decay(col[HALF:] - line[:, :HALF]) * scores[HALF:, :HALF]
                low = decay(col[HALF:] - line[:, HALF:], causal) * scores[HALF:, HALF:]
                tops.append(top.astype(BF16))
                bottoms += [left.astype(BF16), low.astype(BF16)]
            upper_values = jnp.concatenate([v[:HALF, lanes] for v in values], axis=0)
            all_values = jnp.concatenate([v[:, lanes] for v in values], axis=0)
            pieces.append(
                jnp.concatenate(
                    [
                        dot(jnp.concatenate(tops, axis=1), upper_values, NN),
                        dot(jnp.concatenate(bottoms, axis=1), all_values, NN),
                    ],
                    axis=0,
                )
            )
        ssd = jnp.concatenate(pieces, axis=1) + skip * x
        if entering is not None:
            ssd = ssd + dot(c, entering.astype(BF16), NN) * fade_x
        if k + 1 < spans:
            state = dot(b, (x * tail_x).astype(BF16), TN)
            entering = state if entering is None else entering * fade_x[SPAN - 1 :, :] + state
        gated = ssd * silu(z_ref[rows, :].astype(F32))
        inv = lax.rsqrt(jnp.mean(gated * gated, axis=1, keepdims=True) + 1e-05)
        normed_ref[rows, lanes_here] = (gated * inv * gain_ref[...]).astype(BF16)
        inv_ref[pl.program_id(0), rows, :] = inv

    @pl.when(pl.program_id(0) == pl.num_programs(0) - 1)
    def _():
        for load in loads:
            load.wait()


def kept_kernel(global_ref, momentum_ref, kept_ref):
    kept_ref[...] = (global_ref[...] - outer_rate * outer_beta * outer_beta * momentum_ref[...]).astype(BF16)


def project_kernel(chunks, place_ref, weight_ref, normed_ref, target_ref, *part_refs):
    replicas, owned, inner = weight_ref.shape
    held, features = target_ref.shape
    piece = part_refs[0].shape[0] // replicas
    tokens = normed_ref.shape[0]
    eye = (iota((held, held), 0) == iota((held, held), 1)).astype(BF16)
    turned = dot(target_ref[...], eye, TN).reshape(replicas, owned, held)
    here = iota((replicas * piece, tokens), 1) // held == place_ref[0]
    for n, part_ref in zip(chunks, part_refs):
        at = slice(n * piece, (n + 1) * piece)
        part = dot(weight_ref[:, at, :].reshape(replicas * piece, inner), normed_ref[...], NT)
        goal = jnp.concatenate([turned[:, at, :].reshape(replicas * piece, held)] * (tokens // held), axis=1)
        part_ref[...] = (part - jnp.where(here, goal, 0.0)).astype(BF16)


def add_kernel(a_ref, b_ref, sum_ref):
    sum_ref[...] = (a_ref[...].astype(F32) + b_ref[...].astype(F32)).astype(BF16)


def add_squares_kernel(a_ref, b_ref, sum_ref):
    sum_ref[...] = a_ref[...] + b_ref[...]


def gradient_kernel(count, place_ref, *refs):
    cot_refs, (normed_ref, weight_ref, keep_ref, send_ref) = refs[: 2 * count], refs[2 * count :]
    middle = place_ref[1] == 1
    odd = place_ref[2] == 1
    replicas, rows, tile = weight_ref.shape
    piece = rows // count
    cols = pl.ds(pl.multiple_of(pl.program_id(0) * tile, LANES), tile)
    for n in range(count):
        cot = jnp.where(middle, cot_refs[2 * n][...], cot_refs[2 * n + 1][...])
        at = slice(n * piece, (n + 1) * piece)
        weight = weight_ref[:, at, :].reshape(replicas * piece, tile).astype(F32)
        new = weight - inner_rate * dot(cot, normed_ref[:, cols], NN)
        new = new.astype(BF16).reshape(replicas // 2, 2, piece, tile)
        keep_ref[:, at, cols] = jnp.where(odd, new[:, 1], new[:, 0])
        send_ref[:, at, cols] = jnp.where(odd, new[:, 0], new[:, 1])


def backward_kernel(
    begin, place_ref, dt_ref, z_ref, b_ref, c_ref, gain_ref, a_ref, bias_ref, skip_ref, normed_ref, inv_ref, weight_ref, *refs
):
    *cot_refs, dx_ref, dn_ref = refs
    if len(cot_refs) % 2:
        cot_refs = cot_refs[:-1]
    tokens, width = z_ref.shape
    per_group = width // HEAD_DIM
    group = pl.program_id(0) + begin
    first = group * per_group
    here = pl.ds(pl.multiple_of(group * width, LANES), width)
    replicas, owned, _ = weight_ref.shape
    chunks = len(cot_refs) // 2
    piece = owned // chunks
    middle = place_ref[1] == 1
    for n in range(chunks):
        weight = weight_ref[:, n * piece : (n + 1) * piece, :].reshape(replicas * piece, width)
        term = dot(jnp.where(middle, cot_refs[2 * n][...], cot_refs[2 * n + 1][...]), weight, TN)
        dn_ref[...] = term if n == 0 else dn_ref[...] + term
    step, rate = head_tables(dt_ref, a_ref, bias_ref, first, per_group)
    skip = skip_row(skip_ref, first, per_group, width)
    causal = iota((HALF, HALF), 1) >= iota((HALF, HALF), 0)
    spans = tokens // SPAN
    d_state = None
    for k in reversed(range(spans)):
        rows = slice(k * SPAN, (k + 1) * SPAN)
        cum, cum_col, step_x, fade_x, tail_x = span_tables(step, rate, k * SPAN, per_group, width)
        dn = dn_ref[rows, :]
        gain = gain_ref[...]
        normed = normed_ref[rows, here].astype(F32)
        shared = jnp.mean(normed * dn, axis=1, keepdims=True)
        d_gated = inv_ref[group, rows, :] * (gain * dn - (normed / gain) * shared)
        d_ssd = d_gated * silu(z_ref[rows, :].astype(F32))
        values = even_odd(d_ssd)
        b, c = b_ref[rows, :], c_ref[rows, :]
        scores = dot(b, c, NT)
        pieces = []
        for pair in range(per_group // 2):
            lanes = slice(2 * pair * HEAD_DIM, 2 * (pair + 1) * HEAD_DIM)
            tops, bottoms = [], []
            for h in (2 * pair, 2 * pair + 1):
                col, line = cum_col[:, h : h + 1], cum[h : h + 1, :]
                high = decay(line[:, :HALF] - col[:HALF], causal) * scores[:HALF, :HALF]
                right = decay(line[:, HALF:] - col[:HALF]) * scores[:HALF, HALF:]
                low = decay(line[:, HALF:] - col[HALF:], causal) * scores[HALF:, HALF:]
                tops += [high.astype(BF16), right.astype(BF16)]
                bottoms.append(low.astype(BF16))
            lower_values = jnp.concatenate([v[HALF:, lanes] for v in values], axis=0)
            all_values = jnp.concatenate([v[:, lanes] for v in values], axis=0)
            pieces.append(
                jnp.concatenate(
                    [
                        dot(jnp.concatenate(tops, axis=1), all_values, NN),
                        dot(jnp.concatenate(bottoms, axis=1), lower_values, NN),
                    ],
                    axis=0,
                )
            )
        dx = jnp.concatenate(pieces, axis=1) * step_x + skip * d_ssd
        if d_state is not None:
            dx = dx + dot(b, d_state.astype(BF16), NN) * tail_x
        dx_ref[rows, :] = dx.astype(BF16)
        if k > 0:
            own = dot(c, (d_ssd * fade_x).astype(BF16), TN)
            d_state = own if d_state is None else own + d_state * fade_x[SPAN - 1 :, :]


def pick_kernel(count, place_ref, *refs):
    terms, outs = refs[:count], refs[count:]
    my = lax.rem(lax.div(place_ref[3], place_ref[4]), len(outs))
    for mask, out_ref in enumerate(outs):
        at = lax.bitwise_xor(my, jnp.int32(mask))
        total = terms[0][:, at].astype(F32)
        for term in terms[1:]:
            total = total + term[:, at].astype(F32)
        out_ref[...] = total.astype(BF16)


def delta_kernel(count, replicas, global_ref, before_ref, *refs):
    terms, (delta_ref, sent_ref, squares_ref) = refs[:count], refs[count:]
    rows, inner = delta_ref.shape
    total = terms[0][0].astype(F32)
    for term in terms[1:]:
        total = total + term[0].astype(F32)
    delta = global_ref[...] - total / replicas
    delta_ref[...] = delta
    sent_ref[...] = delta.astype(BF16)
    squares = jnp.sum(delta * delta, axis=0, keepdims=True)
    squares = before_ref[...] + jnp.broadcast_to(jnp.sum(squares, axis=1, keepdims=True), before_ref.shape)
    squares_ref[...] = squares


def join_kernel(*refs):
    *parts, out_ref = refs
    lo = 0
    for part in parts:
        out_ref[lo : lo + part.shape[0]] = part[...]
        lo += part.shape[0]


def weight_kernel(sizes, entries, place_ref, kept_ref, global_ref, momentum_ref, *refs):
    count = len(sizes)
    pairs, deltas, squares = refs[: 2 * count], refs[2 * count : 3 * count], refs[3 * count : -3]
    new_ref, new_global_ref, new_momentum_ref = refs[-3:]
    mean = (squares[0][:1, :1] + squares[1][:1, :1]) / entries
    factor = jnp.minimum(1.0, clip_rms / jnp.sqrt(mean + 1e-06))
    at_chip = lax.bitwise_xor(pl.program_id(0), place_ref[3])
    owned = new_ref.shape[0] // 2
    scale = (outer_rate * (1.0 + outer_beta)) * factor

    def one_core(core, side):
        lo = 0
        for n, size in enumerate(sizes):
            rows = slice(core * owned + lo, core * owned + lo + size)
            delta = pairs[2 * n + side][at_chip].astype(F32)
            new_ref[rows, :] = (kept_ref[rows, :].astype(F32) - scale * delta).astype(BF16)
            lo += size

    for own_core in range(2):

        @pl.when(place_ref[2] == own_core)
        def _():
            one_core(own_core, 0)
            one_core(1 - own_core, 1)

    @pl.when(pl.program_id(0) == 0)
    def _():
        lo = 0
        for n, size in enumerate(sizes):
            rows = slice(lo, lo + size)
            lo += size
            clipped = factor * deltas[n][...]
            new_momentum = outer_beta * momentum_ref[rows, :] + clipped
            new_momentum_ref[rows, :] = new_momentum
            new_global_ref[rows, :] = global_ref[rows, :] - outer_rate * (clipped + outer_beta * new_momentum)


def inward(axis_size):
    half = axis_size // 2
    hops = [[(s, s + 1), (axis_size - 1 - s, axis_size - 2 - s)] for s in range(half - 1)]
    return hops, [(half - 1, half), (half, half - 1)]


def in_turn(kernel, inputs, waits, outs):
    def body(*refs):
        end = inputs + waits + outs
        refs[end][...] = jnp.zeros_like(refs[end])
        kernel(*refs[:inputs], *refs[inputs + waits : end], *refs[end + 1 :])

    return body


def stages(replicas):
    bit, left, found = 1, replicas // 2, []
    while left > 1:
        bits = 2 if left >= 4 else 1
        found.append((bit, bits))
        bit, left = bit + bits, left >> bits
    return found


def shards(
    x_in,
    gate_z,
    b_proj,
    c_proj,
    dt_raw,
    a_log,
    dt_bias,
    skip_d,
    norm_gain,
    out_weight,
    global_weight,
    momentum,
    target,
):
    tokens, inner = x_in.shape
    features = out_weight.shape[1]
    replicas = lax.axis_size("replica")
    heads_over = lax.axis_size("tensor")
    groups = b_proj.shape[1] // STATE
    heads = dt_raw.shape[1]
    width = inner // groups
    owned = features // replicas
    chunks = max(2, min(4, owned // 16))
    batches = [list(range(chunks // 2)), list(range(chunks // 2, chunks))]
    piece = owned // chunks
    span_rows = replicas * piece
    place = lax.axis_index("tensor")
    me = lax.axis_index("replica")
    in_middle = (place == heads_over // 2 - 1) | (place == heads_over // 2)
    one = jnp.int32(1)
    places = jnp.stack([place, in_middle.astype(jnp.int32), lax.rem(me, 2), lax.div(me, 2), one]).astype(jnp.int32)
    stored = out_weight[0].reshape(replicas, owned, inner)
    gain = norm_gain.reshape(1, inner)
    dt_rows = dt_raw.T

    smem = pl.BlockSpec(memory_space=pltpu.SMEM)
    vmem = pl.BlockSpec(memory_space=pltpu.VMEM)
    anywhere = pl.BlockSpec(memory_space=pl.ANY)
    inv_spec = pl.BlockSpec((1, tokens, 1), lambda g: (g, 0, 0))
    large = pltpu.CompilerParams(vmem_limit_bytes=20 * 1024 * 1024)
    small = pltpu.CompilerParams(vmem_limit_bytes=12 * 1024 * 1024)
    small_cost = pl.CostEstimate(flops=1, bytes_accessed=1, transcendentals=0)
    large_cost = pl.CostEstimate(flops=30_000_000_000, bytes_accessed=1, transcendentals=0)

    turn = []

    def run(kernel, inputs, in_specs, outs, out_specs, waits=(), **options):
        waits = [*turn[-1:], *waits]
        done = jax.ShapeDtypeStruct((8, LANES), F32)
        *results, ran = pl.pallas_call(
            in_turn(kernel, len(inputs), len(waits), len(outs)),
            in_specs=[*in_specs, *[vmem if v.size <= 8 * LANES or v.shape == (span_rows, tokens) else anywhere for v in waits]],
            out_specs=[*out_specs, vmem],
            out_shape=[*outs, done],
            **options,
        )(*inputs, *waits)
        turn.append(ran)
        return results

    def step(kernel, operands, outs, scalars=(), waits=(), cost=small_cost):
        return run(
            kernel,
            [*scalars, *operands],
            [smem] * len(scalars) + [vmem] * len(operands),
            outs,
            [vmem] * len(outs),
            waits,
            cost_estimate=cost,
            compiler_params=small,
        )

    def shape(*dims, dtype=BF16):
        return jax.ShapeDtypeStruct(dims, dtype)

    def in_hbm(*arrays):
        return [pltpu.with_memory_space_constraint(a, pltpu.HBM) for a in arrays]

    def group_specs(begin):
        wide = pl.BlockSpec((tokens, width), lambda g: (0, g + begin))
        state = pl.BlockSpec((tokens, STATE), lambda g: (0, g + begin))
        dt = pl.BlockSpec((heads // groups, tokens), lambda g: (g + begin, 0))
        return wide, state, dt, pl.BlockSpec((1, width), lambda g: (0, g + begin))

    def exchange(value, mask):
        return lax.ppermute(value, "replica", [(r, r ^ mask) for r in range(replicas)])

    gathered = {}

    def spread_rows(b, sent):
        (bit, bits), *_ = stages(replicas)
        gathered[b] = [sent[None]] + [exchange(sent[None], mask << bit) for mask in range(1, 1 << bits)]

    def join(b, waits=()):
        for at, (bit, bits) in enumerate(stages(replicas)):
            if at > 0:
                gathered[b] = [held] + [exchange(held, mask << bit) for mask in range(1, 1 << bits)]
            one = gathered[b][0]
            out = shape(len(gathered[b]) * one.shape[0], *one.shape[1:])
            (held,) = step(join_kernel, gathered[b], [out], waits=waits if at == 0 else ())
        gathered[b] = [held, exchange(held, 1)]

    by_group, by_state, dt_spec, gain_spec = group_specs(0)
    shared = in_hbm(dt_rows, gate_z, b_proj, c_proj, gain, a_log, dt_bias, skip_d)
    later = [stored, target]
    (kept,) = run(
        kept_kernel,
        in_hbm(global_weight, momentum),
        [pl.BlockSpec((owned, inner), lambda i: (0, 0))] * 2,
        [shape(owned, inner)],
        [pl.BlockSpec((owned, inner), lambda i: (0, 0))],
        grid=(1,),
        cost_estimate=small_cost,
        compiler_params=small,
    )
    (kept_all,) = in_hbm(lax.all_gather(kept, "replica", axis=0, tiled=True))
    weight, goal, normed, inv = run(
        functools.partial(forward_kernel, len(later)),
        [shared[0], *in_hbm(x_in), *shared[1:], *in_hbm(*later)],
        [dt_spec, by_group, by_group, by_state, by_state, gain_spec, smem, smem, smem] + [anywhere] * len(later),
        [pltpu.VMEM(v.shape, v.dtype) for v in later] + [pltpu.VMEM((tokens, inner), BF16), pltpu.VMEM((groups, tokens, 1), F32)],
        [vmem] * (len(later) + 2),
        grid=(groups,),
        scratch_shapes=[pltpu.SemaphoreType.DMA((len(later),))],
        cost_estimate=small_cost,
        compiler_params=large,
    )

    part = shape(span_rows, tokens)

    def project(picked):
        kernel = functools.partial(project_kernel, picked)
        return step(kernel, [weight, normed, goal], [part] * len(picked), scalars=[places])

    in_hops, across = inward(heads_over)
    parts = project([0])
    parts += project(list(range(1, chunks)))
    first_landed = [lax.ppermute(p, "tensor", in_hops[0]) if in_hops else None for p in parts]
    sums, cots = {}, {}

    def sum_side(n, waits=()):
        held = parts[n]
        for at, pairs in enumerate(in_hops):
            landed = first_landed[n] if at == 0 else lax.ppermute(held, "tensor", pairs)
            (held,) = step(add_kernel, [held, landed], [part], waits=waits)
        sums[n] = held

    def sum_all(n, waits=(), cost=small_cost):
        landed = lax.ppermute(sums[n], "tensor", across)
        (mid,) = step(add_kernel, [sums[n], landed], [part], waits=waits, cost=cost)
        out = mid
        for pairs in reversed(in_hops):
            back = lax.ppermute(out, "tensor", [(b, a) for a, b in pairs])
            out = back if pairs is in_hops[0] else jnp.where(in_middle, mid, back)
        cots[n] = (mid, out)

    terms, deltas = {}, {}
    tile = shape(8, LANES, dtype=F32)
    squares = {-1: jnp.zeros((8, LANES), F32)}

    def new_rows(b, waits=()):
        batch = batches[b]
        rows = len(batch) * piece
        col_tile = min(inner, 512)
        keep, send = run(
            functools.partial(gradient_kernel, len(batch)),
            [places, *[c for n in batch for c in cots[n]], normed, *in_hbm(stored)],
            [smem] + [vmem] * (2 * len(batch) + 1) + [pl.BlockSpec((replicas, rows, col_tile), lambda i: (0, b, i))],
            [shape(replicas // 2, rows, inner)] * 2,
            [vmem] * 2,
            waits,
            grid=(inner // col_tile,),
            cost_estimate=small_cost,
            compiler_params=small,
        )
        return [keep, exchange(send, 1)]

    def send_rows(b, held):
        rows, left = len(batches[b]) * piece, replicas // 2
        for bit, bits in stages(replicas):
            ways = 1 << bits
            left //= ways
            cut = [h.reshape(left, ways, rows, inner) for h in held]
            picked = step(
                functools.partial(pick_kernel, len(cut)),
                cut,
                [shape(left, rows, inner)] * ways,
                scalars=[places.at[4].set(1 << (bit - 1))] if bit > 1 else [places],
            )
            held = [picked[0]] + [exchange(picked[mask], mask << bit) for mask in range(1, ways)]
        terms[b] = held

    def own_rows(b, cost=small_cost):
        batch = batches[b]
        rows = len(batch) * piece
        deltas[b], sent, squares[b] = run(
            functools.partial(delta_kernel, len(terms[b]), replicas),
            [*in_hbm(global_weight), squares[b - 1], *terms[b]],
            [pl.BlockSpec((rows, inner), lambda i: (b, 0))] + [vmem] * (1 + len(terms[b])),
            [shape(rows, inner, dtype=F32), shape(rows, inner), tile],
            [vmem] * 3,
            grid=(1,),
            cost_estimate=cost,
            compiler_params=small,
        )
        spread_rows(b, sent)

    def backward(begin, count, so_far):
        wide, state, dt, gain_here = group_specs(begin)
        operands = [places, *shared, normed, inv, *in_hbm(stored)] + [c for n in range(chunks) for c in cots[n]]
        specs = [smem, dt, wide, state, state, gain_here, smem, smem, smem, vmem, vmem]
        specs += [pl.BlockSpec((replicas, owned, width), lambda g: (0, 0, g + begin))] + [vmem] * (2 * chunks)
        aliases = {}
        if so_far is not None:
            aliases = {len(operands): 0}
            operands.append(so_far)
            specs.append(anywhere)
        (grad,) = run(
            functools.partial(backward_kernel, begin),
            operands,
            specs,
            [shape(tokens, inner)],
            [wide],
            grid=(count,),
            scratch_shapes=[pltpu.VMEM((tokens, width), F32)],
            input_output_aliases=aliases,
            cost_estimate=large_cost,
            compiler_params=large,
        )
        return grad

    first, second = range(2)
    for t in range(chunks):
        sum_side(t, [cots[t - 3][1], kept_all] if t >= 3 else [kept_all] if t == chunks - 1 else [])
        if t > 0:
            sum_all(t - 1)
    held_first = new_rows(first)
    sum_all(chunks - 1, [cots[chunks - 2][1]], large_cost)
    send_rows(first, held_first)
    held_second = new_rows(second)
    own_rows(first, large_cost)
    send_rows(second, held_second)
    half = groups // 2
    grad_input = backward(0, half, None) if half else None
    join(first)
    grad_input = backward(half, groups - half, grad_input)
    own_rows(second)
    total = squares[second]
    for axis, bits in (("tensor", range(heads_over.bit_length() - 1)), ("replica", range(1, replicas.bit_length() - 1))):
        for bit in bits:
            pairs = [(r, r ^ (1 << bit)) for r in range(lax.axis_size(axis))]
            (total,) = step(add_squares_kernel, [total, lax.ppermute(total, axis, pairs)], [tile])
    join(second, gathered[first][1:])
    columns = [total, exchange(total, 1)]

    sizes = [len(batch) * piece for batch in batches]
    pair_spec = pl.BlockSpec((2 * owned, inner), lambda r: (r, 0))
    held_spec = pl.BlockSpec((owned, inner), lambda r: (0, 0))
    inputs = [*gathered[first], *gathered[second], deltas[first], deltas[second], *columns]
    new_weight, new_global, new_momentum = run(
        functools.partial(weight_kernel, sizes, features * inner * heads_over),
        [places, kept_all, *in_hbm(global_weight, momentum), *inputs],
        [smem, pair_spec, held_spec, held_spec] + [vmem] * len(inputs),
        [shape(features, inner), shape(owned, inner, dtype=F32), shape(owned, inner, dtype=F32)],
        [pair_spec, held_spec, held_spec],
        grid=(replicas // 2,),
        cost_estimate=small_cost,
        compiler_params=small,
    )
    return (grad_input, new_weight, new_global, new_momentum)


def solution(mesh):
    placed = (
        P("replica", "tensor"),
        P("replica", "tensor"),
        P("replica", "tensor"),
        P("replica", "tensor"),
        P("replica", "tensor"),
        P("tensor"),
        P("tensor"),
        P("tensor"),
        P("tensor"),
        P("replica", None, "tensor"),
        P("replica", "tensor"),
        P("replica", "tensor"),
        P(("replica", "tensor"), None),
    )
    return jax.shard_map(
        shards,
        mesh=mesh,
        in_specs=placed,
        out_specs=(
            P("replica", "tensor"),
            P(None, "tensor"),
            P("replica", "tensor"),
            P("replica", "tensor"),
        ),
        check_vma=False,
    )
```

```python
import functools

import jax
import jax.numpy as jnp
from jax import lax
from jax.experimental import pallas as pl
from jax.experimental.pallas import tpu as pltpu
from jax.sharding import PartitionSpec as P

HEAD_DIM = 64
STATE = 128
SPAN = 256
HALF = SPAN // 2
LANES = 128

inner_rate = 0.001
outer_rate = 0.7
outer_beta = 0.9
clip_rms = 0.005
LOG2E = 1.4426950408889634

F32 = jnp.float32
BF16 = jnp.bfloat16
NN = (((1,), (0,)), ((), ()))
NT = (((1,), (1,)), ((), ()))
TN = (((0,), (0,)), ((), ()))


def dot(a, b, dims):
    return lax.dot_general(a, b, dims, preferred_element_type=F32)


def silu(z):
    return z * (1.0 / (1.0 + jnp.exp(-z)))


def softplus(v):
    return jnp.maximum(v, 0.0) + jnp.log1p(jnp.exp(-jnp.abs(v)))


def iota(shape, axis):
    return lax.broadcasted_iota(jnp.int32, shape, axis)


def thirds(v):
    high = v.astype(BF16).astype(F32)
    middle = (v - high).astype(BF16).astype(F32)
    return jnp.concatenate([high, middle, v - high - middle], axis=0).astype(BF16)


def by_head(refs, first, per_group, tokens):
    row = iota((per_group, tokens), 0)
    rows = []
    for ref in refs:
        value = jnp.zeros((per_group, tokens), F32)
        for h in range(per_group):
            value = jnp.where(row == h, ref[first + h], value)
        rows.append(value)
    return rows


def head_tables(dt_ref, a_ref, bias_ref, first, per_group):
    bias, a_log = by_head([bias_ref, a_ref], first, per_group, dt_ref.shape[1])
    step = softplus(dt_ref[...] + bias)
    return step, -jnp.exp(a_log) * step * LOG2E


def span_tables(step, rate, lo, per_group, width):
    upper = (iota((SPAN, SPAN), 0) <= iota((SPAN, SPAN), 1)).astype(BF16)
    step_k = step[:, lo : lo + SPAN]
    sums = dot(thirds(rate[:, lo : lo + SPAN]), upper, NN)
    cum = sums[:per_group] + sums[per_group : 2 * per_group] + sums[2 * per_group :]
    spread = (iota((3 * per_group, width), 1) // HEAD_DIM == iota((3 * per_group, width), 0) % per_group).astype(BF16)
    turn = (iota((3 * per_group, per_group), 1) == iota((3 * per_group, per_group), 0) % per_group).astype(BF16)
    cum_col = dot(thirds(cum), turn, TN)
    step_x = dot(thirds(step_k), spread, TN)
    fade_x = dot(thirds(jnp.exp2(cum)), spread, TN)
    tail_x = dot(thirds(jnp.exp2(cum[:, SPAN - 1 :] - cum) * step_k), spread, TN)
    return cum, cum_col, step_x, fade_x, tail_x


def skip_row(skip_ref, first, per_group, width):
    head = iota((1, width), 1) // HEAD_DIM
    row = jnp.zeros((1, width), F32)
    for h in range(per_group):
        row = jnp.where(head == h, skip_ref[first + h], row)
    return row


def decay(gap, mask=None):
    return jnp.exp2(gap if mask is None else jnp.where(mask, gap, -1e30))


def even_odd(v):
    first = iota(v.shape, 1) % (2 * HEAD_DIM) < HEAD_DIM
    return jnp.where(first, v, 0.0).astype(BF16), jnp.where(first, 0.0, v).astype(BF16)


def forward_kernel(
    count, dt_ref, x_ref, z_ref, b_ref, c_ref, gain_ref, a_ref, bias_ref, skip_ref, *refs
):
    loads = [pltpu.make_async_copy(refs[n], refs[count + n], refs[-1].at[n]) for n in range(count)]
    normed_ref, inv_ref = refs[2 * count : 2 * count + 2]

    @pl.when(pl.program_id(0) == 0)
    def _():
        for load in loads:
            load.start()

    tokens, width = x_ref.shape
    per_group = width // HEAD_DIM
    first = pl.program_id(0) * per_group
    lanes_here = pl.ds(pl.multiple_of(pl.program_id(0) * width, LANES), width)
    step, rate = head_tables(dt_ref, a_ref, bias_ref, first, per_group)
    skip = skip_row(skip_ref, first, per_group, width)
    causal = iota((HALF, HALF), 0) >= iota((HALF, HALF), 1)
    spans = tokens // SPAN
    entering = None
    for k in range(spans):
        rows = slice(k * SPAN, (k + 1) * SPAN)
        cum, cum_col, step_x, fade_x, tail_x = span_tables(step, rate, k * SPAN, per_group, width)
        x = x_ref[rows, :].astype(F32)
        b, c = b_ref[rows, :], c_ref[rows, :]
        scores = dot(c, b, NT)
        values = even_odd(x * step_x)
        pieces = []
        for pair in range(per_group // 2):
            lanes = slice(2 * pair * HEAD_DIM, 2 * (pair + 1) * HEAD_DIM)
            tops, bottoms = [], []
            for h in (2 * pair, 2 * pair + 1):
                col, line = cum_col[:, h : h + 1], cum[h : h + 1, :]
                top = decay(col[:HALF] - line[:, :HALF], causal) * scores[:HALF, :HALF]
                left = decay(col[HALF:] - line[:, :HALF]) * scores[HALF:, :HALF]
                low = decay(col[HALF:] - line[:, HALF:], causal) * scores[HALF:, HALF:]
                tops.append(top.astype(BF16))
                bottoms += [left.astype(BF16), low.astype(BF16)]
            upper_values = jnp.concatenate([v[:HALF, lanes] for v in values], axis=0)
            all_values = jnp.concatenate([v[:, lanes] for v in values], axis=0)
            pieces.append(
                jnp.concatenate(
                    [
                        dot(jnp.concatenate(tops, axis=1), upper_values, NN),
                        dot(jnp.concatenate(bottoms, axis=1), all_values, NN),
                    ],
                    axis=0,
                )
            )
        ssd = jnp.concatenate(pieces, axis=1) + skip * x
        if entering is not None:
            ssd = ssd + dot(c, entering.astype(BF16), NN) * fade_x
        if k + 1 < spans:
            state = dot(b, (x * tail_x).astype(BF16), TN)
            entering = state if entering is None else entering * fade_x[SPAN - 1 :, :] + state
        gated = ssd * silu(z_ref[rows, :].astype(F32))
        inv = lax.rsqrt(jnp.mean(gated * gated, axis=1, keepdims=True) + 1e-05)
        normed_ref[rows, lanes_here] = (gated * inv * gain_ref[...]).astype(BF16)
        inv_ref[pl.program_id(0), rows, :] = inv

    @pl.when(pl.program_id(0) == pl.num_programs(0) - 1)
    def _():
        for load in loads:
            load.wait()


def kept_kernel(global_ref, momentum_ref, kept_ref):
    kept_ref[...] = (global_ref[...] - outer_rate * outer_beta * outer_beta * momentum_ref[...]).astype(BF16)


def project_kernel(chunks, place_ref, weight_ref, normed_ref, target_ref, *part_refs):
    replicas, owned, inner = weight_ref.shape
    held, features = target_ref.shape
    piece = part_refs[0].shape[0] // replicas
    tokens = normed_ref.shape[0]
    eye = (iota((held, held), 0) == iota((held, held), 1)).astype(BF16)
    turned = dot(target_ref[...], eye, TN).reshape(replicas, owned, held)
    here = iota((replicas * piece, tokens), 1) // held == place_ref[0]
    for n, part_ref in zip(chunks, part_refs):
        at = slice(n * piece, (n + 1) * piece)
        part = dot(weight_ref[:, at, :].reshape(replicas * piece, inner), normed_ref[...], NT)
        goal = jnp.concatenate([turned[:, at, :].reshape(replicas * piece, held)] * (tokens // held), axis=1)
        part_ref[...] = (part - jnp.where(here, goal, 0.0)).astype(BF16)


def gate_kernel(out_ref):
    out_ref[...] = jnp.zeros_like(out_ref)


def add_kernel(a_ref, b_ref, sum_ref):
    sum_ref[...] = (a_ref[...].astype(F32) + b_ref[...].astype(F32)).astype(BF16)


def add_squares_kernel(a_ref, b_ref, sum_ref):
    sum_ref[...] = a_ref[...] + b_ref[...]


def gradient_kernel(batch, place_ref, *refs):
    count = len(batch)
    cot_refs, (normed_ref, weight_ref, keep_ref, send_ref) = refs[: 2 * count], refs[2 * count :]
    middle = place_ref[1] == 1
    odd = place_ref[2] == 1
    replicas, _, inner = weight_ref.shape
    piece = keep_ref.shape[1] // count
    tile = min(inner, 512)
    for n, chunk in enumerate(batch):
        cot = jnp.where(middle, cot_refs[2 * n][...], cot_refs[2 * n + 1][...])
        rows = slice(chunk * piece, (chunk + 1) * piece)
        at = slice(n * piece, (n + 1) * piece)
        for lo in range(0, inner, tile):
            cols = slice(lo, lo + tile)
            weight = weight_ref[:, rows, cols].reshape(replicas * piece, tile).astype(F32)
            new = weight - inner_rate * dot(cot, normed_ref[:, cols], NN)
            new = new.astype(BF16).reshape(replicas // 2, 2, piece, tile)
            keep_ref[:, at, cols] = jnp.where(odd, new[:, 1], new[:, 0])
            send_ref[:, at, cols] = jnp.where(odd, new[:, 0], new[:, 1])


def backward_kernel(
    begin, place_ref, dt_ref, z_ref, b_ref, c_ref, gain_ref, a_ref, bias_ref, skip_ref, normed_ref, inv_ref, weight_ref, *refs
):
    *cot_refs, dx_ref, dn_ref = refs
    if len(cot_refs) % 2:
        cot_refs = cot_refs[:-1]
    tokens, width = z_ref.shape
    per_group = width // HEAD_DIM
    group = pl.program_id(0) + begin
    first = group * per_group
    here = pl.ds(pl.multiple_of(group * width, LANES), width)
    replicas, owned, _ = weight_ref.shape
    chunks = len(cot_refs) // 2
    piece = owned // chunks
    middle = place_ref[1] == 1
    for n in range(chunks):
        weight = weight_ref[:, n * piece : (n + 1) * piece, here].reshape(replicas * piece, width)
        term = dot(jnp.where(middle, cot_refs[2 * n][...], cot_refs[2 * n + 1][...]), weight, TN)
        dn_ref[...] = term if n == 0 else dn_ref[...] + term
    step, rate = head_tables(dt_ref, a_ref, bias_ref, first, per_group)
    skip = skip_row(skip_ref, first, per_group, width)
    causal = iota((HALF, HALF), 1) >= iota((HALF, HALF), 0)
    spans = tokens // SPAN
    d_state = None
    for k in reversed(range(spans)):
        rows = slice(k * SPAN, (k + 1) * SPAN)
        cum, cum_col, step_x, fade_x, tail_x = span_tables(step, rate, k * SPAN, per_group, width)
        dn = dn_ref[rows, :]
        gain = gain_ref[...]
        normed = normed_ref[rows, here].astype(F32)
        shared = jnp.mean(normed * dn, axis=1, keepdims=True)
        d_gated = inv_ref[group, rows, :] * (gain * dn - (normed / gain) * shared)
        d_ssd = d_gated * silu(z_ref[rows, :].astype(F32))
        values = even_odd(d_ssd)
        b, c = b_ref[rows, :], c_ref[rows, :]
        scores = dot(b, c, NT)
        pieces = []
        for pair in range(per_group // 2):
            lanes = slice(2 * pair * HEAD_DIM, 2 * (pair + 1) * HEAD_DIM)
            tops, bottoms = [], []
            for h in (2 * pair, 2 * pair + 1):
                col, line = cum_col[:, h : h + 1], cum[h : h + 1, :]
                high = decay(line[:, :HALF] - col[:HALF], causal) * scores[:HALF, :HALF]
                right = decay(line[:, HALF:] - col[:HALF]) * scores[:HALF, HALF:]
                low = decay(line[:, HALF:] - col[HALF:], causal) * scores[HALF:, HALF:]
                tops += [high.astype(BF16), right.astype(BF16)]
                bottoms.append(low.astype(BF16))
            lower_values = jnp.concatenate([v[HALF:, lanes] for v in values], axis=0)
            all_values = jnp.concatenate([v[:, lanes] for v in values], axis=0)
            pieces.append(
                jnp.concatenate(
                    [
                        dot(jnp.concatenate(tops, axis=1), all_values, NN),
                        dot(jnp.concatenate(bottoms, axis=1), lower_values, NN),
                    ],
                    axis=0,
                )
            )
        dx = jnp.concatenate(pieces, axis=1) * step_x + skip * d_ssd
        if d_state is not None:
            dx = dx + dot(b, d_state.astype(BF16), NN) * tail_x
        dx_ref[rows, :] = dx.astype(BF16)
        if k > 0:
            own = dot(c, (d_ssd * fade_x).astype(BF16), TN)
            d_state = own if d_state is None else own + d_state * fade_x[SPAN - 1 :, :]


def pick_kernel(count, place_ref, *refs):
    terms, outs = refs[:count], refs[count:]
    my = lax.rem(lax.div(place_ref[3], place_ref[4]), len(outs))
    for mask, out_ref in enumerate(outs):
        at = lax.bitwise_xor(my, jnp.int32(mask))
        total = terms[0][:, at].astype(F32)
        for term in terms[1:]:
            total = total + term[:, at].astype(F32)
        out_ref[...] = total.astype(BF16)


def delta_kernel(count, lo, replicas, global_ref, before_ref, *refs):
    terms, (delta_ref, sent_ref, squares_ref) = refs[:count], refs[count:]
    rows, inner = delta_ref.shape
    total = terms[0][0].astype(F32)
    for term in terms[1:]:
        total = total + term[0].astype(F32)
    delta = global_ref[lo : lo + rows, :] - total / replicas
    delta_ref[...] = delta
    sent_ref[...] = delta.astype(BF16)
    squares = jnp.sum(delta * delta, axis=0, keepdims=True)
    squares = before_ref[...] + jnp.broadcast_to(jnp.sum(squares, axis=1, keepdims=True), before_ref.shape)
    squares_ref[...] = squares


def join_kernel(*refs):
    *parts, out_ref = refs
    lo = 0
    for part in parts:
        out_ref[lo : lo + part.shape[0]] = part[...]
        lo += part.shape[0]


def weight_kernel(sizes, entries, place_ref, global_ref, momentum_ref, *refs):
    count = len(sizes)
    pairs, deltas, squares = refs[: 2 * count + 2], refs[2 * count + 2 : 3 * count + 2], refs[3 * count + 2 : -3]
    new_ref, new_global_ref, new_momentum_ref = refs[-3:]
    mean = (squares[0][:1, :1] + squares[1][:1, :1]) / entries
    factor = jnp.minimum(1.0, clip_rms / jnp.sqrt(mean + 1e-06))
    at_chip = lax.bitwise_xor(pl.program_id(0), place_ref[3])
    owned = new_ref.shape[0] // 2
    scale = (outer_rate * (1.0 + outer_beta)) * factor

    def one_core(core, side):
        lo = 0
        for n, size in enumerate(sizes):
            kept = pairs[side][at_chip, lo : lo + size, :].astype(F32)
            delta = pairs[2 * n + 2 + side][at_chip, :size, :].astype(F32)
            new_ref[core * owned + lo : core * owned + lo + size, :] = (kept - scale * delta).astype(BF16)
            lo += size

    for own_core in range(2):

        @pl.when(place_ref[2] == own_core)
        def _():
            one_core(own_core, 0)
            one_core(1 - own_core, 1)

    @pl.when(pl.program_id(0) == 0)
    def _():
        lo = 0
        for n, size in enumerate(sizes):
            rows = slice(lo, lo + size)
            lo += size
            clipped = factor * deltas[n][...]
            new_momentum = outer_beta * momentum_ref[rows, :] + clipped
            new_momentum_ref[rows, :] = new_momentum
            new_global_ref[rows, :] = global_ref[rows, :] - outer_rate * (clipped + outer_beta * new_momentum)


def inward(axis_size):
    half = axis_size // 2
    hops = [[(s, s + 1), (axis_size - 1 - s, axis_size - 2 - s)] for s in range(half - 1)]
    return hops, [(half - 1, half), (half, half - 1)]


def in_turn(kernel, inputs, waits, outs):
    def body(*refs):
        end = inputs + waits + outs
        refs[end][...] = jnp.zeros_like(refs[end])
        kernel(*refs[:inputs], *refs[inputs + waits : end], *refs[end + 1 :])

    return body


def stages(replicas):
    bit, left, found = 1, replicas // 2, []
    while left > 1:
        bits = 2 if left >= 4 else 1
        found.append((bit, bits))
        bit, left = bit + bits, left >> bits
    return found


def shards(
    x_in,
    gate_z,
    b_proj,
    c_proj,
    dt_raw,
    a_log,
    dt_bias,
    skip_d,
    norm_gain,
    out_weight,
    global_weight,
    momentum,
    target,
):
    tokens, inner = x_in.shape
    features = out_weight.shape[1]
    replicas = lax.axis_size("replica")
    heads_over = lax.axis_size("tensor")
    groups = b_proj.shape[1] // STATE
    heads = dt_raw.shape[1]
    width = inner // groups
    owned = features // replicas
    chunks = max(2, min(4, owned // 16))
    batches = [list(range(chunks // 2)), list(range(chunks // 2, chunks))]
    piece = owned // chunks
    span_rows = replicas * piece
    place = lax.axis_index("tensor")
    me = lax.axis_index("replica")
    in_middle = (place == heads_over // 2 - 1) | (place == heads_over // 2)
    one = jnp.int32(1)
    places = jnp.stack([place, in_middle.astype(jnp.int32), lax.rem(me, 2), lax.div(me, 2), one]).astype(jnp.int32)
    stored = out_weight[0].reshape(replicas, owned, inner)
    gain = norm_gain.reshape(1, inner)
    dt_rows = dt_raw.T

    smem = pl.BlockSpec(memory_space=pltpu.SMEM)
    vmem = pl.BlockSpec(memory_space=pltpu.VMEM)
    anywhere = pl.BlockSpec(memory_space=pl.ANY)
    inv_spec = pl.BlockSpec((1, tokens, 1), lambda g: (g, 0, 0))
    large = pltpu.CompilerParams(vmem_limit_bytes=20 * 1024 * 1024)
    small = pltpu.CompilerParams(vmem_limit_bytes=12 * 1024 * 1024)
    small_cost = pl.CostEstimate(flops=1, bytes_accessed=1, transcendentals=0)
    some_cost = pl.CostEstimate(flops=2_000_000_000, bytes_accessed=1, transcendentals=0)
    large_cost = pl.CostEstimate(flops=30_000_000_000, bytes_accessed=1, transcendentals=0)

    turn = []

    def run(kernel, inputs, in_specs, outs, out_specs, waits=(), **options):
        waits = [*turn[-1:], *waits]
        done = jax.ShapeDtypeStruct((8, LANES), F32)
        *results, ran = pl.pallas_call(
            in_turn(kernel, len(inputs), len(waits), len(outs)),
            in_specs=[*in_specs, *[vmem] * len(waits)],
            out_specs=[*out_specs, vmem],
            out_shape=[*outs, done],
            **options,
        )(*inputs, *waits)
        turn.append(ran)
        return results

    def step(kernel, operands, outs, scalars=(), waits=(), cost=small_cost):
        return run(
            kernel,
            [*scalars, *operands],
            [smem] * len(scalars) + [vmem] * len(operands),
            outs,
            [vmem] * len(outs),
            waits,
            cost_estimate=cost,
            compiler_params=small,
        )

    def shape(*dims, dtype=BF16):
        return jax.ShapeDtypeStruct(dims, dtype)

    def in_hbm(*arrays):
        return [pltpu.with_memory_space_constraint(a, pltpu.HBM) for a in arrays]

    def group_specs(begin):
        wide = pl.BlockSpec((tokens, width), lambda g: (0, g + begin))
        state = pl.BlockSpec((tokens, STATE), lambda g: (0, g + begin))
        dt = pl.BlockSpec((heads // groups, tokens), lambda g: (g + begin, 0))
        return wide, state, dt, pl.BlockSpec((1, width), lambda g: (0, g + begin))

    def exchange(value, mask):
        return lax.ppermute(value, "replica", [(r, r ^ mask) for r in range(replicas)])

    gathered = {}

    def spread_rows(b, sent):
        (bit, bits), *_ = stages(replicas)
        gathered[b] = [sent[None]] + [exchange(sent[None], mask << bit) for mask in range(1, 1 << bits)]

    def join(b, waits=()):
        for at, (bit, bits) in enumerate(stages(replicas)):
            if at > 0:
                gathered[b] = [held] + [exchange(held, mask << bit) for mask in range(1, 1 << bits)]
            one = gathered[b][0]
            out = shape(len(gathered[b]) * one.shape[0], *one.shape[1:])
            (held,) = step(join_kernel, gathered[b], [out], waits=waits if at == 0 else ())
        gathered[b] = [held, exchange(held, 1)]

    by_group, by_state, dt_spec, gain_spec = group_specs(0)
    shared = in_hbm(dt_rows, gate_z, b_proj, c_proj, gain, a_log, dt_bias, skip_d)
    later = [stored, target, global_weight, momentum]
    weight, goal, own_global, own_momentum, normed, inv = run(
        functools.partial(forward_kernel, len(later)),
        [shared[0], *in_hbm(x_in), *shared[1:], *in_hbm(*later)],
        [dt_spec, by_group, by_group, by_state, by_state, gain_spec, smem, smem, smem] + [anywhere] * len(later),
        [pltpu.VMEM(v.shape, v.dtype) for v in later] + [pltpu.VMEM((tokens, inner), BF16), pltpu.VMEM((groups, tokens, 1), F32)],
        [vmem] * (len(later) + 2),
        grid=(groups,),
        scratch_shapes=[pltpu.SemaphoreType.DMA((len(later),))],
        cost_estimate=small_cost,
        compiler_params=large,
    )

    part = shape(span_rows, tokens)

    def project(picked):
        kernel = functools.partial(project_kernel, picked)
        return step(kernel, [weight, normed, goal], [part] * len(picked), scalars=[places])

    in_hops, across = inward(heads_over)
    parts = project([0])
    (kept,) = step(kept_kernel, [own_global, own_momentum], [shape(owned, inner)])
    spread_rows("kept", kept)
    parts += project(list(range(1, chunks)))
    first_landed = [lax.ppermute(p, "tensor", in_hops[0]) if in_hops else None for p in parts]
    sums, cots = {}, {}

    def sum_side(n, waits=()):
        held = parts[n]
        for at, pairs in enumerate(in_hops):
            landed = first_landed[n] if at == 0 else lax.ppermute(held, "tensor", pairs)
            (held,) = step(add_kernel, [held, landed], [part], waits=waits)
        sums[n] = held

    def sum_all(n, waits=(), cost=small_cost):
        landed = lax.ppermute(sums[n], "tensor", across)
        (mid,) = step(add_kernel, [sums[n], landed], [part], waits=waits, cost=cost)
        out = mid
        for pairs in reversed(in_hops):
            back = lax.ppermute(out, "tensor", [(b, a) for a, b in pairs])
            out = back if pairs is in_hops[0] else jnp.where(in_middle, mid, back)
        cots[n] = (mid, out)

    terms, deltas = {}, {}
    tile = shape(8, LANES, dtype=F32)
    squares = {-1: jnp.zeros((8, LANES), F32)}

    def new_rows(b, waits=()):
        batch = batches[b]
        rows = len(batch) * piece
        keep, send = step(
            functools.partial(gradient_kernel, batch),
            [c for n in batch for c in cots[n]] + [normed, weight],
            [shape(replicas // 2, rows, inner)] * 2,
            scalars=[places],
            waits=waits,
        )
        return [keep, exchange(send, 1)]

    def send_rows(b, held):
        rows, left = len(batches[b]) * piece, replicas // 2
        for bit, bits in stages(replicas):
            ways = 1 << bits
            left //= ways
            cut = [h.reshape(left, ways, rows, inner) for h in held]
            picked = step(
                functools.partial(pick_kernel, len(cut)),
                cut,
                [shape(left, rows, inner)] * ways,
                scalars=[places.at[4].set(1 << (bit - 1))] if bit > 1 else [places],
            )
            held = [picked[0]] + [exchange(picked[mask], mask << bit) for mask in range(1, ways)]
        terms[b] = held

    def own_rows(b, cost=small_cost):
        batch = batches[b]
        rows = len(batch) * piece
        deltas[b], sent, squares[b] = step(
            functools.partial(delta_kernel, len(terms[b]), batch[0] * piece, replicas),
            [own_global, squares[b - 1], *terms[b]],
            [shape(rows, inner, dtype=F32), shape(rows, inner), tile],
            cost=cost,
        )
        spread_rows(b, sent)

    def backward(begin, count, so_far):
        wide, state, dt, gain_here = group_specs(begin)
        operands = [places, *shared, normed, inv, weight] + [c for n in range(chunks) for c in cots[n]]
        specs = [smem, dt, wide, state, state, gain_here, smem, smem, smem, vmem, vmem, vmem] + [vmem] * (2 * chunks)
        aliases = {}
        if so_far is not None:
            aliases = {len(operands): 0}
            operands.append(so_far)
            specs.append(anywhere)
        (grad,) = run(
            functools.partial(backward_kernel, begin),
            operands,
            specs,
            [shape(tokens, inner)],
            [wide],
            grid=(count,),
            scratch_shapes=[pltpu.VMEM((tokens, width), F32)],
            input_output_aliases=aliases,
            cost_estimate=small_cost,
            compiler_params=large,
        )
        return grad

    first, second = range(2)
    for t in range(chunks):
        sum_side(t, [cots[t - 3][1]] if t >= 3 else [])
        if t == 0:
            join("kept")
        else:
            sum_all(t - 1)
    held_first = new_rows(first)
    sum_all(chunks - 1, cost=large_cost)
    step(gate_kernel, [], [tile], waits=[cots[chunks - 2][1]])
    send_rows(first, held_first)
    held_second = new_rows(second, gathered["kept"][1:])
    own_rows(first, large_cost)
    send_rows(second, held_second)
    half = groups // 2
    grad_input = backward(0, half, None) if half else None
    grad_input = backward(half, groups - half, grad_input)
    own_rows(second, some_cost)
    total = squares[second]
    hops = [("tensor", bit) for bit in range(heads_over.bit_length() - 1)]
    hops += [("replica", bit) for bit in range(1, replicas.bit_length() - 1)]
    for at, (axis, bit) in enumerate(hops):
        if at == len(hops) // 2:
            join(first)
        pairs = [(r, r ^ (1 << bit)) for r in range(lax.axis_size(axis))]
        (total,) = step(add_squares_kernel, [total, lax.ppermute(total, axis, pairs)], [tile])
    join(second, gathered[first][1:])
    columns = [total, exchange(total, 1)]

    sizes = [len(batch) * piece for batch in batches]
    pair_spec = pl.BlockSpec((2 * owned, inner), lambda r: (r, 0))
    held_spec = pl.BlockSpec((owned, inner), lambda r: (0, 0))
    inputs = [own_global, own_momentum, *gathered["kept"], *gathered[first], *gathered[second]]
    inputs += [deltas[first], deltas[second], *columns]
    new_weight, new_global, new_momentum = run(
        functools.partial(weight_kernel, sizes, features * inner * heads_over),
        [places, *inputs],
        [smem] + [vmem] * len(inputs),
        [shape(features, inner), shape(owned, inner, dtype=F32), shape(owned, inner, dtype=F32)],
        [pair_spec, held_spec, held_spec],
        grid=(replicas // 2,),
        cost_estimate=small_cost,
        compiler_params=small,
    )
    return (grad_input, new_weight, new_global, new_momentum)


def solution(mesh):
    placed = (
        P("replica", "tensor"),
        P("replica", "tensor"),
        P("replica", "tensor"),
        P("replica", "tensor"),
        P("replica", "tensor"),
        P("tensor"),
        P("tensor"),
        P("tensor"),
        P("tensor"),
        P("replica", None, "tensor"),
        P("replica", "tensor"),
        P("replica", "tensor"),
        P(("replica", "tensor"), None),
    )
    return jax.shard_map(
        shards,
        mesh=mesh,
        in_specs=placed,
        out_specs=(
            P("replica", "tensor"),
            P(None, "tensor"),
            P("replica", "tensor"),
            P("replica", "tensor"),
        ),
        check_vma=False,
    )
```

```python
import functools

import jax
import jax.numpy as jnp
from jax import lax
from jax.experimental import pallas as pl
from jax.experimental.pallas import tpu as pltpu
from jax.sharding import PartitionSpec as P

HEAD_DIM = 64
STATE = 128
SPAN = 256
HALF = SPAN // 2
LANES = 128

inner_rate = 0.001
outer_rate = 0.7
outer_beta = 0.9
clip_rms = 0.005
LOG2E = 1.4426950408889634

F32 = jnp.float32
BF16 = jnp.bfloat16
NN = (((1,), (0,)), ((), ()))
NT = (((1,), (1,)), ((), ()))
TN = (((0,), (0,)), ((), ()))


def dot(a, b, dims):
    return lax.dot_general(a, b, dims, preferred_element_type=F32)


def silu(z):
    return z * (1.0 / (1.0 + jnp.exp(-z)))


def softplus(v):
    return jnp.maximum(v, 0.0) + jnp.log1p(jnp.exp(-jnp.abs(v)))


def iota(shape, axis):
    return lax.broadcasted_iota(jnp.int32, shape, axis)


def thirds(v):
    high = v.astype(BF16).astype(F32)
    middle = (v - high).astype(BF16).astype(F32)
    return jnp.concatenate([high, middle, v - high - middle], axis=0).astype(BF16)


def by_head(refs, first, per_group, tokens):
    row = iota((per_group, tokens), 0)
    rows = []
    for ref in refs:
        value = jnp.zeros((per_group, tokens), F32)
        for h in range(per_group):
            value = jnp.where(row == h, ref[first + h], value)
        rows.append(value)
    return rows


def head_tables(dt_ref, a_ref, bias_ref, first, per_group):
    bias, a_log = by_head([bias_ref, a_ref], first, per_group, dt_ref.shape[1])
    step = softplus(dt_ref[...] + bias)
    return step, -jnp.exp(a_log) * step * LOG2E


def span_tables(step, rate, lo, per_group, width):
    upper = (iota((SPAN, SPAN), 0) <= iota((SPAN, SPAN), 1)).astype(BF16)
    step_k = step[:, lo : lo + SPAN]
    sums = dot(thirds(rate[:, lo : lo + SPAN]), upper, NN)
    cum = sums[:per_group] + sums[per_group : 2 * per_group] + sums[2 * per_group :]
    spread = (iota((3 * per_group, width), 1) // HEAD_DIM == iota((3 * per_group, width), 0) % per_group).astype(BF16)
    turn = (iota((3 * per_group, per_group), 1) == iota((3 * per_group, per_group), 0) % per_group).astype(BF16)
    cum_col = dot(thirds(cum), turn, TN)
    step_x = dot(thirds(step_k), spread, TN)
    fade_x = dot(thirds(jnp.exp2(cum)), spread, TN)
    tail_x = dot(thirds(jnp.exp2(cum[:, SPAN - 1 :] - cum) * step_k), spread, TN)
    return cum, cum_col, step_x, fade_x, tail_x


def skip_row(skip_ref, first, per_group, width):
    head = iota((1, width), 1) // HEAD_DIM
    row = jnp.zeros((1, width), F32)
    for h in range(per_group):
        row = jnp.where(head == h, skip_ref[first + h], row)
    return row


def decay(gap, mask=None):
    return jnp.exp2(gap if mask is None else jnp.where(mask, gap, -1e30))


def even_odd(v):
    first = iota(v.shape, 1) % (2 * HEAD_DIM) < HEAD_DIM
    return jnp.where(first, v, 0.0).astype(BF16), jnp.where(first, 0.0, v).astype(BF16)


def forward_kernel(
    count, dt_ref, x_ref, z_ref, b_ref, c_ref, gain_ref, a_ref, bias_ref, skip_ref, *refs
):
    loads = [pltpu.make_async_copy(refs[n], refs[count + n], refs[-1].at[n]) for n in range(count)]
    normed_ref, inv_ref = refs[2 * count : 2 * count + 2]

    @pl.when(pl.program_id(0) == 0)
    def _():
        for load in loads:
            load.start()

    tokens, width = x_ref.shape
    per_group = width // HEAD_DIM
    first = pl.program_id(0) * per_group
    lanes_here = pl.ds(pl.multiple_of(pl.program_id(0) * width, LANES), width)
    step, rate = head_tables(dt_ref, a_ref, bias_ref, first, per_group)
    skip = skip_row(skip_ref, first, per_group, width)
    causal = iota((HALF, HALF), 0) >= iota((HALF, HALF), 1)
    spans = tokens // SPAN
    entering = None
    for k in range(spans):
        rows = slice(k * SPAN, (k + 1) * SPAN)
        cum, cum_col, step_x, fade_x, tail_x = span_tables(step, rate, k * SPAN, per_group, width)
        x = x_ref[rows, :].astype(F32)
        b, c = b_ref[rows, :], c_ref[rows, :]
        scores = dot(c, b, NT)
        values = even_odd(x * step_x)
        pieces = []
        for pair in range(per_group // 2):
            lanes = slice(2 * pair * HEAD_DIM, 2 * (pair + 1) * HEAD_DIM)
            tops, bottoms = [], []
            for h in (2 * pair, 2 * pair + 1):
                col, line = cum_col[:, h : h + 1], cum[h : h + 1, :]
                top = decay(col[:HALF] - line[:, :HALF], causal) * scores[:HALF, :HALF]
                left = decay(col[HALF:] - line[:, :HALF]) * scores[HALF:, :HALF]
                low = decay(col[HALF:] - line[:, HALF:], causal) * scores[HALF:, HALF:]
                tops.append(top.astype(BF16))
                bottoms += [left.astype(BF16), low.astype(BF16)]
            upper_values = jnp.concatenate([v[:HALF, lanes] for v in values], axis=0)
            all_values = jnp.concatenate([v[:, lanes] for v in values], axis=0)
            pieces.append(
                jnp.concatenate(
                    [
                        dot(jnp.concatenate(tops, axis=1), upper_values, NN),
                        dot(jnp.concatenate(bottoms, axis=1), all_values, NN),
                    ],
                    axis=0,
                )
            )
        ssd = jnp.concatenate(pieces, axis=1) + skip * x
        if entering is not None:
            ssd = ssd + dot(c, entering.astype(BF16), NN) * fade_x
        if k + 1 < spans:
            state = dot(b, (x * tail_x).astype(BF16), TN)
            entering = state if entering is None else entering * fade_x[SPAN - 1 :, :] + state
        gated = ssd * silu(z_ref[rows, :].astype(F32))
        inv = lax.rsqrt(jnp.mean(gated * gated, axis=1, keepdims=True) + 1e-05)
        normed_ref[rows, lanes_here] = (gated * inv * gain_ref[...]).astype(BF16)
        inv_ref[pl.program_id(0), rows, :] = inv

    @pl.when(pl.program_id(0) == pl.num_programs(0) - 1)
    def _():
        for load in loads:
            load.wait()


def kept_kernel(global_ref, momentum_ref, kept_ref):
    kept_ref[...] = (global_ref[...] - outer_rate * outer_beta * outer_beta * momentum_ref[...]).astype(BF16)


def project_kernel(chunks, place_ref, weight_ref, normed_ref, target_ref, *part_refs):
    replicas, owned, inner = weight_ref.shape
    held, features = target_ref.shape
    piece = part_refs[0].shape[0] // replicas
    tokens = normed_ref.shape[0]
    eye = (iota((held, held), 0) == iota((held, held), 1)).astype(BF16)
    turned = dot(target_ref[...], eye, TN).reshape(replicas, owned, held)
    here = iota((replicas * piece, tokens), 1) // held == place_ref[0]
    for n, part_ref in zip(chunks, part_refs):
        at = slice(n * piece, (n + 1) * piece)
        part = dot(weight_ref[:, at, :].reshape(replicas * piece, inner), normed_ref[...], NT)
        goal = jnp.concatenate([turned[:, at, :].reshape(replicas * piece, held)] * (tokens // held), axis=1)
        part_ref[...] = (part - jnp.where(here, goal, 0.0)).astype(BF16)


def gate_kernel(out_ref):
    out_ref[...] = jnp.zeros_like(out_ref)


def add_kernel(a_ref, b_ref, sum_ref):
    sum_ref[...] = (a_ref[...].astype(F32) + b_ref[...].astype(F32)).astype(BF16)


def add_squares_kernel(*refs):
    *term_refs, sum_ref = refs
    values = [ref[...] for ref in term_refs]
    while len(values) > 1:
        values = [a + b for a, b in zip(values[::2], values[1::2])]
    sum_ref[...] = values[0]


def gradient_kernel(batch, place_ref, *refs):
    count = len(batch)
    cot_refs, (normed_ref, weight_ref, keep_ref, send_ref) = refs[: 2 * count], refs[2 * count :]
    middle = place_ref[1] == 1
    odd = place_ref[2] == 1
    replicas, _, inner = weight_ref.shape
    piece = keep_ref.shape[1] // count
    tile = min(inner, 512)
    for n, chunk in enumerate(batch):
        cot = jnp.where(middle, cot_refs[2 * n][...], cot_refs[2 * n + 1][...])
        rows = slice(chunk * piece, (chunk + 1) * piece)
        at = slice(n * piece, (n + 1) * piece)
        for lo in range(0, inner, tile):
            cols = slice(lo, lo + tile)
            weight = weight_ref[:, rows, cols].reshape(replicas * piece, tile).astype(F32)
            new = weight - inner_rate * dot(cot, normed_ref[:, cols], NN)
            new = new.astype(BF16).reshape(replicas // 2, 2, piece, tile)
            keep_ref[:, at, cols] = jnp.where(odd, new[:, 1], new[:, 0])
            send_ref[:, at, cols] = jnp.where(odd, new[:, 0], new[:, 1])


def backward_kernel(
    begin, place_ref, dt_ref, z_ref, b_ref, c_ref, gain_ref, a_ref, bias_ref, skip_ref, normed_ref, inv_ref, weight_ref, *refs
):
    *cot_refs, dx_ref, dn_ref = refs
    if len(cot_refs) % 2:
        cot_refs = cot_refs[:-1]
    tokens, width = z_ref.shape
    per_group = width // HEAD_DIM
    group = pl.program_id(0) + begin
    first = group * per_group
    here = pl.ds(pl.multiple_of(group * width, LANES), width)
    replicas, owned, _ = weight_ref.shape
    chunks = len(cot_refs) // 2
    piece = owned // chunks
    middle = place_ref[1] == 1
    for n in range(chunks):
        weight = weight_ref[:, n * piece : (n + 1) * piece, here].reshape(replicas * piece, width)
        term = dot(jnp.where(middle, cot_refs[2 * n][...], cot_refs[2 * n + 1][...]), weight, TN)
        dn_ref[...] = term if n == 0 else dn_ref[...] + term
    step, rate = head_tables(dt_ref, a_ref, bias_ref, first, per_group)
    skip = skip_row(skip_ref, first, per_group, width)
    causal = iota((HALF, HALF), 1) >= iota((HALF, HALF), 0)
    spans = tokens // SPAN
    d_state = None
    for k in reversed(range(spans)):
        rows = slice(k * SPAN, (k + 1) * SPAN)
        cum, cum_col, step_x, fade_x, tail_x = span_tables(step, rate, k * SPAN, per_group, width)
        dn = dn_ref[rows, :]
        gain = gain_ref[...]
        normed = normed_ref[rows, here].astype(F32)
        shared = jnp.mean(normed * dn, axis=1, keepdims=True)
        d_gated = inv_ref[group, rows, :] * (gain * dn - (normed / gain) * shared)
        d_ssd = d_gated * silu(z_ref[rows, :].astype(F32))
        values = even_odd(d_ssd)
        b, c = b_ref[rows, :], c_ref[rows, :]
        scores = dot(b, c, NT)
        pieces = []
        for pair in range(per_group // 2):
            lanes = slice(2 * pair * HEAD_DIM, 2 * (pair + 1) * HEAD_DIM)
            tops, bottoms = [], []
            for h in (2 * pair, 2 * pair + 1):
                col, line = cum_col[:, h : h + 1], cum[h : h + 1, :]
                high = decay(line[:, :HALF] - col[:HALF], causal) * scores[:HALF, :HALF]
                right = decay(line[:, HALF:] - col[:HALF]) * scores[:HALF, HALF:]
                low = decay(line[:, HALF:] - col[HALF:], causal) * scores[HALF:, HALF:]
                tops += [high.astype(BF16), right.astype(BF16)]
                bottoms.append(low.astype(BF16))
            lower_values = jnp.concatenate([v[HALF:, lanes] for v in values], axis=0)
            all_values = jnp.concatenate([v[:, lanes] for v in values], axis=0)
            pieces.append(
                jnp.concatenate(
                    [
                        dot(jnp.concatenate(tops, axis=1), all_values, NN),
                        dot(jnp.concatenate(bottoms, axis=1), lower_values, NN),
                    ],
                    axis=0,
                )
            )
        dx = jnp.concatenate(pieces, axis=1) * step_x + skip * d_ssd
        if d_state is not None:
            dx = dx + dot(b, d_state.astype(BF16), NN) * tail_x
        dx_ref[rows, :] = dx.astype(BF16)
        if k > 0:
            own = dot(c, (d_ssd * fade_x).astype(BF16), TN)
            d_state = own if d_state is None else own + d_state * fade_x[SPAN - 1 :, :]


def pick_kernel(count, place_ref, *refs):
    terms, outs = refs[:count], refs[count:]
    my = lax.rem(lax.div(place_ref[3], place_ref[4]), len(outs))
    for mask, out_ref in enumerate(outs):
        at = lax.bitwise_xor(my, jnp.int32(mask))
        total = terms[0][:, at].astype(F32)
        for term in terms[1:]:
            total = total + term[:, at].astype(F32)
        out_ref[...] = total.astype(BF16)


def delta_kernel(count, lo, replicas, global_ref, before_ref, *refs):
    terms, (delta_ref, sent_ref, squares_ref) = refs[:count], refs[count:]
    rows, inner = delta_ref.shape
    total = terms[0][0].astype(F32)
    for term in terms[1:]:
        total = total + term[0].astype(F32)
    delta = global_ref[lo : lo + rows, :] - total / replicas
    delta_ref[...] = delta
    sent_ref[...] = delta.astype(BF16)
    squares = jnp.sum(delta * delta, axis=0, keepdims=True)
    squares = before_ref[...] + jnp.broadcast_to(jnp.sum(squares, axis=1, keepdims=True), before_ref.shape)
    squares_ref[...] = squares


def join_kernel(*refs):
    *parts, out_ref = refs
    lo = 0
    for part in parts:
        out_ref[lo : lo + part.shape[0]] = part[...]
        lo += part.shape[0]


def weight_kernel(sizes, entries, place_ref, global_ref, momentum_ref, *refs):
    count = len(sizes)
    pairs, deltas, squares = refs[: 2 * count + 2], refs[2 * count + 2 : 3 * count + 2], refs[3 * count + 2 : -3]
    new_ref, new_global_ref, new_momentum_ref = refs[-3:]
    mean = (squares[0][:1, :1] + squares[1][:1, :1]) / entries
    factor = jnp.minimum(1.0, clip_rms / jnp.sqrt(mean + 1e-06))
    at_chip = lax.bitwise_xor(pl.program_id(0), place_ref[3])
    owned = new_ref.shape[0] // 2
    scale = (outer_rate * (1.0 + outer_beta)) * factor

    def one_core(core, side):
        lo = 0
        for n, size in enumerate(sizes):
            kept = pairs[side][at_chip, lo : lo + size, :].astype(F32)
            delta = pairs[2 * n + 2 + side][at_chip, :size, :].astype(F32)
            new_ref[core * owned + lo : core * owned + lo + size, :] = (kept - scale * delta).astype(BF16)
            lo += size

    for own_core in range(2):

        @pl.when(place_ref[2] == own_core)
        def _():
            one_core(own_core, 0)
            one_core(1 - own_core, 1)

    @pl.when(pl.program_id(0) == 0)
    def _():
        lo = 0
        for n, size in enumerate(sizes):
            rows = slice(lo, lo + size)
            lo += size
            clipped = factor * deltas[n][...]
            new_momentum = outer_beta * momentum_ref[rows, :] + clipped
            new_momentum_ref[rows, :] = new_momentum
            new_global_ref[rows, :] = global_ref[rows, :] - outer_rate * (clipped + outer_beta * new_momentum)


def inward(axis_size):
    half = axis_size // 2
    hops = [[(s, s + 1), (axis_size - 1 - s, axis_size - 2 - s)] for s in range(half - 1)]
    return hops, [(half - 1, half), (half, half - 1)]


def in_turn(kernel, inputs, waits, outs):
    def body(*refs):
        end = inputs + waits + outs
        refs[end][...] = jnp.zeros_like(refs[end])
        kernel(*refs[:inputs], *refs[inputs + waits : end], *refs[end + 1 :])

    return body


def stages(replicas):
    bit, left, found = 1, replicas // 2, []
    while left > 1:
        bits = 2 if left >= 4 else 1
        found.append((bit, bits))
        bit, left = bit + bits, left >> bits
    return found


def shards(
    x_in,
    gate_z,
    b_proj,
    c_proj,
    dt_raw,
    a_log,
    dt_bias,
    skip_d,
    norm_gain,
    out_weight,
    global_weight,
    momentum,
    target,
):
    tokens, inner = x_in.shape
    features = out_weight.shape[1]
    replicas = lax.axis_size("replica")
    heads_over = lax.axis_size("tensor")
    groups = b_proj.shape[1] // STATE
    heads = dt_raw.shape[1]
    width = inner // groups
    owned = features // replicas
    chunks = max(2, min(4, owned // 16))
    batches = [list(range(chunks // 2)), list(range(chunks // 2, chunks))]
    piece = owned // chunks
    span_rows = replicas * piece
    place = lax.axis_index("tensor")
    me = lax.axis_index("replica")
    in_middle = (place == heads_over // 2 - 1) | (place == heads_over // 2)
    one = jnp.int32(1)
    places = jnp.stack([place, in_middle.astype(jnp.int32), lax.rem(me, 2), lax.div(me, 2), one]).astype(jnp.int32)
    stored = out_weight[0].reshape(replicas, owned, inner)
    gain = norm_gain.reshape(1, inner)
    dt_rows = dt_raw.T

    smem = pl.BlockSpec(memory_space=pltpu.SMEM)
    vmem = pl.BlockSpec(memory_space=pltpu.VMEM)
    anywhere = pl.BlockSpec(memory_space=pl.ANY)
    inv_spec = pl.BlockSpec((1, tokens, 1), lambda g: (g, 0, 0))
    large = pltpu.CompilerParams(vmem_limit_bytes=20 * 1024 * 1024)
    small = pltpu.CompilerParams(vmem_limit_bytes=12 * 1024 * 1024)
    small_cost = pl.CostEstimate(flops=1, bytes_accessed=1, transcendentals=0)
    some_cost = pl.CostEstimate(flops=2_000_000_000, bytes_accessed=1, transcendentals=0)
    large_cost = pl.CostEstimate(flops=30_000_000_000, bytes_accessed=1, transcendentals=0)

    turn = []

    def run(kernel, inputs, in_specs, outs, out_specs, waits=(), **options):
        waits = [*turn[-1:], *waits]
        done = jax.ShapeDtypeStruct((8, LANES), F32)
        *results, ran = pl.pallas_call(
            in_turn(kernel, len(inputs), len(waits), len(outs)),
            in_specs=[*in_specs, *[vmem] * len(waits)],
            out_specs=[*out_specs, vmem],
            out_shape=[*outs, done],
            **options,
        )(*inputs, *waits)
        turn.append(ran)
        return results

    def step(kernel, operands, outs, scalars=(), waits=(), cost=small_cost):
        return run(
            kernel,
            [*scalars, *operands],
            [smem] * len(scalars) + [vmem] * len(operands),
            outs,
            [vmem] * len(outs),
            waits,
            cost_estimate=cost,
            compiler_params=small,
        )

    def shape(*dims, dtype=BF16):
        return jax.ShapeDtypeStruct(dims, dtype)

    def in_hbm(*arrays):
        return [pltpu.with_memory_space_constraint(a, pltpu.HBM) for a in arrays]

    def group_specs(begin):
        wide = pl.BlockSpec((tokens, width), lambda g: (0, g + begin))
        state = pl.BlockSpec((tokens, STATE), lambda g: (0, g + begin))
        dt = pl.BlockSpec((heads // groups, tokens), lambda g: (g + begin, 0))
        return wide, state, dt, pl.BlockSpec((1, width), lambda g: (0, g + begin))

    def exchange(value, mask):
        return lax.ppermute(value, "replica", [(r, r ^ mask) for r in range(replicas)])

    gathered = {}

    def spread_rows(b, sent):
        (bit, bits), *_ = stages(replicas)
        gathered[b] = [sent[None]] + [exchange(sent[None], mask << bit) for mask in range(1, 1 << bits)]

    def join(b, waits=()):
        for at, (bit, bits) in enumerate(stages(replicas)):
            if at > 0:
                gathered[b] = [held] + [exchange(held, mask << bit) for mask in range(1, 1 << bits)]
            one = gathered[b][0]
            out = shape(len(gathered[b]) * one.shape[0], *one.shape[1:])
            (held,) = step(join_kernel, gathered[b], [out], waits=waits if at == 0 else ())
        gathered[b] = [held, exchange(held, 1)]

    by_group, by_state, dt_spec, gain_spec = group_specs(0)
    shared = in_hbm(dt_rows, gate_z, b_proj, c_proj, gain, a_log, dt_bias, skip_d)
    later = [stored, target, global_weight, momentum]
    weight, goal, own_global, own_momentum, normed, inv = run(
        functools.partial(forward_kernel, len(later)),
        [shared[0], *in_hbm(x_in), *shared[1:], *in_hbm(*later)],
        [dt_spec, by_group, by_group, by_state, by_state, gain_spec, smem, smem, smem] + [anywhere] * len(later),
        [pltpu.VMEM(v.shape, v.dtype) for v in later] + [pltpu.VMEM((tokens, inner), BF16), pltpu.VMEM((groups, tokens, 1), F32)],
        [vmem] * (len(later) + 2),
        grid=(groups,),
        scratch_shapes=[pltpu.SemaphoreType.DMA((len(later),))],
        cost_estimate=small_cost,
        compiler_params=large,
    )

    part = shape(span_rows, tokens)

    def project(picked):
        kernel = functools.partial(project_kernel, picked)
        return step(kernel, [weight, normed, goal], [part] * len(picked), scalars=[places])

    in_hops, across = inward(heads_over)
    parts = project([0])
    (kept,) = step(kept_kernel, [own_global, own_momentum], [shape(owned, inner)])
    spread_rows("kept", kept)
    parts += project(list(range(1, chunks)))
    first_landed = [lax.ppermute(p, "tensor", in_hops[0]) if in_hops else None for p in parts]
    sums, cots = {}, {}

    def sum_side(n, waits=()):
        held = parts[n]
        for at, pairs in enumerate(in_hops):
            landed = first_landed[n] if at == 0 else lax.ppermute(held, "tensor", pairs)
            (held,) = step(add_kernel, [held, landed], [part], waits=waits)
        sums[n] = held

    def sum_all(n, waits=(), cost=small_cost):
        landed = lax.ppermute(sums[n], "tensor", across)
        (mid,) = step(add_kernel, [sums[n], landed], [part], waits=waits, cost=cost)
        out = mid
        for pairs in reversed(in_hops):
            back = lax.ppermute(out, "tensor", [(b, a) for a, b in pairs])
            out = back if pairs is in_hops[0] else jnp.where(in_middle, mid, back)
        cots[n] = (mid, out)

    terms, deltas = {}, {}
    tile = shape(8, LANES, dtype=F32)
    squares = {-1: jnp.zeros((8, LANES), F32)}

    def new_rows(b, waits=()):
        batch = batches[b]
        rows = len(batch) * piece
        keep, send = step(
            functools.partial(gradient_kernel, batch),
            [c for n in batch for c in cots[n]] + [normed, weight],
            [shape(replicas // 2, rows, inner)] * 2,
            scalars=[places],
            waits=waits,
        )
        return [keep, exchange(send, 1)]

    def send_rows(b, held):
        rows, left = len(batches[b]) * piece, replicas // 2
        for bit, bits in stages(replicas):
            ways = 1 << bits
            left //= ways
            cut = [h.reshape(left, ways, rows, inner) for h in held]
            picked = step(
                functools.partial(pick_kernel, len(cut)),
                cut,
                [shape(left, rows, inner)] * ways,
                scalars=[places.at[4].set(1 << (bit - 1))] if bit > 1 else [places],
            )
            held = [picked[0]] + [exchange(picked[mask], mask << bit) for mask in range(1, ways)]
        terms[b] = held

    def own_rows(b, cost=small_cost):
        batch = batches[b]
        rows = len(batch) * piece
        deltas[b], sent, squares[b] = step(
            functools.partial(delta_kernel, len(terms[b]), batch[0] * piece, replicas),
            [own_global, squares[b - 1], *terms[b]],
            [shape(rows, inner, dtype=F32), shape(rows, inner), tile],
            cost=cost,
        )
        spread_rows(b, sent)

    def backward(begin, count, so_far):
        wide, state, dt, gain_here = group_specs(begin)
        operands = [places, *shared, normed, inv, weight] + [c for n in range(chunks) for c in cots[n]]
        specs = [smem, dt, wide, state, state, gain_here, smem, smem, smem, vmem, vmem, vmem] + [vmem] * (2 * chunks)
        aliases = {}
        if so_far is not None:
            aliases = {len(operands): 0}
            operands.append(so_far)
            specs.append(anywhere)
        (grad,) = run(
            functools.partial(backward_kernel, begin),
            operands,
            specs,
            [shape(tokens, inner)],
            [wide],
            grid=(count,),
            scratch_shapes=[pltpu.VMEM((tokens, width), F32)],
            input_output_aliases=aliases,
            cost_estimate=small_cost,
            compiler_params=large,
        )
        return grad

    first, second = range(2)
    for t in range(chunks):
        sum_side(t, [cots[t - 3][1]] if t >= 3 else [])
        if t == 0:
            join("kept")
        else:
            sum_all(t - 1)
    held_first = new_rows(first)
    sum_all(chunks - 1, cost=large_cost)
    step(gate_kernel, [], [tile], waits=[cots[chunks - 2][1]])
    send_rows(first, held_first)
    held_second = new_rows(second, gathered["kept"][1:])
    own_rows(first, large_cost)
    send_rows(second, held_second)
    half = groups // 2
    grad_input = backward(0, half, None) if half else None
    grad_input = backward(half, groups - half, grad_input)
    join(first)
    own_rows(second, large_cost)
    total = squares[second]
    for bit in range(heads_over.bit_length() - 1):
        pairs = [(t, t ^ (1 << bit)) for t in range(heads_over)]
        (total,) = step(add_squares_kernel, [total, lax.ppermute(total, "tensor", pairs)], [tile], waits=gathered[first][1:])
    for bit, bits in stages(replicas):
        landed = [exchange(total, mask << bit) for mask in range(1, 1 << bits)]
        (total,) = step(add_squares_kernel, [total, *landed], [tile])
    join(second)
    columns = [total, exchange(total, 1)]

    sizes = [len(batch) * piece for batch in batches]
    pair_spec = pl.BlockSpec((2 * owned, inner), lambda r: (r, 0))
    held_spec = pl.BlockSpec((owned, inner), lambda r: (0, 0))
    inputs = [own_global, own_momentum, *gathered["kept"], *gathered[first], *gathered[second]]
    inputs += [deltas[first], deltas[second], *columns]
    new_weight, new_global, new_momentum = run(
        functools.partial(weight_kernel, sizes, features * inner * heads_over),
        [places, *inputs],
        [smem] + [vmem] * len(inputs),
        [shape(features, inner), shape(owned, inner, dtype=F32), shape(owned, inner, dtype=F32)],
        [pair_spec, held_spec, held_spec],
        grid=(replicas // 2,),
        cost_estimate=small_cost,
        compiler_params=small,
    )
    return (grad_input, new_weight, new_global, new_momentum)


def solution(mesh):
    placed = (
        P("replica", "tensor"),
        P("replica", "tensor"),
        P("replica", "tensor"),
        P("replica", "tensor"),
        P("replica", "tensor"),
        P("tensor"),
        P("tensor"),
        P("tensor"),
        P("tensor"),
        P("replica", None, "tensor"),
        P("replica", "tensor"),
        P("replica", "tensor"),
        P(("replica", "tensor"), None),
    )
    return jax.shard_map(
        shards,
        mesh=mesh,
        in_specs=placed,
        out_specs=(
            P("replica", "tensor"),
            P(None, "tensor"),
            P("replica", "tensor"),
            P("replica", "tensor"),
        ),
        check_vma=False,
    )
```

```python
import functools

import jax
import jax.numpy as jnp
from jax import lax
from jax.experimental import pallas as pl
from jax.experimental.pallas import tpu as pltpu
from jax.sharding import PartitionSpec as P

HEAD_DIM = 64
STATE = 128
SPAN = 256
HALF = SPAN // 2
LANES = 128

inner_rate = 0.001
outer_rate = 0.7
outer_beta = 0.9
clip_rms = 0.005
LOG2E = 1.4426950408889634

F32 = jnp.float32
BF16 = jnp.bfloat16
NN = (((1,), (0,)), ((), ()))
NT = (((1,), (1,)), ((), ()))
TN = (((0,), (0,)), ((), ()))


def dot(a, b, dims):
    return lax.dot_general(a, b, dims, preferred_element_type=F32)


def silu(z):
    return 0.5 * z * (1.0 + jnp.tanh(0.5 * z))


def softplus(v):
    return jnp.maximum(v, 0.0) + jnp.log1p(jnp.exp(-jnp.abs(v)))


def iota(shape, axis):
    return lax.broadcasted_iota(jnp.int32, shape, axis)


def thirds(v):
    high = v.astype(BF16).astype(F32)
    middle = (v - high).astype(BF16).astype(F32)
    return jnp.concatenate([high, middle, v - high - middle], axis=0).astype(BF16)


def by_head(refs, first, per_group, tokens):
    row = iota((per_group, tokens), 0)
    rows = []
    for ref in refs:
        value = jnp.zeros((per_group, tokens), F32)
        for h in range(per_group):
            value = jnp.where(row == h, ref[first + h], value)
        rows.append(value)
    return rows


def head_tables(dt_ref, a_ref, bias_ref, first, per_group):
    bias, a_log = by_head([bias_ref, a_ref], first, per_group, dt_ref.shape[1])
    step = softplus(dt_ref[...] + bias)
    return step, -jnp.exp(a_log) * step * LOG2E


def span_tables(step, rate, lo, per_group, width):
    upper = (iota((SPAN, SPAN), 0) <= iota((SPAN, SPAN), 1)).astype(BF16)
    step_k = step[:, lo : lo + SPAN]
    sums = dot(thirds(rate[:, lo : lo + SPAN]), upper, NN)
    cum = sums[:per_group] + sums[per_group : 2 * per_group] + sums[2 * per_group :]
    spread = (iota((3 * per_group, width), 1) // HEAD_DIM == iota((3 * per_group, width), 0) % per_group).astype(BF16)
    turn = (iota((3 * per_group, per_group), 1) == iota((3 * per_group, per_group), 0) % per_group).astype(BF16)
    cum_col = dot(thirds(cum), turn, TN)
    step_x = dot(thirds(step_k), spread, TN)
    fade_x = dot(thirds(jnp.exp2(cum)), spread, TN)
    tail_x = dot(thirds(jnp.exp2(cum[:, SPAN - 1 :] - cum) * step_k), spread, TN)
    return cum, cum_col, step_x, fade_x, tail_x


def skip_row(skip_ref, first, per_group, width):
    head = iota((1, width), 1) // HEAD_DIM
    row = jnp.zeros((1, width), F32)
    for h in range(per_group):
        row = jnp.where(head == h, skip_ref[first + h], row)
    return row


def decay(gap, mask=None):
    return jnp.exp2(gap if mask is None else jnp.where(mask, gap, -1e30))


def even_odd(v):
    first = iota(v.shape, 1) % (2 * HEAD_DIM) < HEAD_DIM
    return jnp.where(first, v, 0.0).astype(BF16), jnp.where(first, 0.0, v).astype(BF16)


def forward_kernel(
    count, dt_ref, x_ref, z_ref, b_ref, c_ref, gain_ref, a_ref, bias_ref, skip_ref, *refs
):
    loads = [pltpu.make_async_copy(refs[n], refs[count + n], refs[-1].at[n]) for n in range(count)]
    normed_ref, inv_ref = refs[2 * count : 2 * count + 2]

    @pl.when(pl.program_id(0) == 0)
    def _():
        for load in loads:
            load.start()

    tokens, width = x_ref.shape
    per_group = width // HEAD_DIM
    first = pl.program_id(0) * per_group
    lanes_here = pl.ds(pl.multiple_of(pl.program_id(0) * width, LANES), width)
    step, rate = head_tables(dt_ref, a_ref, bias_ref, first, per_group)
    skip = skip_row(skip_ref, first, per_group, width)
    causal = iota((HALF, HALF), 0) >= iota((HALF, HALF), 1)
    spans = tokens // SPAN
    entering = None
    for k in range(spans):
        rows = slice(k * SPAN, (k + 1) * SPAN)
        cum, cum_col, step_x, fade_x, tail_x = span_tables(step, rate, k * SPAN, per_group, width)
        x = x_ref[rows, :].astype(F32)
        b, c = b_ref[rows, :], c_ref[rows, :]
        scores = dot(c, b, NT)
        values = even_odd(x * step_x)
        pieces = []
        for pair in range(per_group // 2):
            lanes = slice(2 * pair * HEAD_DIM, 2 * (pair + 1) * HEAD_DIM)
            tops, bottoms = [], []
            for h in (2 * pair, 2 * pair + 1):
                col, line = cum_col[:, h : h + 1], cum[h : h + 1, :]
                top = decay(col[:HALF] - line[:, :HALF], causal) * scores[:HALF, :HALF]
                left = decay(col[HALF:] - line[:, :HALF]) * scores[HALF:, :HALF]
                low = decay(col[HALF:] - line[:, HALF:], causal) * scores[HALF:, HALF:]
                tops.append(top.astype(BF16))
                bottoms += [left.astype(BF16), low.astype(BF16)]
            upper_values = jnp.concatenate([v[:HALF, lanes] for v in values], axis=0)
            all_values = jnp.concatenate([v[:, lanes] for v in values], axis=0)
            pieces.append(
                jnp.concatenate(
                    [
                        dot(jnp.concatenate(tops, axis=1), upper_values, NN),
                        dot(jnp.concatenate(bottoms, axis=1), all_values, NN),
                    ],
                    axis=0,
                )
            )
        ssd = jnp.concatenate(pieces, axis=1) + skip * x
        if entering is not None:
            ssd = ssd + dot(c, entering.astype(BF16), NN) * fade_x
        if k + 1 < spans:
            state = dot(b, (x * tail_x).astype(BF16), TN)
            entering = state if entering is None else entering * fade_x[SPAN - 1 :, :] + state
        gated = ssd * silu(z_ref[rows, :].astype(F32))
        inv = lax.rsqrt(jnp.mean(gated * gated, axis=1, keepdims=True) + 1e-05)
        normed_ref[rows, lanes_here] = (gated * inv * gain_ref[...]).astype(BF16)
        inv_ref[pl.program_id(0), rows, :] = inv

    @pl.when(pl.program_id(0) == pl.num_programs(0) - 1)
    def _():
        for load in loads:
            load.wait()


def kept_kernel(global_ref, momentum_ref, kept_ref):
    kept_ref[...] = (global_ref[...] - outer_rate * outer_beta * outer_beta * momentum_ref[...]).astype(BF16)


def project_kernel(chunks, place_ref, weight_ref, normed_ref, target_ref, *part_refs):
    replicas, owned, inner = weight_ref.shape
    held, features = target_ref.shape
    piece = part_refs[0].shape[0] // replicas
    tokens = normed_ref.shape[0]
    eye = (iota((held, held), 0) == iota((held, held), 1)).astype(BF16)
    turned = dot(target_ref[...], eye, TN).reshape(replicas, owned, held)
    here = iota((replicas * piece, tokens), 1) // held == place_ref[0]
    for n, part_ref in zip(chunks, part_refs):
        at = slice(n * piece, (n + 1) * piece)
        part = dot(weight_ref[:, at, :].reshape(replicas * piece, inner), normed_ref[...], NT)
        goal = jnp.concatenate([turned[:, at, :].reshape(replicas * piece, held)] * (tokens // held), axis=1)
        part_ref[...] = (part - jnp.where(here, goal, 0.0)).astype(BF16)


def gate_kernel(out_ref):
    out_ref[...] = jnp.zeros_like(out_ref)


def add_kernel(a_ref, b_ref, sum_ref):
    sum_ref[...] = (a_ref[...].astype(F32) + b_ref[...].astype(F32)).astype(BF16)


def add_squares_kernel(*refs):
    *term_refs, sum_ref = refs
    values = [ref[...] for ref in term_refs]
    while len(values) > 1:
        values = [a + b for a, b in zip(values[::2], values[1::2])]
    sum_ref[...] = values[0]


def gradient_kernel(batch, place_ref, *refs):
    count = len(batch)
    cot_refs, (normed_ref, weight_ref, keep_ref, send_ref) = refs[: 2 * count], refs[2 * count :]
    middle = place_ref[1] == 1
    odd = place_ref[2] == 1
    replicas, _, inner = weight_ref.shape
    piece = keep_ref.shape[1] // count
    tile = min(inner, 512)
    for n, chunk in enumerate(batch):
        cot = jnp.where(middle, cot_refs[2 * n][...], cot_refs[2 * n + 1][...])
        rows = slice(chunk * piece, (chunk + 1) * piece)
        at = slice(n * piece, (n + 1) * piece)
        for lo in range(0, inner, tile):
            cols = slice(lo, lo + tile)
            weight = weight_ref[:, rows, cols].reshape(replicas * piece, tile).astype(F32)
            new = weight - inner_rate * dot(cot, normed_ref[:, cols], NN)
            new = new.astype(BF16).reshape(replicas // 2, 2, piece, tile)
            keep_ref[:, at, cols] = jnp.where(odd, new[:, 1], new[:, 0])
            send_ref[:, at, cols] = jnp.where(odd, new[:, 0], new[:, 1])


def backward_kernel(
    begin, place_ref, dt_ref, z_ref, b_ref, c_ref, gain_ref, a_ref, bias_ref, skip_ref, normed_ref, inv_ref, weight_ref, *refs
):
    *cot_refs, dx_ref, dn_ref = refs
    if len(cot_refs) % 2:
        cot_refs = cot_refs[:-1]
    tokens, width = z_ref.shape
    per_group = width // HEAD_DIM
    group = pl.program_id(0) + begin
    first = group * per_group
    here = pl.ds(pl.multiple_of(group * width, LANES), width)
    replicas, owned, _ = weight_ref.shape
    chunks = len(cot_refs) // 2
    piece = owned // chunks
    middle = place_ref[1] == 1
    for n in range(chunks):
        weight = weight_ref[:, n * piece : (n + 1) * piece, here].reshape(replicas * piece, width)
        term = dot(jnp.where(middle, cot_refs[2 * n][...], cot_refs[2 * n + 1][...]), weight, TN)
        dn_ref[...] = term if n == 0 else dn_ref[...] + term
    step, rate = head_tables(dt_ref, a_ref, bias_ref, first, per_group)
    skip = skip_row(skip_ref, first, per_group, width)
    causal = iota((HALF, HALF), 1) >= iota((HALF, HALF), 0)
    spans = tokens // SPAN
    d_state = None
    for k in reversed(range(spans)):
        rows = slice(k * SPAN, (k + 1) * SPAN)
        cum, cum_col, step_x, fade_x, tail_x = span_tables(step, rate, k * SPAN, per_group, width)
        dn = dn_ref[rows, :]
        gain = gain_ref[...]
        normed = normed_ref[rows, here].astype(F32)
        shared = jnp.mean(normed * dn, axis=1, keepdims=True)
        d_gated = inv_ref[group, rows, :] * (gain * dn - (normed / gain) * shared)
        d_ssd = d_gated * silu(z_ref[rows, :].astype(F32))
        values = even_odd(d_ssd)
        b, c = b_ref[rows, :], c_ref[rows, :]
        scores = dot(b, c, NT)
        pieces = []
        for pair in range(per_group // 2):
            lanes = slice(2 * pair * HEAD_DIM, 2 * (pair + 1) * HEAD_DIM)
            tops, bottoms = [], []
            for h in (2 * pair, 2 * pair + 1):
                col, line = cum_col[:, h : h + 1], cum[h : h + 1, :]
                high = decay(line[:, :HALF] - col[:HALF], causal) * scores[:HALF, :HALF]
                right = decay(line[:, HALF:] - col[:HALF]) * scores[:HALF, HALF:]
                low = decay(line[:, HALF:] - col[HALF:], causal) * scores[HALF:, HALF:]
                tops += [high.astype(BF16), right.astype(BF16)]
                bottoms.append(low.astype(BF16))
            lower_values = jnp.concatenate([v[HALF:, lanes] for v in values], axis=0)
            all_values = jnp.concatenate([v[:, lanes] for v in values], axis=0)
            pieces.append(
                jnp.concatenate(
                    [
                        dot(jnp.concatenate(tops, axis=1), all_values, NN),
                        dot(jnp.concatenate(bottoms, axis=1), lower_values, NN),
                    ],
                    axis=0,
                )
            )
        dx = jnp.concatenate(pieces, axis=1) * step_x + skip * d_ssd
        if d_state is not None:
            dx = dx + dot(b, d_state.astype(BF16), NN) * tail_x
        dx_ref[rows, :] = dx.astype(BF16)
        if k > 0:
            own = dot(c, (d_ssd * fade_x).astype(BF16), TN)
            d_state = own if d_state is None else own + d_state * fade_x[SPAN - 1 :, :]


def pick_kernel(count, unit, place_ref, *refs):
    terms, outs = refs[:count], refs[count:]
    my = lax.rem(lax.div(place_ref[3], unit), len(outs))
    for mask, out_ref in enumerate(outs):
        at = lax.bitwise_xor(my, jnp.int32(mask))
        total = terms[0][:, at].astype(F32)
        for term in terms[1:]:
            total = total + term[:, at].astype(F32)
        out_ref[...] = total.astype(BF16)


def delta_kernel(count, lo, replicas, global_ref, before_ref, *refs):
    terms, (delta_ref, sent_ref, squares_ref) = refs[:count], refs[count:]
    rows, inner = delta_ref.shape
    total = terms[0][0].astype(F32)
    for term in terms[1:]:
        total = total + term[0].astype(F32)
    delta = global_ref[lo : lo + rows, :] - total / replicas
    delta_ref[...] = delta
    sent_ref[...] = delta.astype(BF16)
    squares = jnp.sum(delta * delta, axis=0, keepdims=True)
    squares = before_ref[...] + jnp.broadcast_to(jnp.sum(squares, axis=1, keepdims=True), before_ref.shape)
    squares_ref[...] = squares


def join_kernel(*refs):
    *parts, out_ref = refs
    lo = 0
    for part in parts:
        out_ref[lo : lo + part.shape[0]] = part[...]
        lo += part.shape[0]


def weight_kernel(sizes, entries, place_ref, global_ref, momentum_ref, *refs):
    count = len(sizes)
    pairs, deltas, squares = refs[: 2 * count + 2], refs[2 * count + 2 : 3 * count + 2], refs[3 * count + 2 : -3]
    new_ref, new_global_ref, new_momentum_ref = refs[-3:]
    mean = (squares[0][:1, :1] + squares[1][:1, :1]) / entries
    factor = jnp.minimum(1.0, clip_rms / jnp.sqrt(mean + 1e-06))
    at_chip = lax.bitwise_xor(pl.program_id(0), place_ref[3])
    owned = new_ref.shape[0] // 2
    scale = (outer_rate * (1.0 + outer_beta)) * factor

    def one_core(core, side):
        lo = 0
        for n, size in enumerate(sizes):
            kept = pairs[side][at_chip, lo : lo + size, :].astype(F32)
            delta = pairs[2 * n + 2 + side][at_chip, :size, :].astype(F32)
            new_ref[core * owned + lo : core * owned + lo + size, :] = (kept - scale * delta).astype(BF16)
            lo += size

    for own_core in range(2):

        @pl.when(place_ref[2] == own_core)
        def _():
            one_core(own_core, 0)
            one_core(1 - own_core, 1)

    part = new_global_ref.shape[0]
    lo = 0
    for n, size in enumerate(sizes):
        for row in range(0, size, min(size, part)):
            rows = min(size, part)
            at, here = slice(lo + row, lo + row + rows), (lo + row) % part

            @pl.when(pl.program_id(0) == (lo + row) // part)
            def _():
                clipped = factor * deltas[n][row : row + rows, :]
                new_momentum = outer_beta * momentum_ref[at, :] + clipped
                new_momentum_ref[here : here + rows, :] = new_momentum
                new_global = global_ref[at, :] - outer_rate * (clipped + outer_beta * new_momentum)
                new_global_ref[here : here + rows, :] = new_global

        lo += size


def inward(axis_size):
    half = axis_size // 2
    hops = [[(s, s + 1), (axis_size - 1 - s, axis_size - 2 - s)] for s in range(half - 1)]
    return hops, [(half - 1, half), (half, half - 1)]


def in_turn(kernel, inputs, waits, outs):
    def body(*refs):
        end = inputs + waits + outs
        refs[end][...] = jnp.zeros_like(refs[end])
        kernel(*refs[:inputs], *refs[inputs + waits : end], *refs[end + 1 :])

    return body


def stages(replicas, most=2):
    bit, left, found = 1, replicas // 2, []
    while left > 1:
        bits = most if left >= 1 << most else 1
        found.append((bit, bits))
        bit, left = bit + bits, left >> bits
    return found


def shards(
    x_in,
    gate_z,
    b_proj,
    c_proj,
    dt_raw,
    a_log,
    dt_bias,
    skip_d,
    norm_gain,
    out_weight,
    global_weight,
    momentum,
    target,
):
    tokens, inner = x_in.shape
    features = out_weight.shape[1]
    replicas = lax.axis_size("replica")
    heads_over = lax.axis_size("tensor")
    groups = b_proj.shape[1] // STATE
    heads = dt_raw.shape[1]
    width = inner // groups
    owned = features // replicas
    chunks = max(2, min(4, owned // 16))
    batches = [[n] for n in range(chunks // 2)] + [list(range(chunks // 2, chunks))]
    piece = owned // chunks
    span_rows = replicas * piece
    place = lax.axis_index("tensor")
    me = lax.axis_index("replica")
    in_middle = (place == heads_over // 2 - 1) | (place == heads_over // 2)
    places = jnp.stack([place, in_middle.astype(jnp.int32), lax.rem(me, 2), lax.div(me, 2)]).astype(jnp.int32)
    stored = out_weight[0].reshape(replicas, owned, inner)
    gain = norm_gain.reshape(1, inner)
    dt_rows = dt_raw.T

    smem = pl.BlockSpec(memory_space=pltpu.SMEM)
    vmem = pl.BlockSpec(memory_space=pltpu.VMEM)
    anywhere = pl.BlockSpec(memory_space=pl.ANY)
    inv_spec = pl.BlockSpec((1, tokens, 1), lambda g: (g, 0, 0))
    large = pltpu.CompilerParams(vmem_limit_bytes=20 * 1024 * 1024)
    small = pltpu.CompilerParams(vmem_limit_bytes=12 * 1024 * 1024)
    small_cost = pl.CostEstimate(flops=1, bytes_accessed=1, transcendentals=0)
    some_cost = pl.CostEstimate(flops=2_000_000_000, bytes_accessed=1, transcendentals=0)
    large_cost = pl.CostEstimate(flops=30_000_000_000, bytes_accessed=1, transcendentals=0)

    turn = []

    def run(kernel, inputs, in_specs, outs, out_specs, waits=(), **options):
        waits = [*turn[-1:], *waits]
        done = jax.ShapeDtypeStruct((8, LANES), F32)
        *results, ran = pl.pallas_call(
            in_turn(kernel, len(inputs), len(waits), len(outs)),
            in_specs=[*in_specs, *[vmem] * len(waits)],
            out_specs=[*out_specs, vmem],
            out_shape=[*outs, done],
            **options,
        )(*inputs, *waits)
        turn.append(ran)
        return results

    def step(kernel, operands, outs, scalars=(), waits=(), cost=small_cost):
        return run(
            kernel,
            [*scalars, *operands],
            [smem] * len(scalars) + [vmem] * len(operands),
            outs,
            [vmem] * len(outs),
            waits,
            cost_estimate=cost,
            compiler_params=small,
        )

    def shape(*dims, dtype=BF16):
        return jax.ShapeDtypeStruct(dims, dtype)

    def in_hbm(*arrays):
        return [pltpu.with_memory_space_constraint(a, pltpu.HBM) for a in arrays]

    def group_specs(begin):
        wide = pl.BlockSpec((tokens, width), lambda g: (0, g + begin))
        state = pl.BlockSpec((tokens, STATE), lambda g: (0, g + begin))
        dt = pl.BlockSpec((heads // groups, tokens), lambda g: (g + begin, 0))
        return wide, state, dt, pl.BlockSpec((1, width), lambda g: (0, g + begin))

    def exchange(value, mask):
        return lax.ppermute(value, "replica", [(r, r ^ mask) for r in range(replicas)])

    gathered = {}

    def landing(b, some):
        (bit, bits), *_ = some
        return [exchange(gathered[b], mask << bit) for mask in range(1, 1 << bits)]

    def widen(b, some, landed=None):
        for at, (bit, bits) in enumerate(some):
            parts = [gathered[b]] + (landed if at == 0 and landed else landing(b, some[at:]))
            out = shape(len(parts) * parts[0].shape[0], *parts[0].shape[1:])
            (gathered[b],) = step(join_kernel, parts, [out])

    def finish(b):
        gathered[b] = [gathered[b], exchange(gathered[b], 1)]

    by_two, by_one = stages(replicas), stages(replicas, 1)
    by_group, by_state, dt_spec, gain_spec = group_specs(0)
    shared = in_hbm(dt_rows, gate_z, b_proj, c_proj, gain, a_log, dt_bias, skip_d)
    later = [stored, target, global_weight, momentum]
    weight, goal, own_global, own_momentum, normed, inv = run(
        functools.partial(forward_kernel, len(later)),
        [shared[0], *in_hbm(x_in), *shared[1:], *in_hbm(*later)],
        [dt_spec, by_group, by_group, by_state, by_state, gain_spec, smem, smem, smem] + [anywhere] * len(later),
        [pltpu.VMEM(v.shape, v.dtype) for v in later] + [pltpu.VMEM((tokens, inner), BF16), pltpu.VMEM((groups, tokens, 1), F32)],
        [vmem] * (len(later) + 2),
        grid=(groups,),
        scratch_shapes=[pltpu.SemaphoreType.DMA((len(later),))],
        cost_estimate=small_cost,
        compiler_params=large,
    )

    part = shape(span_rows, tokens)

    def project(picked):
        kernel = functools.partial(project_kernel, picked)
        return step(kernel, [weight, normed, goal], [part] * len(picked), scalars=[places])

    in_hops, across = inward(heads_over)
    parts = project([0])
    (kept,) = step(kept_kernel, [own_global, own_momentum], [shape(owned, inner)])
    gathered["kept"] = kept[None]
    kept_landed = landing("kept", by_two)
    parts += project(list(range(1, chunks)))
    first_landed = [lax.ppermute(p, "tensor", in_hops[0]) if in_hops else None for p in parts]
    sums, cots = {}, {}

    def sum_side(n, waits=()):
        held = parts[n]
        for at, pairs in enumerate(in_hops):
            landed = first_landed[n] if at == 0 else lax.ppermute(held, "tensor", pairs)
            (held,) = step(add_kernel, [held, landed], [part], waits=waits)
        sums[n] = held

    def sum_all(n, waits=(), cost=small_cost):
        landed = lax.ppermute(sums[n], "tensor", across)
        (mid,) = step(add_kernel, [sums[n], landed], [part], waits=waits, cost=cost)
        out = mid
        for pairs in reversed(in_hops):
            back = lax.ppermute(out, "tensor", [(b, a) for a, b in pairs])
            out = back if pairs is in_hops[0] else jnp.where(in_middle, mid, back)
        cots[n] = (mid, out)

    held, deltas = {}, {}
    tile = shape(8, LANES, dtype=F32)
    squares = {-1: jnp.zeros((8, LANES), F32)}

    def new_rows(b, waits=()):
        batch = batches[b]
        rows = len(batch) * piece
        keep, send = step(
            functools.partial(gradient_kernel, batch),
            [c for n in batch for c in cots[n]] + [normed, weight],
            [shape(replicas // 2, rows, inner)] * 2,
            scalars=[places],
            waits=waits,
        )
        return [keep, exchange(send, 1)]

    def narrow(b, some, waits=()):
        rows = len(batches[b]) * piece
        for bit, bits in some:
            ways = 1 << bits
            left = held[b][0].shape[0] // ways
            picked = step(
                functools.partial(pick_kernel, len(held[b]), 1 << (bit - 1)),
                [h.reshape(left, ways, rows, inner) for h in held[b]],
                [shape(left, rows, inner)] * ways,
                scalars=[places],
                waits=waits,
            )
            held[b] = [picked[0]] + [exchange(picked[mask], mask << bit) for mask in range(1, ways)]

    def own_rows(b, cost=small_cost, waits=()):
        batch = batches[b]
        rows = len(batch) * piece
        deltas[b], sent, squares[b] = step(
            functools.partial(delta_kernel, len(held[b]), batch[0] * piece, replicas),
            [own_global, squares[b - 1], *held[b]],
            [shape(rows, inner, dtype=F32), shape(rows, inner), tile],
            cost=cost,
            waits=waits,
        )
        gathered[b] = sent[None]

    def backward(begin, count, so_far):
        wide, state, dt, gain_here = group_specs(begin)
        operands = [places, *shared, normed, inv, weight] + [c for n in range(chunks) for c in cots[n]]
        specs = [smem, dt, wide, state, state, gain_here, smem, smem, smem, vmem, vmem, vmem] + [vmem] * (2 * chunks)
        aliases = {}
        if so_far is not None:
            aliases = {len(operands): 0}
            operands.append(so_far)
            specs.append(anywhere)
        (grad,) = run(
            functools.partial(backward_kernel, begin),
            operands,
            specs,
            [shape(tokens, inner)],
            [wide],
            grid=(count,),
            scratch_shapes=[pltpu.VMEM((tokens, width), F32)],
            input_output_aliases=aliases,
            cost_estimate=small_cost,
            compiler_params=large,
        )
        return grad

    end = len(batches) - 1
    early = end > 1
    for t in range(chunks):
        if t == chunks - 1 and early:
            held[0] = new_rows(0)
        sum_side(t, [cots[t - 3][1]] if t >= 3 and not early else [])
        if t == 0:
            widen("kept", by_two, kept_landed)
            finish("kept")
        if t > 0:
            sum_all(t - 1)
    if early:
        narrow(0, by_one[:1])
    held[end - 1] = new_rows(end - 1)
    if early:
        narrow(0, by_one[1:])
    sum_all(chunks - 1, cost=large_cost)
    narrow(end - 1, by_one[:1])
    step(gate_kernel, [], [tile], waits=[cots[chunks - 2][1], gathered["kept"][1]])
    landed = {}
    if early:
        own_rows(0)
        landed[0] = landing(0, by_two)
    narrow(end - 1, by_one[1:])
    own_rows(end - 1, small_cost)
    landed[end - 1] = landing(end - 1, by_two)
    if early:
        widen(0, by_two, landed[0])
        finish(0)
    held[end] = new_rows(end)
    narrow(end, by_two)
    half = groups // 2
    grad_input = backward(0, half, None) if half else None
    grad_input = backward(half, groups - half, grad_input)
    widen(end - 1, by_two, landed[end - 1])
    finish(end - 1)
    own_rows(end, large_cost, [gathered[0][1]] if early else [])
    last_landed = landing(end, by_two)
    total = squares[end]
    for bit in range(heads_over.bit_length() - 1):
        pairs = [(t, t ^ (1 << bit)) for t in range(heads_over)]
        waits = [gathered[b][1] for b in range(end)]
        (total,) = step(add_squares_kernel, [total, lax.ppermute(total, "tensor", pairs)], [tile], waits=waits)
    for bit, bits in by_two:
        landed = [exchange(total, mask << bit) for mask in range(1, 1 << bits)]
        (total,) = step(add_squares_kernel, [total, *landed], [tile])
    widen(end, by_two, last_landed)
    finish(end)
    columns = [total, exchange(total, 1)]

    sizes = [len(batch) * piece for batch in batches]
    pair_spec = pl.BlockSpec((2 * owned, inner), lambda r: (r, 0))
    share = owned // (replicas // 2)
    if share % 8 == 0:
        held_spec = pl.BlockSpec((share, inner), lambda r: (r, 0))
    else:
        held_spec = pl.BlockSpec((owned, inner), lambda r: (0, 0))
    inputs = [own_global, own_momentum, *gathered["kept"], *[v for b in range(end + 1) for v in gathered[b]]]
    inputs += [*[deltas[b] for b in range(end + 1)], *columns]
    new_weight, new_global, new_momentum = run(
        functools.partial(weight_kernel, sizes, features * inner * heads_over),
        [places, *inputs],
        [smem] + [vmem] * len(inputs),
        [shape(features, inner), shape(owned, inner, dtype=F32), shape(owned, inner, dtype=F32)],
        [pair_spec, held_spec, held_spec],
        grid=(replicas // 2,),
        cost_estimate=small_cost,
        compiler_params=small,
    )
    return (grad_input, new_weight, new_global, new_momentum)


def solution(mesh):
    placed = (
        P("replica", "tensor"),
        P("replica", "tensor"),
        P("replica", "tensor"),
        P("replica", "tensor"),
        P("replica", "tensor"),
        P("tensor"),
        P("tensor"),
        P("tensor"),
        P("tensor"),
        P("replica", None, "tensor"),
        P("replica", "tensor"),
        P("replica", "tensor"),
        P(("replica", "tensor"), None),
    )
    return jax.shard_map(
        shards,
        mesh=mesh,
        in_specs=placed,
        out_specs=(
            P("replica", "tensor"),
            P(None, "tensor"),
            P("replica", "tensor"),
            P("replica", "tensor"),
        ),
        check_vma=False,
    )
```

```python
import functools

import jax
import jax.numpy as jnp
from jax import lax
from jax.experimental import pallas as pl
from jax.experimental.pallas import tpu as pltpu
from jax.sharding import PartitionSpec as P

HEAD_DIM = 64
STATE = 128
SPAN = 256
HALF = SPAN // 2
LANES = 128

inner_rate = 0.001
outer_rate = 0.7
outer_beta = 0.9
clip_rms = 0.005
LOG2E = 1.4426950408889634

F32 = jnp.float32
BF16 = jnp.bfloat16
NN = (((1,), (0,)), ((), ()))
NT = (((1,), (1,)), ((), ()))
TN = (((0,), (0,)), ((), ()))


def dot(a, b, dims):
    return lax.dot_general(a, b, dims, preferred_element_type=F32)


def silu(z):
    return 0.5 * z * (1.0 + jnp.tanh(0.5 * z))


def softplus(v):
    return jnp.maximum(v, 0.0) + jnp.log1p(jnp.exp(-jnp.abs(v)))


def iota(shape, axis):
    return lax.broadcasted_iota(jnp.int32, shape, axis)


def thirds(v):
    high = v.astype(BF16).astype(F32)
    middle = (v - high).astype(BF16).astype(F32)
    return jnp.concatenate([high, middle, v - high - middle], axis=0).astype(BF16)


def by_head(refs, first, per_group, tokens):
    row = iota((per_group, tokens), 0)
    rows = []
    for ref in refs:
        value = jnp.zeros((per_group, tokens), F32)
        for h in range(per_group):
            value = jnp.where(row == h, ref[first + h], value)
        rows.append(value)
    return rows


def head_tables(dt_ref, a_ref, bias_ref, first, per_group):
    bias, a_log = by_head([bias_ref, a_ref], first, per_group, dt_ref.shape[1])
    step = softplus(dt_ref[...] + bias)
    return step, -jnp.exp(a_log) * step * LOG2E


def span_tables(step, rate, lo, per_group, width):
    upper = (iota((SPAN, SPAN), 0) <= iota((SPAN, SPAN), 1)).astype(BF16)
    step_k = step[:, lo : lo + SPAN]
    sums = dot(thirds(rate[:, lo : lo + SPAN]), upper, NN)
    cum = sums[:per_group] + sums[per_group : 2 * per_group] + sums[2 * per_group :]
    spread = (iota((3 * per_group, width), 1) // HEAD_DIM == iota((3 * per_group, width), 0) % per_group).astype(BF16)
    turn = (iota((3 * per_group, per_group), 1) == iota((3 * per_group, per_group), 0) % per_group).astype(BF16)
    cum_col = dot(thirds(cum), turn, TN)
    step_x = dot(thirds(step_k), spread, TN)
    fade_x = dot(thirds(jnp.exp2(cum)), spread, TN)
    tail_x = dot(thirds(jnp.exp2(cum[:, SPAN - 1 :] - cum) * step_k), spread, TN)
    return cum, cum_col, step_x, fade_x, tail_x


def skip_row(skip_ref, first, per_group, width):
    head = iota((1, width), 1) // HEAD_DIM
    row = jnp.zeros((1, width), F32)
    for h in range(per_group):
        row = jnp.where(head == h, skip_ref[first + h], row)
    return row


def decay(gap, mask=None):
    return jnp.exp2(gap if mask is None else jnp.where(mask, gap, -1e30))


def even_odd(v):
    first = iota(v.shape, 1) % (2 * HEAD_DIM) < HEAD_DIM
    return jnp.where(first, v, 0.0).astype(BF16), jnp.where(first, 0.0, v).astype(BF16)


def forward_kernel(
    count, dt_ref, x_ref, z_ref, b_ref, c_ref, gain_ref, a_ref, bias_ref, skip_ref, *refs
):
    loads = [pltpu.make_async_copy(refs[n], refs[count + n], refs[-1].at[n]) for n in range(count)]
    normed_ref, inv_ref = refs[2 * count : 2 * count + 2]

    @pl.when(pl.program_id(0) == 0)
    def _():
        for load in loads:
            load.start()

    tokens, width = x_ref.shape
    per_group = width // HEAD_DIM
    first = pl.program_id(0) * per_group
    lanes_here = pl.ds(pl.multiple_of(pl.program_id(0) * width, LANES), width)
    step, rate = head_tables(dt_ref, a_ref, bias_ref, first, per_group)
    skip = skip_row(skip_ref, first, per_group, width)
    causal = iota((HALF, HALF), 0) >= iota((HALF, HALF), 1)
    spans = tokens // SPAN
    entering = None
    for k in range(spans):
        rows = slice(k * SPAN, (k + 1) * SPAN)
        cum, cum_col, step_x, fade_x, tail_x = span_tables(step, rate, k * SPAN, per_group, width)
        x = x_ref[rows, :].astype(F32)
        b, c = b_ref[rows, :], c_ref[rows, :]
        scores = dot(c, b, NT)
        values = even_odd(x * step_x)
        pieces = []
        for pair in range(per_group // 2):
            lanes = slice(2 * pair * HEAD_DIM, 2 * (pair + 1) * HEAD_DIM)
            tops, bottoms = [], []
            for h in (2 * pair, 2 * pair + 1):
                col, line = cum_col[:, h : h + 1], cum[h : h + 1, :]
                top = decay(col[:HALF] - line[:, :HALF], causal) * scores[:HALF, :HALF]
                left = decay(col[HALF:] - line[:, :HALF]) * scores[HALF:, :HALF]
                low = decay(col[HALF:] - line[:, HALF:], causal) * scores[HALF:, HALF:]
                tops.append(top.astype(BF16))
                bottoms += [left.astype(BF16), low.astype(BF16)]
            upper_values = jnp.concatenate([v[:HALF, lanes] for v in values], axis=0)
            all_values = jnp.concatenate([v[:, lanes] for v in values], axis=0)
            pieces.append(
                jnp.concatenate(
                    [
                        dot(jnp.concatenate(tops, axis=1), upper_values, NN),
                        dot(jnp.concatenate(bottoms, axis=1), all_values, NN),
                    ],
                    axis=0,
                )
            )
        ssd = jnp.concatenate(pieces, axis=1) + skip * x
        if entering is not None:
            ssd = ssd + dot(c, entering.astype(BF16), NN) * fade_x
        if k + 1 < spans:
            state = dot(b, (x * tail_x).astype(BF16), TN)
            entering = state if entering is None else entering * fade_x[SPAN - 1 :, :] + state
        gated = ssd * silu(z_ref[rows, :].astype(F32))
        inv = lax.rsqrt(jnp.mean(gated * gated, axis=1, keepdims=True) + 1e-05)
        normed_ref[rows, lanes_here] = (gated * inv * gain_ref[...]).astype(BF16)
        inv_ref[pl.program_id(0), rows, :] = inv

    @pl.when(pl.program_id(0) == pl.num_programs(0) - 1)
    def _():
        for load in loads:
            load.wait()


def kept_kernel(global_ref, momentum_ref, kept_ref):
    kept_ref[...] = (global_ref[...] - outer_rate * outer_beta * outer_beta * momentum_ref[...]).astype(BF16)


def project_kernel(chunks, place_ref, weight_ref, normed_ref, target_ref, *part_refs):
    replicas, owned, inner = weight_ref.shape
    held, features = target_ref.shape
    piece = part_refs[0].shape[0] // replicas
    tokens = normed_ref.shape[0]
    eye = (iota((held, held), 0) == iota((held, held), 1)).astype(BF16)
    turned = dot(target_ref[...], eye, TN).reshape(replicas, owned, held)
    here = iota((replicas * piece, tokens), 1) // held == place_ref[0]
    for n, part_ref in zip(chunks, part_refs):
        at = slice(n * piece, (n + 1) * piece)
        part = dot(weight_ref[:, at, :].reshape(replicas * piece, inner), normed_ref[...], NT)
        goal = jnp.concatenate([turned[:, at, :].reshape(replicas * piece, held)] * (tokens // held), axis=1)
        part_ref[...] = (part - jnp.where(here, goal, 0.0)).astype(BF16)


def gate_kernel(out_ref):
    out_ref[...] = jnp.zeros_like(out_ref)


def add_kernel(a_ref, b_ref, sum_ref):
    sum_ref[...] = (a_ref[...].astype(F32) + b_ref[...].astype(F32)).astype(BF16)


def add_squares_kernel(*refs):
    *term_refs, sum_ref = refs
    values = [ref[...] for ref in term_refs]
    while len(values) > 1:
        values = [a + b for a, b in zip(values[::2], values[1::2])]
    sum_ref[...] = values[0]


def gradient_kernel(batch, place_ref, *refs):
    count = len(batch)
    cot_refs, (normed_ref, weight_ref, keep_ref, send_ref) = refs[: 2 * count], refs[2 * count :]
    middle = place_ref[1] == 1
    odd = place_ref[2] == 1
    replicas, _, inner = weight_ref.shape
    piece = keep_ref.shape[1] // count
    tile = min(inner, 512)
    for n, chunk in enumerate(batch):
        cot = jnp.where(middle, cot_refs[2 * n][...], cot_refs[2 * n + 1][...])
        rows = slice(chunk * piece, (chunk + 1) * piece)
        at = slice(n * piece, (n + 1) * piece)
        for lo in range(0, inner, tile):
            cols = slice(lo, lo + tile)
            weight = weight_ref[:, rows, cols].reshape(replicas * piece, tile).astype(F32)
            new = weight - inner_rate * dot(cot, normed_ref[:, cols], NN)
            new = new.astype(BF16).reshape(replicas // 2, 2, piece, tile)
            keep_ref[:, at, cols] = jnp.where(odd, new[:, 1], new[:, 0])
            send_ref[:, at, cols] = jnp.where(odd, new[:, 0], new[:, 1])


def backward_kernel(
    begin, place_ref, dt_ref, z_ref, b_ref, c_ref, gain_ref, a_ref, bias_ref, skip_ref, normed_ref, inv_ref, weight_ref, *refs
):
    *cot_refs, dx_ref, dn_ref = refs
    if len(cot_refs) % 2:
        cot_refs = cot_refs[:-1]
    tokens, width = z_ref.shape
    per_group = width // HEAD_DIM
    group = pl.program_id(0) + begin
    first = group * per_group
    here = pl.ds(pl.multiple_of(group * width, LANES), width)
    replicas, owned, _ = weight_ref.shape
    chunks = len(cot_refs) // 2
    piece = owned // chunks
    middle = place_ref[1] == 1
    for n in range(chunks):
        weight = weight_ref[:, n * piece : (n + 1) * piece, here].reshape(replicas * piece, width)
        term = dot(jnp.where(middle, cot_refs[2 * n][...], cot_refs[2 * n + 1][...]), weight, TN)
        dn_ref[...] = term if n == 0 else dn_ref[...] + term
    step, rate = head_tables(dt_ref, a_ref, bias_ref, first, per_group)
    skip = skip_row(skip_ref, first, per_group, width)
    causal = iota((HALF, HALF), 1) >= iota((HALF, HALF), 0)
    spans = tokens // SPAN
    d_state = None
    for k in reversed(range(spans)):
        rows = slice(k * SPAN, (k + 1) * SPAN)
        cum, cum_col, step_x, fade_x, tail_x = span_tables(step, rate, k * SPAN, per_group, width)
        dn = dn_ref[rows, :]
        gain = gain_ref[...]
        normed = normed_ref[rows, here].astype(F32)
        shared = jnp.mean(normed * dn, axis=1, keepdims=True)
        d_gated = inv_ref[group, rows, :] * (gain * dn - (normed / gain) * shared)
        d_ssd = d_gated * silu(z_ref[rows, :].astype(F32))
        values = even_odd(d_ssd)
        b, c = b_ref[rows, :], c_ref[rows, :]
        scores = dot(b, c, NT)
        pieces = []
        for pair in range(per_group // 2):
            lanes = slice(2 * pair * HEAD_DIM, 2 * (pair + 1) * HEAD_DIM)
            tops, bottoms = [], []
            for h in (2 * pair, 2 * pair + 1):
                col, line = cum_col[:, h : h + 1], cum[h : h + 1, :]
                high = decay(line[:, :HALF] - col[:HALF], causal) * scores[:HALF, :HALF]
                right = decay(line[:, HALF:] - col[:HALF]) * scores[:HALF, HALF:]
                low = decay(line[:, HALF:] - col[HALF:], causal) * scores[HALF:, HALF:]
                tops += [high.astype(BF16), right.astype(BF16)]
                bottoms.append(low.astype(BF16))
            lower_values = jnp.concatenate([v[HALF:, lanes] for v in values], axis=0)
            all_values = jnp.concatenate([v[:, lanes] for v in values], axis=0)
            pieces.append(
                jnp.concatenate(
                    [
                        dot(jnp.concatenate(tops, axis=1), all_values, NN),
                        dot(jnp.concatenate(bottoms, axis=1), lower_values, NN),
                    ],
                    axis=0,
                )
            )
        dx = jnp.concatenate(pieces, axis=1) * step_x + skip * d_ssd
        if d_state is not None:
            dx = dx + dot(b, d_state.astype(BF16), NN) * tail_x
        dx_ref[rows, :] = dx.astype(BF16)
        if k > 0:
            own = dot(c, (d_ssd * fade_x).astype(BF16), TN)
            d_state = own if d_state is None else own + d_state * fade_x[SPAN - 1 :, :]


def pick_kernel(count, place_ref, *refs):
    terms, outs = refs[:count], refs[count:]
    my = lax.rem(lax.div(place_ref[3], place_ref[4]), len(outs))
    for mask, out_ref in enumerate(outs):
        at = lax.bitwise_xor(my, jnp.int32(mask))
        total = terms[0][:, at].astype(F32)
        for term in terms[1:]:
            total = total + term[:, at].astype(F32)
        out_ref[...] = total.astype(BF16)


def delta_kernel(count, lo, replicas, global_ref, before_ref, *refs):
    terms, earlier, (delta_ref, sent_ref, squares_ref) = refs[:count], refs[count:-3], refs[-3:]
    rows, inner = delta_ref.shape
    total = terms[0][0].astype(F32)
    for term in terms[1:]:
        total = total + term[0].astype(F32)
    delta = global_ref[lo : lo + rows, :] - total / replicas
    delta_ref[...] = delta
    if earlier:
        sent_ref[:lo, :] = earlier[0][...]
    sent_ref[lo:, :] = delta.astype(BF16)
    squares = jnp.sum(delta * delta, axis=0, keepdims=True)
    squares = before_ref[...] + jnp.broadcast_to(jnp.sum(squares, axis=1, keepdims=True), before_ref.shape)
    squares_ref[...] = squares


def join_kernel(*refs):
    *parts, out_ref = refs
    lo = 0
    for part in parts:
        out_ref[lo : lo + part.shape[0]] = part[...]
        lo += part.shape[0]


def weight_kernel(sizes, entries, place_ref, global_ref, momentum_ref, *refs):
    kepts, pairs, (*deltas, own_squares_ref, other_squares_ref) = refs[:2], refs[2:4], refs[4:-3]
    new_ref, new_global_ref, new_momentum_ref = refs[-3:]
    mean = (own_squares_ref[:1, :1] + other_squares_ref[:1, :1]) / entries
    factor = jnp.minimum(1.0, clip_rms / jnp.sqrt(mean + 1e-06))
    at_chip = lax.bitwise_xor(pl.program_id(0), place_ref[3])
    owned = new_ref.shape[0] // 2
    scale = (outer_rate * (1.0 + outer_beta)) * factor

    for own_core in range(2):

        @pl.when(place_ref[2] == own_core)
        def _():
            for core, kept_ref, delta_ref in zip((own_core, 1 - own_core), kepts, pairs):
                new = kept_ref[at_chip].astype(F32) - scale * delta_ref[at_chip].astype(F32)
                new_ref[core * owned : (core + 1) * owned, :] = new.astype(BF16)

    part = new_global_ref.shape[0]
    lo = 0
    for n, size in enumerate(sizes):
        rows = min(size, part)
        for row in range(0, size, rows):
            at, here = slice(lo + row, lo + row + rows), (lo + row) % part

            @pl.when(pl.program_id(0) == (lo + row) // part)
            def _():
                clipped = factor * deltas[n][row : row + rows, :]
                new_momentum = outer_beta * momentum_ref[at, :] + clipped
                new_momentum_ref[here : here + rows, :] = new_momentum
                new_global = global_ref[at, :] - outer_rate * (clipped + outer_beta * new_momentum)
                new_global_ref[here : here + rows, :] = new_global

        lo += size


def inward(axis_size):
    half = axis_size // 2
    hops = [[(s, s + 1), (axis_size - 1 - s, axis_size - 2 - s)] for s in range(half - 1)]
    return hops, [(half - 1, half), (half, half - 1)]


def in_turn(kernel, inputs, waits, outs):
    def body(*refs):
        end = inputs + waits + outs
        refs[end][...] = jnp.zeros_like(refs[end])
        kernel(*refs[:inputs], *refs[inputs + waits : end], *refs[end + 1 :])

    return body


def stages(replicas):
    bit, left, found = 1, replicas // 2, []
    while left > 1:
        bits = 2 if left >= 4 else 1
        found.append((bit, bits))
        bit, left = bit + bits, left >> bits
    return found


def shards(
    x_in,
    gate_z,
    b_proj,
    c_proj,
    dt_raw,
    a_log,
    dt_bias,
    skip_d,
    norm_gain,
    out_weight,
    global_weight,
    momentum,
    target,
):
    tokens, inner = x_in.shape
    features = out_weight.shape[1]
    replicas = lax.axis_size("replica")
    heads_over = lax.axis_size("tensor")
    groups = b_proj.shape[1] // STATE
    heads = dt_raw.shape[1]
    width = inner // groups
    owned = features // replicas
    chunks = max(2, min(4, owned // 16))
    batches = [list(range(chunks // 2)), list(range(chunks // 2, chunks))]
    piece = owned // chunks
    span_rows = replicas * piece
    place = lax.axis_index("tensor")
    me = lax.axis_index("replica")
    in_middle = (place == heads_over // 2 - 1) | (place == heads_over // 2)
    one = jnp.int32(1)
    places = jnp.stack([place, in_middle.astype(jnp.int32), lax.rem(me, 2), lax.div(me, 2), one]).astype(jnp.int32)
    stored = out_weight[0].reshape(replicas, owned, inner)
    gain = norm_gain.reshape(1, inner)
    dt_rows = dt_raw.T

    smem = pl.BlockSpec(memory_space=pltpu.SMEM)
    vmem = pl.BlockSpec(memory_space=pltpu.VMEM)
    anywhere = pl.BlockSpec(memory_space=pl.ANY)
    inv_spec = pl.BlockSpec((1, tokens, 1), lambda g: (g, 0, 0))
    large = pltpu.CompilerParams(vmem_limit_bytes=20 * 1024 * 1024)
    small = pltpu.CompilerParams(vmem_limit_bytes=12 * 1024 * 1024)
    small_cost = pl.CostEstimate(flops=1, bytes_accessed=1, transcendentals=0)
    some_cost = pl.CostEstimate(flops=2_000_000_000, bytes_accessed=1, transcendentals=0)
    large_cost = pl.CostEstimate(flops=30_000_000_000, bytes_accessed=1, transcendentals=0)

    turn = []

    def run(kernel, inputs, in_specs, outs, out_specs, waits=(), **options):
        waits = [*turn[-1:], *waits]
        done = jax.ShapeDtypeStruct((8, LANES), F32)
        *results, ran = pl.pallas_call(
            in_turn(kernel, len(inputs), len(waits), len(outs)),
            in_specs=[*in_specs, *[vmem] * len(waits)],
            out_specs=[*out_specs, vmem],
            out_shape=[*outs, done],
            **options,
        )(*inputs, *waits)
        turn.append(ran)
        return results

    def step(kernel, operands, outs, scalars=(), waits=(), cost=small_cost):
        return run(
            kernel,
            [*scalars, *operands],
            [smem] * len(scalars) + [vmem] * len(operands),
            outs,
            [vmem] * len(outs),
            waits,
            cost_estimate=cost,
            compiler_params=small,
        )

    def shape(*dims, dtype=BF16):
        return jax.ShapeDtypeStruct(dims, dtype)

    def in_hbm(*arrays):
        return [pltpu.with_memory_space_constraint(a, pltpu.HBM) for a in arrays]

    def group_specs(begin):
        wide = pl.BlockSpec((tokens, width), lambda g: (0, g + begin))
        state = pl.BlockSpec((tokens, STATE), lambda g: (0, g + begin))
        dt = pl.BlockSpec((heads // groups, tokens), lambda g: (g + begin, 0))
        return wide, state, dt, pl.BlockSpec((1, width), lambda g: (0, g + begin))

    def exchange(value, mask):
        return lax.ppermute(value, "replica", [(r, r ^ mask) for r in range(replicas)])

    gathered = {}

    def spread_rows(b, sent):
        (bit, bits), *_ = stages(replicas)
        gathered[b] = [sent[None]] + [exchange(sent[None], mask << bit) for mask in range(1, 1 << bits)]

    def join(b, waits=()):
        for at, (bit, bits) in enumerate(stages(replicas)):
            if at > 0:
                gathered[b] = [held] + [exchange(held, mask << bit) for mask in range(1, 1 << bits)]
            one = gathered[b][0]
            out = shape(len(gathered[b]) * one.shape[0], *one.shape[1:])
            (held,) = step(join_kernel, gathered[b], [out], waits=waits if at == 0 else ())
        gathered[b] = [held, exchange(held, 1)]

    by_group, by_state, dt_spec, gain_spec = group_specs(0)
    shared = in_hbm(dt_rows, gate_z, b_proj, c_proj, gain, a_log, dt_bias, skip_d)
    later = [stored, target, global_weight, momentum]
    weight, goal, own_global, own_momentum, normed, inv = run(
        functools.partial(forward_kernel, len(later)),
        [shared[0], *in_hbm(x_in), *shared[1:], *in_hbm(*later)],
        [dt_spec, by_group, by_group, by_state, by_state, gain_spec, smem, smem, smem] + [anywhere] * len(later),
        [pltpu.VMEM(v.shape, v.dtype) for v in later] + [pltpu.VMEM((tokens, inner), BF16), pltpu.VMEM((groups, tokens, 1), F32)],
        [vmem] * (len(later) + 2),
        grid=(groups,),
        scratch_shapes=[pltpu.SemaphoreType.DMA((len(later),))],
        cost_estimate=small_cost,
        compiler_params=large,
    )

    part = shape(span_rows, tokens)

    def project(picked):
        kernel = functools.partial(project_kernel, picked)
        return step(kernel, [weight, normed, goal], [part] * len(picked), scalars=[places])

    in_hops, across = inward(heads_over)
    parts = project([0])
    (kept,) = step(kept_kernel, [own_global, own_momentum], [shape(owned, inner)])
    spread_rows("kept", kept)
    parts += project(list(range(1, chunks)))
    first_landed = [lax.ppermute(p, "tensor", in_hops[0]) if in_hops else None for p in parts]
    sums, cots = {}, {}

    def sum_side(n, waits=()):
        held = parts[n]
        for at, pairs in enumerate(in_hops):
            landed = first_landed[n] if at == 0 else lax.ppermute(held, "tensor", pairs)
            (held,) = step(add_kernel, [held, landed], [part], waits=waits)
        sums[n] = held

    def sum_all(n, waits=(), cost=small_cost):
        landed = lax.ppermute(sums[n], "tensor", across)
        (mid,) = step(add_kernel, [sums[n], landed], [part], waits=waits, cost=cost)
        out = mid
        for pairs in reversed(in_hops):
            back = lax.ppermute(out, "tensor", [(b, a) for a, b in pairs])
            out = back if pairs is in_hops[0] else jnp.where(in_middle, mid, back)
        cots[n] = (mid, out)

    terms, deltas, sent = {}, {}, {}
    tile = shape(8, LANES, dtype=F32)
    squares = {-1: jnp.zeros((8, LANES), F32)}

    def new_rows(b, waits=()):
        batch = batches[b]
        rows = len(batch) * piece
        keep, send = step(
            functools.partial(gradient_kernel, batch),
            [c for n in batch for c in cots[n]] + [normed, weight],
            [shape(replicas // 2, rows, inner)] * 2,
            scalars=[places],
            waits=waits,
        )
        return [keep, exchange(send, 1)]

    def send_rows(b, held):
        rows, left = len(batches[b]) * piece, replicas // 2
        for bit, bits in stages(replicas):
            ways = 1 << bits
            left //= ways
            cut = [h.reshape(left, ways, rows, inner) for h in held]
            picked = step(
                functools.partial(pick_kernel, len(cut)),
                cut,
                [shape(left, rows, inner)] * ways,
                scalars=[places.at[4].set(1 << (bit - 1))] if bit > 1 else [places],
            )
            held = [picked[0]] + [exchange(picked[mask], mask << bit) for mask in range(1, ways)]
        terms[b] = held

    def own_rows(b, cost=small_cost):
        batch = batches[b]
        rows = len(batch) * piece
        deltas[b], sent[b], squares[b] = step(
            functools.partial(delta_kernel, len(terms[b]), batch[0] * piece, replicas),
            [own_global, squares[b - 1], *terms[b], *([sent[b - 1]] if b else [])],
            [shape(rows, inner, dtype=F32), shape(batch[0] * piece + rows, inner), tile],
            cost=cost,
        )

    def backward(begin, count, so_far):
        wide, state, dt, gain_here = group_specs(begin)
        operands = [places, *shared, normed, inv, weight] + [c for n in range(chunks) for c in cots[n]]
        specs = [smem, dt, wide, state, state, gain_here, smem, smem, smem, vmem, vmem, vmem] + [vmem] * (2 * chunks)
        aliases = {}
        if so_far is not None:
            aliases = {len(operands): 0}
            operands.append(so_far)
            specs.append(anywhere)
        (grad,) = run(
            functools.partial(backward_kernel, begin),
            operands,
            specs,
            [shape(tokens, inner)],
            [wide],
            grid=(count,),
            scratch_shapes=[pltpu.VMEM((tokens, width), F32)],
            input_output_aliases=aliases,
            cost_estimate=small_cost,
            compiler_params=large,
        )
        return grad

    first, second = range(2)
    for t in range(chunks):
        sum_side(t, [cots[t - 3][1]] if t >= 3 else [])
        if t == 0:
            join("kept")
        else:
            sum_all(t - 1)
    held_first = new_rows(first)
    sum_all(chunks - 1, cost=large_cost)
    step(gate_kernel, [], [tile], waits=[cots[chunks - 2][1]])
    send_rows(first, held_first)
    held_second = new_rows(second, gathered["kept"][1:])
    own_rows(first, large_cost)
    send_rows(second, held_second)
    grad_input = backward(0, groups, None)
    own_rows(second, large_cost)
    spread_rows("all", sent[second])
    total = squares[second]
    for bit in range(heads_over.bit_length() - 1):
        pairs = [(t, t ^ (1 << bit)) for t in range(heads_over)]
        (total,) = step(add_squares_kernel, [total, lax.ppermute(total, "tensor", pairs)], [tile])
    for bit, bits in stages(replicas):
        landed = [exchange(total, mask << bit) for mask in range(1, 1 << bits)]
        (total,) = step(add_squares_kernel, [total, *landed], [tile])
    join("all")
    columns = [total, exchange(total, 1)]

    sizes = [len(batch) * piece for batch in batches]
    pair_spec = pl.BlockSpec((2 * owned, inner), lambda r: (r, 0))
    share = owned // (replicas // 2)
    if share % 8 == 0:
        held_spec = pl.BlockSpec((share, inner), lambda r: (r, 0))
    else:
        held_spec = pl.BlockSpec((owned, inner), lambda r: (0, 0))
    inputs = [own_global, own_momentum, *gathered["kept"], *gathered["all"]]
    inputs += [deltas[first], deltas[second], *columns]
    new_weight, new_global, new_momentum = run(
        functools.partial(weight_kernel, sizes, features * inner * heads_over),
        [places, *inputs],
        [smem] + [vmem] * len(inputs),
        [shape(features, inner), shape(owned, inner, dtype=F32), shape(owned, inner, dtype=F32)],
        [pair_spec, held_spec, held_spec],
        grid=(replicas // 2,),
        cost_estimate=small_cost,
        compiler_params=small,
    )
    return (grad_input, new_weight, new_global, new_momentum)


def solution(mesh):
    placed = (
        P("replica", "tensor"),
        P("replica", "tensor"),
        P("replica", "tensor"),
        P("replica", "tensor"),
        P("replica", "tensor"),
        P("tensor"),
        P("tensor"),
        P("tensor"),
        P("tensor"),
        P("replica", None, "tensor"),
        P("replica", "tensor"),
        P("replica", "tensor"),
        P(("replica", "tensor"), None),
    )
    return jax.shard_map(
        shards,
        mesh=mesh,
        in_specs=placed,
        out_specs=(
            P("replica", "tensor"),
            P(None, "tensor"),
            P("replica", "tensor"),
            P("replica", "tensor"),
        ),
        check_vma=False,
    )
```

```python
import functools

import jax
import jax.numpy as jnp
from jax import lax
from jax.experimental import pallas as pl
from jax.experimental.pallas import tpu as pltpu
from jax.sharding import PartitionSpec as P

HEAD_DIM = 64
STATE = 128
SPAN = 256
HALF = SPAN // 2
LANES = 128

inner_rate = 0.001
outer_rate = 0.7
outer_beta = 0.9
clip_rms = 0.005
LOG2E = 1.4426950408889634

F32 = jnp.float32
BF16 = jnp.bfloat16
NN = (((1,), (0,)), ((), ()))
NT = (((1,), (1,)), ((), ()))
TN = (((0,), (0,)), ((), ()))


def dot(a, b, dims):
    return lax.dot_general(a, b, dims, preferred_element_type=F32)


def silu(z):
    return 0.5 * z * (1.0 + jnp.tanh(0.5 * z))


def softplus(v):
    return jnp.maximum(v, 0.0) + jnp.log1p(jnp.exp(-jnp.abs(v)))


def iota(shape, axis):
    return lax.broadcasted_iota(jnp.int32, shape, axis)


def thirds(v):
    high = v.astype(BF16).astype(F32)
    middle = (v - high).astype(BF16).astype(F32)
    return jnp.concatenate([high, middle, v - high - middle], axis=0).astype(BF16)


def by_head(refs, first, per_group, tokens):
    row = iota((per_group, tokens), 0)
    rows = []
    for ref in refs:
        value = jnp.zeros((per_group, tokens), F32)
        for h in range(per_group):
            value = jnp.where(row == h, ref[first + h], value)
        rows.append(value)
    return rows


def head_tables(dt_ref, a_ref, bias_ref, first, per_group):
    bias, a_log = by_head([bias_ref, a_ref], first, per_group, dt_ref.shape[1])
    step = softplus(dt_ref[...] + bias)
    return step, -jnp.exp(a_log) * step * LOG2E


def span_tables(step, rate, lo, per_group, width):
    upper = (iota((SPAN, SPAN), 0) <= iota((SPAN, SPAN), 1)).astype(BF16)
    step_k = step[:, lo : lo + SPAN]
    sums = dot(thirds(rate[:, lo : lo + SPAN]), upper, NN)
    cum = sums[:per_group] + sums[per_group : 2 * per_group] + sums[2 * per_group :]
    spread = (iota((3 * per_group, width), 1) // HEAD_DIM == iota((3 * per_group, width), 0) % per_group).astype(BF16)
    turn = (iota((3 * per_group, per_group), 1) == iota((3 * per_group, per_group), 0) % per_group).astype(BF16)
    cum_col = dot(thirds(cum), turn, TN)
    step_x = dot(thirds(step_k), spread, TN)
    fade_x = dot(thirds(jnp.exp2(cum)), spread, TN)
    tail_x = dot(thirds(jnp.exp2(cum[:, SPAN - 1 :] - cum) * step_k), spread, TN)
    return cum, cum_col, step_x, fade_x, tail_x


def skip_row(skip_ref, first, per_group, width):
    head = iota((1, width), 1) // HEAD_DIM
    row = jnp.zeros((1, width), F32)
    for h in range(per_group):
        row = jnp.where(head == h, skip_ref[first + h], row)
    return row


def decay(gap, mask=None):
    return jnp.exp2(gap if mask is None else jnp.where(mask, gap, -1e30))


def even_odd(v):
    first = iota(v.shape, 1) % (2 * HEAD_DIM) < HEAD_DIM
    return jnp.where(first, v, 0.0).astype(BF16), jnp.where(first, 0.0, v).astype(BF16)


def forward_kernel(
    count, dt_ref, x_ref, z_ref, b_ref, c_ref, gain_ref, a_ref, bias_ref, skip_ref, *refs
):
    loads = [pltpu.make_async_copy(refs[n], refs[count + n], refs[-1].at[n]) for n in range(count)]
    normed_ref, inv_ref = refs[2 * count : 2 * count + 2]

    @pl.when(pl.program_id(0) == 0)
    def _():
        for load in loads:
            load.start()

    tokens, width = x_ref.shape
    per_group = width // HEAD_DIM
    first = pl.program_id(0) * per_group
    lanes_here = pl.ds(pl.multiple_of(pl.program_id(0) * width, LANES), width)
    step, rate = head_tables(dt_ref, a_ref, bias_ref, first, per_group)
    skip = skip_row(skip_ref, first, per_group, width)
    causal = iota((HALF, HALF), 0) >= iota((HALF, HALF), 1)
    spans = tokens // SPAN
    entering = None
    for k in range(spans):
        rows = slice(k * SPAN, (k + 1) * SPAN)
        cum, cum_col, step_x, fade_x, tail_x = span_tables(step, rate, k * SPAN, per_group, width)
        x = x_ref[rows, :].astype(F32)
        b, c = b_ref[rows, :], c_ref[rows, :]
        scores = dot(c, b, NT)
        values = even_odd(x * step_x)
        pieces = []
        for pair in range(per_group // 2):
            lanes = slice(2 * pair * HEAD_DIM, 2 * (pair + 1) * HEAD_DIM)
            tops, bottoms = [], []
            for h in (2 * pair, 2 * pair + 1):
                col, line = cum_col[:, h : h + 1], cum[h : h + 1, :]
                top = decay(col[:HALF] - line[:, :HALF], causal) * scores[:HALF, :HALF]
                left = decay(col[HALF:] - line[:, :HALF]) * scores[HALF:, :HALF]
                low = decay(col[HALF:] - line[:, HALF:], causal) * scores[HALF:, HALF:]
                tops.append(top.astype(BF16))
                bottoms += [left.astype(BF16), low.astype(BF16)]
            upper_values = jnp.concatenate([v[:HALF, lanes] for v in values], axis=0)
            all_values = jnp.concatenate([v[:, lanes] for v in values], axis=0)
            pieces.append(
                jnp.concatenate(
                    [
                        dot(jnp.concatenate(tops, axis=1), upper_values, NN),
                        dot(jnp.concatenate(bottoms, axis=1), all_values, NN),
                    ],
                    axis=0,
                )
            )
        ssd = jnp.concatenate(pieces, axis=1) + skip * x
        if entering is not None:
            ssd = ssd + dot(c, entering.astype(BF16), NN) * fade_x
        if k + 1 < spans:
            state = dot(b, (x * tail_x).astype(BF16), TN)
            entering = state if entering is None else entering * fade_x[SPAN - 1 :, :] + state
        gated = ssd * silu(z_ref[rows, :].astype(F32))
        inv = lax.rsqrt(jnp.mean(gated * gated, axis=1, keepdims=True) + 1e-05)
        normed_ref[rows, lanes_here] = (gated * inv * gain_ref[...]).astype(BF16)
        inv_ref[pl.program_id(0), rows, :] = inv

    @pl.when(pl.program_id(0) == pl.num_programs(0) - 1)
    def _():
        for load in loads:
            load.wait()


def kept_kernel(global_ref, momentum_ref, kept_ref):
    kept_ref[...] = (global_ref[...] - outer_rate * outer_beta * outer_beta * momentum_ref[...]).astype(BF16)


def project_kernel(chunks, place_ref, weight_ref, normed_ref, target_ref, *part_refs):
    replicas, owned, inner = weight_ref.shape
    held, features = target_ref.shape
    piece = part_refs[0].shape[0] // replicas
    tokens = normed_ref.shape[0]
    eye = (iota((held, held), 0) == iota((held, held), 1)).astype(BF16)
    turned = dot(target_ref[...], eye, TN).reshape(replicas, owned, held)
    here = iota((replicas * piece, tokens), 1) // held == place_ref[0]
    for n, part_ref in zip(chunks, part_refs):
        at = slice(n * piece, (n + 1) * piece)
        part = dot(weight_ref[:, at, :].reshape(replicas * piece, inner), normed_ref[...], NT)
        goal = jnp.concatenate([turned[:, at, :].reshape(replicas * piece, held)] * (tokens // held), axis=1)
        part_ref[...] = (part - jnp.where(here, goal, 0.0)).astype(BF16)


def gate_kernel(out_ref):
    out_ref[...] = jnp.zeros_like(out_ref)


def add_kernel(a_ref, b_ref, sum_ref):
    sum_ref[...] = (a_ref[...].astype(F32) + b_ref[...].astype(F32)).astype(BF16)


def add_squares_kernel(*refs):
    *term_refs, sum_ref = refs
    values = [ref[...] for ref in term_refs]
    while len(values) > 1:
        values = [a + b for a, b in zip(values[::2], values[1::2])]
    sum_ref[...] = values[0]


def gradient_kernel(batch, place_ref, *refs):
    count = len(batch)
    cot_refs, (normed_ref, weight_ref, keep_ref, send_ref) = refs[: 2 * count], refs[2 * count :]
    middle = place_ref[1] == 1
    odd = place_ref[2] == 1
    replicas, _, inner = weight_ref.shape
    piece = keep_ref.shape[1] // count
    tile = min(inner, 512)
    for n, chunk in enumerate(batch):
        cot = jnp.where(middle, cot_refs[2 * n][...], cot_refs[2 * n + 1][...])
        rows = slice(chunk * piece, (chunk + 1) * piece)
        at = slice(n * piece, (n + 1) * piece)
        for lo in range(0, inner, tile):
            cols = slice(lo, lo + tile)
            weight = weight_ref[:, rows, cols].reshape(replicas * piece, tile).astype(F32)
            new = weight - inner_rate * dot(cot, normed_ref[:, cols], NN)
            new = new.astype(BF16).reshape(replicas // 2, 2, piece, tile)
            keep_ref[:, at, cols] = jnp.where(odd, new[:, 1], new[:, 0])
            send_ref[:, at, cols] = jnp.where(odd, new[:, 0], new[:, 1])


def backward_kernel(
    begin, place_ref, dt_ref, z_ref, b_ref, c_ref, gain_ref, a_ref, bias_ref, skip_ref, normed_ref, inv_ref, weight_ref, *refs
):
    *cot_refs, dx_ref, dn_ref = refs
    if len(cot_refs) % 2:
        cot_refs = cot_refs[:-1]
    tokens, width = z_ref.shape
    per_group = width // HEAD_DIM
    group = pl.program_id(0) + begin
    first = group * per_group
    here = pl.ds(pl.multiple_of(group * width, LANES), width)
    replicas, owned, _ = weight_ref.shape
    chunks = len(cot_refs) // 2
    piece = owned // chunks
    middle = place_ref[1] == 1
    for n in range(chunks):
        weight = weight_ref[:, n * piece : (n + 1) * piece, here].reshape(replicas * piece, width)
        term = dot(jnp.where(middle, cot_refs[2 * n][...], cot_refs[2 * n + 1][...]), weight, TN)
        dn_ref[...] = term if n == 0 else dn_ref[...] + term
    step, rate = head_tables(dt_ref, a_ref, bias_ref, first, per_group)
    skip = skip_row(skip_ref, first, per_group, width)
    causal = iota((HALF, HALF), 1) >= iota((HALF, HALF), 0)
    spans = tokens // SPAN
    d_state = None
    for k in reversed(range(spans)):
        rows = slice(k * SPAN, (k + 1) * SPAN)
        cum, cum_col, step_x, fade_x, tail_x = span_tables(step, rate, k * SPAN, per_group, width)
        dn = dn_ref[rows, :]
        gain = gain_ref[...]
        normed = normed_ref[rows, here].astype(F32)
        shared = jnp.mean(normed * dn, axis=1, keepdims=True)
        d_gated = inv_ref[group, rows, :] * (gain * dn - (normed / gain) * shared)
        d_ssd = d_gated * silu(z_ref[rows, :].astype(F32))
        values = even_odd(d_ssd)
        b, c = b_ref[rows, :], c_ref[rows, :]
        scores = dot(b, c, NT)
        pieces = []
        for pair in range(per_group // 2):
            lanes = slice(2 * pair * HEAD_DIM, 2 * (pair + 1) * HEAD_DIM)
            tops, bottoms = [], []
            for h in (2 * pair, 2 * pair + 1):
                col, line = cum_col[:, h : h + 1], cum[h : h + 1, :]
                high = decay(line[:, :HALF] - col[:HALF], causal) * scores[:HALF, :HALF]
                right = decay(line[:, HALF:] - col[:HALF]) * scores[:HALF, HALF:]
                low = decay(line[:, HALF:] - col[HALF:], causal) * scores[HALF:, HALF:]
                tops += [high.astype(BF16), right.astype(BF16)]
                bottoms.append(low.astype(BF16))
            lower_values = jnp.concatenate([v[HALF:, lanes] for v in values], axis=0)
            all_values = jnp.concatenate([v[:, lanes] for v in values], axis=0)
            pieces.append(
                jnp.concatenate(
                    [
                        dot(jnp.concatenate(tops, axis=1), all_values, NN),
                        dot(jnp.concatenate(bottoms, axis=1), lower_values, NN),
                    ],
                    axis=0,
                )
            )
        dx = jnp.concatenate(pieces, axis=1) * step_x + skip * d_ssd
        if d_state is not None:
            dx = dx + dot(b, d_state.astype(BF16), NN) * tail_x
        dx_ref[rows, :] = dx.astype(BF16)
        if k > 0:
            own = dot(c, (d_ssd * fade_x).astype(BF16), TN)
            d_state = own if d_state is None else own + d_state * fade_x[SPAN - 1 :, :]


def pick_kernel(count, unit, place_ref, *refs):
    terms, outs = refs[:count], refs[count:]
    my = lax.rem(lax.div(place_ref[3], unit), len(outs))
    for mask, out_ref in enumerate(outs):
        at = lax.bitwise_xor(my, jnp.int32(mask))
        total = terms[0][:, at].astype(F32)
        for term in terms[1:]:
            total = total + term[:, at].astype(F32)
        out_ref[...] = total.astype(BF16)


def delta_kernel(count, lo, replicas, global_ref, before_ref, *refs):
    terms, (delta_ref, sent_ref, squares_ref) = refs[:count], refs[count:]
    rows, inner = delta_ref.shape
    total = terms[0][0].astype(F32)
    for term in terms[1:]:
        total = total + term[0].astype(F32)
    delta = global_ref[lo : lo + rows, :] - total / replicas
    delta_ref[...] = delta
    sent_ref[...] = delta.astype(BF16)
    squares = jnp.sum(delta * delta, axis=0, keepdims=True)
    squares = before_ref[...] + jnp.broadcast_to(jnp.sum(squares, axis=1, keepdims=True), before_ref.shape)
    squares_ref[...] = squares


def join_kernel(*refs):
    *parts, out_ref = refs
    lo = 0
    for part in parts:
        out_ref[lo : lo + part.shape[0]] = part[...]
        lo += part.shape[0]


def weight_kernel(sizes, entries, place_ref, global_ref, momentum_ref, *refs):
    count = len(sizes)
    pairs, deltas, squares = refs[: 2 * count + 2], refs[2 * count + 2 : 3 * count + 2], refs[3 * count + 2 : -3]
    new_ref, new_global_ref, new_momentum_ref = refs[-3:]
    mean = (squares[0][:1, :1] + squares[1][:1, :1]) / entries
    factor = jnp.minimum(1.0, clip_rms / jnp.sqrt(mean + 1e-06))
    at_chip = lax.bitwise_xor(pl.program_id(0), place_ref[3])
    owned = new_ref.shape[0] // 2
    scale = (outer_rate * (1.0 + outer_beta)) * factor

    def one_core(core, side):
        lo = 0
        for n, size in enumerate(sizes):
            kept = pairs[side][at_chip, lo : lo + size, :].astype(F32)
            delta = pairs[2 * n + 2 + side][at_chip, :size, :].astype(F32)
            new_ref[core * owned + lo : core * owned + lo + size, :] = (kept - scale * delta).astype(BF16)
            lo += size

    for own_core in range(2):

        @pl.when(place_ref[2] == own_core)
        def _():
            one_core(own_core, 0)
            one_core(1 - own_core, 1)

    part = new_global_ref.shape[0]
    lo = 0
    for n, size in enumerate(sizes):
        for row in range(0, size, min(size, part)):
            rows = min(size, part)
            at, here = slice(lo + row, lo + row + rows), (lo + row) % part

            @pl.when(pl.program_id(0) == (lo + row) // part)
            def _():
                clipped = factor * deltas[n][row : row + rows, :]
                new_momentum = outer_beta * momentum_ref[at, :] + clipped
                new_momentum_ref[here : here + rows, :] = new_momentum
                new_global = global_ref[at, :] - outer_rate * (clipped + outer_beta * new_momentum)
                new_global_ref[here : here + rows, :] = new_global

        lo += size


def inward(axis_size):
    half = axis_size // 2
    hops = [[(s, s + 1), (axis_size - 1 - s, axis_size - 2 - s)] for s in range(half - 1)]
    return hops, [(half - 1, half), (half, half - 1)]


def in_turn(kernel, inputs, waits, outs):
    def body(*refs):
        end = inputs + waits + outs
        refs[end][...] = jnp.zeros_like(refs[end])
        kernel(*refs[:inputs], *refs[inputs + waits : end], *refs[end + 1 :])

    return body


def stages(replicas, most=2):
    bit, left, found = 1, replicas // 2, []
    while left > 1:
        bits = most if left >= 1 << most else 1
        found.append((bit, bits))
        bit, left = bit + bits, left >> bits
    return found


def shards(
    x_in,
    gate_z,
    b_proj,
    c_proj,
    dt_raw,
    a_log,
    dt_bias,
    skip_d,
    norm_gain,
    out_weight,
    global_weight,
    momentum,
    target,
):
    tokens, inner = x_in.shape
    features = out_weight.shape[1]
    replicas = lax.axis_size("replica")
    heads_over = lax.axis_size("tensor")
    groups = b_proj.shape[1] // STATE
    heads = dt_raw.shape[1]
    width = inner // groups
    owned = features // replicas
    chunks = max(2, min(4, owned // 16))
    batches = [[n] for n in range(chunks // 2)] + [list(range(chunks // 2, chunks))]
    piece = owned // chunks
    span_rows = replicas * piece
    place = lax.axis_index("tensor")
    me = lax.axis_index("replica")
    in_middle = (place == heads_over // 2 - 1) | (place == heads_over // 2)
    places = jnp.stack([place, in_middle.astype(jnp.int32), lax.rem(me, 2), lax.div(me, 2)]).astype(jnp.int32)
    stored = out_weight[0].reshape(replicas, owned, inner)
    gain = norm_gain.reshape(1, inner)
    dt_rows = dt_raw.T

    smem = pl.BlockSpec(memory_space=pltpu.SMEM)
    vmem = pl.BlockSpec(memory_space=pltpu.VMEM)
    anywhere = pl.BlockSpec(memory_space=pl.ANY)
    inv_spec = pl.BlockSpec((1, tokens, 1), lambda g: (g, 0, 0))
    large = pltpu.CompilerParams(vmem_limit_bytes=20 * 1024 * 1024)
    small = pltpu.CompilerParams(vmem_limit_bytes=12 * 1024 * 1024)
    small_cost = pl.CostEstimate(flops=1, bytes_accessed=1, transcendentals=0)
    some_cost = pl.CostEstimate(flops=2_000_000_000, bytes_accessed=1, transcendentals=0)
    large_cost = pl.CostEstimate(flops=30_000_000_000, bytes_accessed=1, transcendentals=0)

    turn = []

    def run(kernel, inputs, in_specs, outs, out_specs, waits=(), **options):
        waits = [*turn[-1:], *waits]
        done = jax.ShapeDtypeStruct((8, LANES), F32)
        *results, ran = pl.pallas_call(
            in_turn(kernel, len(inputs), len(waits), len(outs)),
            in_specs=[*in_specs, *[vmem] * len(waits)],
            out_specs=[*out_specs, vmem],
            out_shape=[*outs, done],
            **options,
        )(*inputs, *waits)
        turn.append(ran)
        return results

    def step(kernel, operands, outs, scalars=(), waits=(), cost=small_cost):
        return run(
            kernel,
            [*scalars, *operands],
            [smem] * len(scalars) + [vmem] * len(operands),
            outs,
            [vmem] * len(outs),
            waits,
            cost_estimate=cost,
            compiler_params=small,
        )

    def shape(*dims, dtype=BF16):
        return jax.ShapeDtypeStruct(dims, dtype)

    def in_hbm(*arrays):
        return [pltpu.with_memory_space_constraint(a, pltpu.HBM) for a in arrays]

    def group_specs(begin):
        wide = pl.BlockSpec((tokens, width), lambda g: (0, g + begin))
        state = pl.BlockSpec((tokens, STATE), lambda g: (0, g + begin))
        dt = pl.BlockSpec((heads // groups, tokens), lambda g: (g + begin, 0))
        return wide, state, dt, pl.BlockSpec((1, width), lambda g: (0, g + begin))

    def exchange(value, mask):
        return lax.ppermute(value, "replica", [(r, r ^ mask) for r in range(replicas)])

    gathered = {}

    def landing(b, some):
        (bit, bits), *_ = some
        return [exchange(gathered[b], mask << bit) for mask in range(1, 1 << bits)]

    def widen(b, some, landed=None):
        for at, (bit, bits) in enumerate(some):
            parts = [gathered[b]] + (landed if at == 0 and landed else landing(b, some[at:]))
            out = shape(len(parts) * parts[0].shape[0], *parts[0].shape[1:])
            (gathered[b],) = step(join_kernel, parts, [out])

    def finish(b):
        gathered[b] = [gathered[b], exchange(gathered[b], 1)]

    by_two, by_one = stages(replicas), stages(replicas, 1)
    by_group, by_state, dt_spec, gain_spec = group_specs(0)
    shared = in_hbm(dt_rows, gate_z, b_proj, c_proj, gain, a_log, dt_bias, skip_d)
    later = [stored, target, global_weight, momentum]
    weight, goal, own_global, own_momentum, normed, inv = run(
        functools.partial(forward_kernel, len(later)),
        [shared[0], *in_hbm(x_in), *shared[1:], *in_hbm(*later)],
        [dt_spec, by_group, by_group, by_state, by_state, gain_spec, smem, smem, smem] + [anywhere] * len(later),
        [pltpu.VMEM(v.shape, v.dtype) for v in later] + [pltpu.VMEM((tokens, inner), BF16), pltpu.VMEM((groups, tokens, 1), F32)],
        [vmem] * (len(later) + 2),
        grid=(groups,),
        scratch_shapes=[pltpu.SemaphoreType.DMA((len(later),))],
        cost_estimate=small_cost,
        compiler_params=large,
    )

    part = shape(span_rows, tokens)

    def project(picked):
        kernel = functools.partial(project_kernel, picked)
        return step(kernel, [weight, normed, goal], [part] * len(picked), scalars=[places])

    in_hops, across = inward(heads_over)
    parts = project([0])
    (kept,) = step(kept_kernel, [own_global, own_momentum], [shape(owned, inner)])
    gathered["kept"] = kept[None]
    kept_landed = landing("kept", by_two)
    parts += project(list(range(1, chunks)))
    first_landed = [lax.ppermute(p, "tensor", in_hops[0]) if in_hops else None for p in parts]
    sums, cots = {}, {}

    def sum_side(n, waits=()):
        held = parts[n]
        for at, pairs in enumerate(in_hops):
            landed = first_landed[n] if at == 0 else lax.ppermute(held, "tensor", pairs)
            (held,) = step(add_kernel, [held, landed], [part], waits=waits)
        sums[n] = held

    def sum_all(n, waits=(), cost=small_cost):
        landed = lax.ppermute(sums[n], "tensor", across)
        (mid,) = step(add_kernel, [sums[n], landed], [part], waits=waits, cost=cost)
        out = mid
        for pairs in reversed(in_hops):
            back = lax.ppermute(out, "tensor", [(b, a) for a, b in pairs])
            out = back if pairs is in_hops[0] else jnp.where(in_middle, mid, back)
        cots[n] = (mid, out)

    held, deltas = {}, {}
    tile = shape(8, LANES, dtype=F32)
    squares = {-1: jnp.zeros((8, LANES), F32)}

    def new_rows(b, waits=()):
        batch = batches[b]
        rows = len(batch) * piece
        keep, send = step(
            functools.partial(gradient_kernel, batch),
            [c for n in batch for c in cots[n]] + [normed, weight],
            [shape(replicas // 2, rows, inner)] * 2,
            scalars=[places],
            waits=waits,
        )
        return [keep, exchange(send, 1)]

    def narrow(b, some, waits=()):
        rows = len(batches[b]) * piece
        for bit, bits in some:
            ways = 1 << bits
            left = held[b][0].shape[0] // ways
            picked = step(
                functools.partial(pick_kernel, len(held[b]), 1 << (bit - 1)),
                [h.reshape(left, ways, rows, inner) for h in held[b]],
                [shape(left, rows, inner)] * ways,
                scalars=[places],
                waits=waits,
            )
            held[b] = [picked[0]] + [exchange(picked[mask], mask << bit) for mask in range(1, ways)]

    def own_rows(b, cost=small_cost, waits=()):
        batch = batches[b]
        rows = len(batch) * piece
        deltas[b], sent, squares[b] = step(
            functools.partial(delta_kernel, len(held[b]), batch[0] * piece, replicas),
            [own_global, squares[b - 1], *held[b]],
            [shape(rows, inner, dtype=F32), shape(rows, inner), tile],
            cost=cost,
            waits=waits,
        )
        gathered[b] = sent[None]

    def backward(begin, count, so_far):
        wide, state, dt, gain_here = group_specs(begin)
        operands = [places, *shared, normed, inv, weight] + [c for n in range(chunks) for c in cots[n]]
        specs = [smem, dt, wide, state, state, gain_here, smem, smem, smem, vmem, vmem, vmem] + [vmem] * (2 * chunks)
        aliases = {}
        if so_far is not None:
            aliases = {len(operands): 0}
            operands.append(so_far)
            specs.append(anywhere)
        (grad,) = run(
            functools.partial(backward_kernel, begin),
            operands,
            specs,
            [shape(tokens, inner)],
            [wide],
            grid=(count,),
            scratch_shapes=[pltpu.VMEM((tokens, width), F32)],
            input_output_aliases=aliases,
            cost_estimate=small_cost,
            compiler_params=large,
        )
        return grad

    end = len(batches) - 1
    early = end > 1
    for t in range(chunks):
        if t == chunks - 1 and early:
            held[0] = new_rows(0)
        sum_side(t, [cots[t - 3][1]] if t >= 3 and not early else [])
        if t == 0:
            widen("kept", by_two, kept_landed)
            finish("kept")
        if t > 0:
            sum_all(t - 1)
    if early:
        narrow(0, by_one[:1])
    held[end - 1] = new_rows(end - 1)
    if early:
        narrow(0, by_one[1:])
    sum_all(chunks - 1, cost=large_cost)
    narrow(end - 1, by_one[:1])
    step(gate_kernel, [], [tile], waits=[cots[chunks - 2][1], gathered["kept"][1]])
    landed = {}
    if early:
        own_rows(0)
        landed[0] = landing(0, by_two)
    narrow(end - 1, by_one[1:])
    own_rows(end - 1, small_cost)
    landed[end - 1] = landing(end - 1, by_two)
    if early:
        widen(0, by_two, landed[0])
        finish(0)
    held[end] = new_rows(end)
    narrow(end, by_two)
    grad_input = backward(0, groups, None)
    widen(end - 1, by_two, landed[end - 1])
    finish(end - 1)
    own_rows(end, large_cost, [gathered[0][1]] if early else [])
    last_landed = landing(end, by_two)
    total = squares[end]
    for bit in range(heads_over.bit_length() - 1):
        pairs = [(t, t ^ (1 << bit)) for t in range(heads_over)]
        waits = [gathered[b][1] for b in range(end)]
        (total,) = step(add_squares_kernel, [total, lax.ppermute(total, "tensor", pairs)], [tile], waits=waits)
    for bit, bits in by_one:
        landed = [exchange(total, mask << bit) for mask in range(1, 1 << bits)]
        (total,) = step(add_squares_kernel, [total, *landed], [tile])
    widen(end, by_two, last_landed)
    finish(end)
    columns = [total, exchange(total, 1)]

    sizes = [len(batch) * piece for batch in batches]
    pair_spec = pl.BlockSpec((2 * owned, inner), lambda r: (r, 0))
    share = owned // (replicas // 2)
    if share % 8 == 0:
        held_spec = pl.BlockSpec((share, inner), lambda r: (r, 0))
    else:
        held_spec = pl.BlockSpec((owned, inner), lambda r: (0, 0))
    inputs = [own_global, own_momentum, *gathered["kept"], *[v for b in range(end + 1) for v in gathered[b]]]
    inputs += [*[deltas[b] for b in range(end + 1)], *columns]
    new_weight, new_global, new_momentum = run(
        functools.partial(weight_kernel, sizes, features * inner * heads_over),
        [places, *inputs],
        [smem] + [vmem] * len(inputs),
        [shape(features, inner), shape(owned, inner, dtype=F32), shape(owned, inner, dtype=F32)],
        [pair_spec, held_spec, held_spec],
        grid=(replicas // 2,),
        cost_estimate=small_cost,
        compiler_params=small,
    )
    return (grad_input, new_weight, new_global, new_momentum)


def solution(mesh):
    placed = (
        P("replica", "tensor"),
        P("replica", "tensor"),
        P("replica", "tensor"),
        P("replica", "tensor"),
        P("replica", "tensor"),
        P("tensor"),
        P("tensor"),
        P("tensor"),
        P("tensor"),
        P("replica", None, "tensor"),
        P("replica", "tensor"),
        P("replica", "tensor"),
        P(("replica", "tensor"), None),
    )
    return jax.shard_map(
        shards,
        mesh=mesh,
        in_specs=placed,
        out_specs=(
            P("replica", "tensor"),
            P(None, "tensor"),
            P("replica", "tensor"),
            P("replica", "tensor"),
        ),
        check_vma=False,
    )
```

```python
import functools

import jax
import jax.numpy as jnp
from jax import lax
from jax.experimental import pallas as pl
from jax.experimental.pallas import tpu as pltpu
from jax.sharding import PartitionSpec as P

HEAD_DIM = 64
STATE = 128
SPAN = 256
HALF = SPAN // 2
LANES = 128

inner_rate = 0.001
outer_rate = 0.7
outer_beta = 0.9
clip_rms = 0.005
LOG2E = 1.4426950408889634

F32 = jnp.float32
BF16 = jnp.bfloat16
NN = (((1,), (0,)), ((), ()))
NT = (((1,), (1,)), ((), ()))
TN = (((0,), (0,)), ((), ()))


def dot(a, b, dims):
    return lax.dot_general(a, b, dims, preferred_element_type=F32)


def silu(z):
    return 0.5 * z * (1.0 + jnp.tanh(0.5 * z))


def softplus(v):
    return jnp.maximum(v, 0.0) + jnp.log1p(jnp.exp(-jnp.abs(v)))


def iota(shape, axis):
    return lax.broadcasted_iota(jnp.int32, shape, axis)


def thirds(v):
    high = v.astype(BF16).astype(F32)
    middle = (v - high).astype(BF16).astype(F32)
    return jnp.concatenate([high, middle, v - high - middle], axis=0).astype(BF16)


def by_head(refs, first, per_group, tokens):
    row = iota((per_group, tokens), 0)
    rows = []
    for ref in refs:
        value = jnp.zeros((per_group, tokens), F32)
        for h in range(per_group):
            value = jnp.where(row == h, ref[first + h], value)
        rows.append(value)
    return rows


def head_tables(dt_ref, a_ref, bias_ref, first, per_group):
    bias, a_log = by_head([bias_ref, a_ref], first, per_group, dt_ref.shape[1])
    step = softplus(dt_ref[...] + bias)
    return step, -jnp.exp(a_log) * step * LOG2E


def span_tables(step, rate, lo, per_group, width):
    upper = (iota((SPAN, SPAN), 0) <= iota((SPAN, SPAN), 1)).astype(BF16)
    step_k = step[:, lo : lo + SPAN]
    sums = dot(thirds(rate[:, lo : lo + SPAN]), upper, NN)
    cum = sums[:per_group] + sums[per_group : 2 * per_group] + sums[2 * per_group :]
    spread = (iota((3 * per_group, width), 1) // HEAD_DIM == iota((3 * per_group, width), 0) % per_group).astype(BF16)
    turn = (iota((3 * per_group, per_group), 1) == iota((3 * per_group, per_group), 0) % per_group).astype(BF16)
    cum_col = dot(thirds(cum), turn, TN)
    step_x = dot(thirds(step_k), spread, TN)
    fade_x = dot(thirds(jnp.exp2(cum)), spread, TN)
    tail_x = dot(thirds(jnp.exp2(cum[:, SPAN - 1 :] - cum) * step_k), spread, TN)
    return cum, cum_col, step_x, fade_x, tail_x


def skip_row(skip_ref, first, per_group, width):
    head = iota((1, width), 1) // HEAD_DIM
    row = jnp.zeros((1, width), F32)
    for h in range(per_group):
        row = jnp.where(head == h, skip_ref[first + h], row)
    return row


def decay(gap, mask=None):
    return jnp.exp2(gap if mask is None else jnp.where(mask, gap, -1e30))


def even_odd(v):
    first = iota(v.shape, 1) % (2 * HEAD_DIM) < HEAD_DIM
    return jnp.where(first, v, 0.0).astype(BF16), jnp.where(first, 0.0, v).astype(BF16)


def forward_kernel(
    count, dt_ref, x_ref, z_ref, b_ref, c_ref, gain_ref, a_ref, bias_ref, skip_ref, *refs
):
    loads = [pltpu.make_async_copy(refs[n], refs[count + n], refs[-1].at[n]) for n in range(count)]
    normed_ref, inv_ref = refs[2 * count : 2 * count + 2]

    @pl.when(pl.program_id(0) == 0)
    def _():
        for load in loads:
            load.start()

    tokens, width = x_ref.shape
    per_group = width // HEAD_DIM
    first = pl.program_id(0) * per_group
    lanes_here = pl.ds(pl.multiple_of(pl.program_id(0) * width, LANES), width)
    step, rate = head_tables(dt_ref, a_ref, bias_ref, first, per_group)
    skip = skip_row(skip_ref, first, per_group, width)
    causal = iota((HALF, HALF), 0) >= iota((HALF, HALF), 1)
    spans = tokens // SPAN
    entering = None
    for k in range(spans):
        rows = slice(k * SPAN, (k + 1) * SPAN)
        cum, cum_col, step_x, fade_x, tail_x = span_tables(step, rate, k * SPAN, per_group, width)
        x = x_ref[rows, :].astype(F32)
        b, c = b_ref[rows, :], c_ref[rows, :]
        scores = dot(c, b, NT)
        values = even_odd(x * step_x)
        pieces = []
        for pair in range(per_group // 2):
            lanes = slice(2 * pair * HEAD_DIM, 2 * (pair + 1) * HEAD_DIM)
            tops, bottoms = [], []
            for h in (2 * pair, 2 * pair + 1):
                col, line = cum_col[:, h : h + 1], cum[h : h + 1, :]
                top = decay(col[:HALF] - line[:, :HALF], causal) * scores[:HALF, :HALF]
                left = decay(col[HALF:] - line[:, :HALF]) * scores[HALF:, :HALF]
                low = decay(col[HALF:] - line[:, HALF:], causal) * scores[HALF:, HALF:]
                tops.append(top.astype(BF16))
                bottoms += [left.astype(BF16), low.astype(BF16)]
            upper_values = jnp.concatenate([v[:HALF, lanes] for v in values], axis=0)
            all_values = jnp.concatenate([v[:, lanes] for v in values], axis=0)
            pieces.append(
                jnp.concatenate(
                    [
                        dot(jnp.concatenate(tops, axis=1), upper_values, NN),
                        dot(jnp.concatenate(bottoms, axis=1), all_values, NN),
                    ],
                    axis=0,
                )
            )
        ssd = jnp.concatenate(pieces, axis=1) + skip * x
        if entering is not None:
            ssd = ssd + dot(c, entering.astype(BF16), NN) * fade_x
        if k + 1 < spans:
            state = dot(b, (x * tail_x).astype(BF16), TN)
            entering = state if entering is None else entering * fade_x[SPAN - 1 :, :] + state
        gated = ssd * silu(z_ref[rows, :].astype(F32))
        inv = lax.rsqrt(jnp.mean(gated * gated, axis=1, keepdims=True) + 1e-05)
        normed_ref[rows, lanes_here] = (gated * inv * gain_ref[...]).astype(BF16)
        inv_ref[pl.program_id(0), rows, :] = inv

    @pl.when(pl.program_id(0) == pl.num_programs(0) - 1)
    def _():
        for load in loads:
            load.wait()


def kept_kernel(global_ref, momentum_ref, kept_ref):
    kept_ref[...] = (global_ref[...] - outer_rate * outer_beta * outer_beta * momentum_ref[...]).astype(BF16)


def project_kernel(chunks, place_ref, weight_ref, normed_ref, target_ref, *part_refs):
    replicas, owned, inner = weight_ref.shape
    held, features = target_ref.shape
    piece = part_refs[0].shape[0] // replicas
    tokens = normed_ref.shape[0]
    eye = (iota((held, held), 0) == iota((held, held), 1)).astype(BF16)
    turned = dot(target_ref[...], eye, TN).reshape(replicas, owned, held)
    here = iota((replicas * piece, tokens), 1) // held == place_ref[0]
    for n, part_ref in zip(chunks, part_refs):
        at = slice(n * piece, (n + 1) * piece)
        part = dot(weight_ref[:, at, :].reshape(replicas * piece, inner), normed_ref[...], NT)
        goal = jnp.concatenate([turned[:, at, :].reshape(replicas * piece, held)] * (tokens // held), axis=1)
        part_ref[...] = (part - jnp.where(here, goal, 0.0)).astype(BF16)


def gate_kernel(out_ref):
    out_ref[...] = jnp.zeros_like(out_ref)


def add_kernel(a_ref, b_ref, sum_ref):
    sum_ref[...] = (a_ref[...].astype(F32) + b_ref[...].astype(F32)).astype(BF16)


def add_squares_kernel(*refs):
    *term_refs, sum_ref = refs
    values = [ref[...] for ref in term_refs]
    while len(values) > 1:
        values = [a + b for a, b in zip(values[::2], values[1::2])]
    sum_ref[...] = values[0]


def gradient_kernel(batch, place_ref, *refs):
    count = len(batch)
    cot_refs, (normed_ref, weight_ref, keep_ref, send_ref) = refs[: 2 * count], refs[2 * count :]
    middle = place_ref[1] == 1
    odd = place_ref[2] == 1
    replicas, _, inner = weight_ref.shape
    piece = keep_ref.shape[1] // count
    tile = min(inner, 512)
    for n, chunk in enumerate(batch):
        cot = jnp.where(middle, cot_refs[2 * n][...], cot_refs[2 * n + 1][...])
        rows = slice(chunk * piece, (chunk + 1) * piece)
        at = slice(n * piece, (n + 1) * piece)
        for lo in range(0, inner, tile):
            cols = slice(lo, lo + tile)
            weight = weight_ref[:, rows, cols].reshape(replicas * piece, tile).astype(F32)
            new = weight - inner_rate * dot(cot, normed_ref[:, cols], NN)
            new = new.astype(BF16).reshape(replicas // 2, 2, piece, tile)
            keep_ref[:, at, cols] = jnp.where(odd, new[:, 1], new[:, 0])
            send_ref[:, at, cols] = jnp.where(odd, new[:, 0], new[:, 1])


def backward_kernel(
    begin, place_ref, dt_ref, z_ref, b_ref, c_ref, gain_ref, a_ref, bias_ref, skip_ref, normed_ref, inv_ref, weight_ref, *refs
):
    *cot_refs, dx_ref, dn_ref = refs
    if len(cot_refs) % 2:
        cot_refs = cot_refs[:-1]
    tokens, width = z_ref.shape
    per_group = width // HEAD_DIM
    group = pl.program_id(0) + begin
    first = group * per_group
    here = pl.ds(pl.multiple_of(group * width, LANES), width)
    replicas, owned, _ = weight_ref.shape
    chunks = len(cot_refs) // 2
    piece = owned // chunks
    middle = place_ref[1] == 1
    for n in range(chunks):
        weight = weight_ref[:, n * piece : (n + 1) * piece, here].reshape(replicas * piece, width)
        term = dot(jnp.where(middle, cot_refs[2 * n][...], cot_refs[2 * n + 1][...]), weight, TN)
        dn_ref[...] = term if n == 0 else dn_ref[...] + term
    step, rate = head_tables(dt_ref, a_ref, bias_ref, first, per_group)
    skip = skip_row(skip_ref, first, per_group, width)
    causal = iota((HALF, HALF), 1) >= iota((HALF, HALF), 0)
    spans = tokens // SPAN
    d_state = None
    for k in reversed(range(spans)):
        rows = slice(k * SPAN, (k + 1) * SPAN)
        cum, cum_col, step_x, fade_x, tail_x = span_tables(step, rate, k * SPAN, per_group, width)
        dn = dn_ref[rows, :]
        gain = gain_ref[...]
        normed = normed_ref[rows, here].astype(F32)
        shared = jnp.mean(normed * dn, axis=1, keepdims=True)
        d_gated = inv_ref[group, rows, :] * (gain * dn - (normed / gain) * shared)
        d_ssd = d_gated * silu(z_ref[rows, :].astype(F32))
        values = even_odd(d_ssd)
        b, c = b_ref[rows, :], c_ref[rows, :]
        scores = dot(b, c, NT)
        pieces = []
        for pair in range(per_group // 2):
            lanes = slice(2 * pair * HEAD_DIM, 2 * (pair + 1) * HEAD_DIM)
            tops, bottoms = [], []
            for h in (2 * pair, 2 * pair + 1):
                col, line = cum_col[:, h : h + 1], cum[h : h + 1, :]
                high = decay(line[:, :HALF] - col[:HALF], causal) * scores[:HALF, :HALF]
                right = decay(line[:, HALF:] - col[:HALF]) * scores[:HALF, HALF:]
                low = decay(line[:, HALF:] - col[HALF:], causal) * scores[HALF:, HALF:]
                tops += [high.astype(BF16), right.astype(BF16)]
                bottoms.append(low.astype(BF16))
            lower_values = jnp.concatenate([v[HALF:, lanes] for v in values], axis=0)
            all_values = jnp.concatenate([v[:, lanes] for v in values], axis=0)
            pieces.append(
                jnp.concatenate(
                    [
                        dot(jnp.concatenate(tops, axis=1), all_values, NN),
                        dot(jnp.concatenate(bottoms, axis=1), lower_values, NN),
                    ],
                    axis=0,
                )
            )
        dx = jnp.concatenate(pieces, axis=1) * step_x + skip * d_ssd
        if d_state is not None:
            dx = dx + dot(b, d_state.astype(BF16), NN) * tail_x
        dx_ref[rows, :] = dx.astype(BF16)
        if k > 0:
            own = dot(c, (d_ssd * fade_x).astype(BF16), TN)
            d_state = own if d_state is None else own + d_state * fade_x[SPAN - 1 :, :]


def pick_kernel(count, unit, place_ref, *refs):
    terms, outs = refs[:count], refs[count:]
    my = lax.rem(lax.div(place_ref[3], unit), len(outs))
    for mask, out_ref in enumerate(outs):
        at = lax.bitwise_xor(my, jnp.int32(mask))
        total = terms[0][:, at].astype(F32)
        for term in terms[1:]:
            total = total + term[:, at].astype(F32)
        out_ref[...] = total.astype(BF16)


def delta_kernel(count, lo, replicas, global_ref, before_ref, *refs):
    terms, (delta_ref, sent_ref, squares_ref) = refs[:count], refs[count:]
    rows, inner = delta_ref.shape
    total = terms[0][0].astype(F32)
    for term in terms[1:]:
        total = total + term[0].astype(F32)
    delta = global_ref[lo : lo + rows, :] - total / replicas
    delta_ref[...] = delta
    sent_ref[...] = delta.astype(BF16)
    squares = jnp.sum(delta * delta, axis=0, keepdims=True)
    squares = before_ref[...] + jnp.broadcast_to(jnp.sum(squares, axis=1, keepdims=True), before_ref.shape)
    squares_ref[...] = squares


def join_kernel(*refs):
    *parts, out_ref = refs
    lo = 0
    for part in parts:
        out_ref[lo : lo + part.shape[0]] = part[...]
        lo += part.shape[0]


def pass_kernel(rows_ref, out_ref):
    out_ref[...] = rows_ref[...]


def weight_kernel(sizes, entries, place_ref, global_ref, momentum_ref, *refs):
    count = len(sizes)
    pairs, deltas, squares = refs[: 2 * count + 2], refs[2 * count + 2 : 3 * count + 2], refs[3 * count + 2 : -3]
    new_ref, new_global_ref, new_momentum_ref = refs[-3:]
    mean = (squares[0][:1, :1] + squares[1][:1, :1]) / entries
    factor = jnp.minimum(1.0, clip_rms / jnp.sqrt(mean + 1e-06))
    at_chip = lax.bitwise_xor(pl.program_id(0), place_ref[3])
    owned = new_ref.shape[0] // 2
    scale = (outer_rate * (1.0 + outer_beta)) * factor

    def one_core(core, side):
        lo = 0
        for n, size in enumerate(sizes):
            kept = pairs[side][at_chip, lo : lo + size, :].astype(F32)
            delta = pairs[2 * n + 2 + side][at_chip, :size, :].astype(F32)
            new_ref[core * owned + lo : core * owned + lo + size, :] = (kept - scale * delta).astype(BF16)
            lo += size

    for own_core in range(2):

        @pl.when(place_ref[2] == own_core)
        def _():
            one_core(own_core, 0)
            one_core(1 - own_core, 1)

    part = new_global_ref.shape[0]
    lo = 0
    for n, size in enumerate(sizes):
        for row in range(0, size, min(size, part)):
            rows = min(size, part)
            at, here = slice(lo + row, lo + row + rows), (lo + row) % part

            @pl.when(pl.program_id(0) == (lo + row) // part)
            def _():
                clipped = factor * deltas[n][row : row + rows, :]
                new_momentum = outer_beta * momentum_ref[at, :] + clipped
                new_momentum_ref[here : here + rows, :] = new_momentum
                new_global = global_ref[at, :] - outer_rate * (clipped + outer_beta * new_momentum)
                new_global_ref[here : here + rows, :] = new_global

        lo += size


def inward(axis_size):
    half = axis_size // 2
    hops = [[(s, s + 1), (axis_size - 1 - s, axis_size - 2 - s)] for s in range(half - 1)]
    return hops, [(half - 1, half), (half, half - 1)]


def in_turn(kernel, inputs, waits, outs):
    def body(*refs):
        end = inputs + waits + outs
        refs[end][...] = jnp.zeros_like(refs[end])
        kernel(*refs[:inputs], *refs[inputs + waits : end], *refs[end + 1 :])

    return body


def stages(replicas, most=2):
    bit, left, found = 1, replicas // 2, []
    while left > 1:
        bits = most if left >= 1 << most else 1
        found.append((bit, bits))
        bit, left = bit + bits, left >> bits
    return found


def shards(
    x_in,
    gate_z,
    b_proj,
    c_proj,
    dt_raw,
    a_log,
    dt_bias,
    skip_d,
    norm_gain,
    out_weight,
    global_weight,
    momentum,
    target,
):
    tokens, inner = x_in.shape
    features = out_weight.shape[1]
    replicas = lax.axis_size("replica")
    heads_over = lax.axis_size("tensor")
    groups = b_proj.shape[1] // STATE
    heads = dt_raw.shape[1]
    width = inner // groups
    owned = features // replicas
    chunks = max(2, min(4, owned // 16))
    batches = [[n] for n in range(chunks // 2)] + [list(range(chunks // 2, chunks))]
    piece = owned // chunks
    span_rows = replicas * piece
    place = lax.axis_index("tensor")
    me = lax.axis_index("replica")
    in_middle = (place == heads_over // 2 - 1) | (place == heads_over // 2)
    places = jnp.stack([place, in_middle.astype(jnp.int32), lax.rem(me, 2), lax.div(me, 2)]).astype(jnp.int32)
    stored = out_weight[0].reshape(replicas, owned, inner)
    gain = norm_gain.reshape(1, inner)
    dt_rows = dt_raw.T

    smem = pl.BlockSpec(memory_space=pltpu.SMEM)
    vmem = pl.BlockSpec(memory_space=pltpu.VMEM)
    anywhere = pl.BlockSpec(memory_space=pl.ANY)
    inv_spec = pl.BlockSpec((1, tokens, 1), lambda g: (g, 0, 0))
    large = pltpu.CompilerParams(vmem_limit_bytes=20 * 1024 * 1024)
    small = pltpu.CompilerParams(vmem_limit_bytes=12 * 1024 * 1024)
    small_cost = pl.CostEstimate(flops=1, bytes_accessed=1, transcendentals=0)
    some_cost = pl.CostEstimate(flops=2_000_000_000, bytes_accessed=1, transcendentals=0)
    large_cost = pl.CostEstimate(flops=30_000_000_000, bytes_accessed=1, transcendentals=0)

    turn = []

    def run(kernel, inputs, in_specs, outs, out_specs, waits=(), **options):
        waits = [*turn[-1:], *waits]
        done = jax.ShapeDtypeStruct((8, LANES), F32)
        *results, ran = pl.pallas_call(
            in_turn(kernel, len(inputs), len(waits), len(outs)),
            in_specs=[*in_specs, *[vmem] * len(waits)],
            out_specs=[*out_specs, vmem],
            out_shape=[*outs, done],
            **options,
        )(*inputs, *waits)
        turn.append(ran)
        return results

    def step(kernel, operands, outs, scalars=(), waits=(), cost=small_cost):
        return run(
            kernel,
            [*scalars, *operands],
            [smem] * len(scalars) + [vmem] * len(operands),
            outs,
            [vmem] * len(outs),
            waits,
            cost_estimate=cost,
            compiler_params=small,
        )

    def shape(*dims, dtype=BF16):
        return jax.ShapeDtypeStruct(dims, dtype)

    def in_hbm(*arrays):
        return [pltpu.with_memory_space_constraint(a, pltpu.HBM) for a in arrays]

    def group_specs(begin):
        wide = pl.BlockSpec((tokens, width), lambda g: (0, g + begin))
        state = pl.BlockSpec((tokens, STATE), lambda g: (0, g + begin))
        dt = pl.BlockSpec((heads // groups, tokens), lambda g: (g + begin, 0))
        return wide, state, dt, pl.BlockSpec((1, width), lambda g: (0, g + begin))

    def exchange(value, mask):
        return lax.ppermute(value, "replica", [(r, r ^ mask) for r in range(replicas)])

    gathered = {}

    def landing(b, some):
        (bit, bits), *_ = some
        return [exchange(gathered[b], mask << bit) for mask in range(1, 1 << bits)]

    def widen(b, some, landed=None):
        for at, (bit, bits) in enumerate(some):
            parts = [gathered[b]] + (landed if at == 0 and landed else landing(b, some[at:]))
            out = shape(len(parts) * parts[0].shape[0], *parts[0].shape[1:])
            (gathered[b],) = step(join_kernel, parts, [out])

    def finish(b):
        gathered[b] = [gathered[b], exchange(gathered[b], 1)]

    by_two, by_one = stages(replicas), stages(replicas, 1)
    by_group, by_state, dt_spec, gain_spec = group_specs(0)
    shared = in_hbm(dt_rows, gate_z, b_proj, c_proj, gain, a_log, dt_bias, skip_d)
    later = [stored, target, global_weight, momentum]
    weight, goal, own_global, own_momentum, normed, inv = run(
        functools.partial(forward_kernel, len(later)),
        [shared[0], *in_hbm(x_in), *shared[1:], *in_hbm(*later)],
        [dt_spec, by_group, by_group, by_state, by_state, gain_spec, smem, smem, smem] + [anywhere] * len(later),
        [pltpu.VMEM(v.shape, v.dtype) for v in later] + [pltpu.VMEM((tokens, inner), BF16), pltpu.VMEM((groups, tokens, 1), F32)],
        [vmem] * (len(later) + 2),
        grid=(groups,),
        scratch_shapes=[pltpu.SemaphoreType.DMA((len(later),))],
        cost_estimate=small_cost,
        compiler_params=large,
    )

    part = shape(span_rows, tokens)

    def project(picked):
        kernel = functools.partial(project_kernel, picked)
        return step(kernel, [weight, normed, goal], [part] * len(picked), scalars=[places])

    in_hops, across = inward(heads_over)
    parts = project([0])
    (kept,) = step(kept_kernel, [own_global, own_momentum], [shape(owned, inner)])
    gathered["kept"] = kept[None]
    kept_landed = landing("kept", by_two)
    parts += project(list(range(1, chunks)))
    first_landed = [lax.ppermute(p, "tensor", in_hops[0]) if in_hops else None for p in parts]
    sums, cots = {}, {}

    def sum_side(n, waits=()):
        held = parts[n]
        for at, pairs in enumerate(in_hops):
            landed = first_landed[n] if at == 0 else lax.ppermute(held, "tensor", pairs)
            (held,) = step(add_kernel, [held, landed], [part], waits=waits)
        sums[n] = held

    def sum_all(n, waits=(), cost=small_cost):
        landed = lax.ppermute(sums[n], "tensor", across)
        (mid,) = step(add_kernel, [sums[n], landed], [part], waits=waits, cost=cost)
        out = mid
        for pairs in reversed(in_hops):
            back = lax.ppermute(out, "tensor", [(b, a) for a, b in pairs])
            out = back if pairs is in_hops[0] else jnp.where(in_middle, mid, back)
        cots[n] = (mid, out)

    held, deltas = {}, {}
    tile = shape(8, LANES, dtype=F32)
    squares = {-1: jnp.zeros((8, LANES), F32)}

    def new_rows(b, waits=()):
        batch = batches[b]
        rows = len(batch) * piece
        keep, send = step(
            functools.partial(gradient_kernel, batch),
            [c for n in batch for c in cots[n]] + [normed, weight],
            [shape(replicas // 2, rows, inner)] * 2,
            scalars=[places],
            waits=waits,
        )
        return [keep, exchange(send, 1)]

    def narrow(b, some, waits=()):
        rows = len(batches[b]) * piece
        for bit, bits in some:
            ways = 1 << bits
            left = held[b][0].shape[0] // ways
            picked = step(
                functools.partial(pick_kernel, len(held[b]), 1 << (bit - 1)),
                [h.reshape(left, ways, rows, inner) for h in held[b]],
                [shape(left, rows, inner)] * ways,
                scalars=[places],
                waits=waits,
            )
            held[b] = [picked[0]] + [exchange(picked[mask], mask << bit) for mask in range(1, ways)]

    def own_rows(b, cost=small_cost, waits=()):
        batch = batches[b]
        rows = len(batch) * piece
        deltas[b], sent, squares[b] = step(
            functools.partial(delta_kernel, len(held[b]), batch[0] * piece, replicas),
            [own_global, squares[b - 1], *held[b]],
            [shape(rows, inner, dtype=F32), shape(rows, inner), tile],
            cost=cost,
            waits=waits,
        )
        gathered[b] = sent[None]

    def backward(begin, count, so_far):
        wide, state, dt, gain_here = group_specs(begin)
        operands = [places, *shared, normed, inv, weight] + [c for n in range(chunks) for c in cots[n]]
        specs = [smem, dt, wide, state, state, gain_here, smem, smem, smem, vmem, vmem, vmem] + [vmem] * (2 * chunks)
        aliases = {}
        if so_far is not None:
            aliases = {len(operands): 0}
            operands.append(so_far)
            specs.append(anywhere)
        (grad,) = run(
            functools.partial(backward_kernel, begin),
            operands,
            specs,
            [shape(tokens, inner)],
            [wide],
            grid=(count,),
            scratch_shapes=[pltpu.VMEM((tokens, width), F32)],
            input_output_aliases=aliases,
            cost_estimate=small_cost,
            compiler_params=large,
        )
        return grad

    end = len(batches) - 1
    early = end > 1
    for t in range(chunks):
        if t == chunks - 1 and early:
            held[0] = new_rows(0)
        sum_side(t, [cots[t - 3][1]] if t >= 3 and not early else [])
        if t == 0:
            widen("kept", by_two, kept_landed)
            finish("kept")
        if t > 0:
            sum_all(t - 1)
    if early:
        narrow(0, by_one[:1])
    held[end - 1] = new_rows(end - 1)
    if early:
        narrow(0, by_one[1:])
    sum_all(chunks - 1, cost=large_cost)
    narrow(end - 1, by_one[:1])
    step(gate_kernel, [], [tile], waits=[cots[chunks - 2][1], gathered["kept"][1]])
    landed = {}
    if early:
        own_rows(0)
        landed[0] = landing(0, by_two)
    narrow(end - 1, by_one[1:])
    own_rows(end - 1, small_cost)
    landed[end - 1] = landing(end - 1, by_two)
    if early:
        widen(0, by_two, landed[0])
        finish(0)
    held[end] = new_rows(end)
    narrow(end, by_two)
    grad_input = backward(0, groups, None)
    widen(end - 1, by_two, landed[end - 1])
    finish(end - 1)
    own_rows(end, large_cost, [gathered[0][1]] if early else [])
    (gathered[end],) = step(pass_kernel, [gathered[end]], [shape(*gathered[end].shape)])
    last_landed = landing(end, by_two)
    total = squares[end]
    for bit in range(heads_over.bit_length() - 1):
        pairs = [(t, t ^ (1 << bit)) for t in range(heads_over)]
        waits = [gathered[b][1] for b in range(end)]
        cost = small_cost if bit else large_cost
        landed = lax.ppermute(total, "tensor", pairs)
        (total,) = step(add_squares_kernel, [total, landed], [tile], waits=waits, cost=cost)
    for bit, bits in by_one:
        landed = [exchange(total, mask << bit) for mask in range(1, 1 << bits)]
        (total,) = step(add_squares_kernel, [total, *landed], [tile])
    widen(end, by_two, last_landed)
    finish(end)
    columns = [total, exchange(total, 1)]

    sizes = [len(batch) * piece for batch in batches]
    pair_spec = pl.BlockSpec((2 * owned, inner), lambda r: (r, 0))
    share = owned // (replicas // 2)
    if share % 8 == 0:
        held_spec = pl.BlockSpec((share, inner), lambda r: (r, 0))
    else:
        held_spec = pl.BlockSpec((owned, inner), lambda r: (0, 0))
    inputs = [own_global, own_momentum, *gathered["kept"], *[v for b in range(end + 1) for v in gathered[b]]]
    inputs += [*[deltas[b] for b in range(end + 1)], *columns]
    new_weight, new_global, new_momentum = run(
        functools.partial(weight_kernel, sizes, features * inner * heads_over),
        [places, *inputs],
        [smem] + [vmem] * len(inputs),
        [shape(features, inner), shape(owned, inner, dtype=F32), shape(owned, inner, dtype=F32)],
        [pair_spec, held_spec, held_spec],
        grid=(replicas // 2,),
        cost_estimate=small_cost,
        compiler_params=small,
    )
    return (grad_input, new_weight, new_global, new_momentum)


def solution(mesh):
    placed = (
        P("replica", "tensor"),
        P("replica", "tensor"),
        P("replica", "tensor"),
        P("replica", "tensor"),
        P("replica", "tensor"),
        P("tensor"),
        P("tensor"),
        P("tensor"),
        P("tensor"),
        P("replica", None, "tensor"),
        P("replica", "tensor"),
        P("replica", "tensor"),
        P(("replica", "tensor"), None),
    )
    return jax.shard_map(
        shards,
        mesh=mesh,
        in_specs=placed,
        out_specs=(
            P("replica", "tensor"),
            P(None, "tensor"),
            P("replica", "tensor"),
            P("replica", "tensor"),
        ),
        check_vma=False,
    )
```

```python
import functools

import jax
import jax.numpy as jnp
from jax import lax
from jax.experimental import pallas as pl
from jax.experimental.pallas import tpu as pltpu
from jax.sharding import PartitionSpec as P

HEAD_DIM = 64
STATE = 128
SPAN = 256
HALF = SPAN // 2
LANES = 128

inner_rate = 0.001
outer_rate = 0.7
outer_beta = 0.9
clip_rms = 0.005
LOG2E = 1.4426950408889634

F32 = jnp.float32
BF16 = jnp.bfloat16
NN = (((1,), (0,)), ((), ()))
NT = (((1,), (1,)), ((), ()))
TN = (((0,), (0,)), ((), ()))


def dot(a, b, dims):
    return lax.dot_general(a, b, dims, preferred_element_type=F32)


def silu(z):
    return 0.5 * z * (1.0 + jnp.tanh(0.5 * z))


def softplus(v):
    return jnp.maximum(v, 0.0) + jnp.log1p(jnp.exp(-jnp.abs(v)))


def iota(shape, axis):
    return lax.broadcasted_iota(jnp.int32, shape, axis)


def thirds(v):
    high = v.astype(BF16).astype(F32)
    middle = (v - high).astype(BF16).astype(F32)
    return jnp.concatenate([high, middle, v - high - middle], axis=0).astype(BF16)


def by_head(refs, first, per_group, tokens):
    row = iota((per_group, tokens), 0)
    rows = []
    for ref in refs:
        value = jnp.zeros((per_group, tokens), F32)
        for h in range(per_group):
            value = jnp.where(row == h, ref[first + h], value)
        rows.append(value)
    return rows


def head_tables(dt_ref, a_ref, bias_ref, first, per_group):
    bias, a_log = by_head([bias_ref, a_ref], first, per_group, dt_ref.shape[1])
    step = softplus(dt_ref[...] + bias)
    return step, -jnp.exp(a_log) * step * LOG2E


def span_tables(step, rate, lo, per_group, width):
    upper = (iota((SPAN, SPAN), 0) <= iota((SPAN, SPAN), 1)).astype(BF16)
    step_k = step[:, lo : lo + SPAN]
    sums = dot(thirds(rate[:, lo : lo + SPAN]), upper, NN)
    cum = sums[:per_group] + sums[per_group : 2 * per_group] + sums[2 * per_group :]
    spread = (iota((3 * per_group, width), 1) // HEAD_DIM == iota((3 * per_group, width), 0) % per_group).astype(BF16)
    turn = (iota((3 * per_group, per_group), 1) == iota((3 * per_group, per_group), 0) % per_group).astype(BF16)
    cum_col = dot(thirds(cum), turn, TN)
    step_x = dot(thirds(step_k), spread, TN)
    fade_x = dot(thirds(jnp.exp2(cum)), spread, TN)
    tail_x = dot(thirds(jnp.exp2(cum[:, SPAN - 1 :] - cum) * step_k), spread, TN)
    return cum, cum_col, step_x, fade_x, tail_x


def skip_row(skip_ref, first, per_group, width):
    head = iota((1, width), 1) // HEAD_DIM
    row = jnp.zeros((1, width), F32)
    for h in range(per_group):
        row = jnp.where(head == h, skip_ref[first + h], row)
    return row


def decay(gap, mask=None):
    return jnp.exp2(gap if mask is None else jnp.where(mask, gap, -1e30))


def even_odd(v):
    first = iota(v.shape, 1) % (2 * HEAD_DIM) < HEAD_DIM
    return jnp.where(first, v, 0.0).astype(BF16), jnp.where(first, 0.0, v).astype(BF16)


def forward_kernel(
    count, dt_ref, x_ref, z_ref, b_ref, c_ref, gain_ref, a_ref, bias_ref, skip_ref, *refs
):
    loads = [pltpu.make_async_copy(refs[n], refs[count + n], refs[-1].at[n]) for n in range(count)]
    normed_ref, inv_ref = refs[2 * count : 2 * count + 2]

    @pl.when(pl.program_id(0) == 0)
    def _():
        for load in loads:
            load.start()

    tokens, width = x_ref.shape
    per_group = width // HEAD_DIM
    first = pl.program_id(0) * per_group
    lanes_here = pl.ds(pl.multiple_of(pl.program_id(0) * width, LANES), width)
    step, rate = head_tables(dt_ref, a_ref, bias_ref, first, per_group)
    skip = skip_row(skip_ref, first, per_group, width)
    causal = iota((HALF, HALF), 0) >= iota((HALF, HALF), 1)
    spans = tokens // SPAN
    entering = None
    for k in range(spans):
        rows = slice(k * SPAN, (k + 1) * SPAN)
        cum, cum_col, step_x, fade_x, tail_x = span_tables(step, rate, k * SPAN, per_group, width)
        x = x_ref[rows, :].astype(F32)
        b, c = b_ref[rows, :], c_ref[rows, :]
        scores = dot(c, b, NT)
        values = even_odd(x * step_x)
        pieces = []
        for pair in range(per_group // 2):
            lanes = slice(2 * pair * HEAD_DIM, 2 * (pair + 1) * HEAD_DIM)
            tops, bottoms = [], []
            for h in (2 * pair, 2 * pair + 1):
                col, line = cum_col[:, h : h + 1], cum[h : h + 1, :]
                top = decay(col[:HALF] - line[:, :HALF], causal) * scores[:HALF, :HALF]
                left = decay(col[HALF:] - line[:, :HALF]) * scores[HALF:, :HALF]
                low = decay(col[HALF:] - line[:, HALF:], causal) * scores[HALF:, HALF:]
                tops.append(top.astype(BF16))
                bottoms += [left.astype(BF16), low.astype(BF16)]
            upper_values = jnp.concatenate([v[:HALF, lanes] for v in values], axis=0)
            all_values = jnp.concatenate([v[:, lanes] for v in values], axis=0)
            pieces.append(
                jnp.concatenate(
                    [
                        dot(jnp.concatenate(tops, axis=1), upper_values, NN),
                        dot(jnp.concatenate(bottoms, axis=1), all_values, NN),
                    ],
                    axis=0,
                )
            )
        ssd = jnp.concatenate(pieces, axis=1) + skip * x
        if entering is not None:
            ssd = ssd + dot(c, entering.astype(BF16), NN) * fade_x
        if k + 1 < spans:
            state = dot(b, (x * tail_x).astype(BF16), TN)
            entering = state if entering is None else entering * fade_x[SPAN - 1 :, :] + state
        gated = ssd * silu(z_ref[rows, :].astype(F32))
        inv = lax.rsqrt(jnp.mean(gated * gated, axis=1, keepdims=True) + 1e-05)
        normed_ref[rows, lanes_here] = (gated * inv * gain_ref[...]).astype(BF16)
        inv_ref[pl.program_id(0), rows, :] = inv

    @pl.when(pl.program_id(0) == pl.num_programs(0) - 1)
    def _():
        for load in loads:
            load.wait()


def kept_kernel(global_ref, momentum_ref, kept_ref):
    kept_ref[...] = (global_ref[...] - outer_rate * outer_beta * outer_beta * momentum_ref[...]).astype(BF16)


def project_kernel(chunks, place_ref, weight_ref, normed_ref, target_ref, *part_refs):
    replicas, owned, inner = weight_ref.shape
    held, features = target_ref.shape
    piece = part_refs[0].shape[0] // replicas
    tokens = normed_ref.shape[0]
    eye = (iota((held, held), 0) == iota((held, held), 1)).astype(BF16)
    turned = dot(target_ref[...], eye, TN).reshape(replicas, owned, held)
    here = iota((replicas * piece, tokens), 1) // held == place_ref[0]
    for n, part_ref in zip(chunks, part_refs):
        at = slice(n * piece, (n + 1) * piece)
        part = dot(weight_ref[:, at, :].reshape(replicas * piece, inner), normed_ref[...], NT)
        goal = jnp.concatenate([turned[:, at, :].reshape(replicas * piece, held)] * (tokens // held), axis=1)
        part_ref[...] = (part - jnp.where(here, goal, 0.0)).astype(BF16)


def gate_kernel(out_ref):
    out_ref[...] = jnp.zeros_like(out_ref)


def add_kernel(a_ref, b_ref, sum_ref):
    sum_ref[...] = (a_ref[...].astype(F32) + b_ref[...].astype(F32)).astype(BF16)


def add_squares_kernel(*refs):
    *term_refs, sum_ref = refs
    values = [ref[...] for ref in term_refs]
    while len(values) > 1:
        values = [a + b for a, b in zip(values[::2], values[1::2])]
    sum_ref[...] = values[0]


def gradient_kernel(batch, place_ref, *refs):
    count = len(batch)
    cot_refs, (normed_ref, weight_ref, keep_ref, send_ref) = refs[: 2 * count], refs[2 * count :]
    middle = place_ref[1] == 1
    odd = place_ref[2] == 1
    replicas, _, inner = weight_ref.shape
    piece = keep_ref.shape[1] // count
    tile = min(inner, 512)
    for n, chunk in enumerate(batch):
        cot = jnp.where(middle, cot_refs[2 * n][...], cot_refs[2 * n + 1][...])
        rows = slice(chunk * piece, (chunk + 1) * piece)
        at = slice(n * piece, (n + 1) * piece)
        for lo in range(0, inner, tile):
            cols = slice(lo, lo + tile)
            weight = weight_ref[:, rows, cols].reshape(replicas * piece, tile).astype(F32)
            new = weight - inner_rate * dot(cot, normed_ref[:, cols], NN)
            new = new.astype(BF16).reshape(replicas // 2, 2, piece, tile)
            keep_ref[:, at, cols] = jnp.where(odd, new[:, 1], new[:, 0])
            send_ref[:, at, cols] = jnp.where(odd, new[:, 0], new[:, 1])


def backward_kernel(
    begin, place_ref, dt_ref, z_ref, b_ref, c_ref, gain_ref, a_ref, bias_ref, skip_ref, normed_ref, inv_ref, weight_ref, *refs
):
    *cot_refs, dx_ref, dn_ref = refs
    if len(cot_refs) % 2:
        cot_refs = cot_refs[:-1]
    tokens, width = z_ref.shape
    per_group = width // HEAD_DIM
    group = pl.program_id(0) + begin
    first = group * per_group
    here = pl.ds(pl.multiple_of(group * width, LANES), width)
    replicas, owned, _ = weight_ref.shape
    chunks = len(cot_refs) // 2
    piece = owned // chunks
    middle = place_ref[1] == 1
    for n in range(chunks):
        weight = weight_ref[:, n * piece : (n + 1) * piece, here].reshape(replicas * piece, width)
        term = dot(jnp.where(middle, cot_refs[2 * n][...], cot_refs[2 * n + 1][...]), weight, TN)
        dn_ref[...] = term if n == 0 else dn_ref[...] + term
    step, rate = head_tables(dt_ref, a_ref, bias_ref, first, per_group)
    skip = skip_row(skip_ref, first, per_group, width)
    causal = iota((HALF, HALF), 1) >= iota((HALF, HALF), 0)
    spans = tokens // SPAN
    d_state = None
    for k in reversed(range(spans)):
        rows = slice(k * SPAN, (k + 1) * SPAN)
        cum, cum_col, step_x, fade_x, tail_x = span_tables(step, rate, k * SPAN, per_group, width)
        dn = dn_ref[rows, :]
        gain = gain_ref[...]
        normed = normed_ref[rows, here].astype(F32)
        shared = jnp.mean(normed * dn, axis=1, keepdims=True)
        d_gated = inv_ref[group, rows, :] * (gain * dn - (normed / gain) * shared)
        d_ssd = d_gated * silu(z_ref[rows, :].astype(F32))
        values = even_odd(d_ssd)
        b, c = b_ref[rows, :], c_ref[rows, :]
        scores = dot(b, c, NT)
        pieces = []
        for pair in range(per_group // 2):
            lanes = slice(2 * pair * HEAD_DIM, 2 * (pair + 1) * HEAD_DIM)
            tops, bottoms = [], []
            for h in (2 * pair, 2 * pair + 1):
                col, line = cum_col[:, h : h + 1], cum[h : h + 1, :]
                high = decay(line[:, :HALF] - col[:HALF], causal) * scores[:HALF, :HALF]
                right = decay(line[:, HALF:] - col[:HALF]) * scores[:HALF, HALF:]
                low = decay(line[:, HALF:] - col[HALF:], causal) * scores[HALF:, HALF:]
                tops += [high.astype(BF16), right.astype(BF16)]
                bottoms.append(low.astype(BF16))
            lower_values = jnp.concatenate([v[HALF:, lanes] for v in values], axis=0)
            all_values = jnp.concatenate([v[:, lanes] for v in values], axis=0)
            pieces.append(
                jnp.concatenate(
                    [
                        dot(jnp.concatenate(tops, axis=1), all_values, NN),
                        dot(jnp.concatenate(bottoms, axis=1), lower_values, NN),
                    ],
                    axis=0,
                )
            )
        dx = jnp.concatenate(pieces, axis=1) * step_x + skip * d_ssd
        if d_state is not None:
            dx = dx + dot(b, d_state.astype(BF16), NN) * tail_x
        dx_ref[rows, :] = dx.astype(BF16)
        if k > 0:
            own = dot(c, (d_ssd * fade_x).astype(BF16), TN)
            d_state = own if d_state is None else own + d_state * fade_x[SPAN - 1 :, :]


def pick_kernel(count, unit, place_ref, *refs):
    terms, outs = refs[:count], refs[count:]
    my = lax.rem(lax.div(place_ref[3], unit), len(outs))
    for mask, out_ref in enumerate(outs):
        at = lax.bitwise_xor(my, jnp.int32(mask))
        total = terms[0][:, at].astype(F32)
        for term in terms[1:]:
            total = total + term[:, at].astype(F32)
        out_ref[...] = total.astype(BF16)


def delta_kernel(count, lo, replicas, global_ref, before_ref, *refs):
    terms, (delta_ref, sent_ref, squares_ref) = refs[:count], refs[count:]
    rows, inner = delta_ref.shape
    total = terms[0][0].astype(F32)
    for term in terms[1:]:
        total = total + term[0].astype(F32)
    delta = global_ref[lo : lo + rows, :] - total / replicas
    delta_ref[...] = delta
    sent_ref[...] = delta.astype(BF16)
    squares = jnp.sum(delta * delta, axis=0, keepdims=True)
    squares = before_ref[...] + jnp.broadcast_to(jnp.sum(squares, axis=1, keepdims=True), before_ref.shape)
    squares_ref[...] = squares


def join_kernel(*refs):
    *parts, out_ref = refs
    lo = 0
    for part in parts:
        out_ref[lo : lo + part.shape[0]] = part[...]
        lo += part.shape[0]


def weight_kernel(sizes, entries, place_ref, global_ref, momentum_ref, *refs):
    count = len(sizes)
    pairs, deltas, squares = refs[: 2 * count + 2], refs[2 * count + 2 : 3 * count + 2], refs[3 * count + 2 : -3]
    new_ref, new_global_ref, new_momentum_ref = refs[-3:]
    mean = (squares[0][:1, :1] + squares[1][:1, :1]) / entries
    factor = jnp.minimum(1.0, clip_rms / jnp.sqrt(mean + 1e-06))
    at_chip = lax.bitwise_xor(pl.program_id(0), place_ref[3])
    owned = new_ref.shape[0] // 2
    scale = (outer_rate * (1.0 + outer_beta)) * factor

    def one_core(core, side):
        lo = 0
        for n, size in enumerate(sizes):
            kept = pairs[side][at_chip, lo : lo + size, :].astype(F32)
            delta = pairs[2 * n + 2 + side][at_chip, :size, :].astype(F32)
            new_ref[core * owned + lo : core * owned + lo + size, :] = (kept - scale * delta).astype(BF16)
            lo += size

    for own_core in range(2):

        @pl.when(place_ref[2] == own_core)
        def _():
            one_core(own_core, 0)
            one_core(1 - own_core, 1)

    part = new_global_ref.shape[0]
    lo = 0
    for n, size in enumerate(sizes):
        for row in range(0, size, min(size, part)):
            rows = min(size, part)
            at, here = slice(lo + row, lo + row + rows), (lo + row) % part

            @pl.when(pl.program_id(0) == (lo + row) // part)
            def _():
                clipped = factor * deltas[n][row : row + rows, :]
                new_momentum = outer_beta * momentum_ref[at, :] + clipped
                new_momentum_ref[here : here + rows, :] = new_momentum
                new_global = global_ref[at, :] - outer_rate * (clipped + outer_beta * new_momentum)
                new_global_ref[here : here + rows, :] = new_global

        lo += size


def inward(axis_size):
    half = axis_size // 2
    hops = [[(s, s + 1), (axis_size - 1 - s, axis_size - 2 - s)] for s in range(half - 1)]
    return hops, [(half - 1, half), (half, half - 1)]


def in_turn(kernel, inputs, waits, outs):
    def body(*refs):
        end = inputs + waits + outs
        refs[end][...] = jnp.zeros_like(refs[end])
        kernel(*refs[:inputs], *refs[inputs + waits : end], *refs[end + 1 :])

    return body


def stages(replicas, most=2):
    bit, left, found = 1, replicas // 2, []
    while left > 1:
        bits = most if left >= 1 << most else 1
        found.append((bit, bits))
        bit, left = bit + bits, left >> bits
    return found


def shards(
    x_in,
    gate_z,
    b_proj,
    c_proj,
    dt_raw,
    a_log,
    dt_bias,
    skip_d,
    norm_gain,
    out_weight,
    global_weight,
    momentum,
    target,
):
    tokens, inner = x_in.shape
    features = out_weight.shape[1]
    replicas = lax.axis_size("replica")
    heads_over = lax.axis_size("tensor")
    groups = b_proj.shape[1] // STATE
    heads = dt_raw.shape[1]
    width = inner // groups
    owned = features // replicas
    chunks = max(2, min(4, owned // 16))
    batches = [[n] for n in range(chunks // 2)] + [list(range(chunks // 2, chunks))]
    piece = owned // chunks
    span_rows = replicas * piece
    place = lax.axis_index("tensor")
    me = lax.axis_index("replica")
    in_middle = (place == heads_over // 2 - 1) | (place == heads_over // 2)
    places = jnp.stack([place, in_middle.astype(jnp.int32), lax.rem(me, 2), lax.div(me, 2)]).astype(jnp.int32)
    stored = out_weight[0].reshape(replicas, owned, inner)
    gain = norm_gain.reshape(1, inner)
    dt_rows = dt_raw.T

    smem = pl.BlockSpec(memory_space=pltpu.SMEM)
    vmem = pl.BlockSpec(memory_space=pltpu.VMEM)
    anywhere = pl.BlockSpec(memory_space=pl.ANY)
    inv_spec = pl.BlockSpec((1, tokens, 1), lambda g: (g, 0, 0))
    large = pltpu.CompilerParams(vmem_limit_bytes=20 * 1024 * 1024)
    small = pltpu.CompilerParams(vmem_limit_bytes=12 * 1024 * 1024)
    small_cost = pl.CostEstimate(flops=1, bytes_accessed=1, transcendentals=0)
    some_cost = pl.CostEstimate(flops=2_000_000_000, bytes_accessed=1, transcendentals=0)
    large_cost = pl.CostEstimate(flops=30_000_000_000, bytes_accessed=1, transcendentals=0)

    turn = []

    def run(kernel, inputs, in_specs, outs, out_specs, waits=(), **options):
        waits = [*turn[-1:], *waits]
        done = jax.ShapeDtypeStruct((8, LANES), F32)
        *results, ran = pl.pallas_call(
            in_turn(kernel, len(inputs), len(waits), len(outs)),
            in_specs=[*in_specs, *[vmem] * len(waits)],
            out_specs=[*out_specs, vmem],
            out_shape=[*outs, done],
            **options,
        )(*inputs, *waits)
        turn.append(ran)
        return results

    def step(kernel, operands, outs, scalars=(), waits=(), cost=small_cost):
        return run(
            kernel,
            [*scalars, *operands],
            [smem] * len(scalars) + [vmem] * len(operands),
            outs,
            [vmem] * len(outs),
            waits,
            cost_estimate=cost,
            compiler_params=small,
        )

    def shape(*dims, dtype=BF16):
        return jax.ShapeDtypeStruct(dims, dtype)

    def in_hbm(*arrays):
        return [pltpu.with_memory_space_constraint(a, pltpu.HBM) for a in arrays]

    def group_specs(begin):
        wide = pl.BlockSpec((tokens, width), lambda g: (0, g + begin))
        state = pl.BlockSpec((tokens, STATE), lambda g: (0, g + begin))
        dt = pl.BlockSpec((heads // groups, tokens), lambda g: (g + begin, 0))
        return wide, state, dt, pl.BlockSpec((1, width), lambda g: (0, g + begin))

    def exchange(value, mask):
        return lax.ppermute(value, "replica", [(r, r ^ mask) for r in range(replicas)])

    gathered = {}

    def landing(b, some):
        (bit, bits), *_ = some
        return [exchange(gathered[b], mask << bit) for mask in range(1, 1 << bits)]

    def widen(b, some, landed=None):
        for at, (bit, bits) in enumerate(some):
            parts = [gathered[b]] + (landed if at == 0 and landed else landing(b, some[at:]))
            out = shape(len(parts) * parts[0].shape[0], *parts[0].shape[1:])
            (gathered[b],) = step(join_kernel, parts, [out])

    def finish(b):
        gathered[b] = [gathered[b], exchange(gathered[b], 1)]

    by_two, by_one = stages(replicas), stages(replicas, 1)
    by_group, by_state, dt_spec, gain_spec = group_specs(0)
    shared = in_hbm(dt_rows, gate_z, b_proj, c_proj, gain, a_log, dt_bias, skip_d)
    later = [stored, target, global_weight, momentum]
    weight, goal, own_global, own_momentum, normed, inv = run(
        functools.partial(forward_kernel, len(later)),
        [shared[0], *in_hbm(x_in), *shared[1:], *in_hbm(*later)],
        [dt_spec, by_group, by_group, by_state, by_state, gain_spec, smem, smem, smem] + [anywhere] * len(later),
        [pltpu.VMEM(v.shape, v.dtype) for v in later] + [pltpu.VMEM((tokens, inner), BF16), pltpu.VMEM((groups, tokens, 1), F32)],
        [vmem] * (len(later) + 2),
        grid=(groups,),
        scratch_shapes=[pltpu.SemaphoreType.DMA((len(later),))],
        cost_estimate=small_cost,
        compiler_params=large,
    )

    part = shape(span_rows, tokens)

    def project(picked):
        kernel = functools.partial(project_kernel, picked)
        return step(kernel, [weight, normed, goal], [part] * len(picked), scalars=[places])

    in_hops, across = inward(heads_over)
    parts = project([0])
    (kept,) = step(kept_kernel, [own_global, own_momentum], [shape(owned, inner)])
    gathered["kept"] = kept[None]
    kept_landed = landing("kept", by_two)
    parts += project(list(range(1, chunks)))
    first_landed = [lax.ppermute(p, "tensor", in_hops[0]) if in_hops else None for p in parts]
    sums, cots = {}, {}

    def sum_side(n, waits=()):
        held = parts[n]
        for at, pairs in enumerate(in_hops):
            landed = first_landed[n] if at == 0 else lax.ppermute(held, "tensor", pairs)
            (held,) = step(add_kernel, [held, landed], [part], waits=waits)
        sums[n] = held

    def sum_all(n, waits=(), cost=small_cost):
        landed = lax.ppermute(sums[n], "tensor", across)
        (mid,) = step(add_kernel, [sums[n], landed], [part], waits=waits, cost=cost)
        out = mid
        for pairs in reversed(in_hops):
            back = lax.ppermute(out, "tensor", [(b, a) for a, b in pairs])
            out = back if pairs is in_hops[0] else jnp.where(in_middle, mid, back)
        cots[n] = (mid, out)

    held, deltas = {}, {}
    tile = shape(8, LANES, dtype=F32)
    squares = {-1: jnp.zeros((8, LANES), F32)}

    def new_rows(b, waits=()):
        batch = batches[b]
        rows = len(batch) * piece
        keep, send = step(
            functools.partial(gradient_kernel, batch),
            [c for n in batch for c in cots[n]] + [normed, weight],
            [shape(replicas // 2, rows, inner)] * 2,
            scalars=[places],
            waits=waits,
        )
        return [keep, exchange(send, 1)]

    def narrow(b, some, waits=()):
        rows = len(batches[b]) * piece
        for bit, bits in some:
            ways = 1 << bits
            left = held[b][0].shape[0] // ways
            picked = step(
                functools.partial(pick_kernel, len(held[b]), 1 << (bit - 1)),
                [h.reshape(left, ways, rows, inner) for h in held[b]],
                [shape(left, rows, inner)] * ways,
                scalars=[places],
                waits=waits,
            )
            held[b] = [picked[0]] + [exchange(picked[mask], mask << bit) for mask in range(1, ways)]

    def own_rows(b, cost=small_cost, waits=()):
        batch = batches[b]
        rows = len(batch) * piece
        deltas[b], sent, squares[b] = step(
            functools.partial(delta_kernel, len(held[b]), batch[0] * piece, replicas),
            [own_global, squares[b - 1], *held[b]],
            [shape(rows, inner, dtype=F32), shape(rows, inner), tile],
            cost=cost,
            waits=waits,
        )
        gathered[b] = sent[None]

    def backward(begin, count, so_far):
        wide, state, dt, gain_here = group_specs(begin)
        operands = [places, *shared, normed, inv, weight] + [c for n in range(chunks) for c in cots[n]]
        specs = [smem, dt, wide, state, state, gain_here, smem, smem, smem, vmem, vmem, vmem] + [vmem] * (2 * chunks)
        aliases = {}
        if so_far is not None:
            aliases = {len(operands): 0}
            operands.append(so_far)
            specs.append(anywhere)
        (grad,) = run(
            functools.partial(backward_kernel, begin),
            operands,
            specs,
            [shape(tokens, inner)],
            [wide],
            grid=(count,),
            scratch_shapes=[pltpu.VMEM((tokens, width), F32)],
            input_output_aliases=aliases,
            cost_estimate=small_cost,
            compiler_params=large,
        )
        return grad

    end = len(batches) - 1
    early = end > 1
    for t in range(chunks):
        if t == chunks - 1 and early:
            held[0] = new_rows(0)
        sum_side(t, [cots[t - 3][1]] if t >= 3 and not early else [])
        if t == 0:
            widen("kept", by_two, kept_landed)
            finish("kept")
        if t > 0:
            sum_all(t - 1)
    if early:
        narrow(0, by_one[:1])
    held[end - 1] = new_rows(end - 1)
    if early:
        narrow(0, by_one[1:])
    sum_all(chunks - 1, cost=large_cost)
    narrow(end - 1, by_one[:1])
    step(gate_kernel, [], [tile], waits=[cots[chunks - 2][1], gathered["kept"][1]])
    landed = {}
    if early:
        own_rows(0)
        landed[0] = landing(0, by_two)
    narrow(end - 1, by_one[1:])
    own_rows(end - 1, small_cost)
    landed[end - 1] = landing(end - 1, by_two)
    if early:
        widen(0, by_two, landed[0])
        finish(0)
    held[end] = new_rows(end)
    narrow(end, by_two)
    grad_input = backward(0, groups, None)
    own_rows(end, large_cost, [gathered[0][1]] if early else [])
    last_landed = landing(end, by_two)
    widen(end - 1, by_two, landed[end - 1])
    finish(end - 1)
    total = squares[end]
    for bit in range(heads_over.bit_length() - 1):
        pairs = [(t, t ^ (1 << bit)) for t in range(heads_over)]
        waits = [gathered[b][1] for b in range(end)]
        (total,) = step(add_squares_kernel, [total, lax.ppermute(total, "tensor", pairs)], [tile], waits=waits)
    for bit, bits in by_one:
        landed = [exchange(total, mask << bit) for mask in range(1, 1 << bits)]
        (total,) = step(add_squares_kernel, [total, *landed], [tile])
    widen(end, by_two, last_landed)
    finish(end)
    columns = [total, exchange(total, 1)]

    sizes = [len(batch) * piece for batch in batches]
    pair_spec = pl.BlockSpec((2 * owned, inner), lambda r: (r, 0))
    share = owned // (replicas // 2)
    if share % 8 == 0:
        held_spec = pl.BlockSpec((share, inner), lambda r: (r, 0))
    else:
        held_spec = pl.BlockSpec((owned, inner), lambda r: (0, 0))
    inputs = [own_global, own_momentum, *gathered["kept"], *[v for b in range(end + 1) for v in gathered[b]]]
    inputs += [*[deltas[b] for b in range(end + 1)], *columns]
    new_weight, new_global, new_momentum = run(
        functools.partial(weight_kernel, sizes, features * inner * heads_over),
        [places, *inputs],
        [smem] + [vmem] * len(inputs),
        [shape(features, inner), shape(owned, inner, dtype=F32), shape(owned, inner, dtype=F32)],
        [pair_spec, held_spec, held_spec],
        grid=(replicas // 2,),
        cost_estimate=small_cost,
        compiler_params=small,
    )
    return (grad_input, new_weight, new_global, new_momentum)


def solution(mesh):
    placed = (
        P("replica", "tensor"),
        P("replica", "tensor"),
        P("replica", "tensor"),
        P("replica", "tensor"),
        P("replica", "tensor"),
        P("tensor"),
        P("tensor"),
        P("tensor"),
        P("tensor"),
        P("replica", None, "tensor"),
        P("replica", "tensor"),
        P("replica", "tensor"),
        P(("replica", "tensor"), None),
    )
    return jax.shard_map(
        shards,
        mesh=mesh,
        in_specs=placed,
        out_specs=(
            P("replica", "tensor"),
            P(None, "tensor"),
            P("replica", "tensor"),
            P("replica", "tensor"),
        ),
        check_vma=False,
    )
```
